32 devices in a mesh: groups: 2 (over y), blk: 4 (over z), tile: 2 (over x), pair: 2 (over core).
Axes of the slice: x: 2, y: 2, z: 4, core: 2. Of those that a mesh axis runs over, the one named last changes fastest.
Arguments:
- left_tokens: bfloat16 [4, 1536, 768], P(('groups', 'pair'), 'blk', 'tile'), parts along dimension 0, may hold values from -32 to 32
- right_tokens: bfloat16 [4, 1536, 768], P(('groups', 'pair'), 'blk', 'tile'), parts along dimension 0, may hold values from -32 to 32
- self_qkv: bfloat16 [3, 768, 512], P(None, None, 'tile'), may hold values from -1 to 1
- self_out: bfloat16 [512, 768], P('tile'), may hold values from -0.25 to 0.25
- cross_qkv: bfloat16 [3, 768, 512], P(None, None, 'tile'), may hold values from -1 to 1
- cross_out: bfloat16 [512, 768], P('tile'), may hold values from -0.25 to 0.25
- reassemble: bfloat16 [768, 256], P('tile'), may hold values from -0.21875 to 0.21875
- conv_weight: bfloat16 [3, 3, 256, 256], replicated, may hold values from -0.125 to 0.125
Outputs:
- joined: bfloat16 [4, 12, 128, 256], P(('groups', 'pair'), 'blk', 'tile'), parts along dimension 0
The draws below stay inside these ranges and needn't reach their ends.
There are 2 independent parts, one for each index of `groups`. The reference program is written for one: setup_inputs(seed, part) draws one part's arguments, and reference() takes and returns one part's arrays. A program takes and returns all parts, laid end to end along the dimension named above; an argument that names none is the same for every part. Nothing has to cross between parts.
All inputs are finite; a program needn't handle non-finite values.
Results may differ from the reference program's by a relative error of at most 0.018.
Values may be sent and summed in bfloat16 or wider, within the bound.
No kernel may reach another device: no remote copies, remote signals or barrier semaphores. Data moves between devices by JAX's collectives and lax.ppermute only.
A program may use at most 64 MiB of HBM per device.

```python
import math
import jax
import jax.numpy as jnp
from jax import lax

D = 768
HEADS = 8
HD = 64
CH = 256
GRID_W = 128
PAIRS = 2
GRID_H = 12
LEN = 1536


def token_field(key):
    keys = jax.random.split(key, 3)
    noise = jax.random.truncated_normal(keys[0], -4.0, 4.0, (PAIRS, LEN, D), jnp.float32)
    row_scale = jnp.exp(jax.random.uniform(keys[1], (PAIRS, LEN, 1), jnp.float32, math.log(0.3), math.log(3.0)))
    column_scale = jnp.exp(jax.random.uniform(keys[2], (D,), jnp.float32, math.log(0.2), math.log(2.0)))
    field = noise * column_scale
    return (field * row_scale).astype(jnp.bfloat16)


def projection_weights(key):
    keys = jax.random.split(key, 1)
    columns = HEADS * HD
    scales = jnp.array([1.67, 1.67, 1.0], jnp.float32)[:, None, None] / math.sqrt(D)
    weights = jax.random.truncated_normal(keys[0], -4.0, 4.0, (3, D, columns), jnp.float32) * scales
    return weights.astype(jnp.bfloat16)


def draw_left_tokens(key, part):
    return token_field(jax.random.fold_in(key, 3))


def draw_right_tokens(key, part):
    return token_field(jax.random.fold_in(key, 11))


def draw_self_qkv(key, part):
    return projection_weights(jax.random.fold_in(key, 19))


def draw_cross_qkv(key, part):
    return projection_weights(jax.random.fold_in(key, 29))


def steps_of(rng, shape, pieces, least, largest):
    factor_of = 1.0
    for position, shards_of in pieces:
        draws = jax.random.uniform(jax.random.fold_in(jax.random.fold_in(rng, 6), position), (shards_of,), jnp.float32, least / len(pieces), largest / len(pieces))
        factor_of = factor_of * jnp.repeat(jnp.exp(draws), shape[position] // shards_of).reshape((-1,) + (1,) * (len(shape) - 1 - position))
    return factor_of


def gaussian(key, dims, width, reach, shards=(), held_as=jnp.bfloat16):
    entries = jax.random.normal(key, dims, jnp.float32) * width
    if len(shards) > 0:
        entries = steps_of(key, dims, shards, -0.22, 0.18) * entries
    return jnp.clip(entries, min=-reach, max=reach).astype(held_as)


def setup_inputs(seed: int = 0, part: int = 0) -> dict:
    key_of = jax.random.split(jax.random.key(seed), 9)
    part_keys = jax.random.split(jax.random.fold_in(key_of[8], part), 9)
    return {
        "left_tokens": draw_left_tokens(jax.random.fold_in(jax.random.fold_in(key_of[8], part), 71), part),
        "right_tokens": draw_right_tokens(jax.random.fold_in(jax.random.fold_in(key_of[8], part), 71), part),
        "self_qkv": draw_self_qkv(jax.random.fold_in(key_of[8], 71), part),
        "self_out": gaussian(key_of[3], (HEADS * HD, D), (HEADS * HD) ** -0.5, 0.25, ((0, 2),)),
        "cross_qkv": draw_cross_qkv(jax.random.fold_in(key_of[8], 71), part),
        "cross_out": gaussian(key_of[5], (HEADS * HD, D), (HEADS * HD) ** -0.5, 0.25, ((0, 2),)),
        "reassemble": gaussian(key_of[6], (D, CH), D ** -0.5, 0.21875, ((0, 2),)),
        "conv_weight": gaussian(key_of[7], (3, 3, CH, CH), (9 * CH) ** -0.5, 0.125),
    }


def layer_norm(values):
    widened = values.astype(jnp.float32)
    centred = widened - lax.optimization_barrier(jnp.mean(widened, axis=-1, keepdims=True))
    variance = lax.optimization_barrier(jnp.mean(centred * centred, axis=-1, keepdims=True))
    return (centred * lax.rsqrt(variance + 1e-06)).astype(jnp.bfloat16)

def project_rows(normed, weight):
    return jnp.dot(normed, weight, preferred_element_type=jnp.float32).astype(jnp.bfloat16)

def attention(queries, keys_rows, values_rows):
    block_rows = math.gcd(LEN, 512)
    query_blocks = queries.reshape(LEN // block_rows, block_rows, HEADS, HD)
    keys_wide = keys_rows.reshape(LEN, HEADS, HD).astype(jnp.float32)
    values_wide = values_rows.reshape(LEN, HEADS, HD).astype(jnp.float32)

    def one_block(query_block):
        scores = jnp.einsum('qhd,khd->hqk', query_block.astype(jnp.float32), keys_wide) * HD ** (-0.5)
        maxima = lax.optimization_barrier(jnp.max(scores, axis=2, keepdims=True))
        expanded = jnp.exp(scores - maxima)
        totals = lax.optimization_barrier(jnp.sum(expanded, axis=2))
        rounded = lax.optimization_barrier(expanded.astype(jnp.bfloat16)).astype(jnp.float32)
        mixed = jnp.einsum('hqk,khd->qhd', rounded, values_wide)
        return (mixed / totals.T[:, :, None]).reshape(block_rows, HEADS * HD).astype(jnp.bfloat16)
    return lax.map(one_block, query_blocks).reshape(LEN, HEADS * HD)

def one_pair(left_rows, right_rows, self_qkv, self_out, cross_qkv, cross_out, reassemble, conv_weight):
    left_normed = layer_norm(left_rows)
    right_normed = layer_norm(right_rows)
    self_mixed = attention(project_rows(left_normed, self_qkv[0]), project_rows(left_normed, self_qkv[1]), project_rows(left_normed, self_qkv[2]))
    updated = (left_rows.astype(jnp.float32) + jnp.dot(self_mixed, self_out, preferred_element_type=jnp.float32)).astype(jnp.bfloat16)
    updated_normed = layer_norm(updated)
    cross_mixed = attention(project_rows(updated_normed, cross_qkv[0]), project_rows(right_normed, cross_qkv[1]), project_rows(right_normed, cross_qkv[2]))
    final_tokens = (updated.astype(jnp.float32) + jnp.dot(cross_mixed, cross_out, preferred_element_type=jnp.float32)).astype(jnp.bfloat16)
    feature_map = jnp.dot(final_tokens, reassemble, preferred_element_type=jnp.float32).astype(jnp.bfloat16).reshape(GRID_H, GRID_W, CH)
    activated = jnp.maximum(feature_map, jnp.zeros((), jnp.bfloat16))
    padded = jnp.pad(activated, ((1, 1), (1, 1), (0, 0)))
    stacked = jnp.concatenate([padded[row_shift:row_shift + GRID_H, col_shift:col_shift + GRID_W] for row_shift in range(3) for col_shift in range(3)], axis=-1)
    convolved = jnp.dot(stacked.reshape(GRID_H * GRID_W, 9 * CH), conv_weight.reshape(9 * CH, CH), preferred_element_type=jnp.float32)
    return (feature_map.astype(jnp.float32) + convolved.reshape(GRID_H, GRID_W, CH)).astype(jnp.bfloat16)

def reference(left_tokens, right_tokens, self_qkv, self_out, cross_qkv, cross_out, reassemble, conv_weight):
    results = [one_pair(left_tokens[index], right_tokens[index], self_qkv, self_out, cross_qkv, cross_out, reassemble, conv_weight) for index in range(PAIRS)]
    return jnp.stack(results, axis=0)
```

```python
import functools
import math

import jax
import jax.numpy as jnp
from jax import lax
from jax.experimental import pallas as pl
from jax.experimental.pallas import tpu as pltpu
from jax.sharding import PartitionSpec as P

HD = 64
GRID_W = 128
EDGE = 16
F32 = jnp.float32
BF16 = jnp.bfloat16
QUERY_SCALE = math.log2(math.e) * HD**-0.5
VMEM = pl.BlockSpec(memory_space=pltpu.VMEM)
SMEM = pl.BlockSpec(memory_space=pltpu.SMEM)


def run_kernel(kernel, name, shapes, operands, flops, place=None):
    leading = () if place is None else (place,)
    moved = sum(v.size * 2 for v in operands) + sum(2 * math.prod(s) for s in shapes)
    return pl.pallas_call(
        kernel,
        out_shape=[jax.ShapeDtypeStruct(s, BF16) for s in shapes],
        in_specs=[SMEM] * len(leading) + [VMEM] * len(operands),
        out_specs=[VMEM] * len(shapes),
        compiler_params=pltpu.CompilerParams(vmem_limit_bytes=48 << 20),
        cost_estimate=pl.CostEstimate(flops=flops, bytes_accessed=moved, transcendentals=0),
        name=name,
    )(*leading, *operands)


def normalized(pieces):
    widened = [piece.astype(F32) for piece in pieces]
    width = sum(piece.shape[1] for piece in widened)
    mean = sum(jnp.sum(piece, axis=1, keepdims=True) for piece in widened) / width
    centred = [piece - mean for piece in widened]
    variance = sum(jnp.sum(piece * piece, axis=1, keepdims=True) for piece in centred) / width
    scale = lax.rsqrt(variance + 1e-06)
    return [(piece * scale).astype(BF16) for piece in centred]


def dot(left, right):
    return jnp.dot(left, right, preferred_element_type=F32)


def project_kernel(place, *refs, count, scaled):
    pieces, weight, outs = refs[:count], refs[count], refs[count + 1 :]
    normed = normalized([piece[...] for piece in pieces])
    products = []
    for which in range(weight.shape[0]):
        products.append(
            sum(
                dot(normed[step], weight[which, lax.rem(place[0] + step, count)])
                for step in range(count)
            )
        )
    if scaled:
        outs[0][...] = (products.pop(0) * QUERY_SCALE).astype(BF16)
    columns = weight.shape[3]
    for which, product in enumerate(products):
        outs[-1][:, which * columns : (which + 1) * columns] = product.astype(BF16)


def attend_kernel(query, *refs):
    packs, out = refs[:-1], refs[-1]
    columns = query.shape[1]
    heads = []
    for start in range(0, columns, HD):
        head = slice(start, start + HD)
        values = slice(columns + start, columns + start + HD)
        asked = query[:, head]
        scores = [
            lax.dot_general(
                asked, pack[:, head], (((1,), (1,)), ((), ())), preferred_element_type=F32
            )
            for pack in packs
        ]
        maxima = functools.reduce(
            jnp.maximum, [jnp.max(score, axis=1, keepdims=True) for score in scores]
        )
        total, mixed = 0.0, 0.0
        for score, pack in zip(scores, packs):
            expanded = jnp.exp2(score - maxima)
            total = total + jnp.sum(expanded, axis=1, keepdims=True)
            mixed = mixed + dot(expanded.astype(BF16), pack[:, values])
        heads.append(mixed / total)
    out[...] = jnp.concatenate(heads, axis=1).astype(BF16)


def update_kernel(place, *refs, count):
    mixed, weights = refs[:count], refs[count : 2 * count]
    tokens, query_weight = refs[2 * count : 3 * count], refs[3 * count]
    updated, query = refs[3 * count + 1 :]
    pieces = []
    for step in range(count):
        slot = lax.rem(place[0] + step, count)
        term = sum(dot(mixed[t][...], weights[t][slot]) for t in range(count))
        piece = (tokens[step][...].astype(F32) + term).astype(BF16)
        updated[step] = piece
        pieces.append(piece)
    normed = normalized(pieces)
    product = sum(
        dot(normed[step], query_weight[lax.rem(place[0] + step, count)]) for step in range(count)
    )
    query[...] = (product * QUERY_SCALE).astype(BF16)


def finish_kernel(place, *refs, count, width):
    mixed, weights = refs[:count], refs[count : 2 * count]
    updated, reassemble = refs[2 * count], refs[2 * count + 1 : 3 * count + 1]
    window, board = refs[3 * count + 1], refs[3 * count + 2]
    features = 0.0
    for step in range(count):
        slot = lax.rem(place[0] + step, count)
        term = sum(dot(mixed[t][...], weights[t][slot]) for t in range(count))
        final = (updated[step].astype(F32) + term).astype(BF16)
        features = features + dot(final, reassemble[step][...])
    features = features.astype(BF16)
    band_rows = board.shape[0]
    edge = jnp.zeros((band_rows, EDGE, board.shape[2]), BF16)
    board[:, :EDGE, :] = edge
    board[:, EDGE + GRID_W :, :] = edge
    board[:, EDGE : EDGE + GRID_W, :] = features.reshape(band_rows, GRID_W, board.shape[2])
    start = pl.multiple_of(place[0] * width, EDGE)
    window[...] = board[:, pl.ds(start, width + 2 * EDGE), :]


def conv_kernel(window, above, below, weight, out):
    width = out.shape[1]
    band_rows, channels = out.shape[0], out.shape[2]
    grid = jnp.concatenate([above[...], window[...], below[...]], axis=0).astype(F32)
    active = jnp.maximum(grid, 0.0)
    total = grid[1 : 1 + band_rows, EDGE : EDGE + width, :].reshape(band_rows * width, channels)
    for column in range(3):
        first = EDGE - 1 + column
        shifted = active[:, first : first + width, :].astype(BF16)
        for row in range(3):
            rows = shifted[row : row + band_rows].reshape(band_rows * width, channels)
            total = total + dot(rows, weight[row, column])
    out[...] = total.reshape(out.shape).astype(BF16)


def body(
    left_tokens, right_tokens, self_qkv, self_out, cross_qkv, cross_out, reassemble, conv_weight
):
    bands, tiles, cores = (lax.axis_size(axis) for axis in ("blk", "tile", "pair"))
    half = bands // cores
    both = ("blk", "pair")
    place = lax.axis_index("tile").astype(jnp.int32).reshape(1)
    rows, share = left_tokens.shape[1:]
    columns = self_qkv.shape[2]
    channels = reassemble.shape[1]
    width = GRID_W // tiles
    band_rows = rows // GRID_W

    def home(band, pair):
        return band * cores + pair

    def worker(band, pair):
        shift = (pair - band // half) % cores
        return ((band + shift * half) % bands) * cores + (pair - shift) % cores

    places = [(band, pair) for band in range(bands) for pair in range(cores)]

    def tile_pieces(own):
        others = [
            lax.ppermute(own, "tile", [((i + s) % tiles, i) for i in range(tiles)])
            for s in range(1, tiles)
        ]
        return [own, *others]

    def gathered(pack):
        near = [pack] + [
            lax.ppermute(
                pack,
                "blk",
                [(g * half + (i + s) % half, g * half + i) for g in range(cores) for i in range(half)],
            )
            for s in range(1, half)
        ]
        packs = list(near)
        for s in range(1, cores):
            packs += [
                lax.ppermute(p, "pair", [((i + s) % cores, i) for i in range(cores)]) for p in near
            ]
        if len(packs) > 4:
            size = -(-len(packs) // 4)
            packs = [jnp.concatenate(packs[i : i + size]) for i in range(0, len(packs), size)]
        return packs

    def moved(tokens):
        return lax.ppermute(tokens[0], both, [(home(*p), worker(*p)) for p in places])

    def project(pieces, weights, scaled):
        shapes = [(rows, columns)] * scaled + [(rows, 2 * columns)]
        stacked = weights.reshape(weights.shape[0], tiles, share, columns)
        return run_kernel(
            functools.partial(project_kernel, count=tiles, scaled=scaled),
            "project",
            shapes,
            [*pieces, stacked],
            2 * rows * share * tiles * columns * weights.shape[0],
            place,
        )

    def attend(query, packs):
        keys = sum(p.shape[0] for p in packs)
        return run_kernel(
            attend_kernel, "attend", [(rows, columns)], [query, *packs], 16 * rows * keys * columns
        )[0]

    def feature_blocks(weight):
        return weight.reshape(columns, tiles, share).transpose(1, 0, 2)

    left = tile_pieces(moved(left_tokens))
    self_out_pieces = tile_pieces(feature_blocks(self_out))
    cross_out_pieces = tile_pieces(feature_blocks(cross_out))
    reassemble_pieces = tile_pieces(reassemble)
    query, pack = project(left, self_qkv, True)
    self_packs = gathered(pack)
    right = tile_pieces(moved(right_tokens))
    (pack,) = project(right, cross_qkv[1:], False)
    cross_packs = gathered(pack)

    mixed = tile_pieces(attend(query, self_packs))
    updated, cross_query = run_kernel(
        functools.partial(update_kernel, count=tiles),
        "update",
        [(tiles, rows, share), (rows, columns)],
        [*mixed, *self_out_pieces, *left, cross_qkv[0].reshape(tiles, share, columns)],
        4 * rows * share * tiles * columns * tiles,
        place,
    )
    mixed = tile_pieces(attend(cross_query, cross_packs))
    board = (band_rows, GRID_W + 2 * EDGE, channels)
    operands = [*mixed, *cross_out_pieces, updated, *reassemble_pieces]
    window = pl.pallas_call(
        functools.partial(finish_kernel, count=tiles, width=width),
        out_shape=jax.ShapeDtypeStruct((band_rows, width + 2 * EDGE, channels), BF16),
        in_specs=[SMEM] + [VMEM] * len(operands),
        out_specs=VMEM,
        scratch_shapes=[pltpu.VMEM(board, BF16)],
        compiler_params=pltpu.CompilerParams(vmem_limit_bytes=48 << 20),
        name="finish",
    )(place, *operands)
    back = lax.ppermute(window, both, [(worker(*p), home(*p)) for p in places])
    above = lax.ppermute(
        window[-1:], both, [(worker(b, p), home(b + 1, p)) for b, p in places if b + 1 < bands]
    )
    below = lax.ppermute(
        window[:1], both, [(worker(b, p), home(b - 1, p)) for b, p in places if b > 0]
    )
    (joined,) = run_kernel(
        conv_kernel,
        "join",
        [(band_rows, width, channels)],
        [back, above, below, conv_weight],
        18 * band_rows * width * channels * channels,
    )
    return joined[None]


def solution(mesh):
    placed = (
        P(("groups", "pair"), "blk", "tile"),
        P(("groups", "pair"), "blk", "tile"),
        P(None, None, "tile"),
        P("tile", None),
        P(None, None, "tile"),
        P("tile", None),
        P("tile", None),
        P(),
    )
    return jax.shard_map(
        body,
        mesh=mesh,
        in_specs=placed,
        out_specs=P(("groups", "pair"), "blk", "tile", None),
        check_vma=False,
    )
```

```python
import functools
import math

import jax
import jax.numpy as jnp
from jax import lax
from jax.experimental import pallas as pl
from jax.experimental.pallas import tpu as pltpu
from jax.sharding import PartitionSpec as P

HD = 64
GRID_W = 128
EDGE = 16
F32 = jnp.float32
BF16 = jnp.bfloat16
QUERY_SCALE = math.log2(math.e) * HD**-0.5
VMEM = pl.BlockSpec(memory_space=pltpu.VMEM)
SMEM = pl.BlockSpec(memory_space=pltpu.SMEM)


def run_kernel(kernel, name, shapes, operands, flops=0, place=None, scratch=()):
    leading = () if place is None else (place,)
    return pl.pallas_call(
        kernel,
        out_shape=[jax.ShapeDtypeStruct(*s) for s in shapes],
        in_specs=[SMEM] * len(leading) + [VMEM] * len(operands),
        out_specs=[VMEM] * len(shapes),
        scratch_shapes=scratch,
        compiler_params=pltpu.CompilerParams(vmem_limit_bytes=24 << 20),
        cost_estimate=pl.CostEstimate(flops=flops, bytes_accessed=0, transcendentals=0),
        name=name,
    )(*leading, *operands)


def normalized(pieces):
    widened = [piece.astype(F32) for piece in pieces]
    width = sum(piece.shape[1] for piece in widened)
    mean = sum(jnp.sum(piece, axis=1, keepdims=True) for piece in widened) / width
    centred = [piece - mean for piece in widened]
    variance = sum(jnp.sum(piece * piece, axis=1, keepdims=True) for piece in centred) / width
    scale = lax.rsqrt(variance + 1e-06)
    return [(piece * scale).astype(BF16) for piece in centred]


def dot(left, right):
    return jnp.dot(left, right, preferred_element_type=F32)


def project_kernel(place, *refs, count, scaled):
    pieces, weight, outs = refs[:count], refs[count], refs[count + 1 :]
    normed = normalized([piece[...] for piece in pieces])
    products = []
    for which in range(weight.shape[0]):
        products.append(
            sum(
                dot(normed[step], weight[which, lax.rem(place[0] + step, count)])
                for step in range(count)
            )
        )
    if scaled:
        outs[0][...] = (products.pop(0) * QUERY_SCALE).astype(BF16)
    columns = weight.shape[3]
    for which, product in enumerate(products):
        outs[-1][:, which * columns : (which + 1) * columns] = product.astype(BF16)


def attend_kernel(query, *refs, packed, resumed, final):
    packs = refs[:packed]
    before = refs[packed : packed + 2] if resumed else ()
    outs = refs[packed + len(before) :]
    columns = query.shape[1]
    heads = []
    for index, start in enumerate(range(0, columns, HD)):
        head = slice(start, start + HD)
        values = slice(columns + start, columns + start + HD)
        asked = query[:, head]
        scores = [
            lax.dot_general(
                asked, pack[:, head], (((1,), (1,)), ((), ())), preferred_element_type=F32
            )
            for pack in packs
        ]
        tops = [jnp.max(score, axis=1, keepdims=True) for score in scores]
        total, mixed = 0.0, 0.0
        if resumed:
            stats = before[1][index]
            tops.append(stats[:, :1])
        maxima = functools.reduce(jnp.maximum, tops)
        if resumed:
            correction = jnp.exp2(stats[:, :1] - maxima)
            total = stats[:, 1:2] * correction
            mixed = before[0][index] * correction
        for score, pack in zip(scores, packs):
            expanded = jnp.exp2(score - maxima)
            total = total + jnp.sum(expanded, axis=1, keepdims=True)
            mixed = mixed + dot(expanded.astype(BF16), pack[:, values])
        if final:
            heads.append(mixed / total)
        else:
            outs[0][index] = mixed
            outs[1][index] = jnp.concatenate([maxima, total], axis=1)
    if final:
        outs[0][...] = jnp.concatenate(heads, axis=1).astype(BF16)


def pick(options, slot):
    chosen = options[0]
    for index in range(1, len(options)):
        chosen = jnp.where(slot == index, options[index], chosen)
    return chosen


def shares(mixed, weights, place):
    count = len(mixed)
    whole = sum(dot(m[...], w[...]) for m, w in zip(mixed, weights))
    share = whole.shape[1] // count
    options = [whole[:, i * share : (i + 1) * share] for i in range(count)]
    return [pick(options, lax.rem(place[0] + step, count)) for step in range(count)]


def update_kernel(place, *refs, count):
    mixed, weights = refs[:count], refs[count : 2 * count]
    tokens, query_weight = refs[2 * count : 3 * count], refs[3 * count]
    updated, query = refs[3 * count + 1 :]
    pieces = []
    for step, term in enumerate(shares(mixed, weights, place)):
        piece = (tokens[step][...].astype(F32) + term).astype(BF16)
        updated[step] = piece
        pieces.append(piece)
    normed = normalized(pieces)
    product = sum(
        dot(normed[step], query_weight[lax.rem(place[0] + step, count)]) for step in range(count)
    )
    query[...] = (product * QUERY_SCALE).astype(BF16)


def finish_kernel(place, *refs, count, width):
    mixed, weights = refs[:count], refs[count : 2 * count]
    updated, reassemble = refs[2 * count], refs[2 * count + 1 : 3 * count + 1]
    window, board = refs[3 * count + 1], refs[3 * count + 2]
    features = 0.0
    for step, term in enumerate(shares(mixed, weights, place)):
        final = (updated[step].astype(F32) + term).astype(BF16)
        features = features + dot(final, reassemble[step][...])
    features = features.astype(BF16)
    band_rows = board.shape[0]
    edge = jnp.zeros((band_rows, EDGE, board.shape[2]), BF16)
    board[:, :EDGE, :] = edge
    board[:, EDGE + GRID_W :, :] = edge
    board[:, EDGE : EDGE + GRID_W, :] = features.reshape(band_rows, GRID_W, board.shape[2])
    start = pl.multiple_of(place[0] * width, EDGE)
    window[...] = board[:, pl.ds(start, width + 2 * EDGE), :]


def conv_kernel(window, above, below, weight, out):
    width = out.shape[1]
    band_rows, channels = out.shape[0], out.shape[2]
    grid = jnp.concatenate([above[...], window[...], below[...]], axis=0).astype(F32)
    active = jnp.maximum(grid, 0.0)
    total = grid[1 : 1 + band_rows, EDGE : EDGE + width, :].reshape(band_rows * width, channels)
    for column in range(3):
        first = EDGE - 1 + column
        shifted = active[:, first : first + width, :].astype(BF16)
        for row in range(3):
            rows = shifted[row : row + band_rows].reshape(band_rows * width, channels)
            total = total + dot(rows, weight[row, column])
    out[...] = total.reshape(out.shape).astype(BF16)


def body(
    left_tokens, right_tokens, self_qkv, self_out, cross_qkv, cross_out, reassemble, conv_weight
):
    bands, tiles, cores = (lax.axis_size(axis) for axis in ("blk", "tile", "pair"))
    half = bands // cores
    both = ("blk", "pair")
    place = lax.axis_index("tile").astype(jnp.int32).reshape(1)
    rows, share = left_tokens.shape[1:]
    columns = self_qkv.shape[2]
    channels = reassemble.shape[1]
    width = GRID_W // tiles
    band_rows = rows // GRID_W

    def home(band, pair):
        return band * cores + pair

    def worker(band, pair):
        shift = (pair - band // half) % cores
        return ((band + shift * half) % bands) * cores + (pair - shift) % cores

    places = [(band, pair) for band in range(bands) for pair in range(cores)]

    def tied(values, *others):
        return lax.optimization_barrier((values, others))[0]

    def tile_pieces(own):
        others = [
            lax.ppermute(own, "tile", [((i + s) % tiles, i) for i in range(tiles)])
            for s in range(1, tiles)
        ]
        return [own, *others]

    def neighbours(pack):
        ring = [(g * half, i) for g in range(cores) for i in range(half)]
        return [
            lax.ppermute(pack, "blk", [(g + (i + s) % half, g + i) for g, i in ring])
            for s in range(1, half)
        ]

    def across(pack):
        return [
            lax.ppermute(pack, "pair", [((i + s) % cores, i) for i in range(cores)])
            for s in range(1, cores)
        ]

    def joined_packs(packs):
        return [packs[0] if len(packs) == 1 else jnp.concatenate(packs)]

    def moved(tokens):
        return lax.ppermute(tokens, both, [(home(*p), worker(*p)) for p in places])

    def project(pieces, weights, scaled):
        shapes = [((rows, columns), BF16)] * scaled + [((rows, 2 * columns), BF16)]
        stacked = weights.reshape(weights.shape[0], tiles, share, columns)
        return run_kernel(
            functools.partial(project_kernel, count=tiles, scaled=scaled),
            "project",
            shapes,
            [*pieces, stacked],
            0,
            place,
        )

    def attend(query, packs, state=(), final=False):
        heads = columns // HD
        shapes = [((heads, rows, HD), F32), ((heads, rows, 2), F32)]
        if final:
            shapes = [((rows, columns), BF16)]
        return run_kernel(
            functools.partial(
                attend_kernel, packed=len(packs), resumed=len(state) > 0, final=final
            ),
            "attend",
            shapes,
            [query, *packs, *state],
        )

    left_here = moved(left_tokens[0])
    right = tile_pieces(right_tokens[0])
    (right_pack,) = project(right, cross_qkv[1:], False)
    left_here, right_pack = lax.optimization_barrier((left_here, right_pack))
    right_pack = moved(right_pack)
    left = tile_pieces(left_here)
    query, pack = project(left, self_qkv, True)
    self_out_pieces = tile_pieces(tied(self_out, left))
    beside = neighbours(pack)
    state = attend(query, [pack, *across(pack)])
    beside = tied(beside, state)
    far = [*beside, *[p for b in beside for p in across(b)]]
    far, self_out_pieces = lax.optimization_barrier((far, self_out_pieces))
    (own_mixed,) = attend(query, far if len(far) < 3 else joined_packs(far), state, True)

    mixed = tile_pieces(own_mixed)
    right_pack = tied(right_pack, own_mixed)
    right_beside = neighbours(right_pack)
    near = [right_pack, *across(right_pack)]
    far = [*right_beside, *[p for b in right_beside for p in across(b)]]
    reassemble_pieces = tile_pieces(tied(reassemble, mixed))
    cross_out_pieces = tile_pieces(tied(cross_out, mixed))
    updated, cross_query = run_kernel(
        functools.partial(update_kernel, count=tiles),
        "update",
        [((tiles, rows, share), BF16), ((rows, columns), BF16)],
        [*mixed, *self_out_pieces, *left, cross_qkv[0].reshape(tiles, share, columns)],
        0,
        place,
    )
    state = attend(cross_query, near)
    far = tied(far, state)
    (mixed,) = attend(cross_query, far if len(far) < 3 else joined_packs(far), state, True)
    mixed = tile_pieces(mixed)
    (window,) = run_kernel(
        functools.partial(finish_kernel, count=tiles, width=width),
        "finish",
        [((band_rows, width + 2 * EDGE, channels), BF16)],
        [*mixed, *cross_out_pieces, updated, *reassemble_pieces],
        0,
        place,
        [pltpu.VMEM((band_rows, GRID_W + 2 * EDGE, channels), BF16)],
    )
    back = lax.ppermute(window, both, [(worker(*p), home(*p)) for p in places])
    above = lax.ppermute(
        window[-1:], both, [(worker(b, p), home(b + 1, p)) for b, p in places if b + 1 < bands]
    )
    below = lax.ppermute(
        window[:1], both, [(worker(b, p), home(b - 1, p)) for b, p in places if b > 0]
    )
    (joined,) = run_kernel(
        conv_kernel,
        "join",
        [((band_rows, width, channels), BF16)],
        [back, above, below, conv_weight],
    )
    return joined[None]


def solution(mesh):
    placed = (
        P(("groups", "pair"), "blk", "tile"),
        P(("groups", "pair"), "blk", "tile"),
        P(None, None, "tile"),
        P("tile", None),
        P(None, None, "tile"),
        P("tile", None),
        P("tile", None),
        P(),
    )
    return jax.shard_map(
        body,
        mesh=mesh,
        in_specs=placed,
        out_specs=P(("groups", "pair"), "blk", "tile", None),
        check_vma=False,
    )
```

```python
import functools
import math

import jax
import jax.numpy as jnp
from jax import lax
from jax.experimental import pallas as pl
from jax.experimental.pallas import tpu as pltpu
from jax.sharding import PartitionSpec as P

HD = 64
GRID_W = 128
EDGE = 16
F32 = jnp.float32
BF16 = jnp.bfloat16
QUERY_SCALE = math.log2(math.e) * HD**-0.5
VMEM = pl.BlockSpec(memory_space=pltpu.VMEM)
SMEM = pl.BlockSpec(memory_space=pltpu.SMEM)


def run_kernel(kernel, name, shapes, operands, flops=0, place=None, scratch=()):
    leading = () if place is None else (place,)
    return pl.pallas_call(
        kernel,
        out_shape=[jax.ShapeDtypeStruct(*s) for s in shapes],
        in_specs=[SMEM] * len(leading) + [VMEM] * len(operands),
        out_specs=[VMEM] * len(shapes),
        scratch_shapes=scratch,
        compiler_params=pltpu.CompilerParams(vmem_limit_bytes=24 << 20),
        cost_estimate=pl.CostEstimate(flops=flops, bytes_accessed=0, transcendentals=0),
        name=name,
    )(*leading, *operands)


def normalized(pieces):
    widened = [piece.astype(F32) for piece in pieces]
    width = sum(piece.shape[1] for piece in widened)
    mean = sum(jnp.sum(piece, axis=1, keepdims=True) for piece in widened) / width
    centred = [piece - mean for piece in widened]
    variance = sum(jnp.sum(piece * piece, axis=1, keepdims=True) for piece in centred) / width
    scale = lax.rsqrt(variance + 1e-06)
    return [(piece * scale).astype(BF16) for piece in centred]


def dot(left, right):
    return jnp.dot(left, right, preferred_element_type=F32)


def project_kernel(place, *refs, count, scaled):
    pieces, weight, outs = refs[:count], refs[count], refs[count + 1 :]
    normed = normalized([piece[...] for piece in pieces])
    products = []
    for which in range(weight.shape[0]):
        products.append(
            sum(
                dot(normed[step], weight[which, lax.rem(place[0] + step, count)])
                for step in range(count)
            )
        )
    if scaled:
        outs[0][...] = (products.pop(0) * QUERY_SCALE).astype(BF16)
    columns = weight.shape[3]
    for which, product in enumerate(products):
        outs[-1][:, which * columns : (which + 1) * columns] = product.astype(BF16)


def attend_kernel(query, *refs, packed, resumed, final):
    packs = refs[:packed]
    before = refs[packed : packed + 2] if resumed else ()
    outs = refs[packed + len(before) :]
    columns = query.shape[1]
    heads = []
    for index, start in enumerate(range(0, columns, HD)):
        head = slice(start, start + HD)
        values = slice(columns + start, columns + start + HD)
        asked = query[:, head]
        scores = [
            lax.dot_general(
                asked, pack[:, head], (((1,), (1,)), ((), ())), preferred_element_type=F32
            )
            for pack in packs
        ]
        tops = [jnp.max(score, axis=1, keepdims=True) for score in scores]
        total, mixed = 0.0, 0.0
        if resumed:
            stats = before[1][index]
            tops.append(stats[:, :1])
        maxima = functools.reduce(jnp.maximum, tops)
        if resumed:
            correction = jnp.exp2(stats[:, :1] - maxima)
            total = stats[:, 1:2] * correction
            mixed = before[0][index] * correction
        for score, pack in zip(scores, packs):
            expanded = jnp.exp2(score - maxima)
            total = total + jnp.sum(expanded, axis=1, keepdims=True)
            mixed = mixed + dot(expanded.astype(BF16), pack[:, values])
        if final:
            heads.append(mixed / total)
        else:
            outs[0][index] = mixed
            outs[1][index] = jnp.concatenate([maxima, total], axis=1)
    if final:
        outs[0][...] = jnp.concatenate(heads, axis=1).astype(BF16)


def pick(options, slot):
    chosen = options[0]
    for index in range(1, len(options)):
        chosen = jnp.where(slot == index, options[index], chosen)
    return chosen


def shares(mixed, weights, place):
    count = len(mixed)
    whole = sum(dot(m[...], w[...]) for m, w in zip(mixed, weights))
    share = whole.shape[1] // count
    options = [whole[:, i * share : (i + 1) * share] for i in range(count)]
    return [pick(options, lax.rem(place[0] + step, count)) for step in range(count)]


def update_kernel(place, *refs, count):
    mixed, weights = refs[:count], refs[count : 2 * count]
    tokens, query_weight = refs[2 * count : 3 * count], refs[3 * count]
    updated, query = refs[3 * count + 1 :]
    pieces = []
    for step, term in enumerate(shares(mixed, weights, place)):
        piece = (tokens[step][...].astype(F32) + term).astype(BF16)
        updated[step] = piece
        pieces.append(piece)
    normed = normalized(pieces)
    product = sum(
        dot(normed[step], query_weight[lax.rem(place[0] + step, count)]) for step in range(count)
    )
    query[...] = (product * QUERY_SCALE).astype(BF16)


def finish_kernel(place, *refs, count, width):
    mixed, weights = refs[:count], refs[count : 2 * count]
    updated, reassemble = refs[2 * count], refs[2 * count + 1 : 3 * count + 1]
    window, board = refs[3 * count + 1], refs[3 * count + 2]
    features = 0.0
    for step, term in enumerate(shares(mixed, weights, place)):
        final = (updated[step].astype(F32) + term).astype(BF16)
        features = features + dot(final, reassemble[step][...])
    features = features.astype(BF16)
    band_rows = board.shape[0]
    edge = jnp.zeros((band_rows, EDGE, board.shape[2]), BF16)
    board[:, :EDGE, :] = edge
    board[:, EDGE + GRID_W :, :] = edge
    board[:, EDGE : EDGE + GRID_W, :] = features.reshape(band_rows, GRID_W, board.shape[2])
    start = pl.multiple_of(place[0] * width, EDGE)
    window[...] = board[:, pl.ds(start, width + 2 * EDGE), :]


def conv_kernel(window, above, below, weight, out):
    width = out.shape[1]
    band_rows, channels = out.shape[0], out.shape[2]
    grid = jnp.concatenate([above[...], window[...], below[...]], axis=0).astype(F32)
    active = jnp.maximum(grid, 0.0)
    total = grid[1 : 1 + band_rows, EDGE : EDGE + width, :].reshape(band_rows * width, channels)
    for column in range(3):
        first = EDGE - 1 + column
        shifted = active[:, first : first + width, :].astype(BF16)
        for row in range(3):
            rows = shifted[row : row + band_rows].reshape(band_rows * width, channels)
            total = total + dot(rows, weight[row, column])
    out[...] = total.reshape(out.shape).astype(BF16)


def body(
    left_tokens, right_tokens, self_qkv, self_out, cross_qkv, cross_out, reassemble, conv_weight
):
    bands, tiles, cores = (lax.axis_size(axis) for axis in ("blk", "tile", "pair"))
    half = bands // cores
    both = ("blk", "pair")
    place = lax.axis_index("tile").astype(jnp.int32).reshape(1)
    rows, share = left_tokens.shape[1:]
    columns = self_qkv.shape[2]
    channels = reassemble.shape[1]
    width = GRID_W // tiles
    band_rows = rows // GRID_W

    def home(band, pair):
        return band * cores + pair

    def worker(band, pair):
        shift = (pair - band // half) % cores
        return ((band + shift * half) % bands) * cores + (pair - shift) % cores

    places = [(band, pair) for band in range(bands) for pair in range(cores)]

    def tied(values, *others):
        return lax.optimization_barrier((values, others))[0]

    def tile_pieces(own):
        others = [
            lax.ppermute(own, "tile", [((i + s) % tiles, i) for i in range(tiles)])
            for s in range(1, tiles)
        ]
        return [own, *others]

    def neighbours(pack):
        ring = [(g * half, i) for g in range(cores) for i in range(half)]
        return [
            lax.ppermute(pack, "blk", [(g + (i + s) % half, g + i) for g, i in ring])
            for s in range(1, half)
        ]

    def across(pack):
        return [
            lax.ppermute(pack, "pair", [((i + s) % cores, i) for i in range(cores)])
            for s in range(1, cores)
        ]

    def joined_packs(packs):
        return [packs[0] if len(packs) == 1 else jnp.concatenate(packs)]

    def moved(tokens):
        return lax.ppermute(tokens, both, [(home(*p), worker(*p)) for p in places])

    def project(pieces, weights, scaled):
        shapes = [((rows, columns), BF16)] * scaled + [((rows, 2 * columns), BF16)]
        stacked = weights.reshape(weights.shape[0], tiles, share, columns)
        return run_kernel(
            functools.partial(project_kernel, count=tiles, scaled=scaled),
            "project",
            shapes,
            [*pieces, stacked],
            0,
            place,
        )

    def attend(query, packs, state=(), final=False):
        heads = columns // HD
        shapes = [((heads, rows, HD), F32), ((heads, rows, 2), F32)]
        if final:
            shapes = [((rows, columns), BF16)]
        return run_kernel(
            functools.partial(
                attend_kernel, packed=len(packs), resumed=len(state) > 0, final=final
            ),
            "attend",
            shapes,
            [query, *packs, *state],
        )

    left_here = moved(left_tokens[0])
    right = tile_pieces(right_tokens[0])
    (right_pack,) = project(right, cross_qkv[1:], False)
    left_here, right_pack = lax.optimization_barrier((left_here, right_pack))
    right_pack = moved(right_pack)
    left = tile_pieces(left_here)
    query, pack = project(left, self_qkv, True)
    near = [pack, *across(pack)]
    beside = neighbours(pack)
    query_weight = cross_qkv[0].reshape(tiles, share, columns)
    near, right_pack, query_weight = lax.optimization_barrier((near, right_pack, query_weight))
    self_out_pieces = tile_pieces(tied(self_out, left))
    state = attend(query, near)
    beside, right_pack = tied((beside, right_pack), state)
    far = [*beside, *[p for b in beside for p in across(b)]]
    right_near = [right_pack, *across(right_pack)]
    right_beside = neighbours(right_pack)
    far, self_out_pieces = lax.optimization_barrier((far, self_out_pieces))
    (own_mixed,) = attend(query, far if len(far) < 3 else joined_packs(far), state, True)

    mixed = tile_pieces(own_mixed)
    reassemble_pieces = tile_pieces(tied(reassemble, mixed))
    cross_out_pieces = tile_pieces(tied(cross_out, mixed))
    right_beside = tied(right_beside, mixed)
    right_far = [*right_beside, *[p for b in right_beside for p in across(b)]]
    updated, cross_query = run_kernel(
        functools.partial(update_kernel, count=tiles),
        "update",
        [((tiles, rows, share), BF16), ((rows, columns), BF16)],
        [*mixed, *self_out_pieces, *left, query_weight],
        0,
        place,
    )
    state = attend(cross_query, right_near)
    right_far = tied(right_far, state)
    (mixed,) = attend(
        cross_query, right_far if len(right_far) < 3 else joined_packs(right_far), state, True
    )
    mixed = tile_pieces(mixed)
    (window,) = run_kernel(
        functools.partial(finish_kernel, count=tiles, width=width),
        "finish",
        [((band_rows, width + 2 * EDGE, channels), BF16)],
        [*mixed, *cross_out_pieces, updated, *reassemble_pieces],
        0,
        place,
        [pltpu.VMEM((band_rows, GRID_W + 2 * EDGE, channels), BF16)],
    )
    back = lax.ppermute(window, both, [(worker(*p), home(*p)) for p in places])
    above = lax.ppermute(
        window[-1:], both, [(worker(b, p), home(b + 1, p)) for b, p in places if b + 1 < bands]
    )
    below = lax.ppermute(
        window[:1], both, [(worker(b, p), home(b - 1, p)) for b, p in places if b > 0]
    )
    (joined,) = run_kernel(
        conv_kernel,
        "join",
        [((band_rows, width, channels), BF16)],
        [back, above, below, conv_weight],
    )
    return joined[None]


def solution(mesh):
    placed = (
        P(("groups", "pair"), "blk", "tile"),
        P(("groups", "pair"), "blk", "tile"),
        P(None, None, "tile"),
        P("tile", None),
        P(None, None, "tile"),
        P("tile", None),
        P("tile", None),
        P(),
    )
    return jax.shard_map(
        body,
        mesh=mesh,
        in_specs=placed,
        out_specs=P(("groups", "pair"), "blk", "tile", None),
        check_vma=False,
    )
```

```python
import functools
import math

import jax
import jax.numpy as jnp
from jax import lax
from jax.experimental import pallas as pl
from jax.experimental.pallas import tpu as pltpu
from jax.sharding import PartitionSpec as P

HD = 64
GRID_W = 128
EDGE = 16
F32 = jnp.float32
BF16 = jnp.bfloat16
QUERY_SCALE = math.log2(math.e) * HD**-0.5
VMEM = pl.BlockSpec(memory_space=pltpu.VMEM)
SMEM = pl.BlockSpec(memory_space=pltpu.SMEM)


def run_kernel(kernel, name, shapes, operands, flops=0, place=None, scratch=()):
    leading = () if place is None else (place,)
    return pl.pallas_call(
        kernel,
        out_shape=[jax.ShapeDtypeStruct(*s) for s in shapes],
        in_specs=[SMEM] * len(leading) + [VMEM] * len(operands),
        out_specs=[VMEM] * len(shapes),
        scratch_shapes=scratch,
        compiler_params=pltpu.CompilerParams(vmem_limit_bytes=24 << 20),
        cost_estimate=pl.CostEstimate(flops=flops, bytes_accessed=0, transcendentals=0),
        name=name,
    )(*leading, *operands)


def normalized(pieces):
    widened = [piece.astype(F32) for piece in pieces]
    width = sum(piece.shape[1] for piece in widened)
    mean = sum(jnp.sum(piece, axis=1, keepdims=True) for piece in widened) / width
    centred = [piece - mean for piece in widened]
    variance = sum(jnp.sum(piece * piece, axis=1, keepdims=True) for piece in centred) / width
    scale = lax.rsqrt(variance + 1e-06)
    return [(piece * scale).astype(BF16) for piece in centred]


def dot(left, right):
    return jnp.dot(left, right, preferred_element_type=F32)


def project_kernel(place, *refs, count, scaled):
    pieces, weight, outs = refs[:count], refs[count], refs[count + 1 :]
    normed = normalized([piece[...] for piece in pieces])
    products = []
    for which in range(weight.shape[0]):
        products.append(
            sum(
                dot(normed[step], weight[which, lax.rem(place[0] + step, count)])
                for step in range(count)
            )
        )
    if scaled:
        outs[0][...] = (products.pop(0) * QUERY_SCALE).astype(BF16)
    columns = weight.shape[3]
    for which, product in enumerate(products):
        outs[-1][:, which * columns : (which + 1) * columns] = product.astype(BF16)


def attend_kernel(query, *refs, packed, resumed, final):
    packs = refs[:packed]
    before = refs[packed : packed + 2] if resumed else ()
    outs = refs[packed + len(before) :]
    columns = query.shape[1]
    heads = []
    for index, start in enumerate(range(0, columns, HD)):
        head = slice(start, start + HD)
        values = slice(columns + start, columns + start + HD)
        asked = query[:, head]
        scores = [
            lax.dot_general(
                asked, pack[:, head], (((1,), (1,)), ((), ())), preferred_element_type=F32
            )
            for pack in packs
        ]
        tops = [jnp.max(score, axis=1, keepdims=True) for score in scores]
        total, mixed = 0.0, 0.0
        if resumed:
            stats = before[1][index]
            tops.append(stats[:, :1])
        maxima = functools.reduce(jnp.maximum, tops)
        if resumed:
            correction = jnp.exp2(stats[:, :1] - maxima)
            total = stats[:, 1:2] * correction
            mixed = before[0][index] * correction
        for score, pack in zip(scores, packs):
            expanded = jnp.exp2(score - maxima)
            total = total + jnp.sum(expanded, axis=1, keepdims=True)
            mixed = mixed + dot(expanded.astype(BF16), pack[:, values])
        if final:
            heads.append(mixed / total)
        else:
            outs[0][index] = mixed
            outs[1][index] = jnp.concatenate([maxima, total], axis=1)
    if final:
        outs[0][...] = jnp.concatenate(heads, axis=1).astype(BF16)


def pick(options, slot):
    chosen = options[0]
    for index in range(1, len(options)):
        chosen = jnp.where(slot == index, options[index], chosen)
    return chosen


def shares(mixed, weights, place):
    count = len(mixed)
    whole = sum(dot(m[...], w[...]) for m, w in zip(mixed, weights))
    share = whole.shape[1] // count
    options = [whole[:, i * share : (i + 1) * share] for i in range(count)]
    return [pick(options, lax.rem(place[0] + step, count)) for step in range(count)]


def update_kernel(place, *refs, count):
    mixed, weights = refs[:count], refs[count : 2 * count]
    tokens, query_weight = refs[2 * count : 3 * count], refs[3 * count]
    updated, query = refs[3 * count + 1 :]
    pieces = []
    for step, term in enumerate(shares(mixed, weights, place)):
        piece = (tokens[step][...].astype(F32) + term).astype(BF16)
        updated[step] = piece
        pieces.append(piece)
    normed = normalized(pieces)
    product = sum(
        dot(normed[step], query_weight[lax.rem(place[0] + step, count)]) for step in range(count)
    )
    query[...] = (product * QUERY_SCALE).astype(BF16)


def finish_kernel(place, *refs, count, width):
    mixed, weights = refs[:count], refs[count : 2 * count]
    updated, reassemble = refs[2 * count], refs[2 * count + 1 : 3 * count + 1]
    window, board = refs[3 * count + 1], refs[3 * count + 2]
    features = 0.0
    for step, term in enumerate(shares(mixed, weights, place)):
        final = (updated[step].astype(F32) + term).astype(BF16)
        features = features + dot(final, reassemble[step][...])
    features = features.astype(BF16)
    band_rows = board.shape[0]
    edge = jnp.zeros((band_rows, EDGE, board.shape[2]), BF16)
    board[:, :EDGE, :] = edge
    board[:, EDGE + GRID_W :, :] = edge
    board[:, EDGE : EDGE + GRID_W, :] = features.reshape(band_rows, GRID_W, board.shape[2])
    start = pl.multiple_of(place[0] * width, EDGE)
    window[...] = board[:, pl.ds(start, width + 2 * EDGE), :]


def conv_kernel(window, above, below, weight, out):
    width = out.shape[1]
    band_rows, channels = out.shape[0], out.shape[2]
    grid = jnp.concatenate([above[...], window[...], below[...]], axis=0).astype(F32)
    active = jnp.maximum(grid, 0.0)
    total = grid[1 : 1 + band_rows, EDGE : EDGE + width, :].reshape(band_rows * width, channels)
    for column in range(3):
        first = EDGE - 1 + column
        shifted = active[:, first : first + width, :].astype(BF16)
        for row in range(3):
            rows = shifted[row : row + band_rows].reshape(band_rows * width, channels)
            total = total + dot(rows, weight[row, column])
    out[...] = total.reshape(out.shape).astype(BF16)


def body(
    left_tokens, right_tokens, self_qkv, self_out, cross_qkv, cross_out, reassemble, conv_weight
):
    bands, tiles, cores = (lax.axis_size(axis) for axis in ("blk", "tile", "pair"))
    half = bands // cores
    both = ("blk", "pair")
    place = lax.axis_index("tile").astype(jnp.int32).reshape(1)
    rows, share = left_tokens.shape[1:]
    columns = self_qkv.shape[2]
    channels = reassemble.shape[1]
    width = GRID_W // tiles
    band_rows = rows // GRID_W

    def home(band, pair):
        return band * cores + pair

    def worker(band, pair):
        shift = (pair - band // half) % cores
        return ((band + shift * half) % bands) * cores + (pair - shift) % cores

    places = [(band, pair) for band in range(bands) for pair in range(cores)]

    def tied(values, *others):
        return lax.optimization_barrier((values, others))[0]

    def tile_pieces(own):
        others = [
            lax.ppermute(own, "tile", [((i + s) % tiles, i) for i in range(tiles)])
            for s in range(1, tiles)
        ]
        return [own, *others]

    def neighbours(pack):
        ring = [(g * half, i) for g in range(cores) for i in range(half)]
        return [
            lax.ppermute(pack, "blk", [(g + (i + s) % half, g + i) for g, i in ring])
            for s in range(1, half)
        ]

    def across(pack):
        return [
            lax.ppermute(pack, "pair", [((i + s) % cores, i) for i in range(cores)])
            for s in range(1, cores)
        ]

    def grouped(packs):
        return packs if len(packs) < 3 else [jnp.concatenate(packs)]

    def moved(tokens):
        return lax.ppermute(tokens, both, [(home(*p), worker(*p)) for p in places])

    def project(pieces, weights, scaled):
        shapes = [((rows, columns), BF16)] * scaled + [((rows, 2 * columns), BF16)]
        stacked = weights.reshape(weights.shape[0], tiles, share, columns)
        return run_kernel(
            functools.partial(project_kernel, count=tiles, scaled=scaled),
            "project",
            shapes,
            [*pieces, stacked],
            0,
            place,
        )

    def attend(query, packs, state=(), final=False):
        heads = columns // HD
        shapes = [((heads, rows, HD), F32), ((heads, rows, 2), F32)]
        if final:
            shapes = [((rows, columns), BF16)]
        return run_kernel(
            functools.partial(
                attend_kernel, packed=len(packs), resumed=len(state) > 0, final=final
            ),
            "attend",
            shapes,
            [query, *packs, *state],
        )

    left_here = moved(left_tokens[0])
    left = tile_pieces(left_here)
    right = tile_pieces(right_tokens[0])
    (right_pack,) = project(right, cross_qkv[1:], False)
    right_pack = moved(right_pack)
    query, pack = project(left, self_qkv, True)
    query_weight = cross_qkv[0].reshape(tiles, share, columns)
    near, right_pack, query_weight = lax.optimization_barrier(
        ([pack, *neighbours(pack)], right_pack, query_weight)
    )
    far = [q for p in near for q in across(p)]
    self_out_pieces = tile_pieces(tied(self_out, left))
    reassemble_pieces = tile_pieces(tied(reassemble, left))
    state = attend(query, grouped(near))
    right_pack = tied(right_pack, state)
    right_near = [right_pack, *neighbours(right_pack)]
    far, self_out_pieces, reassemble_pieces = lax.optimization_barrier(
        (far, self_out_pieces, reassemble_pieces)
    )
    (own_mixed,) = attend(query, grouped(far), state, True)

    mixed = tile_pieces(own_mixed)
    updated, cross_query = run_kernel(
        functools.partial(update_kernel, count=tiles),
        "update",
        [((tiles, rows, share), BF16), ((rows, columns), BF16)],
        [*mixed, *self_out_pieces, *left, query_weight],
        0,
        place,
    )
    cross_out_pieces = tile_pieces(tied(cross_out, updated))
    right_near = tied(right_near, updated)
    right_far = [q for p in right_near for q in across(p)]
    state = attend(cross_query, grouped(right_near))
    right_far = tied(right_far, state)
    (mixed,) = attend(cross_query, grouped(right_far), state, True)
    mixed = tile_pieces(mixed)
    (window,) = run_kernel(
        functools.partial(finish_kernel, count=tiles, width=width),
        "finish",
        [((band_rows, width + 2 * EDGE, channels), BF16)],
        [*mixed, *cross_out_pieces, updated, *reassemble_pieces],
        0,
        place,
        [pltpu.VMEM((band_rows, GRID_W + 2 * EDGE, channels), BF16)],
    )
    back = lax.ppermute(window, both, [(worker(*p), home(*p)) for p in places])
    above = lax.ppermute(
        window[-1:], both, [(worker(b, p), home(b + 1, p)) for b, p in places if b + 1 < bands]
    )
    below = lax.ppermute(
        window[:1], both, [(worker(b, p), home(b - 1, p)) for b, p in places if b > 0]
    )
    (joined,) = run_kernel(
        conv_kernel,
        "join",
        [((band_rows, width, channels), BF16)],
        [back, above, below, conv_weight],
    )
    return joined[None]


def solution(mesh):
    placed = (
        P(("groups", "pair"), "blk", "tile"),
        P(("groups", "pair"), "blk", "tile"),
        P(None, None, "tile"),
        P("tile", None),
        P(None, None, "tile"),
        P("tile", None),
        P("tile", None),
        P(),
    )
    return jax.shard_map(
        body,
        mesh=mesh,
        in_specs=placed,
        out_specs=P(("groups", "pair"), "blk", "tile", None),
        check_vma=False,
    )
```

```python
import functools
import math

import jax
import jax.numpy as jnp
from jax import lax
from jax.experimental import pallas as pl
from jax.experimental.pallas import tpu as pltpu
from jax.sharding import PartitionSpec as P

HD = 64
GRID_W = 128
EDGE = 16
F32 = jnp.float32
BF16 = jnp.bfloat16
QUERY_SCALE = math.log2(math.e) * HD**-0.5
VMEM = pl.BlockSpec(memory_space=pltpu.VMEM)
SMEM = pl.BlockSpec(memory_space=pltpu.SMEM)


def run_kernel(kernel, name, shapes, operands, flops=0, place=None, scratch=()):
    leading = () if place is None else (place,)
    return pl.pallas_call(
        kernel,
        out_shape=[jax.ShapeDtypeStruct(*s) for s in shapes],
        in_specs=[SMEM] * len(leading) + [VMEM] * len(operands),
        out_specs=[VMEM] * len(shapes),
        scratch_shapes=scratch,
        compiler_params=pltpu.CompilerParams(vmem_limit_bytes=24 << 20),
        cost_estimate=pl.CostEstimate(flops=flops, bytes_accessed=0, transcendentals=0),
        name=name,
    )(*leading, *operands)


def normalized(pieces):
    widened = [piece.astype(F32) for piece in pieces]
    width = sum(piece.shape[1] for piece in widened)
    mean = sum(jnp.sum(piece, axis=1, keepdims=True) for piece in widened) / width
    centred = [piece - mean for piece in widened]
    variance = sum(jnp.sum(piece * piece, axis=1, keepdims=True) for piece in centred) / width
    scale = lax.rsqrt(variance + 1e-06)
    return [(piece * scale).astype(BF16) for piece in centred]


def dot(left, right):
    return jnp.dot(left, right, preferred_element_type=F32)


def project_kernel(place, *refs, count, scaled, first):
    pieces, weight, outs = refs[:count], refs[count], refs[count + 1 :]
    normed = normalized([piece[...] for piece in pieces])
    products = []
    for which in range(first, weight.shape[0]):
        products.append(
            sum(
                dot(normed[step], weight[which, lax.rem(place[0] + step, count)])
                for step in range(count)
            )
        )
    if scaled:
        outs[0][...] = (products.pop(0) * QUERY_SCALE).astype(BF16)
    columns = weight.shape[3]
    for which, product in enumerate(products):
        outs[-1][:, which * columns : (which + 1) * columns] = product.astype(BF16)


def attend_kernel(query, *refs, packed, resumed, final):
    packs = refs[:packed]
    before = refs[packed : packed + 2] if resumed else ()
    outs = refs[packed + len(before) :]
    columns = query.shape[1]
    heads = []
    for index, start in enumerate(range(0, columns, HD)):
        head = slice(start, start + HD)
        values = slice(columns + start, columns + start + HD)
        asked = query[:, head]
        scores = [
            lax.dot_general(
                asked, pack[:, head], (((1,), (1,)), ((), ())), preferred_element_type=F32
            )
            for pack in packs
        ]
        tops = [jnp.max(score, axis=1, keepdims=True) for score in scores]
        total, mixed = 0.0, 0.0
        if resumed:
            stats = before[1][index]
            tops.append(stats[:, :1])
        maxima = functools.reduce(jnp.maximum, tops)
        if resumed:
            correction = jnp.exp2(stats[:, :1] - maxima)
            total = stats[:, 1:2] * correction
            mixed = before[0][index] * correction
        for score, pack in zip(scores, packs):
            expanded = jnp.exp2(score - maxima)
            total = total + jnp.sum(expanded, axis=1, keepdims=True)
            mixed = mixed + dot(expanded.astype(BF16), pack[:, values])
        if final:
            heads.append(mixed / total)
        else:
            outs[0][index] = mixed
            outs[1][index] = jnp.concatenate([maxima, total], axis=1)
    if final:
        outs[0][...] = jnp.concatenate(heads, axis=1).astype(BF16)


def unpack_kernel(place, *refs):
    halves, outs = refs[:-3], refs[-3:]
    for step, half in enumerate(halves):
        core = lax.rem(place[1] + step, len(halves))
        start = 0
        for out in outs[:2]:
            rows = out.shape[0] // len(halves)
            out[pl.ds(pl.multiple_of(core * rows, rows), rows), :] = half[start : start + rows, :]
            start += rows
        blocks = half.shape[1] // outs[2].shape[1]
        block = outs[2].shape[0] // blocks
        rows = block // len(halves)
        for index in range(blocks):
            first = pl.multiple_of(core * rows + index * block, rows)
            lanes = slice(index * outs[2].shape[1], (index + 1) * outs[2].shape[1])
            outs[2][pl.ds(first, rows), :] = half[start : start + rows, lanes]


def pick(options, slot):
    chosen = options[0]
    for index in range(1, len(options)):
        chosen = jnp.where(slot == index, options[index], chosen)
    return chosen


def shares(mixed, weights, place):
    count = len(mixed)
    whole = sum(dot(m[...], w[...]) for m, w in zip(mixed, weights))
    share = whole.shape[1] // count
    options = [whole[:, i * share : (i + 1) * share] for i in range(count)]
    return [pick(options, lax.rem(place[0] + step, count)) for step in range(count)]


def update_kernel(place, *refs, count):
    mixed, weights = refs[:count], refs[count : 2 * count]
    tokens, query_weight = refs[2 * count : 3 * count], refs[3 * count]
    updated, query = refs[3 * count + 1 :]
    pieces = []
    for step, term in enumerate(shares(mixed, weights, place)):
        piece = (tokens[step][...].astype(F32) + term).astype(BF16)
        updated[step] = piece
        pieces.append(piece)
    normed = normalized(pieces)
    product = sum(
        dot(normed[step], query_weight[lax.rem(place[0] + step, count)]) for step in range(count)
    )
    query[...] = (product * QUERY_SCALE).astype(BF16)


def finish_kernel(place, *refs, count, width):
    mixed, weights = refs[:count], refs[count : 2 * count]
    updated, reassemble = refs[2 * count], refs[2 * count + 1 : 3 * count + 1]
    window, board = refs[3 * count + 1], refs[3 * count + 2]
    features = 0.0
    for step, term in enumerate(shares(mixed, weights, place)):
        final = (updated[step].astype(F32) + term).astype(BF16)
        features = features + dot(final, reassemble[step][...])
    features = features.astype(BF16)
    band_rows = board.shape[0]
    edge = jnp.zeros((band_rows, EDGE, board.shape[2]), BF16)
    board[:, :EDGE, :] = edge
    board[:, EDGE + GRID_W :, :] = edge
    board[:, EDGE : EDGE + GRID_W, :] = features.reshape(band_rows, GRID_W, board.shape[2])
    start = pl.multiple_of(place[0] * width, EDGE)
    window[...] = board[:, pl.ds(start, width + 2 * EDGE), :]


def conv_kernel(window, above, below, weight, out):
    width = out.shape[1]
    band_rows, channels = out.shape[0], out.shape[2]
    grid = jnp.concatenate([above[...], window[...], below[...]], axis=0).astype(F32)
    active = jnp.maximum(grid, 0.0)
    total = grid[1 : 1 + band_rows, EDGE : EDGE + width, :].reshape(band_rows * width, channels)
    for column in range(3):
        first = EDGE - 1 + column
        shifted = active[:, first : first + width, :].astype(BF16)
        for row in range(3):
            rows = shifted[row : row + band_rows].reshape(band_rows * width, channels)
            total = total + dot(rows, weight[row, column])
    out[...] = total.reshape(out.shape).astype(BF16)


def body(
    left_tokens, right_tokens, self_qkv, self_out, cross_qkv, cross_out, reassemble, conv_weight
):
    bands, tiles, cores = (lax.axis_size(axis) for axis in ("blk", "tile", "pair"))
    half = bands // cores
    both = ("blk", "pair")
    place = jnp.stack([lax.axis_index("tile"), lax.axis_index("pair")]).astype(jnp.int32)
    rows, share = left_tokens.shape[1:]
    columns = self_qkv.shape[2]
    channels = reassemble.shape[1]
    width = GRID_W // tiles
    band_rows = rows // GRID_W

    def home(band, pair):
        return band * cores + pair

    def worker(band, pair):
        shift = (pair - band // half) % cores
        return ((band + shift * half) % bands) * cores + (pair - shift) % cores

    places = [(band, pair) for band in range(bands) for pair in range(cores)]

    def tied(values, *others):
        return lax.optimization_barrier((values, others))[0]

    def tile_pieces(own):
        others = [
            lax.ppermute(own, "tile", [((i + s) % tiles, i) for i in range(tiles)])
            for s in range(1, tiles)
        ]
        return [own, *others]

    def neighbours(pack):
        ring = [(g * half, i) for g in range(cores) for i in range(half)]
        return [
            lax.ppermute(pack, "blk", [(g + (i + s) % half, g + i) for g, i in ring])
            for s in range(1, half)
        ]

    def across(pack):
        return [
            lax.ppermute(pack, "pair", [((i + s) % cores, i) for i in range(cores)])
            for s in range(1, cores)
        ]

    def grouped(packs):
        return packs if len(packs) < 3 else [jnp.concatenate(packs)]

    def moved(tokens):
        return lax.ppermute(tokens, both, [(home(*p), worker(*p)) for p in places])

    def project(pieces, weights, scaled, first):
        shapes = [((rows, columns), BF16)] * scaled + [((rows, 2 * columns), BF16)]
        stacked = weights.reshape(weights.shape[0], tiles, share, columns)
        return run_kernel(
            functools.partial(project_kernel, count=tiles, scaled=scaled, first=first),
            "project",
            shapes,
            [*pieces, stacked],
            0,
            place,
        )

    def packed_half():
        parts = [self_out, cross_out]
        blocks = self_out.shape[1] // channels
        height = share // blocks
        parts.append(
            jnp.concatenate(
                [reassemble[i * height : (i + 1) * height] for i in range(blocks)], axis=1
            )
        )
        core = lax.axis_index("pair")
        return jnp.concatenate(
            [
                lax.dynamic_slice_in_dim(p, core * (p.shape[0] // cores), p.shape[0] // cores)
                for p in parts
            ]
        )

    def unpacked(half):
        return run_kernel(
            unpack_kernel,
            "unpack",
            [(w.shape, BF16) for w in (self_out, cross_out, reassemble)],
            [half, *across(half)],
            0,
            place,
        )

    def attend(query, packs, state=(), final=False):
        heads = columns // HD
        shapes = [((heads, rows, HD), F32), ((heads, rows, 2), F32)]
        if final:
            shapes = [((rows, columns), BF16)]
        return run_kernel(
            functools.partial(
                attend_kernel, packed=len(packs), resumed=len(state) > 0, final=final
            ),
            "attend",
            shapes,
            [query, *packs, *state],
        )

    left_here = moved(left_tokens[0])
    left = tile_pieces(left_here)
    right = tile_pieces(right_tokens[0])
    (right_pack,) = project(right, cross_qkv, False, 1)
    right_pack = moved(right_pack)
    query, pack = project(left, self_qkv, True, 0)
    query_weight = cross_qkv[0].reshape(tiles, share, columns)
    beside = neighbours(tied(pack, right_pack))
    halves = tile_pieces(tied(packed_half(), left_here))[1:]
    near, query_weight, halves = lax.optimization_barrier(
        ([pack, *beside], query_weight, halves)
    )
    far = [q for p in near for q in across(p)]
    state = attend(query, grouped(near))
    right_pack = tied(right_pack, state)
    right_near = [right_pack, *neighbours(right_pack)]
    far, halves = lax.optimization_barrier((far, halves))
    others = [unpacked(half) for half in halves]
    (own_mixed,) = attend(query, grouped(far), state, True)

    mixed = tile_pieces(own_mixed)
    updated, cross_query = run_kernel(
        functools.partial(update_kernel, count=tiles),
        "update",
        [((tiles, rows, share), BF16), ((rows, columns), BF16)],
        [*mixed, self_out, *[o[0] for o in others], *left, query_weight],
        0,
        place,
    )
    right_near = tied(right_near, updated)
    right_far = [q for p in right_near for q in across(p)]
    state = attend(cross_query, grouped(right_near))
    right_far = tied(right_far, state)
    (mixed,) = attend(cross_query, grouped(right_far), state, True)
    mixed = tile_pieces(mixed)
    (window,) = run_kernel(
        functools.partial(finish_kernel, count=tiles, width=width),
        "finish",
        [((band_rows, width + 2 * EDGE, channels), BF16)],
        [
            *mixed,
            cross_out,
            *[o[1] for o in others],
            updated,
            reassemble,
            *[o[2] for o in others],
        ],
        0,
        place,
        [pltpu.VMEM((band_rows, GRID_W + 2 * EDGE, channels), BF16)],
    )
    back = lax.ppermute(window, both, [(worker(*p), home(*p)) for p in places])
    above = lax.ppermute(
        window[-1:], both, [(worker(b, p), home(b + 1, p)) for b, p in places if b + 1 < bands]
    )
    below = lax.ppermute(
        window[:1], both, [(worker(b, p), home(b - 1, p)) for b, p in places if b > 0]
    )
    (joined,) = run_kernel(
        conv_kernel,
        "join",
        [((band_rows, width, channels), BF16)],
        [back, above, below, conv_weight],
    )
    return joined[None]


def solution(mesh):
    placed = (
        P(("groups", "pair"), "blk", "tile"),
        P(("groups", "pair"), "blk", "tile"),
        P(None, None, "tile"),
        P("tile", None),
        P(None, None, "tile"),
        P("tile", None),
        P("tile", None),
        P(),
    )
    return jax.shard_map(
        body,
        mesh=mesh,
        in_specs=placed,
        out_specs=P(("groups", "pair"), "blk", "tile", None),
        check_vma=False,
    )
```

```python
import functools
import math

import jax
import jax.numpy as jnp
from jax import lax
from jax.experimental import pallas as pl
from jax.experimental.pallas import tpu as pltpu
from jax.sharding import PartitionSpec as P

HD = 64
GRID_W = 128
EDGE = 16
F32 = jnp.float32
BF16 = jnp.bfloat16
QUERY_SCALE = math.log2(math.e) * HD**-0.5
VMEM = pl.BlockSpec(memory_space=pltpu.VMEM)
SMEM = pl.BlockSpec(memory_space=pltpu.SMEM)
HBM = pl.BlockSpec(memory_space=pl.ANY)


def run_kernel(kernel, name, shapes, operands, flops=0, place=None, scratch=(), space=VMEM):
    leading = () if place is None else (place,)
    return pl.pallas_call(
        kernel,
        out_shape=[jax.ShapeDtypeStruct(*s) for s in shapes],
        in_specs=[SMEM] * len(leading) + [space] * len(operands),
        out_specs=[VMEM] * len(shapes),
        scratch_shapes=scratch,
        compiler_params=pltpu.CompilerParams(vmem_limit_bytes=24 << 20),
        cost_estimate=pl.CostEstimate(flops=flops, bytes_accessed=0, transcendentals=0),
        name=name,
    )(*leading, *operands)


def normalized(pieces):
    widened = [piece.astype(F32) for piece in pieces]
    width = sum(piece.shape[1] for piece in widened)
    mean = sum(jnp.sum(piece, axis=1, keepdims=True) for piece in widened) / width
    centred = [piece - mean for piece in widened]
    variance = sum(jnp.sum(piece * piece, axis=1, keepdims=True) for piece in centred) / width
    scale = lax.rsqrt(variance + 1e-06)
    return [(piece * scale).astype(BF16) for piece in centred]


def dot(left, right):
    return jnp.dot(left, right, preferred_element_type=F32)


def project_kernel(place, *refs, count, scaled, first):
    pieces, weight, outs = refs[:count], refs[count], refs[count + 1 :]
    normed = normalized([piece[...] for piece in pieces])
    products = []
    for which in range(first, weight.shape[0]):
        products.append(
            sum(
                dot(normed[step], weight[which, lax.rem(place[0] + step, count)])
                for step in range(count)
            )
        )
    if scaled:
        outs[0][...] = (products.pop(0) * QUERY_SCALE).astype(BF16)
    columns = weight.shape[3]
    for which, product in enumerate(products):
        outs[-1][:, which * columns : (which + 1) * columns] = product.astype(BF16)


def attend_kernel(query, *refs, packed, resumed, final):
    packs = refs[:packed]
    before = refs[packed : packed + 2] if resumed else ()
    outs = refs[packed + len(before) :]
    columns = query.shape[1]
    heads = []
    for index, start in enumerate(range(0, columns, HD)):
        head = slice(start, start + HD)
        values = slice(columns + start, columns + start + HD)
        asked = query[:, head]
        scores = [
            lax.dot_general(
                asked, pack[:, head], (((1,), (1,)), ((), ())), preferred_element_type=F32
            )
            for pack in packs
        ]
        tops = [jnp.max(score, axis=1, keepdims=True) for score in scores]
        total, mixed = 0.0, 0.0
        if resumed:
            stats = before[1][index]
            tops.append(stats[:, :1])
        maxima = functools.reduce(jnp.maximum, tops)
        if resumed:
            correction = jnp.exp2(stats[:, :1] - maxima)
            total = stats[:, 1:2] * correction
            mixed = before[0][index] * correction
        for score, pack in zip(scores, packs):
            expanded = jnp.exp2(score - maxima)
            total = total + jnp.sum(expanded, axis=1, keepdims=True)
            mixed = mixed + dot(expanded.astype(BF16), pack[:, values])
        if final:
            heads.append(mixed / total)
        else:
            outs[0][index] = mixed
            outs[1][index] = jnp.concatenate([maxima, total], axis=1)
    if final:
        outs[0][...] = jnp.concatenate(heads, axis=1).astype(BF16)


def stage_kernel(place, *refs, cores):
    count = (len(refs) - 2) // 2
    sources, outs, half, sems = refs[:count], refs[count : 2 * count], refs[-2], refs[-1]
    pairs = []
    for source, out in zip(sources, outs):
        pairs.append((source, out))
    first_out, second_out, rows_out = sources[:3]
    start = 0
    for source in (first_out, second_out):
        rows = source.shape[0] // cores
        begin = pl.multiple_of(place[1] * rows, rows)
        pairs.append((source.at[pl.ds(begin, rows)], half.at[pl.ds(start, rows)]))
        start += rows
    blocks = half.shape[1] // rows_out.shape[1]
    block = rows_out.shape[0] // blocks
    rows = block // cores
    for index in range(blocks):
        begin = pl.multiple_of(place[1] * rows + index * block, rows)
        lanes = pl.ds(index * rows_out.shape[1], rows_out.shape[1])
        pairs.append((rows_out.at[pl.ds(begin, rows)], half.at[pl.ds(start, rows), lanes]))
    copies = [pltpu.make_async_copy(a, b, sems.at[i]) for i, (a, b) in enumerate(pairs)]
    for copy in copies:
        copy.start()
    for copy in copies:
        copy.wait()


def unpack_kernel(place, *refs):
    halves, outs = refs[:-3], refs[-3:]
    for step, half in enumerate(halves):
        core = lax.rem(place[1] + step, len(halves))
        start = 0
        for out in outs[:2]:
            rows = out.shape[0] // len(halves)
            out[pl.ds(pl.multiple_of(core * rows, rows), rows), :] = half[start : start + rows, :]
            start += rows
        blocks = half.shape[1] // outs[2].shape[1]
        block = outs[2].shape[0] // blocks
        rows = block // len(halves)
        for index in range(blocks):
            first = pl.multiple_of(core * rows + index * block, rows)
            lanes = slice(index * outs[2].shape[1], (index + 1) * outs[2].shape[1])
            outs[2][pl.ds(first, rows), :] = half[start : start + rows, lanes]


def pick(options, slot):
    chosen = options[0]
    for index in range(1, len(options)):
        chosen = jnp.where(slot == index, options[index], chosen)
    return chosen


def shares(mixed, weights, place):
    count = len(mixed)
    whole = sum(dot(m[...], w[...]) for m, w in zip(mixed, weights))
    share = whole.shape[1] // count
    options = [whole[:, i * share : (i + 1) * share] for i in range(count)]
    return [pick(options, lax.rem(place[0] + step, count)) for step in range(count)]


def update_kernel(place, *refs, count):
    mixed, weights = refs[:count], refs[count : 2 * count]
    tokens, query_weight = refs[2 * count : 3 * count], refs[3 * count]
    updated, query = refs[3 * count + 1 :]
    pieces = []
    for step, term in enumerate(shares(mixed, weights, place)):
        piece = (tokens[step][...].astype(F32) + term).astype(BF16)
        updated[step] = piece
        pieces.append(piece)
    normed = normalized(pieces)
    product = sum(
        dot(normed[step], query_weight[0, lax.rem(place[0] + step, count)])
        for step in range(count)
    )
    query[...] = (product * QUERY_SCALE).astype(BF16)


def finish_kernel(place, *refs, count, width):
    mixed, weights = refs[:count], refs[count : 2 * count]
    updated, reassemble = refs[2 * count], refs[2 * count + 1 : 3 * count + 1]
    window, board = refs[3 * count + 1], refs[3 * count + 2]
    features = 0.0
    for step, term in enumerate(shares(mixed, weights, place)):
        final = (updated[step].astype(F32) + term).astype(BF16)
        features = features + dot(final, reassemble[step][...])
    features = features.astype(BF16)
    band_rows = board.shape[0]
    edge = jnp.zeros((band_rows, EDGE, board.shape[2]), BF16)
    board[:, :EDGE, :] = edge
    board[:, EDGE + GRID_W :, :] = edge
    board[:, EDGE : EDGE + GRID_W, :] = features.reshape(band_rows, GRID_W, board.shape[2])
    start = pl.multiple_of(place[0] * width, EDGE)
    window[...] = board[:, pl.ds(start, width + 2 * EDGE), :]


def conv_kernel(window, above, below, weight, out):
    width = out.shape[1]
    band_rows, channels = out.shape[0], out.shape[2]
    grid = jnp.concatenate([above[...], window[...], below[...]], axis=0).astype(F32)
    active = jnp.maximum(grid, 0.0)
    total = grid[1 : 1 + band_rows, EDGE : EDGE + width, :].reshape(band_rows * width, channels)
    for column in range(3):
        first = EDGE - 1 + column
        shifted = active[:, first : first + width, :].astype(BF16)
        for row in range(3):
            rows = shifted[row : row + band_rows].reshape(band_rows * width, channels)
            total = total + dot(rows, weight[row, column])
    out[...] = total.reshape(out.shape).astype(BF16)


def body(left_tokens, right_tokens, self_qkv, self_out, cross_qkv, cross_out, reassemble, taps):
    bands, tiles, cores = (lax.axis_size(axis) for axis in ("blk", "tile", "pair"))
    span = bands // cores
    both = ("blk", "pair")
    place = jnp.stack([lax.axis_index("tile"), lax.axis_index("pair")]).astype(jnp.int32)
    rows, share = left_tokens.shape[1:]
    columns = self_qkv.shape[2]
    channels = reassemble.shape[1]
    width = GRID_W // tiles
    band_rows = rows // GRID_W

    def home(band, pair):
        return band * cores + pair

    def worker(band, pair):
        shift = (pair - band // span) % cores
        return ((band + shift * span) % bands) * cores + (pair - shift) % cores

    places = [(band, pair) for band in range(bands) for pair in range(cores)]

    def tied(values, *others):
        return lax.optimization_barrier((values, others))[0]

    def tile_pieces(own):
        others = [
            lax.ppermute(own, "tile", [((i + s) % tiles, i) for i in range(tiles)])
            for s in range(1, tiles)
        ]
        return [own, *others]

    def neighbours(pack):
        ring = [(g * span, i) for g in range(cores) for i in range(span)]
        return [
            lax.ppermute(pack, "blk", [(g + (i + s) % span, g + i) for g, i in ring])
            for s in range(1, span)
        ]

    def across(pack):
        return [
            lax.ppermute(pack, "pair", [((i + s) % cores, i) for i in range(cores)])
            for s in range(1, cores)
        ]

    def grouped(packs):
        return packs if len(packs) < 3 else [jnp.concatenate(packs)]

    def moved(tokens):
        return lax.ppermute(tokens, both, [(home(*p), worker(*p)) for p in places])

    def project(pieces, weights, scaled, first):
        shapes = [((rows, columns), BF16)] * scaled + [((rows, 2 * columns), BF16)]
        stacked = weights.reshape(weights.shape[0], tiles, share, columns)
        return run_kernel(
            functools.partial(project_kernel, count=tiles, scaled=scaled, first=first),
            "project",
            shapes,
            [*pieces, stacked],
            0,
            place,
        )

    def staged(weights):
        blocks = weights[0].shape[1] // channels
        height = (weights[0].shape[0] + weights[1].shape[0] + share // blocks) // cores
        shapes = [(w.shape, BF16) for w in weights] + [((height, weights[0].shape[1]), BF16)]
        return run_kernel(
            functools.partial(stage_kernel, cores=cores),
            "stage",
            shapes,
            [pltpu.with_memory_space_constraint(w, pltpu.HBM) for w in weights],
            0,
            place,
            [pltpu.SemaphoreType.DMA((len(weights) + 2 + blocks,))],
            HBM,
        )

    def unpacked(half):
        return run_kernel(
            unpack_kernel,
            "unpack",
            [(w.shape, BF16) for w in (self_out, cross_out, reassemble)],
            [half, *across(half)],
            0,
            place,
        )

    def attend(query, packs, state=(), final=False):
        heads = columns // HD
        shapes = [((heads, rows, HD), F32), ((heads, rows, 2), F32)]
        if final:
            shapes = [((rows, columns), BF16)]
        return run_kernel(
            functools.partial(
                attend_kernel, packed=len(packs), resumed=len(state) > 0, final=final
            ),
            "attend",
            shapes,
            [query, *packs, *state],
        )

    left_here = moved(left_tokens[0])
    self_out, cross_out, reassemble, right_own, self_qkv, cross_qkv, taps, half = staged(
        [self_out, cross_out, reassemble, right_tokens[0], self_qkv, cross_qkv, taps]
    )
    left = tile_pieces(left_here)
    right = [right_own, *tile_pieces(right_tokens[0])[1:]]
    (right_pack,) = project(right, cross_qkv, False, 1)
    right_pack = moved(right_pack)
    query, pack = project(left, self_qkv, True, 0)
    beside = neighbours(tied(pack, right_pack))
    halves = tile_pieces(tied(half, left_here))[1:]
    near, halves = lax.optimization_barrier(([pack, *beside], halves))
    far = [q for p in near for q in across(p)]
    state = attend(query, grouped(near))
    right_pack = tied(right_pack, state)
    right_near = [right_pack, *neighbours(right_pack)]
    far, halves = lax.optimization_barrier((far, halves))
    others = [unpacked(half) for half in halves]
    (own_mixed,) = attend(query, grouped(far), state, True)

    mixed = tile_pieces(own_mixed)
    updated, cross_query = run_kernel(
        functools.partial(update_kernel, count=tiles),
        "update",
        [((tiles, rows, share), BF16), ((rows, columns), BF16)],
        [*mixed, self_out, *[o[0] for o in others], *left,
            cross_qkv.reshape(3, tiles, share, columns)],
        0,
        place,
    )
    right_near = tied(right_near, updated)
    right_far = [q for p in right_near for q in across(p)]
    state = attend(cross_query, grouped(right_near))
    right_far = tied(right_far, state)
    (mixed,) = attend(cross_query, grouped(right_far), state, True)
    mixed = tile_pieces(mixed)
    (window,) = run_kernel(
        functools.partial(finish_kernel, count=tiles, width=width),
        "finish",
        [((band_rows, width + 2 * EDGE, channels), BF16)],
        [
            *mixed,
            cross_out,
            *[o[1] for o in others],
            updated,
            reassemble,
            *[o[2] for o in others],
        ],
        0,
        place,
        [pltpu.VMEM((band_rows, GRID_W + 2 * EDGE, channels), BF16)],
    )
    back = lax.ppermute(window, both, [(worker(*p), home(*p)) for p in places])
    above = lax.ppermute(
        window[-1:], both, [(worker(b, p), home(b + 1, p)) for b, p in places if b + 1 < bands]
    )
    below = lax.ppermute(
        window[:1], both, [(worker(b, p), home(b - 1, p)) for b, p in places if b > 0]
    )
    (joined,) = run_kernel(
        conv_kernel,
        "join",
        [((band_rows, width, channels), BF16)],
        [back, above, below, taps],
    )
    return joined[None]


def solution(mesh):
    placed = (
        P(("groups", "pair"), "blk", "tile"),
        P(("groups", "pair"), "blk", "tile"),
        P(None, None, "tile"),
        P("tile", None),
        P(None, None, "tile"),
        P("tile", None),
        P("tile", None),
        P(),
    )
    return jax.shard_map(
        body,
        mesh=mesh,
        in_specs=placed,
        out_specs=P(("groups", "pair"), "blk", "tile", None),
        check_vma=False,
    )
```

```python
import functools
import math

import jax
import jax.numpy as jnp
from jax import lax
from jax.experimental import pallas as pl
from jax.experimental.pallas import tpu as pltpu
from jax.sharding import PartitionSpec as P

HD = 64
GRID_W = 128
EDGE = 16
F32 = jnp.float32
BF16 = jnp.bfloat16
QUERY_SCALE = math.log2(math.e) * HD**-0.5
VMEM = pl.BlockSpec(memory_space=pltpu.VMEM)
HBM = pl.BlockSpec(memory_space=pl.ANY)


def run_kernel(kernel, name, shapes, operands, scratch=(), space=VMEM):
    return pl.pallas_call(
        kernel,
        out_shape=[jax.ShapeDtypeStruct(*s) for s in shapes],
        in_specs=[space] * len(operands),
        out_specs=[VMEM] * len(shapes),
        scratch_shapes=scratch,
        compiler_params=pltpu.CompilerParams(vmem_limit_bytes=24 << 20),
        cost_estimate=pl.CostEstimate(flops=0, bytes_accessed=0, transcendentals=0),
        name=name,
    )(*operands)


def slot_of(step, count):
    return lax.rem(lax.axis_index("tile") + step, count)


def normalized(pieces):
    widened = [piece.astype(F32) for piece in pieces]
    width = sum(piece.shape[1] for piece in widened)
    mean = sum(jnp.sum(piece, axis=1, keepdims=True) for piece in widened) / width
    centred = [piece - mean for piece in widened]
    variance = sum(jnp.sum(piece * piece, axis=1, keepdims=True) for piece in centred) / width
    scale = lax.rsqrt(variance + 1e-06)
    return [(piece * scale).astype(BF16) for piece in centred]


def dot(left, right):
    return jnp.dot(left, right, preferred_element_type=F32)


def project_kernel(*refs, count, scaled, first):
    pieces, weight, outs = refs[:count], refs[count], refs[count + 1 :]
    normed = normalized([piece[...] for piece in pieces])
    products = []
    for which in range(first, weight.shape[0]):
        products.append(
            sum(dot(normed[step], weight[which, slot_of(step, count)]) for step in range(count))
        )
    if scaled:
        outs[0][...] = (products.pop(0) * QUERY_SCALE).astype(BF16)
    columns = weight.shape[3]
    for which, product in enumerate(products):
        outs[-1][:, which * columns : (which + 1) * columns] = product.astype(BF16)


def attended(query, packs, state, index):
    columns = query.shape[1]
    start = index * HD
    head = slice(start, start + HD)
    values = slice(columns + start, columns + start + HD)
    asked = query[:, head]
    scores = [
        lax.dot_general(asked, pack[:, head], (((1,), (1,)), ((), ())), preferred_element_type=F32)
        for pack in packs
    ]
    tops = [jnp.max(score, axis=1, keepdims=True) for score in scores]
    total, mixed = 0.0, 0.0
    if state:
        before, stats = state[0][index], state[1][index]
        tops.append(stats[:, :1])
    maxima = functools.reduce(jnp.maximum, tops)
    if state:
        correction = jnp.exp2(stats[:, :1] - maxima)
        total = stats[:, 1:2] * correction
        mixed = before * correction
    for score, pack in zip(scores, packs):
        expanded = jnp.exp2(score - maxima)
        total = total + jnp.sum(expanded, axis=1, keepdims=True)
        mixed = mixed + dot(expanded.astype(BF16), pack[:, values])
    return mixed, maxima, total


def begin_kernel(query, *refs):
    packs, (mixed_out, stats_out) = refs[:-2], refs[-2:]
    for index in range(query.shape[1] // HD):
        mixed, maxima, total = attended(query, packs, (), index)
        mixed_out[index] = mixed
        stats_out[index] = jnp.concatenate([maxima, total], axis=1)


def ended(query, packs, state):
    heads = []
    for index in range(query.shape[1] // HD):
        mixed, maxima, total = attended(query, packs, state, index)
        heads.append(mixed / total)
    return jnp.concatenate(heads, axis=1).astype(BF16)


def end_kernel(query, *refs):
    refs[-1][...] = ended(query, refs[:-3], refs[-3:-1])


def fill_board(board, values):
    band_rows, channels = board.shape[0], board.shape[2]
    edge = jnp.zeros((band_rows, EDGE, channels), board.dtype)
    board[:, :EDGE, :] = edge
    board[:, EDGE + GRID_W :, :] = edge
    inner = values.reshape(band_rows, GRID_W, channels)
    board[:, EDGE : EDGE + GRID_W, :] = inner.astype(board.dtype)


def window_of(board, slot, out):
    start = pl.multiple_of(slot * (out.shape[1] - 2 * EDGE), EDGE)
    out[...] = board[:, pl.ds(start, out.shape[1]), :]


def end_map_kernel(query, *refs, count):
    composed, outs, board = refs[-2 - count], refs[-1 - count : -1], refs[-1]
    packs, state = refs[: -4 - count], refs[-4 - count : -2 - count]
    fill_board(board, dot(ended(query, packs, state), composed[...]))
    for step, out in enumerate(outs):
        window_of(board, slot_of(count - step, count), out)


def carry_kernel(updated, *refs):
    pieces, out, board = refs[:-2], refs[-2], refs[-1]
    fill_board(board, sum(dot(updated[i], piece[...]) for i, piece in enumerate(pieces)))
    window_of(board, lax.axis_index("tile"), out)


def add_kernel(*refs):
    refs[-1][...] = sum(ref[...].astype(F32) for ref in refs[:-1]).astype(BF16)


def stage_kernel(*refs, cores):
    count = (len(refs) - 2) // 2
    sources, outs, half, sems = refs[:count], refs[count : 2 * count], refs[-2], refs[-1]
    core = lax.axis_index("pair")
    pairs = list(zip(sources, outs))
    rows = sources[0].shape[0] // cores
    begin = pl.multiple_of(core * rows, rows)
    pairs.append((sources[0].at[pl.ds(begin, rows)], half.at[pl.ds(0, rows)]))
    start = rows
    blocks = half.shape[1] // sources[1].shape[1]
    block = sources[1].shape[0] // blocks
    rows = block // cores
    for index in range(blocks):
        begin = pl.multiple_of(core * rows + index * block, rows)
        lanes = pl.ds(index * sources[1].shape[1], sources[1].shape[1])
        pairs.append((sources[1].at[pl.ds(begin, rows)], half.at[pl.ds(start, rows), lanes]))
    copies = [pltpu.make_async_copy(a, b, sems.at[i]) for i, (a, b) in enumerate(pairs)]
    for copy in copies:
        copy.start()
    for copy in copies:
        copy.wait()


def unpack_kernel(*refs):
    halves, outs = refs[:-2], refs[-2:]
    for step, half in enumerate(halves):
        core = lax.rem(lax.axis_index("pair") + step, len(halves))
        rows = outs[0].shape[0] // len(halves)
        outs[0][pl.ds(pl.multiple_of(core * rows, rows), rows), :] = half[:rows, :]
        start = rows
        blocks = half.shape[1] // outs[1].shape[1]
        block = outs[1].shape[0] // blocks
        rows = block // len(halves)
        for index in range(blocks):
            first = pl.multiple_of(core * rows + index * block, rows)
            lanes = slice(index * outs[1].shape[1], (index + 1) * outs[1].shape[1])
            outs[1][pl.ds(first, rows), :] = half[start : start + rows, lanes]


def pick(options, slot):
    chosen = options[0]
    for index in range(1, len(options)):
        chosen = jnp.where(slot == index, options[index], chosen)
    return chosen


def feature_shares(whole, count):
    share = whole.shape[1] // count
    options = [whole[:, i * share : (i + 1) * share] for i in range(count)]
    return [pick(options, slot_of(step, count)) for step in range(count)]


def compose_kernel(weight, *refs):
    pieces, out = refs[:-1], refs[-1]
    shares = feature_shares(weight[...].astype(F32), len(pieces))
    out[...] = sum(dot(s.astype(BF16), p[...]) for s, p in zip(shares, pieces)).astype(BF16)


def update_kernel(*refs, count):
    mixed, weights = refs[:count], refs[count : 2 * count]
    tokens, query_weight = refs[2 * count : 3 * count], refs[3 * count]
    updated, query = refs[3 * count + 1 :]
    whole = sum(dot(m[...], w[...]) for m, w in zip(mixed, weights))
    pieces = []
    for step, term in enumerate(feature_shares(whole, count)):
        piece = (tokens[step][...].astype(F32) + term).astype(BF16)
        updated[step] = piece
        pieces.append(piece)
    normed = normalized(pieces)
    product = sum(
        dot(normed[step], query_weight[0, slot_of(step, count)]) for step in range(count)
    )
    query[...] = (product * QUERY_SCALE).astype(BF16)


def conv_kernel(window, above, below, weight, out):
    width = out.shape[1]
    band_rows, channels = out.shape[0], out.shape[2]
    grid = jnp.concatenate([above[...], window[...], below[...]], axis=0).astype(F32)
    active = jnp.maximum(grid, 0.0)
    total = grid[1 : 1 + band_rows, EDGE : EDGE + width, :].reshape(band_rows * width, channels)
    for column in range(3):
        first = EDGE - 1 + column
        shifted = active[:, first : first + width, :].astype(BF16)
        for row in range(3):
            rows = shifted[row : row + band_rows].reshape(band_rows * width, channels)
            total = total + dot(rows, weight[row, column])
    out[...] = total.reshape(out.shape).astype(BF16)


def body(left_tokens, right_tokens, self_qkv, self_out, cross_qkv, cross_out, reassemble, taps):
    bands, tiles, cores = (lax.axis_size(axis) for axis in ("blk", "tile", "pair"))
    span = bands // cores
    both = ("blk", "pair")
    rows, share = left_tokens.shape[1:]
    columns = self_qkv.shape[2]
    channels = reassemble.shape[1]
    width = GRID_W // tiles
    band_rows = rows // GRID_W
    heads = columns // HD
    window = (band_rows, width + 2 * EDGE, channels)
    board = (band_rows, GRID_W + 2 * EDGE, channels)

    def home(band, pair):
        return band * cores + pair

    def worker(band, pair):
        shift = (pair - band // span) % cores
        return ((band + shift * span) % bands) * cores + (pair - shift) % cores

    places = [(band, pair) for band in range(bands) for pair in range(cores)]
    there = [(home(*p), worker(*p)) for p in places]
    back = [(worker(*p), home(*p)) for p in places]
    down = [(worker(b, p), worker(b + 1, p)) for b, p in places if b + 1 < bands]
    up = [(worker(b, p), worker(b - 1, p)) for b, p in places if b > 0]

    def tied(values, *others):
        return lax.optimization_barrier((values, others))[0]

    def from_tile(value, step):
        return lax.ppermute(value, "tile", [((i + step) % tiles, i) for i in range(tiles)])

    def tile_pieces(own):
        return [own, *[from_tile(own, s) for s in range(1, tiles)]]

    def neighbours(pack):
        ring = [(g * span, i) for g in range(cores) for i in range(span)]
        return [
            lax.ppermute(pack, "blk", [(g + (i + s) % span, g + i) for g, i in ring])
            for s in range(1, span)
        ]

    def across(pack):
        return [
            lax.ppermute(pack, "pair", [((i + s) % cores, i) for i in range(cores)])
            for s in range(1, cores)
        ]

    def grouped(packs):
        return packs if len(packs) < 3 else [jnp.concatenate(packs)]

    def project(pieces, weights, scaled, first):
        return run_kernel(
            functools.partial(project_kernel, count=tiles, scaled=scaled, first=first),
            "project",
            [((rows, columns), BF16)] * scaled + [((rows, 2 * columns), BF16)],
            [*pieces, weights.reshape(3, tiles, share, columns)],
        )

    def begin(query, packs):
        shapes = [((heads, rows, HD), F32), ((heads, rows, 2), F32)]
        return run_kernel(begin_kernel, "begin", shapes, [query, *grouped(packs)])

    def staged(weights):
        blocks = weights[0].shape[1] // channels
        height = (weights[0].shape[0] + share // blocks) // cores
        return run_kernel(
            functools.partial(stage_kernel, cores=cores),
            "stage",
            [(w.shape, BF16) for w in weights] + [((height, weights[0].shape[1]), BF16)],
            [pltpu.with_memory_space_constraint(w, pltpu.HBM) for w in weights],
            [pltpu.SemaphoreType.DMA((len(weights) + 1 + blocks,))],
            pl.BlockSpec(memory_space=pl.ANY),
        )

    left_here = lax.ppermute(left_tokens[0], both, there)
    self_out, reassemble, cross_out, right_own, self_qkv, cross_qkv, taps, half = staged(
        [self_out, reassemble, cross_out, right_tokens[0], self_qkv, cross_qkv, taps]
    )
    left = tile_pieces(left_here)
    right = [right_own, *[from_tile(right_tokens[0], s) for s in range(1, tiles)]]
    (right_pack,) = project(right, cross_qkv, False, 1)
    right_pack = lax.ppermute(right_pack, both, there)
    query, pack = project(left, self_qkv, True, 0)
    beside = neighbours(tied(pack, right_pack))
    halves = tile_pieces(tied(half, left))[1:]
    near, halves = lax.optimization_barrier(([pack, *beside], halves))
    far = [q for p in near for q in across(p)]
    state = begin(query, near)
    right_pack = tied(right_pack, state)
    right_near = [right_pack, *neighbours(right_pack)]
    others = [
        run_kernel(
            unpack_kernel,
            "unpack",
            [(w.shape, BF16) for w in (self_out, reassemble)],
            [half, *across(half)],
        )
        for half in halves
    ]
    (mixed,) = run_kernel(
        end_kernel, "end", [((rows, columns), BF16)], [query, *grouped(far), *state]
    )

    map_weights = [reassemble, *[other[1] for other in others]]
    (composed,) = run_kernel(
        compose_kernel, "compose", [((columns, channels), BF16)], [cross_out, *map_weights]
    )
    mixed, composed = lax.optimization_barrier((tile_pieces(mixed), composed))
    updated, cross_query = run_kernel(
        functools.partial(update_kernel, count=tiles),
        "update",
        [((tiles, rows, share), BF16), ((rows, columns), BF16)],
        [
            *mixed,
            self_out,
            *[other[0] for other in others],
            *left,
            cross_qkv.reshape(3, tiles, share, columns),
        ],
    )
    right_near = tied(right_near, updated)
    right_far = [q for p in right_near for q in across(p)]
    state = begin(cross_query, right_near)
    right_far = tied(right_far, state)
    maps = run_kernel(
        functools.partial(end_map_kernel, count=tiles),
        "end_map",
        [(window, BF16)] * tiles,
        [cross_query, *grouped(right_far), *state, composed],
        [pltpu.VMEM(board, BF16)],
    )
    (carried,) = run_kernel(
        carry_kernel,
        "carry",
        [(window, F32)],
        [tied(updated, maps), *map_weights],
        [pltpu.VMEM(board, F32)],
    )
    received = [from_tile(part, s) for s, part in enumerate(maps) if s > 0]
    (features,) = run_kernel(add_kernel, "add", [(window, BF16)], [carried, maps[0], *received])
    above = lax.ppermute(features[-1:], both, down)
    below = lax.ppermute(features[:1], both, up)
    (joined,) = run_kernel(
        conv_kernel,
        "join",
        [((band_rows, width, channels), BF16)],
        [features, above, below, taps],
    )
    return lax.ppermute(joined, both, back)[None]


def solution(mesh):
    placed = (
        P(("groups", "pair"), "blk", "tile"),
        P(("groups", "pair"), "blk", "tile"),
        P(None, None, "tile"),
        P("tile", None),
        P(None, None, "tile"),
        P("tile", None),
        P("tile", None),
        P(),
    )
    return jax.shard_map(
        body,
        mesh=mesh,
        in_specs=placed,
        out_specs=P(("groups", "pair"), "blk", "tile", None),
        check_vma=False,
    )
```

```python
import functools
import math

import jax
import jax.numpy as jnp
from jax import lax
from jax.experimental import pallas as pl
from jax.experimental.pallas import tpu as pltpu
from jax.sharding import PartitionSpec as P

HD = 64
GRID_W = 128
EDGE = 16
F32 = jnp.float32
BF16 = jnp.bfloat16
QUERY_SCALE = math.log2(math.e) * HD**-0.5
VMEM = pl.BlockSpec(memory_space=pltpu.VMEM)
HBM = pl.BlockSpec(memory_space=pl.ANY)


def run_kernel(kernel, name, shapes, operands, scratch=(), space=VMEM):
    return pl.pallas_call(
        kernel,
        out_shape=[jax.ShapeDtypeStruct(*s) for s in shapes],
        in_specs=[space] * len(operands),
        out_specs=[VMEM] * len(shapes),
        scratch_shapes=scratch,
        compiler_params=pltpu.CompilerParams(vmem_limit_bytes=24 << 20),
        cost_estimate=pl.CostEstimate(flops=0, bytes_accessed=0, transcendentals=0),
        name=name,
    )(*operands)


def slot_of(step, count):
    return lax.rem(lax.axis_index("tile") + step, count)


def normalized(pieces):
    widened = [piece.astype(F32) for piece in pieces]
    width = sum(piece.shape[1] for piece in widened)
    mean = sum(jnp.sum(piece, axis=1, keepdims=True) for piece in widened) / width
    centred = [piece - mean for piece in widened]
    variance = sum(jnp.sum(piece * piece, axis=1, keepdims=True) for piece in centred) / width
    scale = lax.rsqrt(variance + 1e-06)
    return [(piece * scale).astype(BF16) for piece in centred]


def dot(left, right):
    return jnp.dot(left, right, preferred_element_type=F32)


def project_kernel(*refs, count, scaled, first):
    pieces, weight, outs = refs[:count], refs[count], refs[count + 1 :]
    normed = normalized([piece[...] for piece in pieces])
    products = []
    for which in range(first, weight.shape[0]):
        products.append(
            sum(dot(normed[step], weight[which, slot_of(step, count)]) for step in range(count))
        )
    if scaled:
        outs[0][...] = (products.pop(0) * QUERY_SCALE).astype(BF16)
    columns = weight.shape[3]
    for which, product in enumerate(products):
        outs[-1][:, which * columns : (which + 1) * columns] = product.astype(BF16)


def attended(query, packs, state, index):
    columns = query.shape[1]
    start = index * HD
    head = slice(start, start + HD)
    values = slice(columns + start, columns + start + HD)
    asked = query[:, head]
    scores = [
        lax.dot_general(asked, pack[:, head], (((1,), (1,)), ((), ())), preferred_element_type=F32)
        for pack in packs
    ]
    tops = [jnp.max(score, axis=1, keepdims=True) for score in scores]
    total, mixed = 0.0, 0.0
    if state:
        before, stats = state[0][index], state[1][index]
        tops.append(stats[:, :1])
    maxima = functools.reduce(jnp.maximum, tops)
    if state:
        correction = jnp.exp2(stats[:, :1] - maxima)
        total = stats[:, 1:2] * correction
        mixed = before * correction
    for score, pack in zip(scores, packs):
        expanded = jnp.exp2(score - maxima)
        total = total + jnp.sum(expanded, axis=1, keepdims=True)
        mixed = mixed + dot(expanded.astype(BF16), pack[:, values])
    return mixed, maxima, total


def begin_kernel(query, *refs):
    packs, (mixed_out, stats_out) = refs[:-2], refs[-2:]
    for index in range(query.shape[1] // HD):
        mixed, maxima, total = attended(query, packs, (), index)
        mixed_out[index] = mixed
        stats_out[index] = jnp.concatenate([maxima, total], axis=1)


def ended(query, packs, state):
    heads = []
    for index in range(query.shape[1] // HD):
        mixed, maxima, total = attended(query, packs, state, index)
        heads.append(mixed / total)
    return jnp.concatenate(heads, axis=1).astype(BF16)


def end_kernel(query, *refs):
    refs[-1][...] = ended(query, refs[:-3], refs[-3:-1])


def fill_board(board, values):
    band_rows, channels = board.shape[0], board.shape[2]
    edge = jnp.zeros((band_rows, EDGE, channels), board.dtype)
    board[:, :EDGE, :] = edge
    board[:, EDGE + GRID_W :, :] = edge
    inner = values.reshape(band_rows, GRID_W, channels)
    board[:, EDGE : EDGE + GRID_W, :] = inner.astype(board.dtype)


def window_of(board, slot, out):
    start = pl.multiple_of(slot * (out.shape[1] - 2 * EDGE), EDGE)
    out[...] = board[:, pl.ds(start, out.shape[1]), :].astype(out.dtype)


def end_map_kernel(query, *refs, count):
    composed, outs, board = refs[-2 - count], refs[-1 - count : -1], refs[-1]
    packs, state = refs[: -4 - count], refs[-4 - count : -2 - count]
    fill_board(board, dot(ended(query, packs, state), composed[...]))
    for step, out in enumerate(outs):
        window_of(board, slot_of(count - step, count), out)


def carry_kernel(updated, *refs):
    pieces, out, board = refs[:-2], refs[-2], refs[-1]
    fill_board(board, sum(dot(updated[i], piece[...]) for i, piece in enumerate(pieces)))
    window_of(board, lax.axis_index("tile"), out)


def add_kernel(*refs):
    refs[-1][...] = sum(ref[...].astype(F32) for ref in refs[:-1]).astype(BF16)


def stage_kernel(*refs, cores):
    count = (len(refs) - 2) // 2
    sources, outs, half, sems = refs[:count], refs[count : 2 * count], refs[-2], refs[-1]
    core = lax.axis_index("pair")
    pairs = list(zip(sources, outs))
    rows = sources[0].shape[0] // cores
    begin = pl.multiple_of(core * rows, rows)
    pairs.append((sources[0].at[pl.ds(begin, rows)], half.at[pl.ds(0, rows)]))
    start = rows
    blocks = half.shape[1] // sources[1].shape[1]
    block = sources[1].shape[0] // blocks
    rows = block // cores
    for index in range(blocks):
        begin = pl.multiple_of(core * rows + index * block, rows)
        lanes = pl.ds(index * sources[1].shape[1], sources[1].shape[1])
        pairs.append((sources[1].at[pl.ds(begin, rows)], half.at[pl.ds(start, rows), lanes]))
    copies = [pltpu.make_async_copy(a, b, sems.at[i]) for i, (a, b) in enumerate(pairs)]
    for copy in copies:
        copy.start()
    for copy in copies:
        copy.wait()


def unpack_kernel(*refs):
    halves, outs = refs[:-2], refs[-2:]
    for step, half in enumerate(halves):
        core = lax.rem(lax.axis_index("pair") + step, len(halves))
        rows = outs[0].shape[0] // len(halves)
        outs[0][pl.ds(pl.multiple_of(core * rows, rows), rows), :] = half[:rows, :]
        start = rows
        blocks = half.shape[1] // outs[1].shape[1]
        block = outs[1].shape[0] // blocks
        rows = block // len(halves)
        for index in range(blocks):
            first = pl.multiple_of(core * rows + index * block, rows)
            lanes = slice(index * outs[1].shape[1], (index + 1) * outs[1].shape[1])
            outs[1][pl.ds(first, rows), :] = half[start : start + rows, lanes]


def pick(options, slot):
    chosen = options[0]
    for index in range(1, len(options)):
        chosen = jnp.where(slot == index, options[index], chosen)
    return chosen


def feature_shares(whole, count):
    share = whole.shape[1] // count
    options = [whole[:, i * share : (i + 1) * share] for i in range(count)]
    return [pick(options, slot_of(step, count)) for step in range(count)]


def compose_kernel(weight, *refs):
    pieces, out = refs[:-1], refs[-1]
    shares = feature_shares(weight[...].astype(F32), len(pieces))
    out[...] = sum(dot(s.astype(BF16), p[...]) for s, p in zip(shares, pieces)).astype(BF16)


def update_kernel(*refs, count):
    mixed, weights = refs[:count], refs[count : 2 * count]
    tokens, query_weight = refs[2 * count : 3 * count], refs[3 * count]
    updated, query = refs[3 * count + 1 :]
    whole = sum(dot(m[...], w[...]) for m, w in zip(mixed, weights))
    pieces = []
    for step, term in enumerate(feature_shares(whole, count)):
        piece = (tokens[step][...].astype(F32) + term).astype(BF16)
        updated[step] = piece
        pieces.append(piece)
    normed = normalized(pieces)
    product = sum(
        dot(normed[step], query_weight[0, slot_of(step, count)]) for step in range(count)
    )
    query[...] = (product * QUERY_SCALE).astype(BF16)


def conv_kernel(window, above, below, weight, out):
    width = out.shape[1]
    band_rows, channels = out.shape[0], out.shape[2]
    grid = jnp.concatenate([above[...], window[...], below[...]], axis=0).astype(F32)
    active = jnp.maximum(grid, 0.0)
    total = grid[1 : 1 + band_rows, EDGE : EDGE + width, :].reshape(band_rows * width, channels)
    for column in range(3):
        first = EDGE - 1 + column
        shifted = active[:, first : first + width, :].astype(BF16)
        for row in range(3):
            rows = shifted[row : row + band_rows].reshape(band_rows * width, channels)
            total = total + dot(rows, weight[row, column])
    out[...] = total.reshape(out.shape).astype(BF16)


def body(left_tokens, right_tokens, self_qkv, self_out, cross_qkv, cross_out, reassemble, taps):
    bands, tiles, cores = (lax.axis_size(axis) for axis in ("blk", "tile", "pair"))
    span = bands // cores
    both = ("blk", "pair")
    rows, share = left_tokens.shape[1:]
    columns = self_qkv.shape[2]
    channels = reassemble.shape[1]
    width = GRID_W // tiles
    band_rows = rows // GRID_W
    heads = columns // HD
    window = (band_rows, width + 2 * EDGE, channels)
    board = (band_rows, GRID_W + 2 * EDGE, channels)

    def home(band, pair):
        return band * cores + pair

    def worker(band, pair):
        shift = (pair - band // span) % cores
        return ((band + shift * span) % bands) * cores + (pair - shift) % cores

    places = [(band, pair) for band in range(bands) for pair in range(cores)]
    there = [(home(*p), worker(*p)) for p in places]
    back = [(worker(*p), home(*p)) for p in places]
    down = [(worker(b, p), home(b + 1, p)) for b, p in places if b + 1 < bands]
    up = [(worker(b, p), home(b - 1, p)) for b, p in places if b > 0]
    stays = [home(*p) for p in places if home(*p) == worker(*p)]
    comes = [worker(*p) for p in places if home(*p) != worker(*p)]

    def tile_swaps(value, members, step):
        def flat(position, tile):
            return (position // cores * tiles + tile) * cores + position % cores

        pairs = [(flat(m, (i + step) % tiles), flat(m, i)) for m in members for i in range(tiles)]
        return lax.ppermute(value, ("blk", "tile", "pair"), pairs)

    def tied(values, *others):
        return lax.optimization_barrier((values, others))[0]

    def from_tile(value, step):
        return lax.ppermute(value, "tile", [((i + step) % tiles, i) for i in range(tiles)])

    def tile_pieces(own):
        return [own, *[from_tile(own, s) for s in range(1, tiles)]]

    def neighbours(pack):
        ring = [(g * span, i) for g in range(cores) for i in range(span)]
        return [
            lax.ppermute(pack, "blk", [(g + (i + s) % span, g + i) for g, i in ring])
            for s in range(1, span)
        ]

    def across(pack):
        return [
            lax.ppermute(pack, "pair", [((i + s) % cores, i) for i in range(cores)])
            for s in range(1, cores)
        ]

    def grouped(packs):
        return packs if len(packs) < 3 else [jnp.concatenate(packs)]

    def project(pieces, weights, scaled, first):
        return run_kernel(
            functools.partial(project_kernel, count=tiles, scaled=scaled, first=first),
            "project",
            [((rows, columns), BF16)] * scaled + [((rows, 2 * columns), BF16)],
            [*pieces, weights.reshape(3, tiles, share, columns)],
        )

    def begin(query, packs):
        shapes = [((heads, rows, HD), F32), ((heads, rows, 2), F32)]
        return run_kernel(begin_kernel, "begin", shapes, [query, *grouped(packs)])

    def staged(weights):
        blocks = weights[0].shape[1] // channels
        height = (weights[0].shape[0] + share // blocks) // cores
        return run_kernel(
            functools.partial(stage_kernel, cores=cores),
            "stage",
            [(w.shape, BF16) for w in weights] + [((height, weights[0].shape[1]), BF16)],
            [pltpu.with_memory_space_constraint(w, pltpu.HBM) for w in weights],
            [pltpu.SemaphoreType.DMA((len(weights) + 1 + blocks,))],
            pl.BlockSpec(memory_space=pl.ANY),
        )

    left_here = lax.ppermute(left_tokens[0], both, there)
    steps = range(1, tiles)
    left_early = [tile_swaps(left_tokens[0], stays, s) for s in steps]
    self_out, reassemble, cross_out, right_own, self_qkv, cross_qkv, taps, half = staged(
        [self_out, reassemble, cross_out, right_tokens[0], self_qkv, cross_qkv, taps]
    )
    right = [right_own, *[from_tile(right_tokens[0], s) for s in steps]]
    (right_pack,) = project(right, cross_qkv, False, 1)
    left_here, right_pack = lax.optimization_barrier((left_here, right_pack))
    right_pack = lax.ppermute(right_pack, both, there)
    left_late = [tile_swaps(left_here, comes, s) for s in steps]
    left = [left_here, *[a + b for a, b in zip(left_early, left_late)]]
    query, pack = project(left, self_qkv, True, 0)
    beside = neighbours(pack)
    halves = tile_pieces(tied(half, left))[1:]
    near, halves, right_pack = lax.optimization_barrier(([pack, *beside], halves, right_pack))
    far = [q for p in near for q in across(p)]
    state = begin(query, near)
    right_pack = tied(right_pack, state)
    right_near = [right_pack, *neighbours(right_pack)]
    others = [
        run_kernel(
            unpack_kernel,
            "unpack",
            [(w.shape, BF16) for w in (self_out, reassemble)],
            [half, *across(half)],
        )
        for half in halves
    ]
    (mixed,) = run_kernel(
        end_kernel, "end", [((rows, columns), BF16)], [query, *grouped(far), *state]
    )

    map_weights = [reassemble, *[other[1] for other in others]]
    (composed,) = run_kernel(
        compose_kernel, "compose", [((columns, channels), BF16)], [cross_out, *map_weights]
    )
    mixed, composed = lax.optimization_barrier((tile_pieces(mixed), composed))
    updated, cross_query = run_kernel(
        functools.partial(update_kernel, count=tiles),
        "update",
        [((tiles, rows, share), BF16), ((rows, columns), BF16)],
        [
            *mixed,
            self_out,
            *[other[0] for other in others],
            *left,
            cross_qkv.reshape(3, tiles, share, columns),
        ],
    )
    right_near = tied(right_near, updated)
    right_far = [q for p in right_near for q in across(p)]
    state = begin(cross_query, right_near)
    right_far = tied(right_far, state)
    maps = run_kernel(
        functools.partial(end_map_kernel, count=tiles),
        "end_map",
        [(window, BF16)] * tiles,
        [cross_query, *grouped(right_far), *state, composed],
        [pltpu.VMEM(board, F32)],
    )
    (carried,) = run_kernel(
        carry_kernel,
        "carry",
        [(window, F32)],
        [tied(updated, maps), *map_weights],
        [pltpu.VMEM(board, F32)],
    )
    received = [from_tile(part, s) for s, part in enumerate(maps) if s > 0]
    (features,) = run_kernel(add_kernel, "add", [(window, BF16)], [carried, maps[0], *received])
    above = lax.ppermute(features[-1:], both, down)
    below = lax.ppermute(features[:1], both, up)
    features = lax.ppermute(features, both, back)
    (joined,) = run_kernel(
        conv_kernel,
        "join",
        [((band_rows, width, channels), BF16)],
        [features, above, below, taps],
    )
    return joined[None]


def solution(mesh):
    placed = (
        P(("groups", "pair"), "blk", "tile"),
        P(("groups", "pair"), "blk", "tile"),
        P(None, None, "tile"),
        P("tile", None),
        P(None, None, "tile"),
        P("tile", None),
        P("tile", None),
        P(),
    )
    return jax.shard_map(
        body,
        mesh=mesh,
        in_specs=placed,
        out_specs=P(("groups", "pair"), "blk", "tile", None),
        check_vma=False,
    )
```

```python
import functools
import math

import jax
import jax.numpy as jnp
from jax import lax
from jax.experimental import pallas as pl
from jax.experimental.pallas import tpu as pltpu
from jax.sharding import PartitionSpec as P

HD = 64
GRID_W = 128
EDGE = 16
F32 = jnp.float32
BF16 = jnp.bfloat16
QUERY_SCALE = math.log2(math.e) * HD**-0.5
VMEM = pl.BlockSpec(memory_space=pltpu.VMEM)
HBM = pl.BlockSpec(memory_space=pl.ANY)


def run_kernel(kernel, name, shapes, operands, scratch=(), space=VMEM):
    return pl.pallas_call(
        kernel,
        out_shape=[jax.ShapeDtypeStruct(*s) for s in shapes],
        in_specs=[space] * len(operands),
        out_specs=[VMEM] * len(shapes),
        scratch_shapes=scratch,
        compiler_params=pltpu.CompilerParams(vmem_limit_bytes=24 << 20),
        cost_estimate=pl.CostEstimate(flops=0, bytes_accessed=0, transcendentals=0),
        name=name,
    )(*operands)


def slot_of(step, count):
    return lax.rem(lax.axis_index("tile") + step, count)


def normalized(pieces):
    widened = [piece.astype(F32) for piece in pieces]
    width = sum(piece.shape[1] for piece in widened)
    mean = sum(jnp.sum(piece, axis=1, keepdims=True) for piece in widened) / width
    centred = [piece - mean for piece in widened]
    variance = sum(jnp.sum(piece * piece, axis=1, keepdims=True) for piece in centred) / width
    scale = lax.rsqrt(variance + 1e-06)
    return [(piece * scale).astype(BF16) for piece in centred]


def dot(left, right):
    return jnp.dot(left, right, preferred_element_type=F32)


def project_kernel(*refs, count, scaled, first):
    pieces, weight, outs = refs[:count], refs[count], refs[count + 1 :]
    normed = normalized([piece[...] for piece in pieces])
    products = []
    for which in range(first, weight.shape[0]):
        products.append(
            sum(dot(normed[step], weight[which, slot_of(step, count)]) for step in range(count))
        )
    if scaled:
        outs[0][...] = (products.pop(0) * QUERY_SCALE).astype(BF16)
    columns = weight.shape[3]
    for which, product in enumerate(products):
        outs[-1][:, which * columns : (which + 1) * columns] = product.astype(BF16)


def attended(query, packs, state, index):
    columns = query.shape[1]
    start = index * HD
    head = slice(start, start + HD)
    values = slice(columns + start, columns + start + HD)
    asked = query[:, head]
    scores = [
        lax.dot_general(asked, pack[:, head], (((1,), (1,)), ((), ())), preferred_element_type=F32)
        for pack in packs
    ]
    tops = [jnp.max(score, axis=1, keepdims=True) for score in scores]
    total, mixed = 0.0, 0.0
    if state:
        before, stats = state[0][index], state[1][index]
        tops.append(stats[:, :1])
    maxima = functools.reduce(jnp.maximum, tops)
    if state:
        correction = jnp.exp2(stats[:, :1] - maxima)
        total = stats[:, 1:2] * correction
        mixed = before * correction
    for score, pack in zip(scores, packs):
        expanded = jnp.exp2(score - maxima)
        total = total + jnp.sum(expanded, axis=1, keepdims=True)
        mixed = mixed + dot(expanded.astype(BF16), pack[:, values])
    return mixed, maxima, total


def begin_kernel(query, *refs):
    packs, (mixed_out, stats_out) = refs[:-2], refs[-2:]
    for index in range(query.shape[1] // HD):
        mixed, maxima, total = attended(query, packs, (), index)
        mixed_out[index] = mixed
        stats_out[index] = jnp.concatenate([maxima, total], axis=1)


def ended(query, packs, state):
    heads = []
    for index in range(query.shape[1] // HD):
        mixed, maxima, total = attended(query, packs, state, index)
        heads.append(mixed / total)
    return jnp.concatenate(heads, axis=1).astype(BF16)


def end_kernel(query, *refs):
    refs[-1][...] = ended(query, refs[:-3], refs[-3:-1])


def fill_board(board, values):
    band_rows, channels = board.shape[0], board.shape[2]
    edge = jnp.zeros((band_rows, EDGE, channels), board.dtype)
    board[:, :EDGE, :] = edge
    board[:, EDGE + GRID_W :, :] = edge
    inner = values.reshape(band_rows, GRID_W, channels)
    board[:, EDGE : EDGE + GRID_W, :] = inner.astype(board.dtype)


def window_of(board, slot, out):
    start = pl.multiple_of(slot * (out.shape[1] - 2 * EDGE), EDGE)
    out[...] = board[:, pl.ds(start, out.shape[1]), :].astype(out.dtype)


def end_map_kernel(query, *refs, count):
    composed, outs, board = refs[-2 - count], refs[-1 - count : -1], refs[-1]
    packs, state = refs[: -4 - count], refs[-4 - count : -2 - count]
    fill_board(board, dot(ended(query, packs, state), composed[...]))
    for step, out in enumerate(outs):
        window_of(board, slot_of(count - step, count), out)


def carry_kernel(updated, *refs):
    pieces, out, board = refs[:-2], refs[-2], refs[-1]
    fill_board(board, sum(dot(updated[i], piece[...]) for i, piece in enumerate(pieces)))
    window_of(board, lax.axis_index("tile"), out)


def add_kernel(*refs):
    refs[-1][...] = sum(ref[...].astype(F32) for ref in refs[:-1]).astype(BF16)


def stage_kernel(*refs, cores):
    count = (len(refs) - 2) // 2
    sources, outs, half, sems = refs[:count], refs[count : 2 * count], refs[-2], refs[-1]
    core = lax.axis_index("pair")
    pairs = list(zip(sources, outs))
    rows = sources[0].shape[0] // cores
    begin = pl.multiple_of(core * rows, rows)
    pairs.append((sources[0].at[pl.ds(begin, rows)], half.at[pl.ds(0, rows)]))
    start = rows
    blocks = half.shape[1] // sources[1].shape[1]
    block = sources[1].shape[0] // blocks
    rows = block // cores
    for index in range(blocks):
        begin = pl.multiple_of(core * rows + index * block, rows)
        lanes = pl.ds(index * sources[1].shape[1], sources[1].shape[1])
        pairs.append((sources[1].at[pl.ds(begin, rows)], half.at[pl.ds(start, rows), lanes]))
    copies = [pltpu.make_async_copy(a, b, sems.at[i]) for i, (a, b) in enumerate(pairs)]
    for copy in copies:
        copy.start()
    for copy in copies:
        copy.wait()


def unpack_kernel(*refs):
    halves, outs = refs[:-2], refs[-2:]
    for step, half in enumerate(halves):
        core = lax.rem(lax.axis_index("pair") + step, len(halves))
        rows = outs[0].shape[0] // len(halves)
        outs[0][pl.ds(pl.multiple_of(core * rows, rows), rows), :] = half[:rows, :]
        start = rows
        blocks = half.shape[1] // outs[1].shape[1]
        block = outs[1].shape[0] // blocks
        rows = block // len(halves)
        for index in range(blocks):
            first = pl.multiple_of(core * rows + index * block, rows)
            lanes = slice(index * outs[1].shape[1], (index + 1) * outs[1].shape[1])
            outs[1][pl.ds(first, rows), :] = half[start : start + rows, lanes]


def pick(options, slot):
    chosen = options[0]
    for index in range(1, len(options)):
        chosen = jnp.where(slot == index, options[index], chosen)
    return chosen


def feature_shares(whole, count):
    share = whole.shape[1] // count
    options = [whole[:, i * share : (i + 1) * share] for i in range(count)]
    return [pick(options, slot_of(step, count)) for step in range(count)]


def compose_kernel(weight, *refs):
    pieces, out = refs[:-1], refs[-1]
    shares = feature_shares(weight[...].astype(F32), len(pieces))
    out[...] = sum(dot(s.astype(BF16), p[...]) for s, p in zip(shares, pieces)).astype(BF16)


def update_kernel(*refs, count):
    mixed, weights = refs[:count], refs[count : 2 * count]
    tokens, query_weight = refs[2 * count : 3 * count], refs[3 * count]
    updated, query = refs[3 * count + 1 :]
    whole = sum(dot(m[...], w[...]) for m, w in zip(mixed, weights))
    pieces = []
    for step, term in enumerate(feature_shares(whole, count)):
        piece = (tokens[step][...].astype(F32) + term).astype(BF16)
        updated[step] = piece
        pieces.append(piece)
    normed = normalized(pieces)
    product = sum(
        dot(normed[step], query_weight[0, slot_of(step, count)]) for step in range(count)
    )
    query[...] = (product * QUERY_SCALE).astype(BF16)


def conv_kernel(window, above, below, weight, out):
    width = out.shape[1]
    band_rows, channels = out.shape[0], out.shape[2]
    grid = jnp.concatenate([above[...], window[...], below[...]], axis=0).astype(F32)
    active = jnp.maximum(grid, 0.0)
    total = grid[1 : 1 + band_rows, EDGE : EDGE + width, :].reshape(band_rows * width, channels)
    for column in range(3):
        first = EDGE - 1 + column
        shifted = active[:, first : first + width, :].astype(BF16)
        for row in range(3):
            rows = shifted[row : row + band_rows].reshape(band_rows * width, channels)
            total = total + dot(rows, weight[row, column])
    out[...] = total.reshape(out.shape).astype(BF16)


def body(left_tokens, right_tokens, self_qkv, self_out, cross_qkv, cross_out, reassemble, taps):
    bands, tiles, cores = (lax.axis_size(axis) for axis in ("blk", "tile", "pair"))
    span = bands // cores
    both = ("blk", "pair")
    rows, share = left_tokens.shape[1:]
    columns = self_qkv.shape[2]
    channels = reassemble.shape[1]
    width = GRID_W // tiles
    band_rows = rows // GRID_W
    heads = columns // HD
    window = (band_rows, width + 2 * EDGE, channels)
    board = (band_rows, GRID_W + 2 * EDGE, channels)

    def home(band, pair):
        return band * cores + pair

    def worker(band, pair):
        shift = (pair - band // span) % cores
        return ((band + shift * span) % bands) * cores + (pair - shift) % cores

    places = [(band, pair) for band in range(bands) for pair in range(cores)]
    there = [(home(*p), worker(*p)) for p in places]
    back = [(worker(*p), home(*p)) for p in places]
    down = [(worker(b, p), home(b + 1, p)) for b, p in places if b + 1 < bands]
    up = [(worker(b, p), home(b - 1, p)) for b, p in places if b > 0]
    stays = [home(*p) for p in places if home(*p) == worker(*p)]
    comes = [worker(*p) for p in places if home(*p) != worker(*p)]

    def tile_swaps(value, members, step):
        def flat(position, tile):
            return (position // cores * tiles + tile) * cores + position % cores

        pairs = [(flat(m, (i + step) % tiles), flat(m, i)) for m in members for i in range(tiles)]
        return lax.ppermute(value, ("blk", "tile", "pair"), pairs)

    def tied(values, *others):
        return lax.optimization_barrier((values, others))[0]

    def from_tile(value, step):
        return lax.ppermute(value, "tile", [((i + step) % tiles, i) for i in range(tiles)])

    def tile_pieces(own):
        return [own, *[from_tile(own, s) for s in range(1, tiles)]]

    def neighbours(pack):
        ring = [(g * span, i) for g in range(cores) for i in range(span)]
        return [
            lax.ppermute(pack, "blk", [(g + (i + s) % span, g + i) for g, i in ring])
            for s in range(1, span)
        ]

    def across(pack):
        return [
            lax.ppermute(pack, "pair", [((i + s) % cores, i) for i in range(cores)])
            for s in range(1, cores)
        ]

    def grouped(packs):
        return packs if len(packs) < 3 else [jnp.concatenate(packs)]

    def project(pieces, weights, scaled, first):
        return run_kernel(
            functools.partial(project_kernel, count=tiles, scaled=scaled, first=first),
            "project",
            [((rows, columns), BF16)] * scaled + [((rows, 2 * columns), BF16)],
            [*pieces, weights.reshape(3, tiles, share, columns)],
        )

    def begin(query, packs):
        shapes = [((heads, rows, HD), F32), ((heads, rows, 2), F32)]
        return run_kernel(begin_kernel, "begin", shapes, [query, *grouped(packs)])

    def staged(weights):
        blocks = weights[0].shape[1] // channels
        height = (weights[0].shape[0] + share // blocks) // cores
        return run_kernel(
            functools.partial(stage_kernel, cores=cores),
            "stage",
            [(w.shape, BF16) for w in weights] + [((height, weights[0].shape[1]), BF16)],
            [pltpu.with_memory_space_constraint(w, pltpu.HBM) for w in weights],
            [pltpu.SemaphoreType.DMA((len(weights) + 1 + blocks,))],
            pl.BlockSpec(memory_space=pl.ANY),
        )

    left_here = lax.ppermute(left_tokens[0], both, there)
    steps = range(1, tiles)
    left_early = [tile_swaps(left_tokens[0], stays, s) for s in steps]
    self_out, reassemble, cross_out, right_own, self_qkv, cross_qkv, taps, half = staged(
        [self_out, reassemble, cross_out, right_tokens[0], self_qkv, cross_qkv, taps]
    )
    right = [right_own, *[from_tile(right_tokens[0], s) for s in steps]]
    right, left_early = lax.optimization_barrier((right, left_early))
    (right_pack,) = project(right, cross_qkv, False, 1)
    right_pack = lax.ppermute(right_pack, both, there)
    left_late = [tile_swaps(left_here, comes, s) for s in steps]
    left = [left_here, *[a + b for a, b in zip(left_early, left_late)]]
    query, pack = project(left, self_qkv, True, 0)
    halves = tile_pieces(half)[1:]
    pack, halves = lax.optimization_barrier((pack, halves))
    beside = neighbours(tied(pack, right_pack))
    near = [pack, *beside]
    far = [q for p in near for q in across(p)]
    state = begin(query, near)
    right_pack = tied(right_pack, state)
    right_near = [right_pack, *neighbours(right_pack)]
    others = [
        run_kernel(
            unpack_kernel,
            "unpack",
            [(w.shape, BF16) for w in (self_out, reassemble)],
            [half, *across(half)],
        )
        for half in halves
    ]
    (mixed,) = run_kernel(
        end_kernel, "end", [((rows, columns), BF16)], [query, *grouped(far), *state]
    )

    map_weights = [reassemble, *[other[1] for other in others]]
    (composed,) = run_kernel(
        compose_kernel, "compose", [((columns, channels), BF16)], [cross_out, *map_weights]
    )
    mixed, composed = lax.optimization_barrier((tile_pieces(mixed), composed))
    updated, cross_query = run_kernel(
        functools.partial(update_kernel, count=tiles),
        "update",
        [((tiles, rows, share), BF16), ((rows, columns), BF16)],
        [
            *mixed,
            self_out,
            *[other[0] for other in others],
            *left,
            cross_qkv.reshape(3, tiles, share, columns),
        ],
    )
    right_near = tied(right_near, updated)
    right_far = [q for p in right_near for q in across(p)]
    state = begin(cross_query, right_near)
    right_far = tied(right_far, state)
    maps = run_kernel(
        functools.partial(end_map_kernel, count=tiles),
        "end_map",
        [(window, BF16)] * tiles,
        [cross_query, *grouped(right_far), *state, composed],
        [pltpu.VMEM(board, F32)],
    )
    (carried,) = run_kernel(
        carry_kernel,
        "carry",
        [(window, F32)],
        [tied(updated, maps), *map_weights],
        [pltpu.VMEM(board, F32)],
    )
    received = [from_tile(part, s) for s, part in enumerate(maps) if s > 0]
    (features,) = run_kernel(add_kernel, "add", [(window, BF16)], [carried, maps[0], *received])
    above = lax.ppermute(features[-1:], both, down)
    below = lax.ppermute(features[:1], both, up)
    features = lax.ppermute(features, both, back)
    (joined,) = run_kernel(
        conv_kernel,
        "join",
        [((band_rows, width, channels), BF16)],
        [features, above, below, taps],
    )
    return joined[None]


def solution(mesh):
    placed = (
        P(("groups", "pair"), "blk", "tile"),
        P(("groups", "pair"), "blk", "tile"),
        P(None, None, "tile"),
        P("tile", None),
        P(None, None, "tile"),
        P("tile", None),
        P("tile", None),
        P(),
    )
    return jax.shard_map(
        body,
        mesh=mesh,
        in_specs=placed,
        out_specs=P(("groups", "pair"), "blk", "tile", None),
        check_vma=False,
    )
```

```python
import functools
import math

import jax
import jax.numpy as jnp
from jax import lax
from jax.experimental import pallas as pl
from jax.experimental.pallas import tpu as pltpu
from jax.sharding import PartitionSpec as P

HD = 64
GRID_W = 128
EDGE = 16
F32 = jnp.float32
BF16 = jnp.bfloat16
QUERY_SCALE = math.log2(math.e) * HD**-0.5
VMEM = pl.BlockSpec(memory_space=pltpu.VMEM)
HBM = pl.BlockSpec(memory_space=pl.ANY)


def run_kernel(kernel, name, shapes, operands, scratch=(), space=VMEM):
    return pl.pallas_call(
        kernel,
        out_shape=[jax.ShapeDtypeStruct(*s) for s in shapes],
        in_specs=[space] * len(operands),
        out_specs=[VMEM] * len(shapes),
        scratch_shapes=scratch,
        compiler_params=pltpu.CompilerParams(vmem_limit_bytes=24 << 20),
        cost_estimate=pl.CostEstimate(flops=0, bytes_accessed=0, transcendentals=0),
        name=name,
    )(*operands)


def slot_of(step, count):
    return lax.rem(lax.axis_index("tile") + step, count)


def normalized(pieces):
    widened = [piece.astype(F32) for piece in pieces]
    width = sum(piece.shape[1] for piece in widened)
    mean = sum(jnp.sum(piece, axis=1, keepdims=True) for piece in widened) / width
    centred = [piece - mean for piece in widened]
    variance = sum(jnp.sum(piece * piece, axis=1, keepdims=True) for piece in centred) / width
    scale = lax.rsqrt(variance + 1e-06)
    return [(piece * scale).astype(BF16) for piece in centred]


def dot(left, right):
    return jnp.dot(left, right, preferred_element_type=F32)


def project_kernel(*refs, count, wanted):
    pieces, weight, outs = refs[:count], refs[count], refs[count + 1 :]
    normed = normalized([piece[...] for piece in pieces])
    products = []
    for which in wanted:
        products.append(
            sum(dot(normed[step], weight[which, slot_of(step, count)]) for step in range(count))
        )
    if wanted[0] == 0:
        products[0] = products[0] * QUERY_SCALE
    outs[0][...] = jnp.concatenate([p.astype(BF16) for p in products], axis=1)


def attended(query, packs, state, index):
    columns = query.shape[1]
    start = index * HD
    head = slice(start, start + HD)
    values = slice(columns + start, columns + start + HD)
    asked = query[:, head]
    scores = [
        lax.dot_general(asked, pack[:, head], (((1,), (1,)), ((), ())), preferred_element_type=F32)
        for pack in packs
    ]
    tops = [jnp.max(score, axis=1, keepdims=True) for score in scores]
    total, mixed = 0.0, 0.0
    if state:
        before, stats = state[0][index], state[1][index]
        tops.append(stats[:, :1])
    maxima = functools.reduce(jnp.maximum, tops)
    if state:
        correction = jnp.exp2(stats[:, :1] - maxima)
        total = stats[:, 1:2] * correction
        mixed = before * correction
    for score, pack in zip(scores, packs):
        expanded = jnp.exp2(score - maxima)
        total = total + jnp.sum(expanded, axis=1, keepdims=True)
        mixed = mixed + dot(expanded.astype(BF16), pack[:, values])
    return mixed, maxima, total


def begin_kernel(query, *refs):
    packs, (mixed_out, stats_out) = refs[:-2], refs[-2:]
    for index in range(query.shape[1] // HD):
        mixed, maxima, total = attended(query, packs, (), index)
        mixed_out[index] = mixed
        stats_out[index] = jnp.concatenate([maxima, total], axis=1)


def ended(query, packs, state):
    heads = []
    for index in range(query.shape[1] // HD):
        mixed, maxima, total = attended(query, packs, state, index)
        heads.append(mixed / total)
    return jnp.concatenate(heads, axis=1).astype(BF16)


def end_kernel(query, *refs):
    refs[-1][...] = ended(query, refs[:-3], refs[-3:-1])


def fill_board(board, values):
    band_rows, channels = board.shape[0], board.shape[2]
    edge = jnp.zeros((band_rows, EDGE, channels), board.dtype)
    board[:, :EDGE, :] = edge
    board[:, EDGE + GRID_W :, :] = edge
    inner = values.reshape(band_rows, GRID_W, channels)
    board[:, EDGE : EDGE + GRID_W, :] = inner.astype(board.dtype)


def window_of(board, slot, out):
    start = pl.multiple_of(slot * (out.shape[1] - 2 * EDGE), EDGE)
    out[...] = board[:, pl.ds(start, out.shape[1]), :].astype(out.dtype)


def end_map_kernel(query, *refs, count):
    composed, outs, board = refs[-2 - count], refs[-1 - count : -1], refs[-1]
    packs, state = refs[: -4 - count], refs[-4 - count : -2 - count]
    fill_board(board, dot(ended(query, packs, state), composed[...]))
    for step, out in enumerate(outs):
        window_of(board, slot_of(count - step, count), out)


def carry_kernel(updated, *refs):
    pieces, out, board = refs[:-2], refs[-2], refs[-1]
    fill_board(board, sum(dot(updated[i], piece[...]) for i, piece in enumerate(pieces)))
    window_of(board, lax.axis_index("tile"), out)


def add_kernel(*refs):
    refs[-1][...] = sum(ref[...].astype(F32) for ref in refs[:-1]).astype(BF16)


def stage_kernel(*refs, cores):
    count = (len(refs) - 2) // 2
    sources, outs, half, sems = refs[:count], refs[count : 2 * count], refs[-2], refs[-1]
    core = lax.axis_index("pair")
    pairs = list(zip(sources, outs))
    rows = sources[0].shape[0] // cores
    begin = pl.multiple_of(core * rows, rows)
    pairs.append((sources[0].at[pl.ds(begin, rows)], half.at[pl.ds(0, rows)]))
    start = rows
    blocks = half.shape[1] // sources[1].shape[1]
    block = sources[1].shape[0] // blocks
    rows = block // cores
    for index in range(blocks):
        begin = pl.multiple_of(core * rows + index * block, rows)
        lanes = pl.ds(index * sources[1].shape[1], sources[1].shape[1])
        pairs.append((sources[1].at[pl.ds(begin, rows)], half.at[pl.ds(start, rows), lanes]))
    copies = [pltpu.make_async_copy(a, b, sems.at[i]) for i, (a, b) in enumerate(pairs)]
    for copy in copies:
        copy.start()
    for copy in copies:
        copy.wait()


def unpack_kernel(*refs):
    halves, outs = refs[:-2], refs[-2:]
    for step, half in enumerate(halves):
        core = lax.rem(lax.axis_index("pair") + step, len(halves))
        rows = outs[0].shape[0] // len(halves)
        outs[0][pl.ds(pl.multiple_of(core * rows, rows), rows), :] = half[:rows, :]
        start = rows
        blocks = half.shape[1] // outs[1].shape[1]
        block = outs[1].shape[0] // blocks
        rows = block // len(halves)
        for index in range(blocks):
            first = pl.multiple_of(core * rows + index * block, rows)
            lanes = slice(index * outs[1].shape[1], (index + 1) * outs[1].shape[1])
            outs[1][pl.ds(first, rows), :] = half[start : start + rows, lanes]


def pick(options, slot):
    chosen = options[0]
    for index in range(1, len(options)):
        chosen = jnp.where(slot == index, options[index], chosen)
    return chosen


def feature_shares(whole, count):
    share = whole.shape[1] // count
    options = [whole[:, i * share : (i + 1) * share] for i in range(count)]
    return [pick(options, slot_of(step, count)) for step in range(count)]


def compose_kernel(weight, *refs):
    pieces, out = refs[:-1], refs[-1]
    shares = feature_shares(weight[...].astype(F32), len(pieces))
    out[...] = sum(dot(s.astype(BF16), p[...]) for s, p in zip(shares, pieces)).astype(BF16)


def update_kernel(*refs, count):
    mixed, weights = refs[:count], refs[count : 2 * count]
    tokens, query_weight = refs[2 * count : 3 * count], refs[3 * count]
    updated, query = refs[3 * count + 1 :]
    whole = sum(dot(m[...], w[...]) for m, w in zip(mixed, weights))
    pieces = []
    for step, term in enumerate(feature_shares(whole, count)):
        piece = (tokens[step][...].astype(F32) + term).astype(BF16)
        updated[step] = piece
        pieces.append(piece)
    normed = normalized(pieces)
    product = sum(
        dot(normed[step], query_weight[0, slot_of(step, count)]) for step in range(count)
    )
    query[...] = (product * QUERY_SCALE).astype(BF16)


def conv_kernel(window, above, below, weight, out):
    width = out.shape[1]
    band_rows, channels = out.shape[0], out.shape[2]
    grid = jnp.concatenate([above[...], window[...], below[...]], axis=0).astype(F32)
    active = jnp.maximum(grid, 0.0)
    total = grid[1 : 1 + band_rows, EDGE : EDGE + width, :].reshape(band_rows * width, channels)
    for column in range(3):
        first = EDGE - 1 + column
        shifted = active[:, first : first + width, :].astype(BF16)
        for row in range(3):
            rows = shifted[row : row + band_rows].reshape(band_rows * width, channels)
            total = total + dot(rows, weight[row, column])
    out[...] = total.reshape(out.shape).astype(BF16)


def body(left_tokens, right_tokens, self_qkv, self_out, cross_qkv, cross_out, reassemble, taps):
    bands, tiles, cores = (lax.axis_size(axis) for axis in ("blk", "tile", "pair"))
    span = bands // cores
    both = ("blk", "pair")
    rows, share = left_tokens.shape[1:]
    columns = self_qkv.shape[2]
    channels = reassemble.shape[1]
    width = GRID_W // tiles
    band_rows = rows // GRID_W
    heads = columns // HD
    window = (band_rows, width + 2 * EDGE, channels)
    board = (band_rows, GRID_W + 2 * EDGE, channels)

    def home(band, pair):
        return band * cores + pair

    def worker(band, pair):
        shift = (pair - band // span) % cores
        return ((band + shift * span) % bands) * cores + (pair - shift) % cores

    places = [(band, pair) for band in range(bands) for pair in range(cores)]
    there = [(home(*p), worker(*p)) for p in places]
    back = [(worker(*p), home(*p)) for p in places]
    down = [(worker(b, p), home(b + 1, p)) for b, p in places if b + 1 < bands]
    up = [(worker(b, p), home(b - 1, p)) for b, p in places if b > 0]
    comes = [worker(*p) for p in places if home(*p) != worker(*p)]

    def tile_swaps(value, members, step):
        def flat(position, tile):
            return (position // cores * tiles + tile) * cores + position % cores

        pairs = [(flat(m, (i + step) % tiles), flat(m, i)) for m in members for i in range(tiles)]
        return lax.ppermute(value, ("blk", "tile", "pair"), pairs)

    def tied(values, *others):
        return lax.optimization_barrier((values, others))[0]

    def from_tile(value, step):
        return lax.ppermute(value, "tile", [((i + step) % tiles, i) for i in range(tiles)])

    def tile_pieces(own):
        return [own, *[from_tile(own, s) for s in range(1, tiles)]]

    def neighbours(pack):
        ring = [(g * span, i) for g in range(cores) for i in range(span)]
        return [
            lax.ppermute(pack, "blk", [(g + (i + s) % span, g + i) for g, i in ring])
            for s in range(1, span)
        ]

    def across(pack):
        return [
            lax.ppermute(pack, "pair", [((i + s) % cores, i) for i in range(cores)])
            for s in range(1, cores)
        ]

    def grouped(packs):
        return packs if len(packs) < 3 else [jnp.concatenate(packs)]

    def project(pieces, weights, wanted):
        (projected,) = run_kernel(
            functools.partial(project_kernel, count=tiles, wanted=wanted),
            "project",
            [((rows, columns * len(wanted)), BF16)],
            [*pieces, weights.reshape(3, tiles, share, columns)],
        )
        return projected

    def begin(query, packs):
        shapes = [((heads, rows, HD), F32), ((heads, rows, 2), F32)]
        return run_kernel(begin_kernel, "begin", shapes, [query, *grouped(packs)])

    def staged(weights):
        blocks = weights[0].shape[1] // channels
        height = (weights[0].shape[0] + share // blocks) // cores
        return run_kernel(
            functools.partial(stage_kernel, cores=cores),
            "stage",
            [(w.shape, BF16) for w in weights] + [((height, weights[0].shape[1]), BF16)],
            [pltpu.with_memory_space_constraint(w, pltpu.HBM) for w in weights],
            [pltpu.SemaphoreType.DMA((len(weights) + 1 + blocks,))],
            pl.BlockSpec(memory_space=pl.ANY),
        )

    left_here = lax.ppermute(left_tokens[0], both, there)
    steps = range(1, tiles)
    left_home = [from_tile(left_tokens[0], s) for s in steps]
    right = [from_tile(right_tokens[0], s) for s in steps]
    self_out, reassemble, cross_out, left_own, right_own, self_qkv, cross_qkv, taps, half = staged(
        [self_out, reassemble, cross_out, left_tokens[0], right_tokens[0], self_qkv, cross_qkv, taps]
    )
    pack = project([left_own, *left_home], self_qkv, (1, 2))
    right = tied([right_own, *right], pack)
    right_pack = project(right, cross_qkv, (1, 2))
    pack = lax.ppermute(pack, both, there)
    left_here, right_pack = lax.optimization_barrier((left_here, right_pack))
    right_pack = lax.ppermute(right_pack, both, there)
    settled = lax.axis_index("pair") == lax.axis_index("blk") // span
    left = [left_here]
    for step, early in zip(steps, left_home):
        left.append(jnp.where(settled, early, tile_swaps(left_here, comes, step)))
    query = project(left, self_qkv, (0,))
    halves = tile_pieces(half)[1:]
    beside = neighbours(pack)
    near, right_pack, query, halves = lax.optimization_barrier(
        ([pack, *beside], right_pack, query, halves)
    )
    far = [q for p in near for q in across(p)]
    state = begin(query, near)
    right_pack = tied(right_pack, state)
    right_near = [right_pack, *neighbours(right_pack)]
    others = [
        run_kernel(
            unpack_kernel,
            "unpack",
            [(w.shape, BF16) for w in (self_out, reassemble)],
            [half, *across(half)],
        )
        for half in halves
    ]
    (mixed,) = run_kernel(
        end_kernel, "end", [((rows, columns), BF16)], [query, *grouped(far), *state]
    )

    map_weights = [reassemble, *[other[1] for other in others]]
    (composed,) = run_kernel(
        compose_kernel, "compose", [((columns, channels), BF16)], [cross_out, *map_weights]
    )
    mixed, composed = lax.optimization_barrier((tile_pieces(mixed), composed))
    updated, cross_query = run_kernel(
        functools.partial(update_kernel, count=tiles),
        "update",
        [((tiles, rows, share), BF16), ((rows, columns), BF16)],
        [
            *mixed,
            self_out,
            *[other[0] for other in others],
            *left,
            cross_qkv.reshape(3, tiles, share, columns),
        ],
    )
    right_near = tied(right_near, updated)
    right_far = [q for p in right_near for q in across(p)]
    state = begin(cross_query, right_near)
    right_far = tied(right_far, state)
    maps = run_kernel(
        functools.partial(end_map_kernel, count=tiles),
        "end_map",
        [(window, BF16)] * tiles,
        [cross_query, *grouped(right_far), *state, composed],
        [pltpu.VMEM(board, F32)],
    )
    (carried,) = run_kernel(
        carry_kernel,
        "carry",
        [(window, F32)],
        [tied(updated, maps), *map_weights],
        [pltpu.VMEM(board, F32)],
    )
    received = [from_tile(part, s) for s, part in enumerate(maps) if s > 0]
    (features,) = run_kernel(add_kernel, "add", [(window, BF16)], [carried, maps[0], *received])
    above = lax.ppermute(features[-1:], both, down)
    below = lax.ppermute(features[:1], both, up)
    features = lax.ppermute(features, both, back)
    (joined,) = run_kernel(
        conv_kernel,
        "join",
        [((band_rows, width, channels), BF16)],
        [features, above, below, taps],
    )
    return joined[None]


def solution(mesh):
    placed = (
        P(("groups", "pair"), "blk", "tile"),
        P(("groups", "pair"), "blk", "tile"),
        P(None, None, "tile"),
        P("tile", None),
        P(None, None, "tile"),
        P("tile", None),
        P("tile", None),
        P(),
    )
    return jax.shard_map(
        body,
        mesh=mesh,
        in_specs=placed,
        out_specs=P(("groups", "pair"), "blk", "tile", None),
        check_vma=False,
    )
```

```python
import functools
import math

import jax
import jax.numpy as jnp
from jax import lax
from jax.experimental import pallas as pl
from jax.experimental.pallas import tpu as pltpu
from jax.sharding import PartitionSpec as P

HD = 64
GRID_W = 128
EDGE = 16
F32 = jnp.float32
BF16 = jnp.bfloat16
QUERY_SCALE = math.log2(math.e) * HD**-0.5
VMEM = pl.BlockSpec(memory_space=pltpu.VMEM)
HBM = pl.BlockSpec(memory_space=pl.ANY)


def run_kernel(kernel, name, shapes, operands, scratch=(), space=VMEM):
    return pl.pallas_call(
        kernel,
        out_shape=[jax.ShapeDtypeStruct(*s) for s in shapes],
        in_specs=[space] * len(operands),
        out_specs=[VMEM] * len(shapes),
        scratch_shapes=scratch,
        compiler_params=pltpu.CompilerParams(vmem_limit_bytes=24 << 20),
        cost_estimate=pl.CostEstimate(flops=0, bytes_accessed=0, transcendentals=0),
        name=name,
    )(*operands)


def slot_of(step, count):
    return lax.rem(lax.axis_index("tile") + step, count)


def normalized(pieces):
    widened = [piece.astype(F32) for piece in pieces]
    width = sum(piece.shape[1] for piece in widened)
    mean = sum(jnp.sum(piece, axis=1, keepdims=True) for piece in widened) / width
    centred = [piece - mean for piece in widened]
    variance = sum(jnp.sum(piece * piece, axis=1, keepdims=True) for piece in centred) / width
    scale = lax.rsqrt(variance + 1e-06)
    return [(piece * scale).astype(BF16) for piece in centred]


def dot(left, right):
    return jnp.dot(left, right, preferred_element_type=F32)


def project_kernel(*refs, count, pairs, scaled, first):
    pieces = [piece[...] for piece in refs[:count]]
    weight, outs = refs[count + pairs], refs[count + pairs + 1 :]
    for index in range(pairs):
        place = count - pairs + index
        pieces[place] = pieces[place] + refs[count + index][...]
    normed = normalized(pieces)
    if scaled:
        for out, piece in zip(outs[2:], pieces[1:]):
            out[...] = piece
    products = []
    for which in range(first, weight.shape[0]):
        products.append(
            sum(dot(normed[step], weight[which, slot_of(step, count)]) for step in range(count))
        )
    if scaled:
        outs[0][...] = (products.pop(0) * QUERY_SCALE).astype(BF16)
    columns = weight.shape[3]
    for which, product in enumerate(products):
        outs[scaled][:, which * columns : (which + 1) * columns] = product.astype(BF16)


def attended(query, packs, state, index):
    columns = query.shape[1]
    start = index * HD
    head = slice(start, start + HD)
    values = slice(columns + start, columns + start + HD)
    asked = query[:, head]
    scores = [
        lax.dot_general(asked, pack[:, head], (((1,), (1,)), ((), ())), preferred_element_type=F32)
        for pack in packs
    ]
    tops = [jnp.max(score, axis=1, keepdims=True) for score in scores]
    total, mixed = 0.0, 0.0
    if state:
        before, stats = state[0][index], state[1][index]
        tops.append(stats[:, :1])
    maxima = functools.reduce(jnp.maximum, tops)
    if state:
        correction = jnp.exp2(stats[:, :1] - maxima)
        total = stats[:, 1:2] * correction
        mixed = before * correction
    for score, pack in zip(scores, packs):
        expanded = jnp.exp2(score - maxima)
        total = total + jnp.sum(expanded, axis=1, keepdims=True)
        mixed = mixed + dot(expanded.astype(BF16), pack[:, values])
    return mixed, maxima, total


def begin_kernel(query, *refs):
    packs, (mixed_out, stats_out) = refs[:-2], refs[-2:]
    for index in range(query.shape[1] // HD):
        mixed, maxima, total = attended(query, packs, (), index)
        mixed_out[index] = mixed
        stats_out[index] = jnp.concatenate([maxima, total], axis=1)


def ended(query, packs, state):
    heads = []
    for index in range(query.shape[1] // HD):
        mixed, maxima, total = attended(query, packs, state, index)
        heads.append(mixed / total)
    return jnp.concatenate(heads, axis=1).astype(BF16)


def end_kernel(query, *refs):
    refs[-1][...] = ended(query, refs[:-3], refs[-3:-1])


def fill_board(board, values):
    band_rows, channels = board.shape[0], board.shape[2]
    edge = jnp.zeros((band_rows, EDGE, channels), board.dtype)
    board[:, :EDGE, :] = edge
    board[:, EDGE + GRID_W :, :] = edge
    inner = values.reshape(band_rows, GRID_W, channels)
    board[:, EDGE : EDGE + GRID_W, :] = inner.astype(board.dtype)


def window_of(board, slot, out):
    start = pl.multiple_of(slot * (out.shape[1] - 2 * EDGE), EDGE)
    out[...] = board[:, pl.ds(start, out.shape[1]), :].astype(out.dtype)


def end_map_kernel(query, *refs, count):
    composed, outs, board = refs[-2 - count], refs[-1 - count : -1], refs[-1]
    packs, state = refs[: -4 - count], refs[-4 - count : -2 - count]
    fill_board(board, dot(ended(query, packs, state), composed[...]))
    for step, out in enumerate(outs):
        window_of(board, slot_of(count - step, count), out)


def carry_kernel(updated, *refs):
    pieces, out, board = refs[:-2], refs[-2], refs[-1]
    fill_board(board, sum(dot(updated[i], piece[...]) for i, piece in enumerate(pieces)))
    window_of(board, lax.axis_index("tile"), out)


def add_kernel(*refs):
    refs[-1][...] = sum(ref[...].astype(F32) for ref in refs[:-1]).astype(BF16)


def stage_kernel(*refs, cores):
    count = (len(refs) - 2) // 2
    sources, outs, half, sems = refs[:count], refs[count : 2 * count], refs[-2], refs[-1]
    core = lax.axis_index("pair")
    pairs = list(zip(sources, outs))
    rows = sources[0].shape[0] // cores
    begin = pl.multiple_of(core * rows, rows)
    pairs.append((sources[0].at[pl.ds(begin, rows)], half.at[pl.ds(0, rows)]))
    start = rows
    blocks = half.shape[1] // sources[1].shape[1]
    block = sources[1].shape[0] // blocks
    rows = block // cores
    for index in range(blocks):
        begin = pl.multiple_of(core * rows + index * block, rows)
        lanes = pl.ds(index * sources[1].shape[1], sources[1].shape[1])
        pairs.append((sources[1].at[pl.ds(begin, rows)], half.at[pl.ds(start, rows), lanes]))
    copies = [pltpu.make_async_copy(a, b, sems.at[i]) for i, (a, b) in enumerate(pairs)]
    for copy in copies:
        copy.start()
    for copy in copies:
        copy.wait()


def unpack_kernel(*refs):
    halves, outs = refs[:-2], refs[-2:]
    for step, half in enumerate(halves):
        core = lax.rem(lax.axis_index("pair") + step, len(halves))
        rows = outs[0].shape[0] // len(halves)
        outs[0][pl.ds(pl.multiple_of(core * rows, rows), rows), :] = half[:rows, :]
        start = rows
        blocks = half.shape[1] // outs[1].shape[1]
        block = outs[1].shape[0] // blocks
        rows = block // len(halves)
        for index in range(blocks):
            first = pl.multiple_of(core * rows + index * block, rows)
            lanes = slice(index * outs[1].shape[1], (index + 1) * outs[1].shape[1])
            outs[1][pl.ds(first, rows), :] = half[start : start + rows, lanes]


def pick(options, slot):
    chosen = options[0]
    for index in range(1, len(options)):
        chosen = jnp.where(slot == index, options[index], chosen)
    return chosen


def feature_shares(whole, count):
    share = whole.shape[1] // count
    options = [whole[:, i * share : (i + 1) * share] for i in range(count)]
    return [pick(options, slot_of(step, count)) for step in range(count)]


def compose_kernel(weight, *refs):
    pieces, out = refs[:-1], refs[-1]
    shares = feature_shares(weight[...].astype(F32), len(pieces))
    out[...] = sum(dot(s.astype(BF16), p[...]) for s, p in zip(shares, pieces)).astype(BF16)


def update_kernel(*refs, count):
    mixed, weights = refs[:count], refs[count : 2 * count]
    tokens, query_weight = refs[2 * count : 3 * count], refs[3 * count]
    updated, query = refs[3 * count + 1 :]
    whole = sum(dot(m[...], w[...]) for m, w in zip(mixed, weights))
    pieces = []
    for step, term in enumerate(feature_shares(whole, count)):
        piece = (tokens[step][...].astype(F32) + term).astype(BF16)
        updated[step] = piece
        pieces.append(piece)
    normed = normalized(pieces)
    product = sum(
        dot(normed[step], query_weight[0, slot_of(step, count)]) for step in range(count)
    )
    query[...] = (product * QUERY_SCALE).astype(BF16)


def conv_kernel(window, above, below, weight, out):
    width = out.shape[1]
    band_rows, channels = out.shape[0], out.shape[2]
    grid = jnp.concatenate([above[...], window[...], below[...]], axis=0).astype(F32)
    active = jnp.maximum(grid, 0.0)
    total = grid[1 : 1 + band_rows, EDGE : EDGE + width, :].reshape(band_rows * width, channels)
    for column in range(3):
        first = EDGE - 1 + column
        shifted = active[:, first : first + width, :].astype(BF16)
        for row in range(3):
            rows = shifted[row : row + band_rows].reshape(band_rows * width, channels)
            total = total + dot(rows, weight[row, column])
    out[...] = total.reshape(out.shape).astype(BF16)


def body(left_tokens, right_tokens, self_qkv, self_out, cross_qkv, cross_out, reassemble, taps):
    bands, tiles, cores = (lax.axis_size(axis) for axis in ("blk", "tile", "pair"))
    span = bands // cores
    both = ("blk", "pair")
    rows, share = left_tokens.shape[1:]
    columns = self_qkv.shape[2]
    channels = reassemble.shape[1]
    width = GRID_W // tiles
    band_rows = rows // GRID_W
    heads = columns // HD
    window = (band_rows, width + 2 * EDGE, channels)
    board = (band_rows, GRID_W + 2 * EDGE, channels)

    def home(band, pair):
        return band * cores + pair

    def worker(band, pair):
        shift = (pair - band // span) % cores
        return ((band + shift * span) % bands) * cores + (pair - shift) % cores

    places = [(band, pair) for band in range(bands) for pair in range(cores)]
    there = [(home(*p), worker(*p)) for p in places]
    back = [(worker(*p), home(*p)) for p in places]
    down = [(worker(b, p), home(b + 1, p)) for b, p in places if b + 1 < bands]
    up = [(worker(b, p), home(b - 1, p)) for b, p in places if b > 0]
    stays = [home(*p) for p in places if home(*p) == worker(*p)]
    comes = [worker(*p) for p in places if home(*p) != worker(*p)]

    def tile_swaps(value, members, step):
        def flat(position, tile):
            return (position // cores * tiles + tile) * cores + position % cores

        pairs = [(flat(m, (i + step) % tiles), flat(m, i)) for m in members for i in range(tiles)]
        return lax.ppermute(value, ("blk", "tile", "pair"), pairs)

    def tied(values, *others):
        return lax.optimization_barrier((values, others))[0]

    def from_tile(value, step):
        return lax.ppermute(value, "tile", [((i + step) % tiles, i) for i in range(tiles)])

    def tile_pieces(own):
        return [own, *[from_tile(own, s) for s in range(1, tiles)]]

    def beside_swaps(value, members, step):
        def source(member):
            band, core = member // cores, member % cores
            return (band // span * span + (band % span + step) % span) * cores + core

        return lax.ppermute(value, both, [(source(m), m) for m in members])

    def neighbours(pack):
        ring = [(g * span, i) for g in range(cores) for i in range(span)]
        return [
            lax.ppermute(pack, "blk", [(g + (i + s) % span, g + i) for g, i in ring])
            for s in range(1, span)
        ]

    def across(pack):
        return [
            lax.ppermute(pack, "pair", [((i + s) % cores, i) for i in range(cores)])
            for s in range(1, cores)
        ]

    def grouped(packs):
        return packs if len(packs) < 3 else [jnp.concatenate(packs)]

    def project(pieces, weights, scaled, first, pairs=()):
        shapes = [((rows, columns), BF16)] * scaled + [((rows, 2 * columns), BF16)]
        return run_kernel(
            functools.partial(
                project_kernel, count=tiles, pairs=len(pairs), scaled=scaled, first=first
            ),
            "project",
            shapes + [((rows, share), BF16)] * (scaled * (tiles - 1)),
            [*pieces, *pairs, weights.reshape(3, tiles, share, columns)],
        )

    def begin(query, packs):
        shapes = [((heads, rows, HD), F32), ((heads, rows, 2), F32)]
        return run_kernel(begin_kernel, "begin", shapes, [query, *grouped(packs)])

    def staged(weights):
        blocks = weights[0].shape[1] // channels
        height = (weights[0].shape[0] + share // blocks) // cores
        return run_kernel(
            functools.partial(stage_kernel, cores=cores),
            "stage",
            [(w.shape, BF16) for w in weights] + [((height, weights[0].shape[1]), BF16)],
            [pltpu.with_memory_space_constraint(w, pltpu.HBM) for w in weights],
            [pltpu.SemaphoreType.DMA((len(weights) + 1 + blocks,))],
            pl.BlockSpec(memory_space=pl.ANY),
        )

    steps, hops = range(1, tiles), range(1, span)
    left_here = lax.ppermute(left_tokens[0], both, there)
    beside_early = [beside_swaps(left_tokens[0], stays, s) for s in hops]
    left_early = [tile_swaps(left_tokens[0], stays, s) for s in steps]
    self_out, reassemble, cross_out, right_own, self_qkv, cross_qkv, taps, half = staged(
        [self_out, reassemble, cross_out, right_tokens[0], self_qkv, cross_qkv, taps]
    )
    right = [right_own, *[from_tile(right_tokens[0], s) for s in steps]]
    right, left_early, beside_early = lax.optimization_barrier((right, left_early, beside_early))
    far_early = [[tile_swaps(b, stays, s) for s in steps] for b in beside_early]
    (right_pack,) = project(right, cross_qkv, False, 1)
    right_pack = lax.ppermute(right_pack, both, there)
    beside_late = [beside_swaps(left_here, comes, s) for s in hops]
    left_late = [tile_swaps(left_here, comes, s) for s in steps]
    left_late, beside_late, far_early = lax.optimization_barrier(
        (left_late, beside_late, far_early)
    )
    far_late = [[tile_swaps(b, comes, s) for s in steps] for b in beside_late]
    query, pack, *left_rest = project(
        [left_here, *left_early], self_qkv, True, 0, left_late
    )
    left = [left_here, *left_rest]
    near, right_pack = lax.optimization_barrier(([pack, *across(pack)], right_pack))
    state = begin(query, near)
    far_late = tied(far_late, state)
    beside = [
        project([early, *more], self_qkv, False, 1, [late, *rest])[0]
        for early, late, more, rest in zip(beside_early, beside_late, far_early, far_late)
    ]
    far = [*beside, *[q for p in beside for q in across(p)]]
    halves = tile_pieces(tied(half, far))[1:]
    right_pack = tied(right_pack, state)
    right_near = [right_pack, *neighbours(right_pack)]
    (mixed,) = run_kernel(
        end_kernel, "end", [((rows, columns), BF16)], [query, *grouped(far), *state]
    )
    halves = tied(halves, mixed)
    others = [
        run_kernel(
            unpack_kernel,
            "unpack",
            [(w.shape, BF16) for w in (self_out, reassemble)],
            [half, *across(half)],
        )
        for half in halves
    ]

    map_weights = [reassemble, *[other[1] for other in others]]
    (composed,) = run_kernel(
        compose_kernel, "compose", [((columns, channels), BF16)], [cross_out, *map_weights]
    )
    mixed, composed = lax.optimization_barrier((tile_pieces(mixed), composed))
    updated, cross_query = run_kernel(
        functools.partial(update_kernel, count=tiles),
        "update",
        [((tiles, rows, share), BF16), ((rows, columns), BF16)],
        [
            *mixed,
            self_out,
            *[other[0] for other in others],
            *left,
            cross_qkv.reshape(3, tiles, share, columns),
        ],
    )
    right_near = tied(right_near, updated)
    right_far = [q for p in right_near for q in across(p)]
    state = begin(cross_query, right_near)
    right_far = tied(right_far, state)
    maps = run_kernel(
        functools.partial(end_map_kernel, count=tiles),
        "end_map",
        [(window, BF16)] * tiles,
        [cross_query, *grouped(right_far), *state, composed],
        [pltpu.VMEM(board, F32)],
    )
    (carried,) = run_kernel(
        carry_kernel,
        "carry",
        [(window, F32)],
        [tied(updated, maps), *map_weights],
        [pltpu.VMEM(board, F32)],
    )
    received = [from_tile(part, s) for s, part in enumerate(maps) if s > 0]
    (features,) = run_kernel(add_kernel, "add", [(window, BF16)], [carried, maps[0], *received])
    above = lax.ppermute(features[-1:], both, down)
    below = lax.ppermute(features[:1], both, up)
    features = lax.ppermute(features, both, back)
    (joined,) = run_kernel(
        conv_kernel,
        "join",
        [((band_rows, width, channels), BF16)],
        [features, above, below, taps],
    )
    return joined[None]


def solution(mesh):
    placed = (
        P(("groups", "pair"), "blk", "tile"),
        P(("groups", "pair"), "blk", "tile"),
        P(None, None, "tile"),
        P("tile", None),
        P(None, None, "tile"),
        P("tile", None),
        P("tile", None),
        P(),
    )
    return jax.shard_map(
        body,
        mesh=mesh,
        in_specs=placed,
        out_specs=P(("groups", "pair"), "blk", "tile", None),
        check_vma=False,
    )
```

```python
import functools
import math

import jax
import jax.numpy as jnp
from jax import lax
from jax.experimental import pallas as pl
from jax.experimental.pallas import tpu as pltpu
from jax.sharding import PartitionSpec as P

HD = 64
GRID_W = 128
EDGE = 16
F32 = jnp.float32
BF16 = jnp.bfloat16
QUERY_SCALE = math.log2(math.e) * HD**-0.5
VMEM = pl.BlockSpec(memory_space=pltpu.VMEM)
HBM = pl.BlockSpec(memory_space=pl.ANY)


def run_kernel(kernel, name, shapes, operands, scratch=(), space=VMEM):
    return pl.pallas_call(
        kernel,
        out_shape=[jax.ShapeDtypeStruct(*s) for s in shapes],
        in_specs=[space] * len(operands),
        out_specs=[VMEM] * len(shapes),
        scratch_shapes=scratch,
        compiler_params=pltpu.CompilerParams(vmem_limit_bytes=24 << 20),
        cost_estimate=pl.CostEstimate(flops=0, bytes_accessed=0, transcendentals=0),
        name=name,
    )(*operands)


def slot_of(step, count):
    return lax.rem(lax.axis_index("tile") + step, count)


def normalized(pieces):
    widened = [piece.astype(F32) for piece in pieces]
    width = sum(piece.shape[1] for piece in widened)
    mean = sum(jnp.sum(piece, axis=1, keepdims=True) for piece in widened) / width
    centred = [piece - mean for piece in widened]
    variance = sum(jnp.sum(piece * piece, axis=1, keepdims=True) for piece in centred) / width
    scale = lax.rsqrt(variance + 1e-06)
    return [(piece * scale).astype(BF16) for piece in centred]


def dot(left, right):
    return jnp.dot(left, right, preferred_element_type=F32)


def project_kernel(*refs, count, scaled, first):
    pieces, weight, outs = refs[:count], refs[count], refs[count + 1 :]
    normed = normalized([piece[...] for piece in pieces])
    products = []
    for which in range(first, weight.shape[0]):
        products.append(
            sum(dot(normed[step], weight[which, slot_of(step, count)]) for step in range(count))
        )
    if scaled:
        outs[0][...] = (products.pop(0) * QUERY_SCALE).astype(BF16)
    columns = weight.shape[3]
    for which, product in enumerate(products):
        outs[-1][:, which * columns : (which + 1) * columns] = product.astype(BF16)


def attended(query, packs, state, index):
    columns = query.shape[1]
    start = index * HD
    head = slice(start, start + HD)
    values = slice(columns + start, columns + start + HD)
    asked = query[:, head]
    scores = [
        lax.dot_general(asked, pack[:, head], (((1,), (1,)), ((), ())), preferred_element_type=F32)
        for pack in packs
    ]
    tops = [jnp.max(score, axis=1, keepdims=True) for score in scores]
    total, mixed = 0.0, 0.0
    if state:
        before, stats = state[0][index], state[1][index]
        tops.append(stats[:, :1])
    maxima = functools.reduce(jnp.maximum, tops)
    if state:
        correction = jnp.exp2(stats[:, :1] - maxima)
        total = stats[:, 1:2] * correction
        mixed = before * correction
    for score, pack in zip(scores, packs):
        expanded = jnp.exp2(score - maxima)
        total = total + jnp.sum(expanded, axis=1, keepdims=True)
        mixed = mixed + dot(expanded.astype(BF16), pack[:, values])
    return mixed, maxima, total


def begin_kernel(query, *refs):
    packs, (mixed_out, stats_out) = refs[:-2], refs[-2:]
    for index in range(query.shape[1] // HD):
        mixed, maxima, total = attended(query, packs, (), index)
        mixed_out[index] = mixed
        stats_out[index] = jnp.concatenate([maxima, total], axis=1)


def ended(query, packs, state):
    heads = []
    for index in range(query.shape[1] // HD):
        mixed, maxima, total = attended(query, packs, state, index)
        heads.append(mixed / total)
    return jnp.concatenate(heads, axis=1).astype(BF16)


def end_kernel(query, *refs):
    refs[-1][...] = ended(query, refs[:-3], refs[-3:-1])


def fill_board(board, values):
    band_rows, channels = board.shape[0], board.shape[2]
    edge = jnp.zeros((band_rows, EDGE, channels), board.dtype)
    board[:, :EDGE, :] = edge
    board[:, EDGE + GRID_W :, :] = edge
    inner = values.reshape(band_rows, GRID_W, channels)
    board[:, EDGE : EDGE + GRID_W, :] = inner.astype(board.dtype)


def window_of(board, slot, out):
    start = pl.multiple_of(slot * (out.shape[1] - 2 * EDGE), EDGE)
    out[...] = board[:, pl.ds(start, out.shape[1]), :].astype(out.dtype)


def end_map_kernel(query, *refs, count):
    composed, outs, board = refs[-2 - count], refs[-1 - count : -1], refs[-1]
    packs, state = refs[: -4 - count], refs[-4 - count : -2 - count]
    fill_board(board, dot(ended(query, packs, state), composed[...]))
    for step, out in enumerate(outs):
        window_of(board, slot_of(count - step, count), out)


def carry_kernel(updated, *refs):
    pieces, out, board = refs[:-2], refs[-2], refs[-1]
    fill_board(board, sum(dot(updated[i], piece[...]) for i, piece in enumerate(pieces)))
    window_of(board, lax.axis_index("tile"), out)


def add_kernel(*refs):
    refs[-1][...] = sum(ref[...].astype(F32) for ref in refs[:-1]).astype(BF16)


def stage_kernel(*refs, cores):
    count = (len(refs) - 2) // 2
    sources, outs, half, sems = refs[:count], refs[count : 2 * count], refs[-2], refs[-1]
    core = lax.axis_index("pair")
    pairs = list(zip(sources, outs))
    rows = sources[0].shape[0] // cores
    begin = pl.multiple_of(core * rows, rows)
    pairs.append((sources[0].at[pl.ds(begin, rows)], half.at[pl.ds(0, rows)]))
    start = rows
    blocks = half.shape[1] // sources[1].shape[1]
    block = sources[1].shape[0] // blocks
    rows = block // cores
    for index in range(blocks):
        begin = pl.multiple_of(core * rows + index * block, rows)
        lanes = pl.ds(index * sources[1].shape[1], sources[1].shape[1])
        pairs.append((sources[1].at[pl.ds(begin, rows)], half.at[pl.ds(start, rows), lanes]))
    copies = [pltpu.make_async_copy(a, b, sems.at[i]) for i, (a, b) in enumerate(pairs)]
    for copy in copies:
        copy.start()
    for copy in copies:
        copy.wait()


def unpack_kernel(*refs):
    halves, outs = refs[:-2], refs[-2:]
    for step, half in enumerate(halves):
        core = lax.rem(lax.axis_index("pair") + step, len(halves))
        rows = outs[0].shape[0] // len(halves)
        outs[0][pl.ds(pl.multiple_of(core * rows, rows), rows), :] = half[:rows, :]
        start = rows
        blocks = half.shape[1] // outs[1].shape[1]
        block = outs[1].shape[0] // blocks
        rows = block // len(halves)
        for index in range(blocks):
            first = pl.multiple_of(core * rows + index * block, rows)
            lanes = slice(index * outs[1].shape[1], (index + 1) * outs[1].shape[1])
            outs[1][pl.ds(first, rows), :] = half[start : start + rows, lanes]


def pick(options, slot):
    chosen = options[0]
    for index in range(1, len(options)):
        chosen = jnp.where(slot == index, options[index], chosen)
    return chosen


def feature_shares(whole, count):
    share = whole.shape[1] // count
    options = [whole[:, i * share : (i + 1) * share] for i in range(count)]
    return [pick(options, slot_of(step, count)) for step in range(count)]


def compose_kernel(weight, *refs):
    pieces, out = refs[:-1], refs[-1]
    shares = feature_shares(weight[...].astype(F32), len(pieces))
    out[...] = sum(dot(s.astype(BF16), p[...]) for s, p in zip(shares, pieces)).astype(BF16)


def update_kernel(*refs, count):
    mixed, weights = refs[:count], refs[count : 2 * count]
    tokens, query_weight = refs[2 * count : 3 * count], refs[3 * count]
    updated, query = refs[3 * count + 1 :]
    whole = sum(dot(m[...], w[...]) for m, w in zip(mixed, weights))
    pieces = []
    for step, term in enumerate(feature_shares(whole, count)):
        piece = (tokens[step][...].astype(F32) + term).astype(BF16)
        updated[step] = piece
        pieces.append(piece)
    normed = normalized(pieces)
    product = sum(
        dot(normed[step], query_weight[0, slot_of(step, count)]) for step in range(count)
    )
    query[...] = (product * QUERY_SCALE).astype(BF16)


def conv_kernel(window, above, below, weight, out):
    width = out.shape[1]
    band_rows, channels = out.shape[0], out.shape[2]
    grid = jnp.concatenate([above[...], window[...], below[...]], axis=0).astype(F32)
    active = jnp.maximum(grid, 0.0)
    total = grid[1 : 1 + band_rows, EDGE : EDGE + width, :].reshape(band_rows * width, channels)
    for column in range(3):
        first = EDGE - 1 + column
        shifted = active[:, first : first + width, :].astype(BF16)
        for row in range(3):
            rows = shifted[row : row + band_rows].reshape(band_rows * width, channels)
            total = total + dot(rows, weight[row, column])
    out[...] = total.reshape(out.shape).astype(BF16)


def body(left_tokens, right_tokens, self_qkv, self_out, cross_qkv, cross_out, reassemble, taps):
    bands, tiles, cores = (lax.axis_size(axis) for axis in ("blk", "tile", "pair"))
    span = bands // cores
    both = ("blk", "pair")
    rows, share = left_tokens.shape[1:]
    columns = self_qkv.shape[2]
    channels = reassemble.shape[1]
    width = GRID_W // tiles
    band_rows = rows // GRID_W
    heads = columns // HD
    window = (band_rows, width + 2 * EDGE, channels)
    board = (band_rows, GRID_W + 2 * EDGE, channels)

    def home(band, pair):
        return band * cores + pair

    def worker(band, pair):
        shift = (pair - band // span) % cores
        return ((band + shift * span) % bands) * cores + (pair - shift) % cores

    places = [(band, pair) for band in range(bands) for pair in range(cores)]
    there = [(home(*p), worker(*p)) for p in places]
    back = [(worker(*p), home(*p)) for p in places]
    down = [(worker(b, p), home(b + 1, p)) for b, p in places if b + 1 < bands]
    up = [(worker(b, p), home(b - 1, p)) for b, p in places if b > 0]

    def fetched(value, step):
        def flat(position, tile):
            return (position // cores * tiles + tile) * cores + position % cores

        pairs = [(flat(s, (i + step) % tiles), flat(d, i)) for s, d in there for i in range(tiles)]
        return lax.ppermute(value, ("blk", "tile", "pair"), pairs)

    def tied(values, *others):
        return lax.optimization_barrier((values, others))[0]

    def from_tile(value, step):
        return lax.ppermute(value, "tile", [((i + step) % tiles, i) for i in range(tiles)])

    def tile_pieces(own):
        return [own, *[from_tile(own, s) for s in range(1, tiles)]]

    def neighbours(pack):
        ring = [(g * span, i) for g in range(cores) for i in range(span)]
        return [
            lax.ppermute(pack, "blk", [(g + (i + s) % span, g + i) for g, i in ring])
            for s in range(1, span)
        ]

    def across(pack):
        return [
            lax.ppermute(pack, "pair", [((i + s) % cores, i) for i in range(cores)])
            for s in range(1, cores)
        ]

    def grouped(packs):
        return packs if len(packs) < 3 else [jnp.concatenate(packs)]

    def project(pieces, weights, scaled, first):
        return run_kernel(
            functools.partial(project_kernel, count=tiles, scaled=scaled, first=first),
            "project",
            [((rows, columns), BF16)] * scaled + [((rows, 2 * columns), BF16)],
            [*pieces, weights.reshape(3, tiles, share, columns)],
        )

    def begin(query, packs):
        shapes = [((heads, rows, HD), F32), ((heads, rows, 2), F32)]
        return run_kernel(begin_kernel, "begin", shapes, [query, *grouped(packs)])

    def staged(weights):
        blocks = weights[0].shape[1] // channels
        height = (weights[0].shape[0] + share // blocks) // cores
        return run_kernel(
            functools.partial(stage_kernel, cores=cores),
            "stage",
            [(w.shape, BF16) for w in weights] + [((height, weights[0].shape[1]), BF16)],
            [pltpu.with_memory_space_constraint(w, pltpu.HBM) for w in weights],
            [pltpu.SemaphoreType.DMA((len(weights) + 1 + blocks,))],
            pl.BlockSpec(memory_space=pl.ANY),
        )

    steps = range(1, tiles)
    left = [fetched(left_tokens[0], step) for step in range(tiles)]
    self_out, reassemble, cross_out, right_own, self_qkv, cross_qkv, taps, half = staged(
        [self_out, reassemble, cross_out, right_tokens[0], self_qkv, cross_qkv, taps]
    )
    right = [right_own, *[from_tile(right_tokens[0], s) for s in steps]]
    (right_pack,) = project(right, cross_qkv, False, 1)
    left, right_pack = lax.optimization_barrier((left, right_pack))
    query, pack = project(left, self_qkv, True, 0)
    right_pack = lax.ppermute(tied(right_pack, pack), both, there)
    beside = neighbours(pack)
    near = [pack, *beside]
    far = [q for p in near for q in across(p)]
    state = begin(query, near)
    right_pack = tied(right_pack, state)
    right_near = [right_pack, *neighbours(right_pack)]
    halves = tile_pieces(tied(half, beside))[1:]
    (mixed,) = run_kernel(
        end_kernel, "end", [((rows, columns), BF16)], [query, *grouped(far), *state]
    )
    halves = tied(halves, mixed)
    others = [
        run_kernel(
            unpack_kernel,
            "unpack",
            [(w.shape, BF16) for w in (self_out, reassemble)],
            [half, *across(half)],
        )
        for half in halves
    ]
    map_weights = [reassemble, *[other[1] for other in others]]
    (composed,) = run_kernel(
        compose_kernel, "compose", [((columns, channels), BF16)], [cross_out, *map_weights]
    )
    mixed, composed = lax.optimization_barrier((tile_pieces(mixed), composed))
    updated, cross_query = run_kernel(
        functools.partial(update_kernel, count=tiles),
        "update",
        [((tiles, rows, share), BF16), ((rows, columns), BF16)],
        [
            *mixed,
            self_out,
            *[other[0] for other in others],
            *left,
            cross_qkv.reshape(3, tiles, share, columns),
        ],
    )
    right_near = tied(right_near, updated)
    right_far = [q for p in right_near for q in across(p)]
    state = begin(cross_query, right_near)
    right_far = tied(right_far, state)
    maps = run_kernel(
        functools.partial(end_map_kernel, count=tiles),
        "end_map",
        [(window, BF16)] * tiles,
        [cross_query, *grouped(right_far), *state, composed],
        [pltpu.VMEM(board, F32)],
    )
    (carried,) = run_kernel(
        carry_kernel,
        "carry",
        [(window, F32)],
        [tied(updated, maps), *map_weights],
        [pltpu.VMEM(board, F32)],
    )
    received = [from_tile(part, s) for s, part in enumerate(maps) if s > 0]
    (features,) = run_kernel(add_kernel, "add", [(window, BF16)], [carried, maps[0], *received])
    above = lax.ppermute(features[-1:], both, down)
    below = lax.ppermute(features[:1], both, up)
    features = lax.ppermute(features, both, back)
    (joined,) = run_kernel(
        conv_kernel,
        "join",
        [((band_rows, width, channels), BF16)],
        [features, above, below, taps],
    )
    return joined[None]


def solution(mesh):
    placed = (
        P(("groups", "pair"), "blk", "tile"),
        P(("groups", "pair"), "blk", "tile"),
        P(None, None, "tile"),
        P("tile", None),
        P(None, None, "tile"),
        P("tile", None),
        P("tile", None),
        P(),
    )
    return jax.shard_map(
        body,
        mesh=mesh,
        in_specs=placed,
        out_specs=P(("groups", "pair"), "blk", "tile", None),
        check_vma=False,
    )
```

```python
import functools
import math

import jax
import jax.numpy as jnp
from jax import lax
from jax.experimental import pallas as pl
from jax.experimental.pallas import tpu as pltpu
from jax.sharding import PartitionSpec as P

HD = 64
GRID_W = 128
EDGE = 16
F32 = jnp.float32
BF16 = jnp.bfloat16
QUERY_SCALE = math.log2(math.e) * HD**-0.5
VMEM = pl.BlockSpec(memory_space=pltpu.VMEM)
HBM = pl.BlockSpec(memory_space=pl.ANY)


def run_kernel(kernel, name, shapes, operands, scratch=(), space=VMEM):
    return pl.pallas_call(
        kernel,
        out_shape=[jax.ShapeDtypeStruct(*s) for s in shapes],
        in_specs=[space] * len(operands),
        out_specs=[VMEM] * len(shapes),
        scratch_shapes=scratch,
        compiler_params=pltpu.CompilerParams(vmem_limit_bytes=24 << 20),
        cost_estimate=pl.CostEstimate(flops=0, bytes_accessed=0, transcendentals=0),
        name=name,
    )(*operands)


def slot_of(step, count):
    return lax.rem(lax.axis_index("tile") + step, count)


def normalized(pieces):
    widened = [piece.astype(F32) for piece in pieces]
    width = sum(piece.shape[1] for piece in widened)
    mean = sum(jnp.sum(piece, axis=1, keepdims=True) for piece in widened) / width
    centred = [piece - mean for piece in widened]
    variance = sum(jnp.sum(piece * piece, axis=1, keepdims=True) for piece in centred) / width
    scale = lax.rsqrt(variance + 1e-06)
    return [(piece * scale).astype(BF16) for piece in centred]


def dot(left, right):
    return jnp.dot(left, right, preferred_element_type=F32)


def project_kernel(*refs, count, scaled, first):
    pieces, weight, outs = refs[:count], refs[count], refs[count + 1 :]
    normed = normalized([piece[...] for piece in pieces])
    products = []
    for which in range(first, weight.shape[0]):
        products.append(
            sum(dot(normed[step], weight[which, slot_of(step, count)]) for step in range(count))
        )
    if scaled:
        outs[0][...] = (products.pop(0) * QUERY_SCALE).astype(BF16)
    columns = weight.shape[3]
    for which, product in enumerate(products):
        outs[-1][:, which * columns : (which + 1) * columns] = product.astype(BF16)


def attended(query, packs, state, index):
    columns = query.shape[1]
    start = index * HD
    head = slice(start, start + HD)
    values = slice(columns + start, columns + start + HD)
    asked = query[:, head]
    scores = [
        lax.dot_general(asked, pack[:, head], (((1,), (1,)), ((), ())), preferred_element_type=F32)
        for pack in packs
    ]
    tops = [jnp.max(score, axis=1, keepdims=True) for score in scores]
    total, mixed = 0.0, 0.0
    if state:
        before, stats = state[0][index], state[1][index]
        tops.append(stats[:, :1])
    maxima = functools.reduce(jnp.maximum, tops)
    if state:
        correction = jnp.exp2(stats[:, :1] - maxima)
        total = stats[:, 1:2] * correction
        mixed = before * correction
    for score, pack in zip(scores, packs):
        expanded = jnp.exp2(score - maxima)
        total = total + jnp.sum(expanded, axis=1, keepdims=True)
        mixed = mixed + dot(expanded.astype(BF16), pack[:, values])
    return mixed, maxima, total


def begin_kernel(query, *refs):
    packs, (mixed_out, stats_out) = refs[:-2], refs[-2:]
    for index in range(query.shape[1] // HD):
        mixed, maxima, total = attended(query, packs, (), index)
        mixed_out[index] = mixed
        stats_out[index] = jnp.concatenate([maxima, total], axis=1)


def ended(query, packs, state):
    heads = []
    for index in range(query.shape[1] // HD):
        mixed, maxima, total = attended(query, packs, state, index)
        heads.append(mixed / total)
    return jnp.concatenate(heads, axis=1).astype(BF16)


def end_kernel(query, *refs):
    refs[-1][...] = ended(query, refs[:-3], refs[-3:-1])


def fill_board(board, values):
    band_rows, channels = board.shape[0], board.shape[2]
    edge = jnp.zeros((band_rows, EDGE, channels), board.dtype)
    board[:, :EDGE, :] = edge
    board[:, EDGE + GRID_W :, :] = edge
    inner = values.reshape(band_rows, GRID_W, channels)
    board[:, EDGE : EDGE + GRID_W, :] = inner.astype(board.dtype)


def window_of(board, slot, out):
    start = pl.multiple_of(slot * (out.shape[1] - 2 * EDGE), EDGE)
    out[...] = board[:, pl.ds(start, out.shape[1]), :].astype(out.dtype)


def end_map_kernel(query, *refs, count):
    composed, outs, board = refs[-2 - count], refs[-1 - count : -1], refs[-1]
    packs, state = refs[: -4 - count], refs[-4 - count : -2 - count]
    fill_board(board, dot(ended(query, packs, state), composed[...]))
    for step, out in enumerate(outs):
        window_of(board, slot_of(count - step, count), out)


def carry_kernel(updated, *refs):
    pieces, out, board = refs[:-2], refs[-2], refs[-1]
    fill_board(board, sum(dot(updated[i], piece[...]) for i, piece in enumerate(pieces)))
    window_of(board, lax.axis_index("tile"), out)


def add_kernel(*refs):
    refs[-1][...] = sum(ref[...].astype(F32) for ref in refs[:-1]).astype(BF16)


def stage_kernel(*refs, cores):
    count = (len(refs) - 2) // 2
    sources, outs, half, sems = refs[:count], refs[count : 2 * count], refs[-2], refs[-1]
    core = lax.axis_index("pair")
    pairs = list(zip(sources, outs))
    rows = sources[0].shape[0] // cores
    begin = pl.multiple_of(core * rows, rows)
    pairs.append((sources[0].at[pl.ds(begin, rows)], half.at[pl.ds(0, rows)]))
    start = rows
    blocks = half.shape[1] // sources[1].shape[1]
    block = sources[1].shape[0] // blocks
    rows = block // cores
    for index in range(blocks):
        begin = pl.multiple_of(core * rows + index * block, rows)
        lanes = pl.ds(index * sources[1].shape[1], sources[1].shape[1])
        pairs.append((sources[1].at[pl.ds(begin, rows)], half.at[pl.ds(start, rows), lanes]))
    copies = [pltpu.make_async_copy(a, b, sems.at[i]) for i, (a, b) in enumerate(pairs)]
    for copy in copies:
        copy.start()
    for copy in copies:
        copy.wait()


def unpack_kernel(*refs):
    halves, outs = refs[:-2], refs[-2:]
    for step, half in enumerate(halves):
        core = lax.rem(lax.axis_index("pair") + step, len(halves))
        rows = outs[0].shape[0] // len(halves)
        outs[0][pl.ds(pl.multiple_of(core * rows, rows), rows), :] = half[:rows, :]
        start = rows
        blocks = half.shape[1] // outs[1].shape[1]
        block = outs[1].shape[0] // blocks
        rows = block // len(halves)
        for index in range(blocks):
            first = pl.multiple_of(core * rows + index * block, rows)
            lanes = slice(index * outs[1].shape[1], (index + 1) * outs[1].shape[1])
            outs[1][pl.ds(first, rows), :] = half[start : start + rows, lanes]


def pick(options, slot):
    chosen = options[0]
    for index in range(1, len(options)):
        chosen = jnp.where(slot == index, options[index], chosen)
    return chosen


def feature_shares(whole, count):
    share = whole.shape[1] // count
    options = [whole[:, i * share : (i + 1) * share] for i in range(count)]
    return [pick(options, slot_of(step, count)) for step in range(count)]


def compose_kernel(weight, *refs):
    pieces, out = refs[:-1], refs[-1]
    shares = feature_shares(weight[...].astype(F32), len(pieces))
    out[...] = sum(dot(s.astype(BF16), p[...]) for s, p in zip(shares, pieces)).astype(BF16)


def update_kernel(*refs, count):
    mixed, weights = refs[:count], refs[count : 2 * count]
    tokens, query_weight = refs[2 * count : 3 * count], refs[3 * count]
    updated, query = refs[3 * count + 1 :]
    whole = sum(dot(m[...], w[...]) for m, w in zip(mixed, weights))
    pieces = []
    for step, term in enumerate(feature_shares(whole, count)):
        piece = (tokens[step][...].astype(F32) + term).astype(BF16)
        updated[step] = piece
        pieces.append(piece)
    normed = normalized(pieces)
    product = sum(
        dot(normed[step], query_weight[0, slot_of(step, count)]) for step in range(count)
    )
    query[...] = (product * QUERY_SCALE).astype(BF16)


def conv_kernel(window, above, below, weight, out):
    width = out.shape[1]
    band_rows, channels = out.shape[0], out.shape[2]
    grid = jnp.concatenate([above[...], window[...], below[...]], axis=0).astype(F32)
    active = jnp.maximum(grid, 0.0)
    total = grid[1 : 1 + band_rows, EDGE : EDGE + width, :].reshape(band_rows * width, channels)
    for column in range(3):
        first = EDGE - 1 + column
        shifted = active[:, first : first + width, :].astype(BF16)
        for row in range(3):
            rows = shifted[row : row + band_rows].reshape(band_rows * width, channels)
            total = total + dot(rows, weight[row, column])
    out[...] = total.reshape(out.shape).astype(BF16)


def body(left_tokens, right_tokens, self_qkv, self_out, cross_qkv, cross_out, reassemble, taps):
    bands, tiles, cores = (lax.axis_size(axis) for axis in ("blk", "tile", "pair"))
    span = bands // cores
    both = ("blk", "pair")
    rows, share = left_tokens.shape[1:]
    columns = self_qkv.shape[2]
    channels = reassemble.shape[1]
    width = GRID_W // tiles
    band_rows = rows // GRID_W
    heads = columns // HD
    window = (band_rows, width + 2 * EDGE, channels)
    board = (band_rows, GRID_W + 2 * EDGE, channels)

    def home(band, pair):
        return band * cores + pair

    def worker(band, pair):
        shift = (pair - band // span) % cores
        return ((band + shift * span) % bands) * cores + (pair - shift) % cores

    places = [(band, pair) for band in range(bands) for pair in range(cores)]
    there = [(home(*p), worker(*p)) for p in places]
    back = [(worker(*p), home(*p)) for p in places]
    down = [(worker(b, p), home(b + 1, p)) for b, p in places if b + 1 < bands]
    up = [(worker(b, p), home(b - 1, p)) for b, p in places if b > 0]

    def fetched(value, step):
        def flat(position, tile):
            return (position // cores * tiles + tile) * cores + position % cores

        pairs = [(flat(s, (i + step) % tiles), flat(d, i)) for s, d in there for i in range(tiles)]
        return lax.ppermute(value, ("blk", "tile", "pair"), pairs)

    def tied(values, *others):
        return lax.optimization_barrier((values, others))[0]

    def from_tile(value, step):
        return lax.ppermute(value, "tile", [((i + step) % tiles, i) for i in range(tiles)])

    def tile_pieces(own):
        return [own, *[from_tile(own, s) for s in range(1, tiles)]]

    def neighbours(pack):
        ring = [(g * span, i) for g in range(cores) for i in range(span)]
        return [
            lax.ppermute(pack, "blk", [(g + (i + s) % span, g + i) for g, i in ring])
            for s in range(1, span)
        ]

    def across(pack):
        return [
            lax.ppermute(pack, "pair", [((i + s) % cores, i) for i in range(cores)])
            for s in range(1, cores)
        ]

    def grouped(packs):
        return packs if len(packs) < 3 else [jnp.concatenate(packs)]

    def project(pieces, weights, scaled, first):
        return run_kernel(
            functools.partial(project_kernel, count=tiles, scaled=scaled, first=first),
            "project",
            [((rows, columns), BF16)] * scaled + [((rows, 2 * columns), BF16)],
            [*pieces, weights.reshape(3, tiles, share, columns)],
        )

    def begin(query, packs):
        shapes = [((heads, rows, HD), F32), ((heads, rows, 2), F32)]
        return run_kernel(begin_kernel, "begin", shapes, [query, *grouped(packs)])

    def staged(weights):
        blocks = weights[0].shape[1] // channels
        height = (weights[0].shape[0] + share // blocks) // cores
        return run_kernel(
            functools.partial(stage_kernel, cores=cores),
            "stage",
            [(w.shape, BF16) for w in weights] + [((height, weights[0].shape[1]), BF16)],
            [pltpu.with_memory_space_constraint(w, pltpu.HBM) for w in weights],
            [pltpu.SemaphoreType.DMA((len(weights) + 1 + blocks,))],
            pl.BlockSpec(memory_space=pl.ANY),
        )

    steps = range(1, tiles)
    left = [fetched(left_tokens[0], step) for step in range(tiles)]
    self_out, reassemble, cross_out, right_own, self_qkv, cross_qkv, taps, half = staged(
        [self_out, reassemble, cross_out, right_tokens[0], self_qkv, cross_qkv, taps]
    )
    right = [right_own, *[from_tile(right_tokens[0], s) for s in steps]]
    (right_pack,) = project(right, cross_qkv, False, 1)
    left, right_pack = lax.optimization_barrier((left, right_pack))
    query, pack = project(left, self_qkv, True, 0)
    beside = neighbours(pack)
    halves = tile_pieces(tied(half, pack))[1:]
    right_pack = lax.ppermute(tied(right_pack, beside), both, there)
    near, halves = lax.optimization_barrier(([pack, *beside], halves))
    far = [q for p in near for q in across(p)]
    state = begin(query, near)
    halves = tied(halves, state)
    (mixed,) = run_kernel(
        end_kernel, "end", [((rows, columns), BF16)], [query, *grouped(far), *state]
    )
    others = [
        run_kernel(
            unpack_kernel,
            "unpack",
            [(w.shape, BF16) for w in (self_out, reassemble)],
            [half, *across(half)],
        )
        for half in halves
    ]
    map_weights = [reassemble, *[other[1] for other in others]]
    (composed,) = run_kernel(
        compose_kernel, "compose", [((columns, channels), BF16)], [cross_out, *map_weights]
    )
    right_pack = tied(right_pack, composed)
    right_near = [right_pack, *across(right_pack)]
    right_beside = neighbours(right_pack)
    mixed, composed = lax.optimization_barrier((tile_pieces(mixed), composed))
    updated, cross_query = run_kernel(
        functools.partial(update_kernel, count=tiles),
        "update",
        [((tiles, rows, share), BF16), ((rows, columns), BF16)],
        [
            *mixed,
            self_out,
            *[other[0] for other in others],
            *left,
            cross_qkv.reshape(3, tiles, share, columns),
        ],
    )
    state = begin(cross_query, right_near)
    right_beside = tied(right_beside, state)
    right_far = [*right_beside, *[q for p in right_beside for q in across(p)]]
    maps = run_kernel(
        functools.partial(end_map_kernel, count=tiles),
        "end_map",
        [(window, BF16)] * tiles,
        [cross_query, *grouped(right_far), *state, composed],
        [pltpu.VMEM(board, F32)],
    )
    (carried,) = run_kernel(
        carry_kernel,
        "carry",
        [(window, F32)],
        [tied(updated, maps), *map_weights],
        [pltpu.VMEM(board, F32)],
    )
    received = [from_tile(part, s) for s, part in enumerate(maps) if s > 0]
    (features,) = run_kernel(add_kernel, "add", [(window, BF16)], [carried, maps[0], *received])
    above = lax.ppermute(features[-1:], both, down)
    below = lax.ppermute(features[:1], both, up)
    features = lax.ppermute(features, both, back)
    (joined,) = run_kernel(
        conv_kernel,
        "join",
        [((band_rows, width, channels), BF16)],
        [features, above, below, taps],
    )
    return joined[None]


def solution(mesh):
    placed = (
        P(("groups", "pair"), "blk", "tile"),
        P(("groups", "pair"), "blk", "tile"),
        P(None, None, "tile"),
        P("tile", None),
        P(None, None, "tile"),
        P("tile", None),
        P("tile", None),
        P(),
    )
    return jax.shard_map(
        body,
        mesh=mesh,
        in_specs=placed,
        out_specs=P(("groups", "pair"), "blk", "tile", None),
        check_vma=False,
    )
```

```python
import functools
import math

import jax
import jax.numpy as jnp
from jax import lax
from jax.experimental import pallas as pl
from jax.experimental.pallas import tpu as pltpu
from jax.sharding import PartitionSpec as P

HD = 64
GRID_W = 128
EDGE = 16
F32 = jnp.float32
BF16 = jnp.bfloat16
QUERY_SCALE = math.log2(math.e) * HD**-0.5
VMEM = pl.BlockSpec(memory_space=pltpu.VMEM)
HBM = pl.BlockSpec(memory_space=pl.ANY)


def run_kernel(kernel, name, shapes, operands, scratch=(), space=VMEM):
    return pl.pallas_call(
        kernel,
        out_shape=[jax.ShapeDtypeStruct(*s) for s in shapes],
        in_specs=[space] * len(operands),
        out_specs=[VMEM] * len(shapes),
        scratch_shapes=scratch,
        compiler_params=pltpu.CompilerParams(vmem_limit_bytes=24 << 20),
        cost_estimate=pl.CostEstimate(flops=0, bytes_accessed=0, transcendentals=0),
        name=name,
    )(*operands)


def slot_of(step, count):
    return lax.rem(lax.axis_index("tile") + step, count)


def normalized(pieces):
    widened = [piece.astype(F32) for piece in pieces]
    width = sum(piece.shape[1] for piece in widened)
    mean = sum(jnp.sum(piece, axis=1, keepdims=True) for piece in widened) / width
    centred = [piece - mean for piece in widened]
    variance = sum(jnp.sum(piece * piece, axis=1, keepdims=True) for piece in centred) / width
    scale = lax.rsqrt(variance + 1e-06)
    return [(piece * scale).astype(BF16) for piece in centred]


def dot(left, right):
    return jnp.dot(left, right, preferred_element_type=F32)


def project_kernel(*refs, count, scaled, first):
    pieces, weight, outs = refs[:count], refs[count], refs[count + 1 :]
    normed = normalized([piece[...] for piece in pieces])
    products = []
    for which in range(first, weight.shape[0]):
        products.append(
            sum(dot(normed[step], weight[which, slot_of(step, count)]) for step in range(count))
        )
    if scaled:
        outs[0][...] = (products.pop(0) * QUERY_SCALE).astype(BF16)
    columns = weight.shape[3]
    for which, product in enumerate(products):
        outs[-1][:, which * columns : (which + 1) * columns] = product.astype(BF16)


def attended(query, packs, index):
    columns = query.shape[1]
    start = index * HD
    head = slice(start, start + HD)
    values = slice(columns + start, columns + start + HD)
    asked = query[:, head]
    scores = [
        lax.dot_general(asked, pack[:, head], (((1,), (1,)), ((), ())), preferred_element_type=F32)
        for pack in packs
    ]
    maxima = functools.reduce(
        jnp.maximum, [jnp.max(score, axis=1, keepdims=True) for score in scores]
    )
    mixed = 0.0
    for score, pack in zip(scores, packs):
        value = pack[:, values]
        widened = jnp.concatenate([value, jnp.ones_like(value)], axis=1)
        mixed = mixed + dot(jnp.exp2(score - maxima).astype(BF16), widened)
    return mixed, maxima


def begin_kernel(query, *refs):
    packs, (mixed_out, maxima_out) = refs[:-2], refs[-2:]
    for index in range(query.shape[1] // HD):
        mixed_out[index], maxima_out[index] = attended(query, packs, index)


def ended(query, packs, state):
    heads = []
    for index in range(query.shape[1] // HD):
        mixed, maxima = attended(query, packs, index)
        if state:
            before = state[1][index]
            highest = jnp.maximum(maxima, before)
            mixed = mixed * jnp.exp2(maxima - highest)
            mixed = mixed + state[0][index] * jnp.exp2(before - highest)
        heads.append(mixed[:, :HD] / mixed[:, HD:])
    return jnp.concatenate(heads, axis=1).astype(BF16)


def end_kernel(query, *refs):
    refs[-1][...] = ended(query, refs[:-3], refs[-3:-1])


def fill_board(board, values):
    band_rows, channels = board.shape[0], board.shape[2]
    edge = jnp.zeros((band_rows, EDGE, channels), board.dtype)
    board[:, :EDGE, :] = edge
    board[:, EDGE + GRID_W :, :] = edge
    inner = values.reshape(band_rows, GRID_W, channels)
    board[:, EDGE : EDGE + GRID_W, :] = inner.astype(board.dtype)


def window_of(board, slot, out):
    start = pl.multiple_of(slot * (out.shape[1] - 2 * EDGE), EDGE)
    out[...] = board[:, pl.ds(start, out.shape[1]), :].astype(out.dtype)


def end_map_kernel(query, *refs, count):
    composed, outs, board = refs[-2 - count], refs[-1 - count : -1], refs[-1]
    fill_board(board, dot(ended(query, refs[: -2 - count], ()), composed[...]))
    for step, out in enumerate(outs):
        window_of(board, slot_of(count - step, count), out)


def carry_kernel(updated, *refs):
    pieces, out, board = refs[:-2], refs[-2], refs[-1]
    fill_board(board, sum(dot(updated[i], piece[...]) for i, piece in enumerate(pieces)))
    window_of(board, lax.axis_index("tile"), out)


def add_kernel(*refs):
    refs[-1][...] = sum(ref[...].astype(F32) for ref in refs[:-1]).astype(BF16)


def stage_kernel(*refs, cores):
    count = (len(refs) - 2) // 2
    sources, outs, half, sems = refs[:count], refs[count : 2 * count], refs[-2], refs[-1]
    core = lax.axis_index("pair")
    pairs = list(zip(sources, outs))
    rows = sources[0].shape[0] // cores
    begin = pl.multiple_of(core * rows, rows)
    pairs.append((sources[0].at[pl.ds(begin, rows)], half.at[pl.ds(0, rows)]))
    start = rows
    blocks = half.shape[1] // sources[1].shape[1]
    block = sources[1].shape[0] // blocks
    rows = block // cores
    for index in range(blocks):
        begin = pl.multiple_of(core * rows + index * block, rows)
        lanes = pl.ds(index * sources[1].shape[1], sources[1].shape[1])
        pairs.append((sources[1].at[pl.ds(begin, rows)], half.at[pl.ds(start, rows), lanes]))
    copies = [pltpu.make_async_copy(a, b, sems.at[i]) for i, (a, b) in enumerate(pairs)]
    for copy in copies:
        copy.start()
    for copy in copies:
        copy.wait()


def unpack_kernel(*refs):
    halves, outs = refs[:-2], refs[-2:]
    for step, half in enumerate(halves):
        core = lax.rem(lax.axis_index("pair") + step, len(halves))
        rows = outs[0].shape[0] // len(halves)
        outs[0][pl.ds(pl.multiple_of(core * rows, rows), rows), :] = half[:rows, :]
        start = rows
        blocks = half.shape[1] // outs[1].shape[1]
        block = outs[1].shape[0] // blocks
        rows = block // len(halves)
        for index in range(blocks):
            first = pl.multiple_of(core * rows + index * block, rows)
            lanes = slice(index * outs[1].shape[1], (index + 1) * outs[1].shape[1])
            outs[1][pl.ds(first, rows), :] = half[start : start + rows, lanes]


def pick(options, slot):
    chosen = options[0]
    for index in range(1, len(options)):
        chosen = jnp.where(slot == index, options[index], chosen)
    return chosen


def feature_shares(whole, count):
    share = whole.shape[1] // count
    options = [whole[:, i * share : (i + 1) * share] for i in range(count)]
    return [pick(options, slot_of(step, count)) for step in range(count)]


def compose_kernel(weight, *refs):
    pieces, out = refs[:-1], refs[-1]
    shares = feature_shares(weight[...].astype(F32), len(pieces))
    out[...] = sum(dot(s.astype(BF16), p[...]) for s, p in zip(shares, pieces)).astype(BF16)


def update_kernel(*refs, count):
    mixed, weights = refs[:count], refs[count : 2 * count]
    tokens, query_weight = refs[2 * count : 3 * count], refs[3 * count]
    updated, query = refs[3 * count + 1 :]
    whole = sum(dot(m[...], w[...]) for m, w in zip(mixed, weights))
    pieces = []
    for step, term in enumerate(feature_shares(whole, count)):
        piece = (tokens[step][...].astype(F32) + term).astype(BF16)
        updated[step] = piece
        pieces.append(piece)
    normed = normalized(pieces)
    product = sum(
        dot(normed[step], query_weight[0, slot_of(step, count)]) for step in range(count)
    )
    query[...] = (product * QUERY_SCALE).astype(BF16)


def conv_kernel(window, above, below, weight, out):
    width = out.shape[1]
    band_rows, channels = out.shape[0], out.shape[2]
    grid = jnp.concatenate([above[...], window[...], below[...]], axis=0).astype(F32)
    active = jnp.maximum(grid, 0.0)
    total = grid[1 : 1 + band_rows, EDGE : EDGE + width, :].reshape(band_rows * width, channels)
    for column in range(3):
        first = EDGE - 1 + column
        shifted = active[:, first : first + width, :].astype(BF16)
        for row in range(3):
            rows = shifted[row : row + band_rows].reshape(band_rows * width, channels)
            total = total + dot(rows, weight[row, column])
    out[...] = total.reshape(out.shape).astype(BF16)


def body(left_tokens, right_tokens, self_qkv, self_out, cross_qkv, cross_out, reassemble, taps):
    bands, tiles, cores = (lax.axis_size(axis) for axis in ("blk", "tile", "pair"))
    span = bands // cores
    both = ("blk", "pair")
    rows, share = left_tokens.shape[1:]
    columns = self_qkv.shape[2]
    channels = reassemble.shape[1]
    width = GRID_W // tiles
    band_rows = rows // GRID_W
    heads = columns // HD
    window = (band_rows, width + 2 * EDGE, channels)
    board = (band_rows, GRID_W + 2 * EDGE, channels)

    def home(band, pair):
        return band * cores + pair

    def worker(band, pair):
        shift = (pair - band // span) % cores
        return ((band + shift * span) % bands) * cores + (pair - shift) % cores

    places = [(band, pair) for band in range(bands) for pair in range(cores)]
    there = [(home(*p), worker(*p)) for p in places]
    back = [(worker(*p), home(*p)) for p in places]
    down = [(worker(b, p), home(b + 1, p)) for b, p in places if b + 1 < bands]
    up = [(worker(b, p), home(b - 1, p)) for b, p in places if b > 0]

    def fetched(value, step):
        def flat(position, tile):
            return (position // cores * tiles + tile) * cores + position % cores

        pairs = [(flat(s, (i + step) % tiles), flat(d, i)) for s, d in there for i in range(tiles)]
        return lax.ppermute(value, ("blk", "tile", "pair"), pairs)

    def tied(values, *others):
        return lax.optimization_barrier((values, others))[0]

    def from_tile(value, step):
        return lax.ppermute(value, "tile", [((i + step) % tiles, i) for i in range(tiles)])

    def tile_pieces(own):
        return [own, *[from_tile(own, s) for s in range(1, tiles)]]

    def neighbours(pack):
        ring = [(g * span, i) for g in range(cores) for i in range(span)]
        return [
            lax.ppermute(pack, "blk", [(g + (i + s) % span, g + i) for g, i in ring])
            for s in range(1, span)
        ]

    def across(pack):
        return [
            lax.ppermute(pack, "pair", [((i + s) % cores, i) for i in range(cores)])
            for s in range(1, cores)
        ]

    def grouped(packs):
        return packs if len(packs) < 5 else [jnp.concatenate(packs)]

    def project(pieces, weights, scaled, first):
        return run_kernel(
            functools.partial(project_kernel, count=tiles, scaled=scaled, first=first),
            "project",
            [((rows, columns), BF16)] * scaled + [((rows, 2 * columns), BF16)],
            [*pieces, weights.reshape(3, tiles, share, columns)],
        )

    def begin(query, packs):
        shapes = [((heads, rows, 2 * HD), F32), ((heads, rows, 1), F32)]
        return run_kernel(begin_kernel, "begin", shapes, [query, *grouped(packs)])

    def staged(weights):
        blocks = weights[0].shape[1] // channels
        height = (weights[0].shape[0] + share // blocks) // cores
        return run_kernel(
            functools.partial(stage_kernel, cores=cores),
            "stage",
            [(w.shape, BF16) for w in weights] + [((height, weights[0].shape[1]), BF16)],
            [pltpu.with_memory_space_constraint(w, pltpu.HBM) for w in weights],
            [pltpu.SemaphoreType.DMA((len(weights) + 1 + blocks,))],
            pl.BlockSpec(memory_space=pl.ANY),
        )

    steps = range(1, tiles)
    left = [fetched(left_tokens[0], step) for step in range(tiles)]
    self_out, reassemble, cross_out, right_own, self_qkv, cross_qkv, taps, half = staged(
        [self_out, reassemble, cross_out, right_tokens[0], self_qkv, cross_qkv, taps]
    )
    right = [right_own, *[from_tile(right_tokens[0], s) for s in steps]]
    (right_pack,) = project(right, cross_qkv, False, 1)
    left, right_pack = lax.optimization_barrier((left, right_pack))
    query, pack = project(left, self_qkv, True, 0)
    right_pack = lax.ppermute(tied(right_pack, pack), both, there)
    beside = neighbours(pack)
    halves = tile_pieces(half)[1:]
    others = [
        run_kernel(
            unpack_kernel,
            "unpack",
            [(w.shape, BF16) for w in (self_out, reassemble)],
            [half, *across(half)],
        )
        for half in halves
    ]
    map_weights = [reassemble, *[other[1] for other in others]]
    (composed,) = run_kernel(
        compose_kernel, "compose", [((columns, channels), BF16)], [cross_out, *map_weights]
    )
    near, others, composed, map_weights = lax.optimization_barrier(
        ([pack, *beside], others, composed, map_weights)
    )
    far = [q for p in near for q in across(p)]
    state = begin(query, near)
    right_pack = tied(right_pack, state)
    right_near = [right_pack, *neighbours(right_pack)]
    (mixed,) = run_kernel(
        end_kernel, "end", [((rows, columns), BF16)], [query, *grouped(far), *state]
    )
    mixed = tile_pieces(mixed)
    right_near = tied(right_near, mixed)
    right_far = [q for p in right_near for q in across(p)]
    updated, cross_query = run_kernel(
        functools.partial(update_kernel, count=tiles),
        "update",
        [((tiles, rows, share), BF16), ((rows, columns), BF16)],
        [
            *mixed,
            self_out,
            *[other[0] for other in others],
            *left,
            cross_qkv.reshape(3, tiles, share, columns),
        ],
    )
    maps = run_kernel(
        functools.partial(end_map_kernel, count=tiles),
        "end_map",
        [(window, BF16)] * tiles,
        [cross_query, *grouped([*right_near, *right_far]), composed],
        [pltpu.VMEM(board, F32)],
    )
    (carried,) = run_kernel(
        carry_kernel,
        "carry",
        [(window, F32)],
        [tied(updated, maps), *map_weights],
        [pltpu.VMEM(board, F32)],
    )
    received = [from_tile(part, s) for s, part in enumerate(maps) if s > 0]
    (features,) = run_kernel(add_kernel, "add", [(window, BF16)], [carried, maps[0], *received])
    above = lax.ppermute(features[-1:], both, down)
    below = lax.ppermute(features[:1], both, up)
    features = lax.ppermute(features, both, back)
    (joined,) = run_kernel(
        conv_kernel,
        "join",
        [((band_rows, width, channels), BF16)],
        [features, above, below, taps],
    )
    return joined[None]


def solution(mesh):
    placed = (
        P(("groups", "pair"), "blk", "tile"),
        P(("groups", "pair"), "blk", "tile"),
        P(None, None, "tile"),
        P("tile", None),
        P(None, None, "tile"),
        P("tile", None),
        P("tile", None),
        P(),
    )
    return jax.shard_map(
        body,
        mesh=mesh,
        in_specs=placed,
        out_specs=P(("groups", "pair"), "blk", "tile", None),
        check_vma=False,
    )
```

```python
import functools
import math

import jax
import jax.numpy as jnp
from jax import lax
from jax.experimental import pallas as pl
from jax.experimental.pallas import tpu as pltpu
from jax.sharding import PartitionSpec as P

HD = 64
GRID_W = 128
EDGE = 16
F32 = jnp.float32
BF16 = jnp.bfloat16
QUERY_SCALE = math.log2(math.e) * HD**-0.5
VMEM = pl.BlockSpec(memory_space=pltpu.VMEM)
HBM = pl.BlockSpec(memory_space=pl.ANY)


def run_kernel(kernel, name, shapes, operands, scratch=(), space=VMEM):
    return pl.pallas_call(
        kernel,
        out_shape=[jax.ShapeDtypeStruct(*s) for s in shapes],
        in_specs=[space] * len(operands),
        out_specs=[VMEM] * len(shapes),
        scratch_shapes=scratch,
        compiler_params=pltpu.CompilerParams(vmem_limit_bytes=24 << 20),
        cost_estimate=pl.CostEstimate(flops=0, bytes_accessed=0, transcendentals=0),
        name=name,
    )(*operands)


def slot_of(step, count):
    return lax.rem(lax.axis_index("tile") + step, count)


def normalized(pieces):
    widened = [piece.astype(F32) for piece in pieces]
    width = sum(piece.shape[1] for piece in widened)
    mean = sum(jnp.sum(piece, axis=1, keepdims=True) for piece in widened) / width
    centred = [piece - mean for piece in widened]
    variance = sum(jnp.sum(piece * piece, axis=1, keepdims=True) for piece in centred) / width
    scale = lax.rsqrt(variance + 1e-06)
    return [(piece * scale).astype(BF16) for piece in centred]


def dot(left, right):
    return jnp.dot(left, right, preferred_element_type=F32)


def project_kernel(*refs, count, scaled, first):
    pieces, weight, outs = refs[:count], refs[count], refs[count + 1 :]
    normed = normalized([piece[...] for piece in pieces])
    products = []
    for which in range(first, weight.shape[0]):
        products.append(
            sum(dot(normed[step], weight[which, slot_of(step, count)]) for step in range(count))
        )
    if scaled:
        outs[0][...] = (products.pop(0) * QUERY_SCALE).astype(BF16)
    columns = weight.shape[3]
    for which, product in enumerate(products):
        outs[-1][:, which * columns : (which + 1) * columns] = product.astype(BF16)


def attended(query, packs, index):
    columns = query.shape[1]
    start = index * HD
    head = slice(start, start + HD)
    values = slice(columns + start, columns + start + HD)
    asked = query[:, head]
    scores = [
        lax.dot_general(asked, pack[:, head], (((1,), (1,)), ((), ())), preferred_element_type=F32)
        for pack in packs
    ]
    maxima = functools.reduce(
        jnp.maximum, [jnp.max(score, axis=1, keepdims=True) for score in scores]
    )
    mixed = 0.0
    for score, pack in zip(scores, packs):
        value = pack[:, values]
        widened = jnp.concatenate([value, jnp.ones_like(value)], axis=1)
        mixed = mixed + dot(jnp.exp2(score - maxima).astype(BF16), widened)
    return mixed, maxima


def begin_kernel(query, *refs):
    packs, (mixed_out, maxima_out) = refs[:-2], refs[-2:]
    for index in range(query.shape[1] // HD):
        mixed_out[index], maxima_out[index] = attended(query, packs, index)


def ended(query, packs, state):
    heads = []
    for index in range(query.shape[1] // HD):
        mixed, maxima = attended(query, packs, index)
        if state:
            before = state[1][index]
            highest = jnp.maximum(maxima, before)
            mixed = mixed * jnp.exp2(maxima - highest)
            mixed = mixed + state[0][index] * jnp.exp2(before - highest)
        heads.append(mixed[:, :HD] / mixed[:, HD:])
    return jnp.concatenate(heads, axis=1).astype(BF16)


def end_kernel(query, *refs):
    refs[-1][...] = ended(query, refs[:-3], refs[-3:-1])


def fill_board(board, values):
    band_rows, channels = board.shape[0], board.shape[2]
    edge = jnp.zeros((band_rows, EDGE, channels), board.dtype)
    board[:, :EDGE, :] = edge
    board[:, EDGE + GRID_W :, :] = edge
    inner = values.reshape(band_rows, GRID_W, channels)
    board[:, EDGE : EDGE + GRID_W, :] = inner.astype(board.dtype)


def window_of(board, slot, out):
    start = pl.multiple_of(slot * (out.shape[1] - 2 * EDGE), EDGE)
    out[...] = board[:, pl.ds(start, out.shape[1]), :].astype(out.dtype)


def end_map_kernel(query, *refs, count):
    carried, composed, outs, board = refs[-3 - count], refs[-2 - count], refs[-1 - count : -1], refs[-1]
    fill_board(board, dot(ended(query, refs[: -3 - count], ()), composed[...]))
    for step, out in enumerate(outs):
        start = pl.multiple_of(slot_of(count - step, count) * (out.shape[1] - 2 * EDGE), EDGE)
        part = board[:, pl.ds(start, out.shape[1]), :]
        out[...] = (part if step else part + carried[...]).astype(BF16)


def carry_kernel(updated, *refs):
    pieces, out, board = refs[:-2], refs[-2], refs[-1]
    fill_board(board, sum(dot(updated[i], piece[...]) for i, piece in enumerate(pieces)))
    window_of(board, lax.axis_index("tile"), out)


def stage_kernel(*refs, cores):
    count = (len(refs) - 2) // 2
    sources, outs, half, sems = refs[:count], refs[count : 2 * count], refs[-2], refs[-1]
    core = lax.axis_index("pair")
    pairs = list(zip(sources, outs))
    rows = sources[0].shape[0] // cores
    begin = pl.multiple_of(core * rows, rows)
    pairs.append((sources[0].at[pl.ds(begin, rows)], half.at[pl.ds(0, rows)]))
    start = rows
    blocks = half.shape[1] // sources[1].shape[1]
    block = sources[1].shape[0] // blocks
    rows = block // cores
    for index in range(blocks):
        begin = pl.multiple_of(core * rows + index * block, rows)
        lanes = pl.ds(index * sources[1].shape[1], sources[1].shape[1])
        pairs.append((sources[1].at[pl.ds(begin, rows)], half.at[pl.ds(start, rows), lanes]))
    copies = [pltpu.make_async_copy(a, b, sems.at[i]) for i, (a, b) in enumerate(pairs)]
    for copy in copies:
        copy.start()
    for copy in copies:
        copy.wait()


def unpack_kernel(*refs):
    halves, outs = refs[:-2], refs[-2:]
    for step, half in enumerate(halves):
        core = lax.rem(lax.axis_index("pair") + step, len(halves))
        rows = outs[0].shape[0] // len(halves)
        outs[0][pl.ds(pl.multiple_of(core * rows, rows), rows), :] = half[:rows, :]
        start = rows
        blocks = half.shape[1] // outs[1].shape[1]
        block = outs[1].shape[0] // blocks
        rows = block // len(halves)
        for index in range(blocks):
            first = pl.multiple_of(core * rows + index * block, rows)
            lanes = slice(index * outs[1].shape[1], (index + 1) * outs[1].shape[1])
            outs[1][pl.ds(first, rows), :] = half[start : start + rows, lanes]


def pick(options, slot):
    chosen = options[0]
    for index in range(1, len(options)):
        chosen = jnp.where(slot == index, options[index], chosen)
    return chosen


def feature_shares(whole, count):
    share = whole.shape[1] // count
    options = [whole[:, i * share : (i + 1) * share] for i in range(count)]
    return [pick(options, slot_of(step, count)) for step in range(count)]


def compose_kernel(weight, *refs):
    pieces, out = refs[:-1], refs[-1]
    shares = feature_shares(weight[...].astype(F32), len(pieces))
    out[...] = sum(dot(s.astype(BF16), p[...]) for s, p in zip(shares, pieces)).astype(BF16)


def update_kernel(*refs, count):
    mixed, weights = refs[:count], refs[count : 2 * count]
    tokens, query_weight = refs[2 * count : 3 * count], refs[3 * count]
    updated, query = refs[3 * count + 1 :]
    whole = sum(dot(m[...], w[...]) for m, w in zip(mixed, weights))
    pieces = []
    for step, term in enumerate(feature_shares(whole, count)):
        piece = (tokens[step][...].astype(F32) + term).astype(BF16)
        updated[step] = piece
        pieces.append(piece)
    normed = normalized(pieces)
    product = sum(
        dot(normed[step], query_weight[0, slot_of(step, count)]) for step in range(count)
    )
    query[...] = (product * QUERY_SCALE).astype(BF16)


def conv_kernel(*refs):
    weight, out = refs[-2:]
    width = out.shape[1]
    band_rows, channels = out.shape[0], out.shape[2]
    count = (len(refs) - 2) // 3

    def summed(parts):
        return sum(part[...].astype(F32) for part in parts).astype(BF16)

    above, window, below = (summed(refs[i * count : (i + 1) * count]) for i in range(3))
    grid = jnp.concatenate([above, window, below], axis=0).astype(F32)
    active = jnp.maximum(grid, 0.0)
    total = grid[1 : 1 + band_rows, EDGE : EDGE + width, :].reshape(band_rows * width, channels)
    for column in range(3):
        first = EDGE - 1 + column
        shifted = active[:, first : first + width, :].astype(BF16)
        for row in range(3):
            rows = shifted[row : row + band_rows].reshape(band_rows * width, channels)
            total = total + dot(rows, weight[row, column])
    out[...] = total.reshape(out.shape).astype(BF16)


def body(left_tokens, right_tokens, self_qkv, self_out, cross_qkv, cross_out, reassemble, taps):
    bands, tiles, cores = (lax.axis_size(axis) for axis in ("blk", "tile", "pair"))
    span = bands // cores
    both = ("blk", "pair")
    rows, share = left_tokens.shape[1:]
    columns = self_qkv.shape[2]
    channels = reassemble.shape[1]
    width = GRID_W // tiles
    band_rows = rows // GRID_W
    heads = columns // HD
    window = (band_rows, width + 2 * EDGE, channels)
    board = (band_rows, GRID_W + 2 * EDGE, channels)

    def home(band, pair):
        return band * cores + pair

    def worker(band, pair):
        shift = (pair - band // span) % cores
        return ((band + shift * span) % bands) * cores + (pair - shift) % cores

    places = [(band, pair) for band in range(bands) for pair in range(cores)]
    there = [(home(*p), worker(*p)) for p in places]
    back = [(worker(*p), home(*p)) for p in places]
    down = [(worker(b, p), home(b + 1, p)) for b, p in places if b + 1 < bands]
    up = [(worker(b, p), home(b - 1, p)) for b, p in places if b > 0]

    def fetched(value, step, moves=there):
        def flat(position, tile):
            return (position // cores * tiles + tile) * cores + position % cores

        pairs = [(flat(s, (i + step) % tiles), flat(d, i)) for s, d in moves for i in range(tiles)]
        return lax.ppermute(value, ("blk", "tile", "pair"), pairs)

    def tied(values, *others):
        return lax.optimization_barrier((values, others))[0]

    def from_tile(value, step):
        return lax.ppermute(value, "tile", [((i + step) % tiles, i) for i in range(tiles)])

    def tile_pieces(own):
        return [own, *[from_tile(own, s) for s in range(1, tiles)]]

    def neighbours(pack):
        ring = [(g * span, i) for g in range(cores) for i in range(span)]
        return [
            lax.ppermute(pack, "blk", [(g + (i + s) % span, g + i) for g, i in ring])
            for s in range(1, span)
        ]

    def across(pack):
        return [
            lax.ppermute(pack, "pair", [((i + s) % cores, i) for i in range(cores)])
            for s in range(1, cores)
        ]

    def grouped(packs):
        return packs if len(packs) < 5 else [jnp.concatenate(packs)]

    def project(pieces, weights, scaled, first):
        return run_kernel(
            functools.partial(project_kernel, count=tiles, scaled=scaled, first=first),
            "project",
            [((rows, columns), BF16)] * scaled + [((rows, 2 * columns), BF16)],
            [*pieces, weights.reshape(3, tiles, share, columns)],
        )

    def begin(query, packs):
        shapes = [((heads, rows, 2 * HD), F32), ((heads, rows, 1), F32)]
        return run_kernel(begin_kernel, "begin", shapes, [query, *grouped(packs)])

    def staged(weights):
        blocks = weights[0].shape[1] // channels
        height = (weights[0].shape[0] + share // blocks) // cores
        return run_kernel(
            functools.partial(stage_kernel, cores=cores),
            "stage",
            [(w.shape, BF16) for w in weights] + [((height, weights[0].shape[1]), BF16)],
            [pltpu.with_memory_space_constraint(w, pltpu.HBM) for w in weights],
            [pltpu.SemaphoreType.DMA((len(weights) + 1 + blocks,))],
            pl.BlockSpec(memory_space=pl.ANY),
        )

    steps = range(1, tiles)
    left = [fetched(left_tokens[0], step) for step in range(tiles)]
    self_out, reassemble, cross_out, right_own, self_qkv, cross_qkv, taps, half = staged(
        [self_out, reassemble, cross_out, right_tokens[0], self_qkv, cross_qkv, taps]
    )
    right = [right_own, *[from_tile(right_tokens[0], s) for s in steps]]
    (right_pack,) = project(right, cross_qkv, False, 1)
    left, right_pack = lax.optimization_barrier((left, right_pack))
    query, pack = project(left, self_qkv, True, 0)
    right_pack = lax.ppermute(tied(right_pack, pack), both, there)
    beside = neighbours(pack)
    halves = tile_pieces(half)[1:]
    others = [
        run_kernel(
            unpack_kernel,
            "unpack",
            [(w.shape, BF16) for w in (self_out, reassemble)],
            [half, *across(half)],
        )
        for half in halves
    ]
    map_weights = [reassemble, *[other[1] for other in others]]
    (composed,) = run_kernel(
        compose_kernel, "compose", [((columns, channels), BF16)], [cross_out, *map_weights]
    )
    near, others, composed, map_weights = lax.optimization_barrier(
        ([pack, *beside], others, composed, map_weights)
    )
    far = [q for p in near for q in across(p)]
    state = begin(query, near)
    right_pack = tied(right_pack, state)
    right_near = [right_pack, *neighbours(right_pack)]
    (mixed,) = run_kernel(
        end_kernel, "end", [((rows, columns), BF16)], [query, *grouped(far), *state]
    )
    mixed = tile_pieces(mixed)
    right_near = tied(right_near, mixed)
    right_far = [q for p in right_near for q in across(p)]
    updated, cross_query = run_kernel(
        functools.partial(update_kernel, count=tiles),
        "update",
        [((tiles, rows, share), BF16), ((rows, columns), BF16)],
        [
            *mixed,
            self_out,
            *[other[0] for other in others],
            *left,
            cross_qkv.reshape(3, tiles, share, columns),
        ],
    )
    (carried,) = run_kernel(
        carry_kernel,
        "carry",
        [(window, F32)],
        [updated, *map_weights],
        [pltpu.VMEM(board, F32)],
    )
    maps = run_kernel(
        functools.partial(end_map_kernel, count=tiles),
        "end_map",
        [(window, BF16)] * tiles,
        [cross_query, *grouped([*right_near, *right_far]), carried, composed],
        [pltpu.VMEM(board, F32)],
    )
    above = [fetched(part[-1:], s, down) for s, part in enumerate(maps)]
    below = [fetched(part[:1], s, up) for s, part in enumerate(maps)]
    middle = [fetched(part, s, back) for s, part in enumerate(maps)]
    (joined,) = run_kernel(
        conv_kernel,
        "join",
        [((band_rows, width, channels), BF16)],
        [*above, *middle, *below, taps],
    )
    return joined[None]


def solution(mesh):
    placed = (
        P(("groups", "pair"), "blk", "tile"),
        P(("groups", "pair"), "blk", "tile"),
        P(None, None, "tile"),
        P("tile", None),
        P(None, None, "tile"),
        P("tile", None),
        P("tile", None),
        P(),
    )
    return jax.shard_map(
        body,
        mesh=mesh,
        in_specs=placed,
        out_specs=P(("groups", "pair"), "blk", "tile", None),
        check_vma=False,
    )
```

```python
import functools
import math

import jax
import jax.numpy as jnp
from jax import lax
from jax.experimental import pallas as pl
from jax.experimental.pallas import tpu as pltpu
from jax.sharding import PartitionSpec as P

HD = 64
GRID_W = 128
EDGE = 16
F32 = jnp.float32
BF16 = jnp.bfloat16
QUERY_SCALE = math.log2(math.e) * HD**-0.5
VMEM = pl.BlockSpec(memory_space=pltpu.VMEM)
HBM = pl.BlockSpec(memory_space=pl.ANY)


def run_kernel(kernel, name, shapes, operands, scratch=(), space=VMEM):
    return pl.pallas_call(
        kernel,
        out_shape=[jax.ShapeDtypeStruct(*s) for s in shapes],
        in_specs=[space] * len(operands),
        out_specs=[VMEM] * len(shapes),
        scratch_shapes=scratch,
        compiler_params=pltpu.CompilerParams(vmem_limit_bytes=24 << 20),
        cost_estimate=pl.CostEstimate(flops=0, bytes_accessed=0, transcendentals=0),
        name=name,
    )(*operands)


def slot_of(step, count):
    return lax.rem(lax.axis_index("tile") + step, count)


def normalized(pieces):
    widened = [piece.astype(F32) for piece in pieces]
    width = sum(piece.shape[1] for piece in widened)
    mean = sum(jnp.sum(piece, axis=1, keepdims=True) for piece in widened) / width
    centred = [piece - mean for piece in widened]
    variance = sum(jnp.sum(piece * piece, axis=1, keepdims=True) for piece in centred) / width
    scale = lax.rsqrt(variance + 1e-06)
    return [(piece * scale).astype(BF16) for piece in centred]


def dot(left, right):
    return jnp.dot(left, right, preferred_element_type=F32)


def project_kernel(*refs, count, scaled, first):
    pieces, weight, outs = refs[:count], refs[count], refs[count + 1 :]
    normed = normalized([piece[...] for piece in pieces])
    products = []
    for which in range(first, weight.shape[0]):
        products.append(
            sum(dot(normed[step], weight[which, slot_of(step, count)]) for step in range(count))
        )
    if scaled:
        outs[0][...] = (products.pop(0) * QUERY_SCALE).astype(BF16)
    columns = weight.shape[3]
    for which, product in enumerate(products):
        outs[-1][:, which * columns : (which + 1) * columns] = product.astype(BF16)


def attended(query, packs, index):
    columns = query.shape[1]
    start = index * HD
    head = slice(start, start + HD)
    values = slice(columns + start, columns + start + HD)
    asked = query[:, head]
    scores = [
        lax.dot_general(asked, pack[:, head], (((1,), (1,)), ((), ())), preferred_element_type=F32)
        for pack in packs
    ]
    maxima = functools.reduce(
        jnp.maximum, [jnp.max(score, axis=1, keepdims=True) for score in scores]
    )
    mixed = 0.0
    for score, pack in zip(scores, packs):
        value = pack[:, values]
        widened = jnp.concatenate([value, jnp.ones_like(value)], axis=1)
        mixed = mixed + dot(jnp.exp2(score - maxima).astype(BF16), widened)
    return mixed, maxima


def begin_kernel(query, *refs):
    packs, (mixed_out, maxima_out) = refs[:-2], refs[-2:]
    for index in range(query.shape[1] // HD):
        mixed_out[index], maxima_out[index] = attended(query, packs, index)


def ended(query, packs, state):
    heads = []
    for index in range(query.shape[1] // HD):
        mixed, maxima = attended(query, packs, index)
        if state:
            before = state[1][index]
            highest = jnp.maximum(maxima, before)
            mixed = mixed * jnp.exp2(maxima - highest)
            mixed = mixed + state[0][index] * jnp.exp2(before - highest)
        heads.append(mixed[:, :HD] / mixed[:, HD:])
    return jnp.concatenate(heads, axis=1).astype(BF16)


def end_kernel(query, *refs):
    refs[-1][...] = ended(query, refs[:-3], refs[-3:-1])


def fill_board(board, values):
    band_rows, channels = board.shape[0], board.shape[2]
    edge = jnp.zeros((band_rows, EDGE, channels), board.dtype)
    board[:, :EDGE, :] = edge
    board[:, EDGE + GRID_W :, :] = edge
    inner = values.reshape(band_rows, GRID_W, channels)
    board[:, EDGE : EDGE + GRID_W, :] = inner.astype(board.dtype)


def window_of(board, slot, out):
    start = pl.multiple_of(slot * (out.shape[1] - 2 * EDGE), EDGE)
    out[...] = board[:, pl.ds(start, out.shape[1]), :].astype(out.dtype)


def end_map_kernel(query, *refs, count):
    composed, outs, board = refs[-2 - count], refs[-1 - count : -1], refs[-1]
    fill_board(board, dot(ended(query, refs[: -2 - count], ()), composed[...]))
    for step, out in enumerate(outs):
        window_of(board, slot_of(count - step, count), out)


def carry_kernel(updated, *refs):
    pieces, out, board = refs[:-2], refs[-2], refs[-1]
    fill_board(board, sum(dot(updated[i], piece[...]) for i, piece in enumerate(pieces)))
    window_of(board, lax.axis_index("tile"), out)


def add_kernel(*refs):
    refs[-1][...] = sum(ref[...].astype(F32) for ref in refs[:-1]).astype(BF16)


def stage_kernel(*refs, cores):
    count = (len(refs) - 2) // 2
    sources, outs, half, sems = refs[:count], refs[count : 2 * count], refs[-2], refs[-1]
    core = lax.axis_index("pair")
    pairs = list(zip(sources, outs))
    rows = sources[0].shape[0] // cores
    begin = pl.multiple_of(core * rows, rows)
    pairs.append((sources[0].at[pl.ds(begin, rows)], half.at[pl.ds(0, rows)]))
    start = rows
    blocks = half.shape[1] // sources[1].shape[1]
    block = sources[1].shape[0] // blocks
    rows = block // cores
    for index in range(blocks):
        begin = pl.multiple_of(core * rows + index * block, rows)
        lanes = pl.ds(index * sources[1].shape[1], sources[1].shape[1])
        pairs.append((sources[1].at[pl.ds(begin, rows)], half.at[pl.ds(start, rows), lanes]))
    copies = [pltpu.make_async_copy(a, b, sems.at[i]) for i, (a, b) in enumerate(pairs)]
    for copy in copies:
        copy.start()
    for copy in copies:
        copy.wait()


def unpack_kernel(*refs):
    halves, outs = refs[:-2], refs[-2:]
    for step, half in enumerate(halves):
        core = lax.rem(lax.axis_index("pair") + step, len(halves))
        rows = outs[0].shape[0] // len(halves)
        outs[0][pl.ds(pl.multiple_of(core * rows, rows), rows), :] = half[:rows, :]
        start = rows
        blocks = half.shape[1] // outs[1].shape[1]
        block = outs[1].shape[0] // blocks
        rows = block // len(halves)
        for index in range(blocks):
            first = pl.multiple_of(core * rows + index * block, rows)
            lanes = slice(index * outs[1].shape[1], (index + 1) * outs[1].shape[1])
            outs[1][pl.ds(first, rows), :] = half[start : start + rows, lanes]


def pick(options, slot):
    chosen = options[0]
    for index in range(1, len(options)):
        chosen = jnp.where(slot == index, options[index], chosen)
    return chosen


def feature_shares(whole, count):
    share = whole.shape[1] // count
    options = [whole[:, i * share : (i + 1) * share] for i in range(count)]
    return [pick(options, slot_of(step, count)) for step in range(count)]


def compose_kernel(weight, *refs):
    pieces, out = refs[:-1], refs[-1]
    shares = feature_shares(weight[...].astype(F32), len(pieces))
    out[...] = sum(dot(s.astype(BF16), p[...]) for s, p in zip(shares, pieces)).astype(BF16)


def update_kernel(*refs, count):
    mixed, weights = refs[:count], refs[count : 2 * count]
    tokens, query_weight = refs[2 * count : 3 * count], refs[3 * count]
    updated, query = refs[3 * count + 1 :]
    whole = sum(dot(m[...], w[...]) for m, w in zip(mixed, weights))
    pieces = []
    for step, term in enumerate(feature_shares(whole, count)):
        piece = (tokens[step][...].astype(F32) + term).astype(BF16)
        updated[step] = piece
        pieces.append(piece)
    normed = normalized(pieces)
    product = sum(
        dot(normed[step], query_weight[0, slot_of(step, count)]) for step in range(count)
    )
    query[...] = (product * QUERY_SCALE).astype(BF16)


def conv_kernel(window, above, below, weight, out):
    width = out.shape[1]
    band_rows, channels = out.shape[0], out.shape[2]
    grid = jnp.concatenate([above[...], window[...], below[...]], axis=0).astype(F32)
    active = jnp.maximum(grid, 0.0)
    total = grid[1 : 1 + band_rows, EDGE : EDGE + width, :].reshape(band_rows * width, channels)
    for column in range(3):
        first = EDGE - 1 + column
        shifted = active[:, first : first + width, :].astype(BF16)
        for row in range(3):
            rows = shifted[row : row + band_rows].reshape(band_rows * width, channels)
            total = total + dot(rows, weight[row, column])
    out[...] = total.reshape(out.shape).astype(BF16)


def body(left_tokens, right_tokens, self_qkv, self_out, cross_qkv, cross_out, reassemble, taps):
    bands, tiles, cores = (lax.axis_size(axis) for axis in ("blk", "tile", "pair"))
    span = bands // cores
    both = ("blk", "pair")
    rows, share = left_tokens.shape[1:]
    columns = self_qkv.shape[2]
    channels = reassemble.shape[1]
    width = GRID_W // tiles
    band_rows = rows // GRID_W
    heads = columns // HD
    window = (band_rows, width + 2 * EDGE, channels)
    board = (band_rows, GRID_W + 2 * EDGE, channels)

    def home(band, pair):
        return band * cores + pair

    def worker(band, pair):
        part, index = divmod(band, span)
        if part == pair:
            return band * cores + pair
        shift = (pair - part) % cores
        return (pair * span + span - 1 - index) * cores + (pair - shift) % cores

    places = [(band, pair) for band in range(bands) for pair in range(cores)]
    there = [(home(*p), worker(*p)) for p in places]
    back = [(worker(*p), home(*p)) for p in places]
    down = [(worker(b, p), home(b + 1, p)) for b, p in places if b + 1 < bands]
    up = [(worker(b, p), home(b - 1, p)) for b, p in places if b > 0]

    def fetched(value, step):
        def flat(position, tile):
            return (position // cores * tiles + tile) * cores + position % cores

        pairs = [(flat(s, (i + step) % tiles), flat(d, i)) for s, d in there for i in range(tiles)]
        return lax.ppermute(value, ("blk", "tile", "pair"), pairs)

    def tied(values, *others):
        return lax.optimization_barrier((values, others))[0]

    def from_tile(value, step):
        return lax.ppermute(value, "tile", [((i + step) % tiles, i) for i in range(tiles)])

    def tile_pieces(own):
        return [own, *[from_tile(own, s) for s in range(1, tiles)]]

    def neighbours(pack):
        ring = [(g * span, i) for g in range(cores) for i in range(span)]
        return [
            lax.ppermute(pack, "blk", [(g + (i + s) % span, g + i) for g, i in ring])
            for s in range(1, span)
        ]

    def across(pack):
        return [
            lax.ppermute(pack, "pair", [((i + s) % cores, i) for i in range(cores)])
            for s in range(1, cores)
        ]

    def grouped(packs):
        return packs if len(packs) < 5 else [jnp.concatenate(packs)]

    def project(pieces, weights, scaled, first):
        return run_kernel(
            functools.partial(project_kernel, count=tiles, scaled=scaled, first=first),
            "project",
            [((rows, columns), BF16)] * scaled + [((rows, 2 * columns), BF16)],
            [*pieces, weights.reshape(3, tiles, share, columns)],
        )

    def begin(query, packs):
        shapes = [((heads, rows, 2 * HD), F32), ((heads, rows, 1), F32)]
        return run_kernel(begin_kernel, "begin", shapes, [query, *grouped(packs)])

    def staged(weights):
        blocks = weights[0].shape[1] // channels
        height = (weights[0].shape[0] + share // blocks) // cores
        return run_kernel(
            functools.partial(stage_kernel, cores=cores),
            "stage",
            [(w.shape, BF16) for w in weights] + [((height, weights[0].shape[1]), BF16)],
            [pltpu.with_memory_space_constraint(w, pltpu.HBM) for w in weights],
            [pltpu.SemaphoreType.DMA((len(weights) + 1 + blocks,))],
            pl.BlockSpec(memory_space=pl.ANY),
        )

    steps = range(1, tiles)
    left = [fetched(left_tokens[0], step) for step in range(tiles)]
    self_out, reassemble, cross_out, right_own, self_qkv, cross_qkv, taps, half = staged(
        [self_out, reassemble, cross_out, right_tokens[0], self_qkv, cross_qkv, taps]
    )
    right = [right_own, *[from_tile(right_tokens[0], s) for s in steps]]
    (right_pack,) = project(right, cross_qkv, False, 1)
    left, right_pack = lax.optimization_barrier((left, right_pack))
    query, pack = project(left, self_qkv, True, 0)
    right_pack = lax.ppermute(tied(right_pack, pack), both, there)
    beside = neighbours(pack)
    halves = tile_pieces(half)[1:]
    others = [
        run_kernel(
            unpack_kernel,
            "unpack",
            [(w.shape, BF16) for w in (self_out, reassemble)],
            [half, *across(half)],
        )
        for half in halves
    ]
    map_weights = [reassemble, *[other[1] for other in others]]
    (composed,) = run_kernel(
        compose_kernel, "compose", [((columns, channels), BF16)], [cross_out, *map_weights]
    )
    near, others, composed, map_weights = lax.optimization_barrier(
        ([pack, *beside], others, composed, map_weights)
    )
    far = [q for p in near for q in across(p)]
    state = begin(query, near)
    right_pack = tied(right_pack, state)
    right_near = [right_pack, *neighbours(right_pack)]
    (mixed,) = run_kernel(
        end_kernel, "end", [((rows, columns), BF16)], [query, *grouped(far), *state]
    )
    mixed = tile_pieces(mixed)
    right_near = tied(right_near, mixed)
    right_far = [q for p in right_near for q in across(p)]
    updated, cross_query = run_kernel(
        functools.partial(update_kernel, count=tiles),
        "update",
        [((tiles, rows, share), BF16), ((rows, columns), BF16)],
        [
            *mixed,
            self_out,
            *[other[0] for other in others],
            *left,
            cross_qkv.reshape(3, tiles, share, columns),
        ],
    )
    maps = run_kernel(
        functools.partial(end_map_kernel, count=tiles),
        "end_map",
        [(window, BF16)] * tiles,
        [cross_query, *grouped([*right_near, *right_far]), composed],
        [pltpu.VMEM(board, F32)],
    )
    (carried,) = run_kernel(
        carry_kernel,
        "carry",
        [(window, F32)],
        [tied(updated, maps), *map_weights],
        [pltpu.VMEM(board, F32)],
    )
    received = [from_tile(part, s) for s, part in enumerate(maps) if s > 0]
    (features,) = run_kernel(add_kernel, "add", [(window, BF16)], [carried, maps[0], *received])
    above = lax.ppermute(features[-1:], both, down)
    below = lax.ppermute(features[:1], both, up)
    features = lax.ppermute(features, both, back)
    (joined,) = run_kernel(
        conv_kernel,
        "join",
        [((band_rows, width, channels), BF16)],
        [features, above, below, taps],
    )
    return joined[None]


def solution(mesh):
    placed = (
        P(("groups", "pair"), "blk", "tile"),
        P(("groups", "pair"), "blk", "tile"),
        P(None, None, "tile"),
        P("tile", None),
        P(None, None, "tile"),
        P("tile", None),
        P("tile", None),
        P(),
    )
    return jax.shard_map(
        body,
        mesh=mesh,
        in_specs=placed,
        out_specs=P(("groups", "pair"), "blk", "tile", None),
        check_vma=False,
    )
```

```python
import functools
import math

import jax
import jax.numpy as jnp
from jax import lax
from jax.experimental import pallas as pl
from jax.experimental.pallas import tpu as pltpu
from jax.sharding import PartitionSpec as P

HD = 64
GRID_W = 128
EDGE = 16
F32 = jnp.float32
BF16 = jnp.bfloat16
QUERY_SCALE = math.log2(math.e) * HD**-0.5
VMEM = pl.BlockSpec(memory_space=pltpu.VMEM)
HBM = pl.BlockSpec(memory_space=pl.ANY)


def run_kernel(kernel, name, shapes, operands, scratch=(), space=VMEM):
    return pl.pallas_call(
        kernel,
        out_shape=[jax.ShapeDtypeStruct(*s) for s in shapes],
        in_specs=[space] * len(operands),
        out_specs=[VMEM] * len(shapes),
        scratch_shapes=scratch,
        compiler_params=pltpu.CompilerParams(vmem_limit_bytes=24 << 20),
        cost_estimate=pl.CostEstimate(flops=0, bytes_accessed=0, transcendentals=0),
        name=name,
    )(*operands)


def slot_of(step, count):
    return lax.rem(lax.axis_index("tile") + step, count)


def normalized(pieces):
    widened = [piece.astype(F32) for piece in pieces]
    width = sum(piece.shape[1] for piece in widened)
    mean = sum(jnp.sum(piece, axis=1, keepdims=True) for piece in widened) / width
    centred = [piece - mean for piece in widened]
    variance = sum(jnp.sum(piece * piece, axis=1, keepdims=True) for piece in centred) / width
    scale = lax.rsqrt(variance + 1e-06)
    return [(piece * scale).astype(BF16) for piece in centred]


def dot(left, right):
    return jnp.dot(left, right, preferred_element_type=F32)


def project_kernel(*refs, count, scaled, first):
    pieces, weight, outs = refs[:count], refs[count], refs[count + 1 :]
    normed = normalized([piece[...] for piece in pieces])
    products = []
    for which in range(first, weight.shape[0]):
        products.append(
            sum(dot(normed[step], weight[which, slot_of(step, count)]) for step in range(count))
        )
    if scaled:
        outs[0][...] = (products.pop(0) * QUERY_SCALE).astype(BF16)
    columns = weight.shape[3]
    for which, product in enumerate(products):
        outs[-1][:, which * columns : (which + 1) * columns] = product.astype(BF16)


def attended(query, packs, index):
    columns = query.shape[1]
    start = index * HD
    head = slice(start, start + HD)
    values = slice(columns + start, columns + start + HD)
    asked = query[:, head]
    scores = [
        lax.dot_general(asked, pack[:, head], (((1,), (1,)), ((), ())), preferred_element_type=F32)
        for pack in packs
    ]
    maxima = functools.reduce(
        jnp.maximum, [jnp.max(score, axis=1, keepdims=True) for score in scores]
    )
    mixed = 0.0
    for score, pack in zip(scores, packs):
        value = pack[:, values]
        widened = jnp.concatenate([value, jnp.ones_like(value)], axis=1)
        mixed = mixed + dot(jnp.exp2(score - maxima).astype(BF16), widened)
    return mixed, maxima


def begin_kernel(query, *refs):
    packs, (mixed_out, maxima_out) = refs[:-2], refs[-2:]
    for index in range(query.shape[1] // HD):
        mixed_out[index], maxima_out[index] = attended(query, packs, index)


def ended(query, packs, state):
    heads = []
    for index in range(query.shape[1] // HD):
        mixed, maxima = attended(query, packs, index)
        if state:
            before = state[1][index]
            highest = jnp.maximum(maxima, before)
            mixed = mixed * jnp.exp2(maxima - highest)
            mixed = mixed + state[0][index] * jnp.exp2(before - highest)
        heads.append(mixed[:, :HD] / mixed[:, HD:])
    return jnp.concatenate(heads, axis=1).astype(BF16)


def end_kernel(query, *refs):
    refs[-1][...] = ended(query, refs[:-3], refs[-3:-1])


def fill_board(board, values):
    band_rows, channels = board.shape[0], board.shape[2]
    edge = jnp.zeros((band_rows, EDGE, channels), board.dtype)
    board[:, :EDGE, :] = edge
    board[:, EDGE + GRID_W :, :] = edge
    inner = values.reshape(band_rows, GRID_W, channels)
    board[:, EDGE : EDGE + GRID_W, :] = inner.astype(board.dtype)


def window_of(board, slot, out):
    start = pl.multiple_of(slot * (out.shape[1] - 2 * EDGE), EDGE)
    out[...] = board[:, pl.ds(start, out.shape[1]), :].astype(out.dtype)


def end_map_kernel(query, *refs, count):
    composed, outs, board = refs[-2 - count], refs[-1 - count : -1], refs[-1]
    fill_board(board, dot(ended(query, refs[: -2 - count], ()), composed[...]))
    for step, out in enumerate(outs):
        window_of(board, slot_of(count - step, count), out)


def carry_kernel(updated, *refs):
    pieces, out, board = refs[:-2], refs[-2], refs[-1]
    fill_board(board, sum(dot(updated[i], piece[...]) for i, piece in enumerate(pieces)))
    window_of(board, lax.axis_index("tile"), out)


def add_kernel(*refs):
    refs[-1][...] = sum(ref[...].astype(F32) for ref in refs[:-1]).astype(BF16)


def stage_kernel(*refs, cores):
    count = (len(refs) - 2) // 2
    sources, outs, half, sems = refs[:count], refs[count : 2 * count], refs[-2], refs[-1]
    core = lax.axis_index("pair")
    pairs = list(zip(sources, outs))
    rows = sources[0].shape[0] // cores
    begin = pl.multiple_of(core * rows, rows)
    pairs.append((sources[0].at[pl.ds(begin, rows)], half.at[pl.ds(0, rows)]))
    start = rows
    blocks = half.shape[1] // sources[1].shape[1]
    block = sources[1].shape[0] // blocks
    rows = block // cores
    for index in range(blocks):
        begin = pl.multiple_of(core * rows + index * block, rows)
        lanes = pl.ds(index * sources[1].shape[1], sources[1].shape[1])
        pairs.append((sources[1].at[pl.ds(begin, rows)], half.at[pl.ds(start, rows), lanes]))
    copies = [pltpu.make_async_copy(a, b, sems.at[i]) for i, (a, b) in enumerate(pairs)]
    for copy in copies:
        copy.start()
    for copy in copies:
        copy.wait()


def unpack_kernel(*refs):
    halves, outs = refs[:-2], refs[-2:]
    for step, half in enumerate(halves):
        core = lax.rem(lax.axis_index("pair") + step, len(halves))
        rows = outs[0].shape[0] // len(halves)
        outs[0][pl.ds(pl.multiple_of(core * rows, rows), rows), :] = half[:rows, :]
        start = rows
        blocks = half.shape[1] // outs[1].shape[1]
        block = outs[1].shape[0] // blocks
        rows = block // len(halves)
        for index in range(blocks):
            first = pl.multiple_of(core * rows + index * block, rows)
            lanes = slice(index * outs[1].shape[1], (index + 1) * outs[1].shape[1])
            outs[1][pl.ds(first, rows), :] = half[start : start + rows, lanes]


def pick(options, slot):
    chosen = options[0]
    for index in range(1, len(options)):
        chosen = jnp.where(slot == index, options[index], chosen)
    return chosen


def feature_shares(whole, count):
    share = whole.shape[1] // count
    options = [whole[:, i * share : (i + 1) * share] for i in range(count)]
    return [pick(options, slot_of(step, count)) for step in range(count)]


def compose_kernel(weight, *refs):
    pieces, out = refs[:-1], refs[-1]
    shares = feature_shares(weight[...].astype(F32), len(pieces))
    out[...] = sum(dot(s.astype(BF16), p[...]) for s, p in zip(shares, pieces)).astype(BF16)


def update_kernel(*refs, count):
    mixed, weights = refs[:count], refs[count : 2 * count]
    tokens, query_weight = refs[2 * count : 3 * count], refs[3 * count]
    updated, query = refs[3 * count + 1 :]
    whole = sum(dot(m[...], w[...]) for m, w in zip(mixed, weights))
    pieces = []
    for step, term in enumerate(feature_shares(whole, count)):
        piece = (tokens[step][...].astype(F32) + term).astype(BF16)
        updated[step] = piece
        pieces.append(piece)
    normed = normalized(pieces)
    product = sum(
        dot(normed[step], query_weight[0, slot_of(step, count)]) for step in range(count)
    )
    query[...] = (product * QUERY_SCALE).astype(BF16)


def conv_kernel(window, above, below, weight, out):
    width = out.shape[1]
    band_rows, channels = out.shape[0], out.shape[2]
    grid = jnp.concatenate([above[...], window[...], below[...]], axis=0).astype(F32)
    active = jnp.maximum(grid, 0.0)
    total = grid[1 : 1 + band_rows, EDGE : EDGE + width, :].reshape(band_rows * width, channels)
    for column in range(3):
        first = EDGE - 1 + column
        shifted = active[:, first : first + width, :].astype(BF16)
        for row in range(3):
            rows = shifted[row : row + band_rows].reshape(band_rows * width, channels)
            total = total + dot(rows, weight[row, column])
    out[...] = total.reshape(out.shape).astype(BF16)


def body(left_tokens, right_tokens, self_qkv, self_out, cross_qkv, cross_out, reassemble, taps):
    bands, tiles, cores = (lax.axis_size(axis) for axis in ("blk", "tile", "pair"))
    span = bands // cores
    both = ("blk", "pair")
    rows, share = left_tokens.shape[1:]
    columns = self_qkv.shape[2]
    channels = reassemble.shape[1]
    width = GRID_W // tiles
    band_rows = rows // GRID_W
    heads = columns // HD
    window = (band_rows, width + 2 * EDGE, channels)
    board = (band_rows, GRID_W + 2 * EDGE, channels)

    def home(band, pair):
        return band * cores + pair

    def worker(band, pair):
        return pair * bands + band

    places = [(band, pair) for band in range(bands) for pair in range(cores)]
    there = [(home(*p), worker(*p)) for p in places]
    back = [(worker(*p), home(*p)) for p in places]
    down = [(worker(b, p), home(b + 1, p)) for b, p in places if b + 1 < bands]
    up = [(worker(b, p), home(b - 1, p)) for b, p in places if b > 0]

    def fetched(value, step):
        def flat(position, tile):
            return (position // cores * tiles + tile) * cores + position % cores

        pairs = [(flat(s, (i + step) % tiles), flat(d, i)) for s, d in there for i in range(tiles)]
        return lax.ppermute(value, ("blk", "tile", "pair"), pairs)

    def tied(values, *others):
        return lax.optimization_barrier((values, others))[0]

    def from_tile(value, step):
        return lax.ppermute(value, "tile", [((i + step) % tiles, i) for i in range(tiles)])

    def tile_pieces(own):
        return [own, *[from_tile(own, s) for s in range(1, tiles)]]

    def neighbours(pack):
        ring = [(g * span, i) for g in range(cores) for i in range(span)]
        return [
            lax.ppermute(pack, "blk", [(g + (i + s) % span, g + i) for g, i in ring])
            for s in range(1, span)
        ]

    def across(pack):
        return [
            lax.ppermute(pack, "pair", [((i + s) % cores, i) for i in range(cores)])
            for s in range(1, cores)
        ]

    def grouped(packs):
        return packs if len(packs) < 5 else [jnp.concatenate(packs)]

    def project(pieces, weights, scaled, first):
        return run_kernel(
            functools.partial(project_kernel, count=tiles, scaled=scaled, first=first),
            "project",
            [((rows, columns), BF16)] * scaled + [((rows, 2 * columns), BF16)],
            [*pieces, weights.reshape(3, tiles, share, columns)],
        )

    def begin(query, packs):
        shapes = [((heads, rows, 2 * HD), F32), ((heads, rows, 1), F32)]
        return run_kernel(begin_kernel, "begin", shapes, [query, *grouped(packs)])

    def staged(weights):
        blocks = weights[0].shape[1] // channels
        height = (weights[0].shape[0] + share // blocks) // cores
        return run_kernel(
            functools.partial(stage_kernel, cores=cores),
            "stage",
            [(w.shape, BF16) for w in weights] + [((height, weights[0].shape[1]), BF16)],
            [pltpu.with_memory_space_constraint(w, pltpu.HBM) for w in weights],
            [pltpu.SemaphoreType.DMA((len(weights) + 1 + blocks,))],
            pl.BlockSpec(memory_space=pl.ANY),
        )

    steps = range(1, tiles)
    left = [fetched(left_tokens[0], step) for step in range(tiles)]
    self_out, reassemble, cross_out, right_own, self_qkv, cross_qkv, taps, half = staged(
        [self_out, reassemble, cross_out, right_tokens[0], self_qkv, cross_qkv, taps]
    )
    right = [right_own, *[from_tile(right_tokens[0], s) for s in steps]]
    (right_pack,) = project(right, cross_qkv, False, 1)
    left, right_pack = lax.optimization_barrier((left, right_pack))
    query, pack = project(left, self_qkv, True, 0)
    right_pack = lax.ppermute(tied(right_pack, pack), both, there)
    beside = neighbours(pack)
    halves = tile_pieces(half)[1:]
    others = [
        run_kernel(
            unpack_kernel,
            "unpack",
            [(w.shape, BF16) for w in (self_out, reassemble)],
            [half, *across(half)],
        )
        for half in halves
    ]
    map_weights = [reassemble, *[other[1] for other in others]]
    (composed,) = run_kernel(
        compose_kernel, "compose", [((columns, channels), BF16)], [cross_out, *map_weights]
    )
    near, others, composed, map_weights = lax.optimization_barrier(
        ([pack, *beside], others, composed, map_weights)
    )
    far = [q for p in near for q in across(p)]
    state = begin(query, near)
    right_pack = tied(right_pack, state)
    right_near = [right_pack, *neighbours(right_pack)]
    (mixed,) = run_kernel(
        end_kernel, "end", [((rows, columns), BF16)], [query, *grouped(far), *state]
    )
    mixed = tile_pieces(mixed)
    right_near = tied(right_near, mixed)
    right_far = [q for p in right_near for q in across(p)]
    updated, cross_query = run_kernel(
        functools.partial(update_kernel, count=tiles),
        "update",
        [((tiles, rows, share), BF16), ((rows, columns), BF16)],
        [
            *mixed,
            self_out,
            *[other[0] for other in others],
            *left,
            cross_qkv.reshape(3, tiles, share, columns),
        ],
    )
    maps = run_kernel(
        functools.partial(end_map_kernel, count=tiles),
        "end_map",
        [(window, BF16)] * tiles,
        [cross_query, *grouped([*right_near, *right_far]), composed],
        [pltpu.VMEM(board, F32)],
    )
    (carried,) = run_kernel(
        carry_kernel,
        "carry",
        [(window, F32)],
        [tied(updated, maps), *map_weights],
        [pltpu.VMEM(board, F32)],
    )
    received = [from_tile(part, s) for s, part in enumerate(maps) if s > 0]
    (features,) = run_kernel(add_kernel, "add", [(window, BF16)], [carried, maps[0], *received])
    above = lax.ppermute(features[-1:], both, down)
    below = lax.ppermute(features[:1], both, up)
    features = lax.ppermute(features, both, back)
    (joined,) = run_kernel(
        conv_kernel,
        "join",
        [((band_rows, width, channels), BF16)],
        [features, above, below, taps],
    )
    return joined[None]


def solution(mesh):
    placed = (
        P(("groups", "pair"), "blk", "tile"),
        P(("groups", "pair"), "blk", "tile"),
        P(None, None, "tile"),
        P("tile", None),
        P(None, None, "tile"),
        P("tile", None),
        P("tile", None),
        P(),
    )
    return jax.shard_map(
        body,
        mesh=mesh,
        in_specs=placed,
        out_specs=P(("groups", "pair"), "blk", "tile", None),
        check_vma=False,
    )
```

```python
import functools
import math

import jax
import jax.numpy as jnp
from jax import lax
from jax.experimental import pallas as pl
from jax.experimental.pallas import tpu as pltpu
from jax.sharding import PartitionSpec as P

HD = 64
GRID_W = 128
EDGE = 16
F32 = jnp.float32
BF16 = jnp.bfloat16
QUERY_SCALE = math.log2(math.e) * HD**-0.5
VMEM = pl.BlockSpec(memory_space=pltpu.VMEM)
HBM = pl.BlockSpec(memory_space=pl.ANY)


def run_kernel(kernel, name, shapes, operands, scratch=(), space=VMEM):
    return pl.pallas_call(
        kernel,
        out_shape=[jax.ShapeDtypeStruct(*s) for s in shapes],
        in_specs=[space] * len(operands),
        out_specs=[VMEM] * len(shapes),
        scratch_shapes=scratch,
        compiler_params=pltpu.CompilerParams(vmem_limit_bytes=24 << 20),
        cost_estimate=pl.CostEstimate(flops=0, bytes_accessed=0, transcendentals=0),
        name=name,
    )(*operands)


def slot_of(step, count):
    return lax.rem(lax.axis_index("tile") + step, count)


def normalized(pieces):
    widened = [piece.astype(F32) for piece in pieces]
    width = sum(piece.shape[1] for piece in widened)
    mean = sum(jnp.sum(piece, axis=1, keepdims=True) for piece in widened) / width
    centred = [piece - mean for piece in widened]
    variance = sum(jnp.sum(piece * piece, axis=1, keepdims=True) for piece in centred) / width
    scale = lax.rsqrt(variance + 1e-06)
    return [(piece * scale).astype(BF16) for piece in centred]


def dot(left, right):
    return jnp.dot(left, right, preferred_element_type=F32)


def project_kernel(*refs, count, scaled, first):
    pieces, weight, outs = refs[:count], refs[count], refs[count + 1 :]
    normed = normalized([piece[...] for piece in pieces])
    products = []
    for which in range(first, weight.shape[0]):
        products.append(
            sum(dot(normed[step], weight[which, slot_of(step, count)]) for step in range(count))
        )
    if scaled:
        outs[0][...] = (products.pop(0) * QUERY_SCALE).astype(BF16)
    columns = weight.shape[3]
    for which, product in enumerate(products):
        outs[-1][:, which * columns : (which + 1) * columns] = product.astype(BF16)


def attended(query, packs, index):
    columns = query.shape[1]
    start = index * HD
    head = slice(start, start + HD)
    values = slice(columns + start, columns + start + HD)
    asked = query[:, head]
    scores = [
        lax.dot_general(asked, pack[:, head], (((1,), (1,)), ((), ())), preferred_element_type=F32)
        for pack in packs
    ]
    maxima = functools.reduce(
        jnp.maximum, [jnp.max(score, axis=1, keepdims=True) for score in scores]
    )
    mixed = 0.0
    for score, pack in zip(scores, packs):
        value = pack[:, values]
        widened = jnp.concatenate([value, jnp.ones_like(value)], axis=1)
        mixed = mixed + dot(jnp.exp2(score - maxima).astype(BF16), widened)
    return mixed, maxima


def begin_kernel(query, *refs):
    packs, (mixed_out, maxima_out) = refs[:-2], refs[-2:]
    for index in range(query.shape[1] // HD):
        mixed_out[index], maxima_out[index] = attended(query, packs, index)


def ended(query, packs, state):
    heads = []
    for index in range(query.shape[1] // HD):
        mixed, maxima = attended(query, packs, index)
        if state:
            before = state[1][index]
            highest = jnp.maximum(maxima, before)
            mixed = mixed * jnp.exp2(maxima - highest)
            mixed = mixed + state[0][index] * jnp.exp2(before - highest)
        heads.append(mixed[:, :HD] / mixed[:, HD:])
    return jnp.concatenate(heads, axis=1).astype(BF16)


def end_kernel(query, *refs):
    refs[-1][...] = ended(query, refs[:-3], refs[-3:-1])


def fill_board(board, values):
    band_rows, channels = board.shape[0], board.shape[2]
    edge = jnp.zeros((band_rows, EDGE, channels), board.dtype)
    board[:, :EDGE, :] = edge
    board[:, EDGE + GRID_W :, :] = edge
    inner = values.reshape(band_rows, GRID_W, channels)
    board[:, EDGE : EDGE + GRID_W, :] = inner.astype(board.dtype)


def window_of(board, slot, out):
    start = pl.multiple_of(slot * (out.shape[1] - 2 * EDGE), EDGE)
    out[...] = board[:, pl.ds(start, out.shape[1]), :].astype(out.dtype)


def end_map_kernel(query, *refs, count):
    composed, outs, board = refs[-2 - count], refs[-1 - count : -1], refs[-1]
    fill_board(board, dot(ended(query, refs[: -2 - count], ()), composed[...]))
    for step, out in enumerate(outs):
        window_of(board, slot_of(count - step, count), out)


def carry_kernel(updated, *refs):
    pieces, out, board = refs[:-2], refs[-2], refs[-1]
    fill_board(board, sum(dot(updated[i], piece[...]) for i, piece in enumerate(pieces)))
    window_of(board, lax.axis_index("tile"), out)


def add_kernel(*refs):
    refs[-1][...] = sum(ref[...].astype(F32) for ref in refs[:-1]).astype(BF16)


def stage_kernel(*refs, cores):
    count = (len(refs) - 2) // 2
    sources, outs, half, sems = refs[:count], refs[count : 2 * count], refs[-2], refs[-1]
    core = lax.axis_index("pair")
    pairs = list(zip(sources, outs))
    rows = sources[0].shape[0] // cores
    begin = pl.multiple_of(core * rows, rows)
    pairs.append((sources[0].at[pl.ds(begin, rows)], half.at[pl.ds(0, rows)]))
    start = rows
    blocks = half.shape[1] // sources[1].shape[1]
    block = sources[1].shape[0] // blocks
    rows = block // cores
    for index in range(blocks):
        begin = pl.multiple_of(core * rows + index * block, rows)
        lanes = pl.ds(index * sources[1].shape[1], sources[1].shape[1])
        pairs.append((sources[1].at[pl.ds(begin, rows)], half.at[pl.ds(start, rows), lanes]))
    copies = [pltpu.make_async_copy(a, b, sems.at[i]) for i, (a, b) in enumerate(pairs)]
    for copy in copies:
        copy.start()
    for copy in copies:
        copy.wait()


def unpack_kernel(*refs):
    halves, outs = refs[:-2], refs[-2:]
    for step, half in enumerate(halves):
        core = lax.rem(lax.axis_index("pair") + step, len(halves))
        rows = outs[0].shape[0] // len(halves)
        outs[0][pl.ds(pl.multiple_of(core * rows, rows), rows), :] = half[:rows, :]
        start = rows
        blocks = half.shape[1] // outs[1].shape[1]
        block = outs[1].shape[0] // blocks
        rows = block // len(halves)
        for index in range(blocks):
            first = pl.multiple_of(core * rows + index * block, rows)
            lanes = slice(index * outs[1].shape[1], (index + 1) * outs[1].shape[1])
            outs[1][pl.ds(first, rows), :] = half[start : start + rows, lanes]


def pick(options, slot):
    chosen = options[0]
    for index in range(1, len(options)):
        chosen = jnp.where(slot == index, options[index], chosen)
    return chosen


def feature_shares(whole, count):
    share = whole.shape[1] // count
    options = [whole[:, i * share : (i + 1) * share] for i in range(count)]
    return [pick(options, slot_of(step, count)) for step in range(count)]


def compose_kernel(weight, *refs):
    pieces, out = refs[:-1], refs[-1]
    shares = feature_shares(weight[...].astype(F32), len(pieces))
    out[...] = sum(dot(s.astype(BF16), p[...]) for s, p in zip(shares, pieces)).astype(BF16)


def update_kernel(*refs, count):
    mixed, weights = refs[:count], refs[count : 2 * count]
    tokens, query_weight = refs[2 * count : 3 * count], refs[3 * count]
    updated, query = refs[3 * count + 1 :]
    whole = sum(dot(m[...], w[...]) for m, w in zip(mixed, weights))
    pieces = []
    for step, term in enumerate(feature_shares(whole, count)):
        piece = (tokens[step][...].astype(F32) + term).astype(BF16)
        updated[step] = piece
        pieces.append(piece)
    normed = normalized(pieces)
    product = sum(
        dot(normed[step], query_weight[0, slot_of(step, count)]) for step in range(count)
    )
    query[...] = (product * QUERY_SCALE).astype(BF16)


def conv_kernel(window, above, below, weight, out):
    width = out.shape[1]
    band_rows, channels = out.shape[0], out.shape[2]
    grid = jnp.concatenate([above[...], window[...], below[...]], axis=0).astype(F32)
    active = jnp.maximum(grid, 0.0)
    total = grid[1 : 1 + band_rows, EDGE : EDGE + width, :].reshape(band_rows * width, channels)
    for column in range(3):
        first = EDGE - 1 + column
        shifted = active[:, first : first + width, :].astype(BF16)
        for row in range(3):
            rows = shifted[row : row + band_rows].reshape(band_rows * width, channels)
            total = total + dot(rows, weight[row, column])
    out[...] = total.reshape(out.shape).astype(BF16)


def body(left_tokens, right_tokens, self_qkv, self_out, cross_qkv, cross_out, reassemble, taps):
    bands, tiles, cores = (lax.axis_size(axis) for axis in ("blk", "tile", "pair"))
    span = bands // cores
    both = ("blk", "pair")
    rows, share = left_tokens.shape[1:]
    columns = self_qkv.shape[2]
    channels = reassemble.shape[1]
    width = GRID_W // tiles
    band_rows = rows // GRID_W
    heads = columns // HD
    window = (band_rows, width + 2 * EDGE, channels)
    board = (band_rows, GRID_W + 2 * EDGE, channels)

    def home(band, pair):
        return band * cores + pair

    def worker(band, pair):
        part, index = divmod(band, span)
        if part == pair:
            return band * cores + pair
        shift = (pair - part) % cores
        return (pair * span + span - 1 - index) * cores + (pair - shift) % cores

    places = [(band, pair) for band in range(bands) for pair in range(cores)]
    there = [(home(*p), worker(*p)) for p in places]
    back = [(worker(*p), home(*p)) for p in places]
    down = [(worker(b, p), home(b + 1, p)) for b, p in places if b + 1 < bands]
    up = [(worker(b, p), home(b - 1, p)) for b, p in places if b > 0]

    def fetched(value, step):
        def flat(position, tile):
            return (position // cores * tiles + tile) * cores + position % cores

        pairs = [(flat(s, (i + step) % tiles), flat(d, i)) for s, d in there for i in range(tiles)]
        return lax.ppermute(value, ("blk", "tile", "pair"), pairs)

    def tied(values, *others):
        return lax.optimization_barrier((values, others))[0]

    def from_tile(value, step):
        return lax.ppermute(value, "tile", [((i + step) % tiles, i) for i in range(tiles)])

    def tile_pieces(own):
        return [own, *[from_tile(own, s) for s in range(1, tiles)]]

    def neighbours(pack):
        ring = [(g * span, i) for g in range(cores) for i in range(span)]
        return [
            lax.ppermute(pack, "blk", [(g + (i + s) % span, g + i) for g, i in ring])
            for s in range(1, span)
        ]

    def across(pack):
        return [
            lax.ppermute(pack, "pair", [((i + s) % cores, i) for i in range(cores)])
            for s in range(1, cores)
        ]

    def grouped(packs):
        return packs if len(packs) < 5 else [jnp.concatenate(packs)]

    def project(pieces, weights, scaled, first):
        return run_kernel(
            functools.partial(project_kernel, count=tiles, scaled=scaled, first=first),
            "project",
            [((rows, columns), BF16)] * scaled + [((rows, 2 * columns), BF16)],
            [*pieces, weights.reshape(3, tiles, share, columns)],
        )

    def begin(query, packs):
        shapes = [((heads, rows, 2 * HD), F32), ((heads, rows, 1), F32)]
        return run_kernel(begin_kernel, "begin", shapes, [query, *grouped(packs)])

    def staged(weights):
        blocks = weights[0].shape[1] // channels
        height = (weights[0].shape[0] + share // blocks) // cores
        return run_kernel(
            functools.partial(stage_kernel, cores=cores),
            "stage",
            [(w.shape, BF16) for w in weights] + [((height, weights[0].shape[1]), BF16)],
            [pltpu.with_memory_space_constraint(w, pltpu.HBM) for w in weights],
            [pltpu.SemaphoreType.DMA((len(weights) + 1 + blocks,))],
            pl.BlockSpec(memory_space=pl.ANY),
        )

    steps = range(1, tiles)
    left = [fetched(left_tokens[0], step) for step in range(tiles)]
    self_out, reassemble, cross_out, right_own, self_qkv, cross_qkv, taps, half = staged(
        [self_out, reassemble, cross_out, right_tokens[0], self_qkv, cross_qkv, taps]
    )
    right = [right_own, *[from_tile(right_tokens[0], s) for s in steps]]
    (right_pack,) = project(right, cross_qkv, False, 1)
    left, right_pack = lax.optimization_barrier((left, right_pack))
    query, pack = project(left, self_qkv, True, 0)
    right_pack = lax.ppermute(tied(right_pack, pack), both, there)
    beside = neighbours(pack)
    halves = tile_pieces(half)[1:]
    others = [
        run_kernel(
            unpack_kernel,
            "unpack",
            [(w.shape, BF16) for w in (self_out, reassemble)],
            [half, *across(half)],
        )
        for half in halves
    ]
    map_weights = [reassemble, *[other[1] for other in others]]
    (composed,) = run_kernel(
        compose_kernel, "compose", [((columns, channels), BF16)], [cross_out, *map_weights]
    )
    near, others, composed, map_weights, right_pack = lax.optimization_barrier(
        ([pack, *beside], others, composed, map_weights, right_pack)
    )
    far = [q for p in near for q in across(p)]
    state = begin(query, near)
    right_near = [right_pack, *neighbours(right_pack)]
    (mixed,) = run_kernel(
        end_kernel, "end", [((rows, columns), BF16)], [query, *grouped(far), *state]
    )
    mixed = tile_pieces(mixed)
    right_near = tied(right_near, mixed)
    right_far = [q for p in right_near for q in across(p)]
    updated, cross_query = run_kernel(
        functools.partial(update_kernel, count=tiles),
        "update",
        [((tiles, rows, share), BF16), ((rows, columns), BF16)],
        [
            *mixed,
            self_out,
            *[other[0] for other in others],
            *left,
            cross_qkv.reshape(3, tiles, share, columns),
        ],
    )
    maps = run_kernel(
        functools.partial(end_map_kernel, count=tiles),
        "end_map",
        [(window, BF16)] * tiles,
        [cross_query, *grouped([*right_near, *right_far]), composed],
        [pltpu.VMEM(board, F32)],
    )
    (carried,) = run_kernel(
        carry_kernel,
        "carry",
        [(window, F32)],
        [tied(updated, maps), *map_weights],
        [pltpu.VMEM(board, F32)],
    )
    received = [from_tile(part, s) for s, part in enumerate(maps) if s > 0]
    (features,) = run_kernel(add_kernel, "add", [(window, BF16)], [carried, maps[0], *received])
    above = lax.ppermute(features[-1:], both, down)
    below = lax.ppermute(features[:1], both, up)
    features = lax.ppermute(features, both, back)
    (joined,) = run_kernel(
        conv_kernel,
        "join",
        [((band_rows, width, channels), BF16)],
        [features, above, below, taps],
    )
    return joined[None]


def solution(mesh):
    placed = (
        P(("groups", "pair"), "blk", "tile"),
        P(("groups", "pair"), "blk", "tile"),
        P(None, None, "tile"),
        P("tile", None),
        P(None, None, "tile"),
        P("tile", None),
        P("tile", None),
        P(),
    )
    return jax.shard_map(
        body,
        mesh=mesh,
        in_specs=placed,
        out_specs=P(("groups", "pair"), "blk", "tile", None),
        check_vma=False,
    )
```

```python
import functools
import math

import jax
import jax.numpy as jnp
from jax import lax
from jax.experimental import pallas as pl
from jax.experimental.pallas import tpu as pltpu
from jax.sharding import PartitionSpec as P

HD = 64
GRID_W = 128
EDGE = 16
F32 = jnp.float32
BF16 = jnp.bfloat16
QUERY_SCALE = math.log2(math.e) * HD**-0.5
VMEM = pl.BlockSpec(memory_space=pltpu.VMEM)
HBM = pl.BlockSpec(memory_space=pl.ANY)


def run_kernel(kernel, name, shapes, operands, scratch=(), space=VMEM):
    return pl.pallas_call(
        kernel,
        out_shape=[jax.ShapeDtypeStruct(*s) for s in shapes],
        in_specs=[space] * len(operands),
        out_specs=[VMEM] * len(shapes),
        scratch_shapes=scratch,
        compiler_params=pltpu.CompilerParams(vmem_limit_bytes=24 << 20),
        cost_estimate=pl.CostEstimate(flops=0, bytes_accessed=0, transcendentals=0),
        name=name,
    )(*operands)


def slot_of(step, count):
    return lax.rem(lax.axis_index("tile") + step, count)


def normalized(pieces):
    widened = [piece.astype(F32) for piece in pieces]
    width = sum(piece.shape[1] for piece in widened)
    mean = sum(jnp.sum(piece, axis=1, keepdims=True) for piece in widened) / width
    centred = [piece - mean for piece in widened]
    variance = sum(jnp.sum(piece * piece, axis=1, keepdims=True) for piece in centred) / width
    scale = lax.rsqrt(variance + 1e-06)
    return [(piece * scale).astype(BF16) for piece in centred]


def dot(left, right):
    return jnp.dot(left, right, preferred_element_type=F32)


def project_kernel(*refs, count, scaled, first):
    pieces, weight, outs = refs[:count], refs[count], refs[count + 1 :]
    normed = normalized([piece[...] for piece in pieces])
    products = []
    for which in range(first, weight.shape[0]):
        products.append(
            sum(dot(normed[step], weight[which, slot_of(step, count)]) for step in range(count))
        )
    if scaled:
        outs[0][...] = (products.pop(0) * QUERY_SCALE).astype(BF16)
    columns = weight.shape[3]
    for which, product in enumerate(products):
        outs[-1][:, which * columns : (which + 1) * columns] = product.astype(BF16)


def attended(query, packs, index):
    columns = query.shape[1]
    start = index * HD
    head = slice(start, start + HD)
    values = slice(columns + start, columns + start + HD)
    asked = query[:, head]
    scores = [
        lax.dot_general(asked, pack[:, head], (((1,), (1,)), ((), ())), preferred_element_type=F32)
        for pack in packs
    ]
    maxima = functools.reduce(
        jnp.maximum, [jnp.max(score, axis=1, keepdims=True) for score in scores]
    )
    mixed = 0.0
    for score, pack in zip(scores, packs):
        value = pack[:, values]
        widened = jnp.concatenate([value, jnp.ones_like(value)], axis=1)
        mixed = mixed + dot(jnp.exp2(score - maxima).astype(BF16), widened)
    return mixed, maxima


def begin_kernel(query, *refs):
    packs, (mixed_out, maxima_out) = refs[:-2], refs[-2:]
    for index in range(query.shape[1] // HD):
        mixed_out[index], maxima_out[index] = attended(query, packs, index)


def ended(query, packs, state):
    heads = []
    for index in range(query.shape[1] // HD):
        mixed, maxima = attended(query, packs, index)
        if state:
            before = state[1][index]
            highest = jnp.maximum(maxima, before)
            mixed = mixed * jnp.exp2(maxima - highest)
            mixed = mixed + state[0][index] * jnp.exp2(before - highest)
        heads.append(mixed[:, :HD] / mixed[:, HD:])
    return jnp.concatenate(heads, axis=1).astype(BF16)


def end_kernel(query, *refs):
    refs[-1][...] = ended(query, refs[:-3], refs[-3:-1])


def fill_board(board, values):
    band_rows, channels = board.shape[0], board.shape[2]
    edge = jnp.zeros((band_rows, EDGE, channels), board.dtype)
    board[:, :EDGE, :] = edge
    board[:, EDGE + GRID_W :, :] = edge
    inner = values.reshape(band_rows, GRID_W, channels)
    board[:, EDGE : EDGE + GRID_W, :] = inner.astype(board.dtype)


def window_of(board, slot, out):
    start = pl.multiple_of(slot * (out.shape[1] - 2 * EDGE), EDGE)
    out[...] = board[:, pl.ds(start, out.shape[1]), :].astype(out.dtype)


def end_map_kernel(query, *refs, count):
    composed, outs, board = refs[-2 - count], refs[-1 - count : -1], refs[-1]
    fill_board(board, dot(ended(query, refs[: -2 - count], ()), composed[...]))
    for step, out in enumerate(outs):
        window_of(board, slot_of(count - step, count), out)


def carry_kernel(updated, *refs):
    pieces, out, board = refs[:-2], refs[-2], refs[-1]
    fill_board(board, sum(dot(updated[i], piece[...]) for i, piece in enumerate(pieces)))
    window_of(board, lax.axis_index("tile"), out)


def add_kernel(*refs):
    refs[-1][...] = sum(ref[...].astype(F32) for ref in refs[:-1]).astype(BF16)


def stage_kernel(*refs, cores):
    count = (len(refs) - 2) // 2
    sources, outs, half, sems = refs[:count], refs[count : 2 * count], refs[-2], refs[-1]
    core = lax.axis_index("pair")
    pairs = list(zip(sources, outs))
    rows = sources[0].shape[0] // cores
    begin = pl.multiple_of(core * rows, rows)
    pairs.append((sources[0].at[pl.ds(begin, rows)], half.at[pl.ds(0, rows)]))
    start = rows
    blocks = half.shape[1] // sources[1].shape[1]
    block = sources[1].shape[0] // blocks
    rows = block // cores
    for index in range(blocks):
        begin = pl.multiple_of(core * rows + index * block, rows)
        lanes = pl.ds(index * sources[1].shape[1], sources[1].shape[1])
        pairs.append((sources[1].at[pl.ds(begin, rows)], half.at[pl.ds(start, rows), lanes]))
    copies = [pltpu.make_async_copy(a, b, sems.at[i]) for i, (a, b) in enumerate(pairs)]
    for copy in copies:
        copy.start()
    for copy in copies:
        copy.wait()


def unpack_kernel(*refs):
    halves, outs = refs[:-2], refs[-2:]
    for step, half in enumerate(halves):
        core = lax.rem(lax.axis_index("pair") + step, len(halves))
        rows = outs[0].shape[0] // len(halves)
        outs[0][pl.ds(pl.multiple_of(core * rows, rows), rows), :] = half[:rows, :]
        start = rows
        blocks = half.shape[1] // outs[1].shape[1]
        block = outs[1].shape[0] // blocks
        rows = block // len(halves)
        for index in range(blocks):
            first = pl.multiple_of(core * rows + index * block, rows)
            lanes = slice(index * outs[1].shape[1], (index + 1) * outs[1].shape[1])
            outs[1][pl.ds(first, rows), :] = half[start : start + rows, lanes]


def pick(options, slot):
    chosen = options[0]
    for index in range(1, len(options)):
        chosen = jnp.where(slot == index, options[index], chosen)
    return chosen


def feature_shares(whole, count):
    share = whole.shape[1] // count
    options = [whole[:, i * share : (i + 1) * share] for i in range(count)]
    return [pick(options, slot_of(step, count)) for step in range(count)]


def compose_kernel(weight, *refs):
    pieces, out = refs[:-1], refs[-1]
    shares = feature_shares(weight[...].astype(F32), len(pieces))
    out[...] = sum(dot(s.astype(BF16), p[...]) for s, p in zip(shares, pieces)).astype(BF16)


def update_kernel(*refs, count):
    mixed, weights = refs[:count], refs[count : 2 * count]
    tokens, query_weight = refs[2 * count : 3 * count], refs[3 * count]
    updated, query = refs[3 * count + 1 :]
    whole = sum(dot(m[...], w[...]) for m, w in zip(mixed, weights))
    pieces = []
    for step, term in enumerate(feature_shares(whole, count)):
        piece = (tokens[step][...].astype(F32) + term).astype(BF16)
        updated[step] = piece
        pieces.append(piece)
    normed = normalized(pieces)
    product = sum(
        dot(normed[step], query_weight[0, slot_of(step, count)]) for step in range(count)
    )
    query[...] = (product * QUERY_SCALE).astype(BF16)


def conv_kernel(window, above, below, weight, out):
    width = out.shape[1]
    band_rows, channels = out.shape[0], out.shape[2]
    grid = jnp.concatenate([above[...], window[...], below[...]], axis=0).astype(F32)
    active = jnp.maximum(grid, 0.0)
    total = grid[1 : 1 + band_rows, EDGE : EDGE + width, :].reshape(band_rows * width, channels)
    for column in range(3):
        first = EDGE - 1 + column
        shifted = active[:, first : first + width, :].astype(BF16)
        for row in range(3):
            rows = shifted[row : row + band_rows].reshape(band_rows * width, channels)
            total = total + dot(rows, weight[row, column])
    out[...] = total.reshape(out.shape).astype(BF16)


def body(left_tokens, right_tokens, self_qkv, self_out, cross_qkv, cross_out, reassemble, taps):
    bands, tiles, cores = (lax.axis_size(axis) for axis in ("blk", "tile", "pair"))
    span = bands // cores
    both = ("blk", "pair")
    rows, share = left_tokens.shape[1:]
    columns = self_qkv.shape[2]
    channels = reassemble.shape[1]
    width = GRID_W // tiles
    band_rows = rows // GRID_W
    heads = columns // HD
    window = (band_rows, width + 2 * EDGE, channels)
    board = (band_rows, GRID_W + 2 * EDGE, channels)

    def home(band, pair):
        return band * cores + pair

    def worker(band, pair):
        part, index = divmod(band, span)
        if part == pair:
            return band * cores + pair
        shift = (pair - part) % cores
        return (pair * span + span - 1 - index) * cores + (pair - shift) % cores

    places = [(band, pair) for band in range(bands) for pair in range(cores)]
    there = [(home(*p), worker(*p)) for p in places]
    back = [(worker(*p), home(*p)) for p in places]
    down = [(worker(b, p), home(b + 1, p)) for b, p in places if b + 1 < bands]
    up = [(worker(b, p), home(b - 1, p)) for b, p in places if b > 0]

    def fetched(value, step):
        def flat(position, tile):
            return (position // cores * tiles + tile) * cores + position % cores

        pairs = [(flat(s, (i + step) % tiles), flat(d, i)) for s, d in there for i in range(tiles)]
        return lax.ppermute(value, ("blk", "tile", "pair"), pairs)

    def tied(values, *others):
        return lax.optimization_barrier((values, others))[0]

    def from_tile(value, step):
        return lax.ppermute(value, "tile", [((i + step) % tiles, i) for i in range(tiles)])

    def tile_pieces(own):
        return [own, *[from_tile(own, s) for s in range(1, tiles)]]

    def neighbours(pack):
        ring = [(g * span, i) for g in range(cores) for i in range(span)]
        return [
            lax.ppermute(pack, "blk", [(g + (i + s) % span, g + i) for g, i in ring])
            for s in range(1, span)
        ]

    def across(pack):
        return [
            lax.ppermute(pack, "pair", [((i + s) % cores, i) for i in range(cores)])
            for s in range(1, cores)
        ]

    def grouped(packs):
        return packs if len(packs) < 5 else [jnp.concatenate(packs)]

    def project(pieces, weights, scaled, first):
        return run_kernel(
            functools.partial(project_kernel, count=tiles, scaled=scaled, first=first),
            "project",
            [((rows, columns), BF16)] * scaled + [((rows, 2 * columns), BF16)],
            [*pieces, weights.reshape(3, tiles, share, columns)],
        )

    def begin(query, packs):
        shapes = [((heads, rows, 2 * HD), F32), ((heads, rows, 1), F32)]
        return run_kernel(begin_kernel, "begin", shapes, [query, *grouped(packs)])

    def staged(weights):
        blocks = weights[0].shape[1] // channels
        height = (weights[0].shape[0] + share // blocks) // cores
        return run_kernel(
            functools.partial(stage_kernel, cores=cores),
            "stage",
            [(w.shape, BF16) for w in weights] + [((height, weights[0].shape[1]), BF16)],
            [pltpu.with_memory_space_constraint(w, pltpu.HBM) for w in weights],
            [pltpu.SemaphoreType.DMA((len(weights) + 1 + blocks,))],
            pl.BlockSpec(memory_space=pl.ANY),
        )

    steps = range(1, tiles)
    left = [fetched(left_tokens[0], step) for step in range(tiles)]
    self_out, reassemble, cross_out, right_own, self_qkv, cross_qkv, taps, half = staged(
        [self_out, reassemble, cross_out, right_tokens[0], self_qkv, cross_qkv, taps]
    )
    right = [right_own, *[from_tile(right_tokens[0], s) for s in steps]]
    (right_pack,) = project(right, cross_qkv, False, 1)
    left, right_pack = lax.optimization_barrier((left, right_pack))
    query, pack = project(left, self_qkv, True, 0)
    right_pack = lax.ppermute(tied(right_pack, pack), both, there)
    beside = neighbours(pack)
    near = [pack, *across(pack)]
    halves = tile_pieces(half)[1:]
    others = [
        run_kernel(
            unpack_kernel,
            "unpack",
            [(w.shape, BF16) for w in (self_out, reassemble)],
            [half, *across(half)],
        )
        for half in halves
    ]
    map_weights = [reassemble, *[other[1] for other in others]]
    (composed,) = run_kernel(
        compose_kernel, "compose", [((columns, channels), BF16)], [cross_out, *map_weights]
    )
    state = begin(query, near)
    beside, others, composed, map_weights, state = lax.optimization_barrier(
        (beside, others, composed, map_weights, state)
    )
    far = [*beside, *[q for p in beside for q in across(p)]]
    right_pack = tied(right_pack, beside)
    right_near = [right_pack, *neighbours(right_pack)]
    (mixed,) = run_kernel(
        end_kernel, "end", [((rows, columns), BF16)], [query, *grouped(far), *state]
    )
    mixed = tile_pieces(mixed)
    right_near = tied(right_near, mixed)
    right_far = [q for p in right_near for q in across(p)]
    updated, cross_query = run_kernel(
        functools.partial(update_kernel, count=tiles),
        "update",
        [((tiles, rows, share), BF16), ((rows, columns), BF16)],
        [
            *mixed,
            self_out,
            *[other[0] for other in others],
            *left,
            cross_qkv.reshape(3, tiles, share, columns),
        ],
    )
    maps = run_kernel(
        functools.partial(end_map_kernel, count=tiles),
        "end_map",
        [(window, BF16)] * tiles,
        [cross_query, *grouped([*right_near, *right_far]), composed],
        [pltpu.VMEM(board, F32)],
    )
    (carried,) = run_kernel(
        carry_kernel,
        "carry",
        [(window, F32)],
        [tied(updated, maps), *map_weights],
        [pltpu.VMEM(board, F32)],
    )
    received = [from_tile(part, s) for s, part in enumerate(maps) if s > 0]
    (features,) = run_kernel(add_kernel, "add", [(window, BF16)], [carried, maps[0], *received])
    above = lax.ppermute(features[-1:], both, down)
    below = lax.ppermute(features[:1], both, up)
    features = lax.ppermute(features, both, back)
    (joined,) = run_kernel(
        conv_kernel,
        "join",
        [((band_rows, width, channels), BF16)],
        [features, above, below, taps],
    )
    return joined[None]


def solution(mesh):
    placed = (
        P(("groups", "pair"), "blk", "tile"),
        P(("groups", "pair"), "blk", "tile"),
        P(None, None, "tile"),
        P("tile", None),
        P(None, None, "tile"),
        P("tile", None),
        P("tile", None),
        P(),
    )
    return jax.shard_map(
        body,
        mesh=mesh,
        in_specs=placed,
        out_specs=P(("groups", "pair"), "blk", "tile", None),
        check_vma=False,
    )
```

```python
import functools
import math

import jax
import jax.numpy as jnp
from jax import lax
from jax.experimental import pallas as pl
from jax.experimental.pallas import tpu as pltpu
from jax.sharding import PartitionSpec as P

HD = 64
GRID_W = 128
EDGE = 8
F32 = jnp.float32
BF16 = jnp.bfloat16
QUERY_SCALE = math.log2(math.e) * HD**-0.5
VMEM = pl.BlockSpec(memory_space=pltpu.VMEM)
HBM = pl.BlockSpec(memory_space=pl.ANY)


def run_kernel(kernel, name, shapes, operands, scratch=(), space=VMEM):
    return pl.pallas_call(
        kernel,
        out_shape=[jax.ShapeDtypeStruct(*s) for s in shapes],
        in_specs=[space] * len(operands),
        out_specs=[VMEM] * len(shapes),
        scratch_shapes=scratch,
        compiler_params=pltpu.CompilerParams(vmem_limit_bytes=24 << 20),
        cost_estimate=pl.CostEstimate(flops=0, bytes_accessed=0, transcendentals=0),
        name=name,
    )(*operands)


def slot_of(step, count):
    return lax.rem(lax.axis_index("tile") + step, count)


def normalized(pieces):
    widened = [piece.astype(F32) for piece in pieces]
    width = sum(piece.shape[1] for piece in widened)
    mean = sum(jnp.sum(piece, axis=1, keepdims=True) for piece in widened) / width
    centred = [piece - mean for piece in widened]
    variance = sum(jnp.sum(piece * piece, axis=1, keepdims=True) for piece in centred) / width
    scale = lax.rsqrt(variance + 1e-06)
    return [(piece * scale).astype(BF16) for piece in centred]


def dot(left, right):
    return jnp.dot(left, right, preferred_element_type=F32)


def project_kernel(*refs, count, scaled, first):
    pieces, weight, outs = refs[:count], refs[count], refs[count + 1 :]
    normed = normalized([piece[...] for piece in pieces])
    products = []
    for which in range(first, weight.shape[0]):
        products.append(
            sum(dot(normed[step], weight[which, slot_of(step, count)]) for step in range(count))
        )
    if scaled:
        outs[0][...] = (products.pop(0) * QUERY_SCALE).astype(BF16)
    columns = weight.shape[3]
    for which, product in enumerate(products):
        outs[-1][:, which * columns : (which + 1) * columns] = product.astype(BF16)


def attended(query, packs, index):
    columns = query.shape[1]
    start = index * HD
    head = slice(start, start + HD)
    values = slice(columns + start, columns + start + HD)
    asked = query[:, head]
    scores = [
        lax.dot_general(asked, pack[:, head], (((1,), (1,)), ((), ())), preferred_element_type=F32)
        for pack in packs
    ]
    maxima = functools.reduce(
        jnp.maximum, [jnp.max(score, axis=1, keepdims=True) for score in scores]
    )
    mixed = 0.0
    for score, pack in zip(scores, packs):
        value = pack[:, values]
        widened = jnp.concatenate([value, jnp.ones_like(value)], axis=1)
        mixed = mixed + dot(jnp.exp2(score - maxima).astype(BF16), widened)
    return mixed, maxima


def begin_kernel(query, *refs):
    packs, (mixed_out, maxima_out) = refs[:-2], refs[-2:]
    for index in range(query.shape[1] // HD):
        mixed_out[index], maxima_out[index] = attended(query, packs, index)


def ended(query, packs, state):
    heads = []
    for index in range(query.shape[1] // HD):
        mixed, maxima = attended(query, packs, index)
        if state:
            before = state[1][index]
            highest = jnp.maximum(maxima, before)
            mixed = mixed * jnp.exp2(maxima - highest)
            mixed = mixed + state[0][index] * jnp.exp2(before - highest)
        heads.append(mixed[:, :HD] / mixed[:, HD:])
    return jnp.concatenate(heads, axis=1).astype(BF16)


def end_kernel(query, *refs):
    refs[-1][...] = ended(query, refs[:-3], refs[-3:-1])


def fill_board(board, values):
    band_rows, channels = board.shape[0], board.shape[2]
    edge = jnp.zeros((band_rows, EDGE, channels), board.dtype)
    board[:, :EDGE, :] = edge
    board[:, EDGE + GRID_W :, :] = edge
    inner = values.reshape(band_rows, GRID_W, channels)
    board[:, EDGE : EDGE + GRID_W, :] = inner.astype(board.dtype)


def window_of(board, slot, out):
    width = out.shape[1] - 2 * EDGE
    start = pl.multiple_of(slot * width, width)
    out[...] = board[:, pl.ds(start, out.shape[1]), :].astype(out.dtype)


def end_map_kernel(query, *refs, count):
    composed, outs, board = refs[-2 - count], refs[-1 - count : -1], refs[-1]
    fill_board(board, dot(ended(query, refs[: -2 - count], ()), composed[...]))
    for step, out in enumerate(outs):
        window_of(board, slot_of(count - step, count), out)


def carry_kernel(updated, *refs):
    pieces, out, board = refs[:-2], refs[-2], refs[-1]
    fill_board(board, sum(dot(updated[i], piece[...]) for i, piece in enumerate(pieces)))
    window_of(board, lax.axis_index("tile"), out)


def add_kernel(*refs):
    refs[-1][...] = sum(ref[...].astype(F32) for ref in refs[:-1]).astype(BF16)


def stage_kernel(*refs, cores):
    count = (len(refs) - 2) // 2
    sources, outs, half, sems = refs[:count], refs[count : 2 * count], refs[-2], refs[-1]
    core = lax.axis_index("pair")
    pairs = list(zip(sources, outs))
    rows = sources[0].shape[0] // cores
    begin = pl.multiple_of(core * rows, rows)
    pairs.append((sources[0].at[pl.ds(begin, rows)], half.at[pl.ds(0, rows)]))
    start = rows
    blocks = half.shape[1] // sources[1].shape[1]
    block = sources[1].shape[0] // blocks
    rows = block // cores
    for index in range(blocks):
        begin = pl.multiple_of(core * rows + index * block, rows)
        lanes = pl.ds(index * sources[1].shape[1], sources[1].shape[1])
        pairs.append((sources[1].at[pl.ds(begin, rows)], half.at[pl.ds(start, rows), lanes]))
    copies = [pltpu.make_async_copy(a, b, sems.at[i]) for i, (a, b) in enumerate(pairs)]
    for copy in copies:
        copy.start()
    for copy in copies:
        copy.wait()


def unpack_kernel(*refs):
    halves, outs = refs[:-2], refs[-2:]
    for step, half in enumerate(halves):
        core = lax.rem(lax.axis_index("pair") + step, len(halves))
        rows = outs[0].shape[0] // len(halves)
        outs[0][pl.ds(pl.multiple_of(core * rows, rows), rows), :] = half[:rows, :]
        start = rows
        blocks = half.shape[1] // outs[1].shape[1]
        block = outs[1].shape[0] // blocks
        rows = block // len(halves)
        for index in range(blocks):
            first = pl.multiple_of(core * rows + index * block, rows)
            lanes = slice(index * outs[1].shape[1], (index + 1) * outs[1].shape[1])
            outs[1][pl.ds(first, rows), :] = half[start : start + rows, lanes]


def pick(options, slot):
    chosen = options[0]
    for index in range(1, len(options)):
        chosen = jnp.where(slot == index, options[index], chosen)
    return chosen


def feature_shares(whole, count):
    share = whole.shape[1] // count
    options = [whole[:, i * share : (i + 1) * share] for i in range(count)]
    return [pick(options, slot_of(step, count)) for step in range(count)]


def compose_kernel(weight, *refs):
    pieces, out = refs[:-1], refs[-1]
    shares = feature_shares(weight[...].astype(F32), len(pieces))
    out[...] = sum(dot(s.astype(BF16), p[...]) for s, p in zip(shares, pieces)).astype(BF16)


def update_kernel(*refs, count):
    mixed, weights = refs[:count], refs[count : 2 * count]
    tokens, query_weight = refs[2 * count : 3 * count], refs[3 * count]
    updated, query = refs[3 * count + 1 :]
    whole = sum(dot(m[...], w[...]) for m, w in zip(mixed, weights))
    pieces = []
    for step, term in enumerate(feature_shares(whole, count)):
        piece = (tokens[step][...].astype(F32) + term).astype(BF16)
        updated[step] = piece
        pieces.append(piece)
    normed = normalized(pieces)
    product = sum(
        dot(normed[step], query_weight[0, slot_of(step, count)]) for step in range(count)
    )
    query[...] = (product * QUERY_SCALE).astype(BF16)


def conv_kernel(window, above, below, weight, out):
    width = out.shape[1]
    band_rows, channels = out.shape[0], out.shape[2]
    grid = jnp.concatenate([above[...], window[...], below[...]], axis=0).astype(F32)
    active = jnp.maximum(grid, 0.0)
    total = grid[1 : 1 + band_rows, EDGE : EDGE + width, :].reshape(band_rows * width, channels)
    for column in range(3):
        first = EDGE - 1 + column
        shifted = active[:, first : first + width, :].astype(BF16)
        for row in range(3):
            rows = shifted[row : row + band_rows].reshape(band_rows * width, channels)
            total = total + dot(rows, weight[row, column])
    out[...] = total.reshape(out.shape).astype(BF16)


def body(left_tokens, right_tokens, self_qkv, self_out, cross_qkv, cross_out, reassemble, taps):
    bands, tiles, cores = (lax.axis_size(axis) for axis in ("blk", "tile", "pair"))
    span = bands // cores
    both = ("blk", "pair")
    rows, share = left_tokens.shape[1:]
    columns = self_qkv.shape[2]
    channels = reassemble.shape[1]
    width = GRID_W // tiles
    band_rows = rows // GRID_W
    heads = columns // HD
    window = (band_rows, width + 2 * EDGE, channels)
    board = (band_rows, GRID_W + 2 * EDGE, channels)

    def home(band, pair):
        return band * cores + pair

    def worker(band, pair):
        part, index = divmod(band, span)
        if part == pair:
            return band * cores + pair
        shift = (pair - part) % cores
        return (pair * span + span - 1 - index) * cores + (pair - shift) % cores

    places = [(band, pair) for band in range(bands) for pair in range(cores)]
    there = [(home(*p), worker(*p)) for p in places]
    back = [(worker(*p), home(*p)) for p in places]
    down = [(worker(b, p), home(b + 1, p)) for b, p in places if b + 1 < bands]
    up = [(worker(b, p), home(b - 1, p)) for b, p in places if b > 0]

    def fetched(value, step):
        def flat(position, tile):
            return (position // cores * tiles + tile) * cores + position % cores

        pairs = [(flat(s, (i + step) % tiles), flat(d, i)) for s, d in there for i in range(tiles)]
        return lax.ppermute(value, ("blk", "tile", "pair"), pairs)

    def tied(values, *others):
        return lax.optimization_barrier((values, others))[0]

    def from_tile(value, step):
        return lax.ppermute(value, "tile", [((i + step) % tiles, i) for i in range(tiles)])

    def tile_pieces(own):
        return [own, *[from_tile(own, s) for s in range(1, tiles)]]

    def neighbours(pack):
        ring = [(g * span, i) for g in range(cores) for i in range(span)]
        return [
            lax.ppermute(pack, "blk", [(g + (i + s) % span, g + i) for g, i in ring])
            for s in range(1, span)
        ]

    def across(pack):
        return [
            lax.ppermute(pack, "pair", [((i + s) % cores, i) for i in range(cores)])
            for s in range(1, cores)
        ]

    def grouped(packs):
        return packs if len(packs) < 5 else [jnp.concatenate(packs)]

    def project(pieces, weights, scaled, first):
        return run_kernel(
            functools.partial(project_kernel, count=tiles, scaled=scaled, first=first),
            "project",
            [((rows, columns), BF16)] * scaled + [((rows, 2 * columns), BF16)],
            [*pieces, weights.reshape(3, tiles, share, columns)],
        )

    def begin(query, packs):
        shapes = [((heads, rows, 2 * HD), F32), ((heads, rows, 1), F32)]
        return run_kernel(begin_kernel, "begin", shapes, [query, *grouped(packs)])

    def staged(weights):
        blocks = weights[0].shape[1] // channels
        height = (weights[0].shape[0] + share // blocks) // cores
        return run_kernel(
            functools.partial(stage_kernel, cores=cores),
            "stage",
            [(w.shape, BF16) for w in weights] + [((height, weights[0].shape[1]), BF16)],
            [pltpu.with_memory_space_constraint(w, pltpu.HBM) for w in weights],
            [pltpu.SemaphoreType.DMA((len(weights) + 1 + blocks,))],
            pl.BlockSpec(memory_space=pl.ANY),
        )

    steps = range(1, tiles)
    left = [fetched(left_tokens[0], step) for step in range(tiles)]
    self_out, reassemble, cross_out, right_own, self_qkv, cross_qkv, taps, half = staged(
        [self_out, reassemble, cross_out, right_tokens[0], self_qkv, cross_qkv, taps]
    )
    right = [right_own, *[from_tile(tied(right_tokens[0], half), s) for s in steps]]
    query, pack = project(left, self_qkv, True, 0)
    (right_pack,) = project(tied(right, pack), cross_qkv, False, 1)
    right_pack = lax.ppermute(right_pack, both, there)
    beside = neighbours(pack)
    near = [pack, *across(pack)]
    halves = tile_pieces(half)[1:]
    others = [
        run_kernel(
            unpack_kernel,
            "unpack",
            [(w.shape, BF16) for w in (self_out, reassemble)],
            [half, *across(half)],
        )
        for half in halves
    ]
    map_weights = [reassemble, *[other[1] for other in others]]
    (composed,) = run_kernel(
        compose_kernel, "compose", [((columns, channels), BF16)], [cross_out, *map_weights]
    )
    state = begin(query, near)
    beside, others, composed, map_weights, state = lax.optimization_barrier(
        (beside, others, composed, map_weights, state)
    )
    far = [*beside, *[q for p in beside for q in across(p)]]
    right_pack = tied(right_pack, beside)
    right_near = [right_pack, *neighbours(right_pack)]
    (mixed,) = run_kernel(
        end_kernel, "end", [((rows, columns), BF16)], [query, *grouped(far), *state]
    )
    mixed = tile_pieces(mixed)
    right_near = tied(right_near, mixed)
    right_far = [q for p in right_near for q in across(p)]
    updated, cross_query = run_kernel(
        functools.partial(update_kernel, count=tiles),
        "update",
        [((tiles, rows, share), BF16), ((rows, columns), BF16)],
        [
            *mixed,
            self_out,
            *[other[0] for other in others],
            *left,
            cross_qkv.reshape(3, tiles, share, columns),
        ],
    )
    maps = run_kernel(
        functools.partial(end_map_kernel, count=tiles),
        "end_map",
        [(window, BF16)] * tiles,
        [cross_query, *grouped([*right_near, *right_far]), composed],
        [pltpu.VMEM(board, F32)],
    )
    (carried,) = run_kernel(
        carry_kernel,
        "carry",
        [(window, F32)],
        [tied(updated, maps), *map_weights],
        [pltpu.VMEM(board, F32)],
    )
    received = [from_tile(part, s) for s, part in enumerate(maps) if s > 0]
    (features,) = run_kernel(add_kernel, "add", [(window, BF16)], [carried, maps[0], *received])
    above = lax.ppermute(features[-1:], both, down)
    below = lax.ppermute(features[:1], both, up)
    features = lax.ppermute(features, both, back)
    (joined,) = run_kernel(
        conv_kernel,
        "join",
        [((band_rows, width, channels), BF16)],
        [features, above, below, taps],
    )
    return joined[None]


def solution(mesh):
    placed = (
        P(("groups", "pair"), "blk", "tile"),
        P(("groups", "pair"), "blk", "tile"),
        P(None, None, "tile"),
        P("tile", None),
        P(None, None, "tile"),
        P("tile", None),
        P("tile", None),
        P(),
    )
    return jax.shard_map(
        body,
        mesh=mesh,
        in_specs=placed,
        out_specs=P(("groups", "pair"), "blk", "tile", None),
        check_vma=False,
    )
```

```python
import functools
import math

import jax
import jax.numpy as jnp
from jax import lax
from jax.experimental import pallas as pl
from jax.experimental.pallas import tpu as pltpu
from jax.sharding import PartitionSpec as P

HD = 64
GRID_W = 128
EDGE = 8
F32 = jnp.float32
BF16 = jnp.bfloat16
QUERY_SCALE = math.log2(math.e) * HD**-0.5
VMEM = pl.BlockSpec(memory_space=pltpu.VMEM)
HBM = pl.BlockSpec(memory_space=pl.ANY)


def run_kernel(kernel, name, shapes, operands, scratch=(), space=VMEM):
    return pl.pallas_call(
        kernel,
        out_shape=[jax.ShapeDtypeStruct(*s) for s in shapes],
        in_specs=[space] * len(operands),
        out_specs=[VMEM] * len(shapes),
        scratch_shapes=scratch,
        compiler_params=pltpu.CompilerParams(vmem_limit_bytes=24 << 20),
        cost_estimate=pl.CostEstimate(flops=0, bytes_accessed=0, transcendentals=0),
        name=name,
    )(*operands)


def slot_of(step, count):
    return lax.rem(lax.axis_index("tile") + step, count)


def normalized(pieces):
    widened = [piece.astype(F32) for piece in pieces]
    width = sum(piece.shape[1] for piece in widened)
    mean = sum(jnp.sum(piece, axis=1, keepdims=True) for piece in widened) / width
    centred = [piece - mean for piece in widened]
    variance = sum(jnp.sum(piece * piece, axis=1, keepdims=True) for piece in centred) / width
    scale = lax.rsqrt(variance + 1e-06)
    return [(piece * scale).astype(BF16) for piece in centred]


def dot(left, right):
    return jnp.dot(left, right, preferred_element_type=F32)


def project_kernel(*refs, count, scaled, first):
    pieces, weight, outs = refs[:count], refs[count], refs[count + 1 :]
    normed = normalized([piece[...] for piece in pieces])
    products = []
    for which in range(first, weight.shape[0]):
        products.append(
            sum(dot(normed[step], weight[which, slot_of(step, count)]) for step in range(count))
        )
    if scaled:
        outs[0][...] = (products.pop(0) * QUERY_SCALE).astype(BF16)
    columns = weight.shape[3]
    for which, product in enumerate(products):
        outs[-1][:, which * columns : (which + 1) * columns] = product.astype(BF16)


def attended(query, packs, index):
    columns = query.shape[1]
    start = index * HD
    head = slice(start, start + HD)
    values = slice(columns + start, columns + start + HD)
    asked = query[:, head]
    scores = [
        lax.dot_general(asked, pack[:, head], (((1,), (1,)), ((), ())), preferred_element_type=F32)
        for pack in packs
    ]
    maxima = functools.reduce(
        jnp.maximum, [jnp.max(score, axis=1, keepdims=True) for score in scores]
    )
    mixed = 0.0
    for score, pack in zip(scores, packs):
        value = pack[:, values]
        widened = jnp.concatenate([value, jnp.ones_like(value)], axis=1)
        mixed = mixed + dot(jnp.exp2(score - maxima).astype(BF16), widened)
    return mixed, maxima


def begin_kernel(query, *refs):
    packs, (mixed_out, maxima_out) = refs[:-2], refs[-2:]
    for index in range(query.shape[1] // HD):
        mixed_out[index], maxima_out[index] = attended(query, packs, index)


def ended(query, packs, state):
    heads = []
    for index in range(query.shape[1] // HD):
        mixed, maxima = attended(query, packs, index)
        if state:
            before = state[1][index]
            highest = jnp.maximum(maxima, before)
            mixed = mixed * jnp.exp2(maxima - highest)
            mixed = mixed + state[0][index] * jnp.exp2(before - highest)
        heads.append(mixed[:, :HD] / mixed[:, HD:])
    return jnp.concatenate(heads, axis=1).astype(BF16)


def end_kernel(query, *refs):
    refs[-1][...] = ended(query, refs[:-3], refs[-3:-1])


def fill_board(board, values):
    band_rows, channels = board.shape[0], board.shape[2]
    edge = jnp.zeros((band_rows, EDGE, channels), board.dtype)
    board[:, :EDGE, :] = edge
    board[:, EDGE + GRID_W :, :] = edge
    inner = values.reshape(band_rows, GRID_W, channels)
    board[:, EDGE : EDGE + GRID_W, :] = inner.astype(board.dtype)


def window_of(board, slot, out):
    width = out.shape[1] - 2 * EDGE
    start = pl.multiple_of(slot * width, width)
    out[...] = board[:, pl.ds(start, out.shape[1]), :].astype(out.dtype)


def end_map_kernel(query, *refs, count):
    composed, outs, board = refs[-2 - count], refs[-1 - count : -1], refs[-1]
    fill_board(board, dot(ended(query, refs[: -2 - count], ()), composed[...]))
    for step, out in enumerate(outs):
        window_of(board, slot_of(count - step, count), out)


def carry_kernel(updated, *refs):
    pieces, out, board = refs[:-2], refs[-2], refs[-1]
    fill_board(board, sum(dot(updated[i], piece[...]) for i, piece in enumerate(pieces)))
    window_of(board, lax.axis_index("tile"), out)


def add_kernel(*refs):
    refs[-1][...] = sum(ref[...].astype(F32) for ref in refs[:-1]).astype(BF16)


def stage_kernel(*refs, cores):
    count = (len(refs) - 2) // 2
    sources, outs, half, sems = refs[:count], refs[count : 2 * count], refs[-2], refs[-1]
    core = lax.axis_index("pair")
    pairs = list(zip(sources, outs))
    rows = sources[0].shape[0] // cores
    begin = pl.multiple_of(core * rows, rows)
    pairs.append((sources[0].at[pl.ds(begin, rows)], half.at[pl.ds(0, rows)]))
    start = rows
    blocks = half.shape[1] // sources[1].shape[1]
    block = sources[1].shape[0] // blocks
    rows = block // cores
    for index in range(blocks):
        begin = pl.multiple_of(core * rows + index * block, rows)
        lanes = pl.ds(index * sources[1].shape[1], sources[1].shape[1])
        pairs.append((sources[1].at[pl.ds(begin, rows)], half.at[pl.ds(start, rows), lanes]))
    copies = [pltpu.make_async_copy(a, b, sems.at[i]) for i, (a, b) in enumerate(pairs)]
    for copy in copies:
        copy.start()
    for copy in copies:
        copy.wait()


def unpack_kernel(*refs):
    halves, outs = refs[:-2], refs[-2:]
    for step, half in enumerate(halves):
        core = lax.rem(lax.axis_index("pair") + step, len(halves))
        rows = outs[0].shape[0] // len(halves)
        outs[0][pl.ds(pl.multiple_of(core * rows, rows), rows), :] = half[:rows, :]
        start = rows
        blocks = half.shape[1] // outs[1].shape[1]
        block = outs[1].shape[0] // blocks
        rows = block // len(halves)
        for index in range(blocks):
            first = pl.multiple_of(core * rows + index * block, rows)
            lanes = slice(index * outs[1].shape[1], (index + 1) * outs[1].shape[1])
            outs[1][pl.ds(first, rows), :] = half[start : start + rows, lanes]


def pick(options, slot):
    chosen = options[0]
    for index in range(1, len(options)):
        chosen = jnp.where(slot == index, options[index], chosen)
    return chosen


def feature_shares(whole, count):
    share = whole.shape[1] // count
    options = [whole[:, i * share : (i + 1) * share] for i in range(count)]
    return [pick(options, slot_of(step, count)) for step in range(count)]


def compose_kernel(weight, *refs):
    pieces, out = refs[:-1], refs[-1]
    shares = feature_shares(weight[...].astype(F32), len(pieces))
    out[...] = sum(dot(s.astype(BF16), p[...]) for s, p in zip(shares, pieces)).astype(BF16)


def update_kernel(*refs, count):
    mixed, weights = refs[:count], refs[count : 2 * count]
    tokens, query_weight = refs[2 * count : 3 * count], refs[3 * count]
    updated, query = refs[3 * count + 1 :]
    whole = sum(dot(m[...], w[...]) for m, w in zip(mixed, weights))
    pieces = []
    for step, term in enumerate(feature_shares(whole, count)):
        piece = (tokens[step][...].astype(F32) + term).astype(BF16)
        updated[step] = piece
        pieces.append(piece)
    normed = normalized(pieces)
    product = sum(
        dot(normed[step], query_weight[0, slot_of(step, count)]) for step in range(count)
    )
    query[...] = (product * QUERY_SCALE).astype(BF16)


def conv_kernel(window, above, below, weight, out):
    width = out.shape[1]
    band_rows, channels = out.shape[0], out.shape[2]
    grid = jnp.concatenate([above[...], window[...], below[...]], axis=0).astype(F32)
    active = jnp.maximum(grid, 0.0)
    total = grid[1 : 1 + band_rows, EDGE : EDGE + width, :].reshape(band_rows * width, channels)
    for column in range(3):
        first = EDGE - 1 + column
        shifted = active[:, first : first + width, :].astype(BF16)
        for row in range(3):
            rows = shifted[row : row + band_rows].reshape(band_rows * width, channels)
            total = total + dot(rows, weight[row, column])
    out[...] = total.reshape(out.shape).astype(BF16)


def body(left_tokens, right_tokens, self_qkv, self_out, cross_qkv, cross_out, reassemble, taps):
    bands, tiles, cores = (lax.axis_size(axis) for axis in ("blk", "tile", "pair"))
    span = bands // cores
    both = ("blk", "pair")
    rows, share = left_tokens.shape[1:]
    columns = self_qkv.shape[2]
    channels = reassemble.shape[1]
    width = GRID_W // tiles
    band_rows = rows // GRID_W
    heads = columns // HD
    window = (band_rows, width + 2 * EDGE, channels)
    board = (band_rows, GRID_W + 2 * EDGE, channels)

    def home(band, pair):
        return band * cores + pair

    def worker(band, pair):
        part, index = divmod(band, span)
        if part == pair:
            return band * cores + pair
        shift = (pair - part) % cores
        return (pair * span + span - 1 - index) * cores + (pair - shift) % cores

    places = [(band, pair) for band in range(bands) for pair in range(cores)]
    there = [(home(*p), worker(*p)) for p in places]
    back = [(worker(*p), home(*p)) for p in places]
    down = [(worker(b, p), home(b + 1, p)) for b, p in places if b + 1 < bands]
    up = [(worker(b, p), home(b - 1, p)) for b, p in places if b > 0]

    def fetched(value, step):
        def flat(position, tile):
            return (position // cores * tiles + tile) * cores + position % cores

        pairs = [(flat(s, (i + step) % tiles), flat(d, i)) for s, d in there for i in range(tiles)]
        return lax.ppermute(value, ("blk", "tile", "pair"), pairs)

    def tied(values, *others):
        return lax.optimization_barrier((values, others))[0]

    def from_tile(value, step):
        return lax.ppermute(value, "tile", [((i + step) % tiles, i) for i in range(tiles)])

    def tile_pieces(own):
        return [own, *[from_tile(own, s) for s in range(1, tiles)]]

    def neighbours(pack):
        ring = [(g * span, i) for g in range(cores) for i in range(span)]
        return [
            lax.ppermute(pack, "blk", [(g + (i + s) % span, g + i) for g, i in ring])
            for s in range(1, span)
        ]

    def across(pack):
        return [
            lax.ppermute(pack, "pair", [((i + s) % cores, i) for i in range(cores)])
            for s in range(1, cores)
        ]

    def grouped(packs):
        return packs if len(packs) < 5 else [jnp.concatenate(packs)]

    def project(pieces, weights, scaled, first):
        return run_kernel(
            functools.partial(project_kernel, count=tiles, scaled=scaled, first=first),
            "project",
            [((rows, columns), BF16)] * scaled + [((rows, 2 * columns), BF16)],
            [*pieces, weights.reshape(3, tiles, share, columns)],
        )

    def begin(query, packs):
        shapes = [((heads, rows, 2 * HD), F32), ((heads, rows, 1), F32)]
        return run_kernel(begin_kernel, "begin", shapes, [query, *grouped(packs)])

    def staged(weights):
        blocks = weights[0].shape[1] // channels
        height = (weights[0].shape[0] + share // blocks) // cores
        return run_kernel(
            functools.partial(stage_kernel, cores=cores),
            "stage",
            [(w.shape, BF16) for w in weights] + [((height, weights[0].shape[1]), BF16)],
            [pltpu.with_memory_space_constraint(w, pltpu.HBM) for w in weights],
            [pltpu.SemaphoreType.DMA((len(weights) + 1 + blocks,))],
            pl.BlockSpec(memory_space=pl.ANY),
        )

    steps = range(1, tiles)
    left = [fetched(left_tokens[0], step) for step in range(tiles)]
    self_out, reassemble, cross_out, right_own, self_qkv, cross_qkv, taps, half = staged(
        [self_out, reassemble, cross_out, right_tokens[0], self_qkv, cross_qkv, taps]
    )
    right = [right_own, *[from_tile(tied(right_tokens[0], half), s) for s in steps]]
    query, pack = project(left, self_qkv, True, 0)
    (right_pack,) = project(tied(right, pack), cross_qkv, False, 1)
    beside = neighbours(pack)
    near = [pack, *beside]
    far = [q for p in near for q in across(p)]
    state = begin(query, near)
    halves = tile_pieces(tied(half, right_pack))[1:]
    right_pack = lax.ppermute(right_pack, both, there)
    others = [
        run_kernel(
            unpack_kernel,
            "unpack",
            [(w.shape, BF16) for w in (self_out, reassemble)],
            [half, *across(half)],
        )
        for half in halves
    ]
    map_weights = [reassemble, *[other[1] for other in others]]
    (composed,) = run_kernel(
        compose_kernel, "compose", [((columns, channels), BF16)], [cross_out, *map_weights]
    )
    far, others, composed, map_weights, right_pack = lax.optimization_barrier(
        (far, others, composed, map_weights, right_pack)
    )
    (mixed,) = run_kernel(
        end_kernel, "end", [((rows, columns), BF16)], [query, *grouped(far), *state]
    )
    right_pack = tied(right_pack, mixed)
    right_near = [right_pack, *neighbours(right_pack)]
    mixed = tile_pieces(mixed)
    right_near = tied(right_near, mixed)
    right_far = [q for p in right_near for q in across(p)]
    updated, cross_query = run_kernel(
        functools.partial(update_kernel, count=tiles),
        "update",
        [((tiles, rows, share), BF16), ((rows, columns), BF16)],
        [
            *mixed,
            self_out,
            *[other[0] for other in others],
            *left,
            cross_qkv.reshape(3, tiles, share, columns),
        ],
    )
    maps = run_kernel(
        functools.partial(end_map_kernel, count=tiles),
        "end_map",
        [(window, BF16)] * tiles,
        [cross_query, *grouped([*right_near, *right_far]), composed],
        [pltpu.VMEM(board, F32)],
    )
    (carried,) = run_kernel(
        carry_kernel,
        "carry",
        [(window, F32)],
        [tied(updated, maps), *map_weights],
        [pltpu.VMEM(board, F32)],
    )
    received = [from_tile(part, s) for s, part in enumerate(maps) if s > 0]
    (features,) = run_kernel(add_kernel, "add", [(window, BF16)], [carried, maps[0], *received])
    above = lax.ppermute(features[-1:], both, down)
    below = lax.ppermute(features[:1], both, up)
    features = lax.ppermute(features, both, back)
    (joined,) = run_kernel(
        conv_kernel,
        "join",
        [((band_rows, width, channels), BF16)],
        [features, above, below, taps],
    )
    return joined[None]


def solution(mesh):
    placed = (
        P(("groups", "pair"), "blk", "tile"),
        P(("groups", "pair"), "blk", "tile"),
        P(None, None, "tile"),
        P("tile", None),
        P(None, None, "tile"),
        P("tile", None),
        P("tile", None),
        P(),
    )
    return jax.shard_map(
        body,
        mesh=mesh,
        in_specs=placed,
        out_specs=P(("groups", "pair"), "blk", "tile", None),
        check_vma=False,
    )
```

```python
import functools
import math

import jax
import jax.numpy as jnp
from jax import lax
from jax.experimental import pallas as pl
from jax.experimental.pallas import tpu as pltpu
from jax.sharding import PartitionSpec as P

HD = 64
GRID_W = 128
EDGE = 8
F32 = jnp.float32
BF16 = jnp.bfloat16
QUERY_SCALE = math.log2(math.e) * HD**-0.5
VMEM = pl.BlockSpec(memory_space=pltpu.VMEM)
HBM = pl.BlockSpec(memory_space=pl.ANY)


def run_kernel(kernel, name, shapes, operands, scratch=(), space=VMEM):
    return pl.pallas_call(
        kernel,
        out_shape=[jax.ShapeDtypeStruct(*s) for s in shapes],
        in_specs=[space] * len(operands),
        out_specs=[VMEM] * len(shapes),
        scratch_shapes=scratch,
        compiler_params=pltpu.CompilerParams(vmem_limit_bytes=24 << 20),
        cost_estimate=pl.CostEstimate(flops=0, bytes_accessed=0, transcendentals=0),
        name=name,
    )(*operands)


def slot_of(step, count):
    return lax.rem(lax.axis_index("tile") + step, count)


def normalized(pieces):
    widened = [piece.astype(F32) for piece in pieces]
    width = sum(piece.shape[1] for piece in widened)
    mean = sum(jnp.sum(piece, axis=1, keepdims=True) for piece in widened) / width
    centred = [piece - mean for piece in widened]
    variance = sum(jnp.sum(piece * piece, axis=1, keepdims=True) for piece in centred) / width
    scale = lax.rsqrt(variance + 1e-06)
    return [(piece * scale).astype(BF16) for piece in centred]


def dot(left, right):
    return jnp.dot(left, right, preferred_element_type=F32)


def project_kernel(*refs, count, scaled, first):
    pieces, weight, outs = refs[:count], refs[count], refs[count + 1 :]
    normed = normalized([piece[...] for piece in pieces])
    products = []
    for which in range(first, weight.shape[0]):
        products.append(
            sum(dot(normed[step], weight[which, slot_of(step, count)]) for step in range(count))
        )
    if scaled:
        outs[0][...] = (products.pop(0) * QUERY_SCALE).astype(BF16)
    columns = weight.shape[3]
    for which, product in enumerate(products):
        outs[-1][:, which * columns : (which + 1) * columns] = product.astype(BF16)


def attended(query, packs, index):
    columns = query.shape[1]
    start = index * HD
    head = slice(start, start + HD)
    values = slice(columns + start, columns + start + HD)
    asked = query[:, head]
    scores = [
        lax.dot_general(asked, pack[:, head], (((1,), (1,)), ((), ())), preferred_element_type=F32)
        for pack in packs
    ]
    maxima = functools.reduce(
        jnp.maximum, [jnp.max(score, axis=1, keepdims=True) for score in scores]
    )
    mixed = 0.0
    for score, pack in zip(scores, packs):
        value = pack[:, values]
        widened = jnp.concatenate([value, jnp.ones_like(value)], axis=1)
        mixed = mixed + dot(jnp.exp2(score - maxima).astype(BF16), widened)
    return mixed, maxima


def begin_kernel(query, *refs):
    packs, (mixed_out, maxima_out) = refs[:-2], refs[-2:]
    for index in range(query.shape[1] // HD):
        mixed_out[index], maxima_out[index] = attended(query, packs, index)


def ended(query, packs, state):
    heads = []
    for index in range(query.shape[1] // HD):
        mixed, maxima = attended(query, packs, index)
        if state:
            before = state[1][index]
            highest = jnp.maximum(maxima, before)
            mixed = mixed * jnp.exp2(maxima - highest)
            mixed = mixed + state[0][index] * jnp.exp2(before - highest)
        heads.append(mixed[:, :HD] / mixed[:, HD:])
    return jnp.concatenate(heads, axis=1).astype(BF16)


def end_kernel(query, *refs):
    refs[-1][...] = ended(query, refs[:-3], refs[-3:-1])


def fill_board(board, values):
    band_rows, channels = board.shape[0], board.shape[2]
    edge = jnp.zeros((band_rows, EDGE, channels), board.dtype)
    board[:, :EDGE, :] = edge
    board[:, EDGE + GRID_W :, :] = edge
    inner = values.reshape(band_rows, GRID_W, channels)
    board[:, EDGE : EDGE + GRID_W, :] = inner.astype(board.dtype)


def window_of(board, slot, out):
    width = out.shape[1] - 2 * EDGE
    start = pl.multiple_of(slot * width, width)
    out[...] = board[:, pl.ds(start, out.shape[1]), :].astype(out.dtype)


def end_map_kernel(query, *refs, count):
    composed, outs, board = refs[-2 - count], refs[-1 - count : -1], refs[-1]
    fill_board(board, dot(ended(query, refs[: -2 - count], ()), composed[...]))
    for step, out in enumerate(outs):
        window_of(board, slot_of(count - step, count), out)


def carry_kernel(updated, *refs):
    pieces, out, board = refs[:-2], refs[-2], refs[-1]
    fill_board(board, sum(dot(updated[i], piece[...]) for i, piece in enumerate(pieces)))
    window_of(board, lax.axis_index("tile"), out)


def add_kernel(*refs):
    refs[-1][...] = sum(ref[...].astype(F32) for ref in refs[:-1]).astype(BF16)


def stage_kernel(*refs, cores):
    count = (len(refs) - 2) // 2
    sources, outs, half, sems = refs[:count], refs[count : 2 * count], refs[-2], refs[-1]
    core = lax.axis_index("pair")
    pairs = list(zip(sources, outs))
    rows = sources[0].shape[0] // cores
    begin = pl.multiple_of(core * rows, rows)
    pairs.append((sources[0].at[pl.ds(begin, rows)], half.at[pl.ds(0, rows)]))
    start = rows
    blocks = half.shape[1] // sources[1].shape[1]
    block = sources[1].shape[0] // blocks
    rows = block // cores
    for index in range(blocks):
        begin = pl.multiple_of(core * rows + index * block, rows)
        lanes = pl.ds(index * sources[1].shape[1], sources[1].shape[1])
        pairs.append((sources[1].at[pl.ds(begin, rows)], half.at[pl.ds(start, rows), lanes]))
    copies = [pltpu.make_async_copy(a, b, sems.at[i]) for i, (a, b) in enumerate(pairs)]
    for copy in copies:
        copy.start()
    for copy in copies:
        copy.wait()


def unpack_kernel(*refs):
    halves, outs = refs[:-2], refs[-2:]
    for step, half in enumerate(halves):
        core = lax.rem(lax.axis_index("pair") + step, len(halves))
        rows = outs[0].shape[0] // len(halves)
        outs[0][pl.ds(pl.multiple_of(core * rows, rows), rows), :] = half[:rows, :]
        start = rows
        blocks = half.shape[1] // outs[1].shape[1]
        block = outs[1].shape[0] // blocks
        rows = block // len(halves)
        for index in range(blocks):
            first = pl.multiple_of(core * rows + index * block, rows)
            lanes = slice(index * outs[1].shape[1], (index + 1) * outs[1].shape[1])
            outs[1][pl.ds(first, rows), :] = half[start : start + rows, lanes]


def pick(options, slot):
    chosen = options[0]
    for index in range(1, len(options)):
        chosen = jnp.where(slot == index, options[index], chosen)
    return chosen


def feature_shares(whole, count):
    share = whole.shape[1] // count
    options = [whole[:, i * share : (i + 1) * share] for i in range(count)]
    return [pick(options, slot_of(step, count)) for step in range(count)]


def compose_kernel(weight, *refs):
    pieces, out = refs[:-1], refs[-1]
    shares = feature_shares(weight[...].astype(F32), len(pieces))
    out[...] = sum(dot(s.astype(BF16), p[...]) for s, p in zip(shares, pieces)).astype(BF16)


def update_kernel(*refs, count):
    mixed, weights = refs[:count], refs[count : 2 * count]
    tokens, query_weight = refs[2 * count : 3 * count], refs[3 * count]
    updated, query = refs[3 * count + 1 :]
    whole = sum(dot(m[...], w[...]) for m, w in zip(mixed, weights))
    pieces = []
    for step, term in enumerate(feature_shares(whole, count)):
        piece = (tokens[step][...].astype(F32) + term).astype(BF16)
        updated[step] = piece
        pieces.append(piece)
    normed = normalized(pieces)
    product = sum(
        dot(normed[step], query_weight[0, slot_of(step, count)]) for step in range(count)
    )
    query[...] = (product * QUERY_SCALE).astype(BF16)


def conv_kernel(window, above, below, weight, out):
    width = out.shape[1]
    band_rows, channels = out.shape[0], out.shape[2]
    grid = jnp.concatenate([above[...], window[...], below[...]], axis=0).astype(F32)
    active = jnp.maximum(grid, 0.0)
    total = grid[1 : 1 + band_rows, EDGE : EDGE + width, :].reshape(band_rows * width, channels)
    for column in range(3):
        first = EDGE - 1 + column
        shifted = active[:, first : first + width, :].astype(BF16)
        for row in range(3):
            rows = shifted[row : row + band_rows].reshape(band_rows * width, channels)
            total = total + dot(rows, weight[row, column])
    out[...] = total.reshape(out.shape).astype(BF16)


def body(left_tokens, right_tokens, self_qkv, self_out, cross_qkv, cross_out, reassemble, taps):
    bands, tiles, cores = (lax.axis_size(axis) for axis in ("blk", "tile", "pair"))
    span = bands // cores
    both = ("blk", "pair")
    rows, share = left_tokens.shape[1:]
    columns = self_qkv.shape[2]
    channels = reassemble.shape[1]
    width = GRID_W // tiles
    band_rows = rows // GRID_W
    heads = columns // HD
    window = (band_rows, width + 2 * EDGE, channels)
    board = (band_rows, GRID_W + 2 * EDGE, channels)

    def home(band, pair):
        return band * cores + pair

    def worker(band, pair):
        part, index = divmod(band, span)
        if part == pair:
            return band * cores + pair
        shift = (pair - part) % cores
        return (pair * span + span - 1 - index) * cores + (pair - shift) % cores

    places = [(band, pair) for band in range(bands) for pair in range(cores)]
    there = [(home(*p), worker(*p)) for p in places]
    back = [(worker(*p), home(*p)) for p in places]
    down = [(worker(b, p), home(b + 1, p)) for b, p in places if b + 1 < bands]
    up = [(worker(b, p), home(b - 1, p)) for b, p in places if b > 0]

    stays = [home(*p) for p in places if home(*p) == worker(*p)]
    comes = [worker(*p) for p in places if home(*p) != worker(*p)]

    def fetched(value, step):
        def flat(position, tile):
            return (position // cores * tiles + tile) * cores + position % cores

        pairs = [(flat(s, (i + step) % tiles), flat(d, i)) for s, d in there for i in range(tiles)]
        return lax.ppermute(value, ("blk", "tile", "pair"), pairs)

    def tied(values, *others):
        return lax.optimization_barrier((values, others))[0]

    def from_tile(value, step):
        return lax.ppermute(value, "tile", [((i + step) % tiles, i) for i in range(tiles)])

    def tile_pieces(own):
        return [own, *[from_tile(own, s) for s in range(1, tiles)]]

    def neighbours(pack, members):
        def source(member, step):
            band, core = divmod(member, cores)
            return (band // span * span + (band % span + step) % span) * cores + core

        return [
            lax.ppermute(pack, both, [(source(m, s), m) for m in members]) for s in range(1, span)
        ]

    def across(pack):
        return [
            lax.ppermute(pack, "pair", [((i + s) % cores, i) for i in range(cores)])
            for s in range(1, cores)
        ]

    def grouped(packs):
        return packs if len(packs) < 5 else [jnp.concatenate(packs)]

    def project(pieces, weights, scaled, first):
        return run_kernel(
            functools.partial(project_kernel, count=tiles, scaled=scaled, first=first),
            "project",
            [((rows, columns), BF16)] * scaled + [((rows, 2 * columns), BF16)],
            [*pieces, weights.reshape(3, tiles, share, columns)],
        )

    def begin(query, packs):
        shapes = [((heads, rows, 2 * HD), F32), ((heads, rows, 1), F32)]
        return run_kernel(begin_kernel, "begin", shapes, [query, *grouped(packs)])

    def staged(weights):
        blocks = weights[0].shape[1] // channels
        height = (weights[0].shape[0] + share // blocks) // cores
        return run_kernel(
            functools.partial(stage_kernel, cores=cores),
            "stage",
            [(w.shape, BF16) for w in weights] + [((height, weights[0].shape[1]), BF16)],
            [pltpu.with_memory_space_constraint(w, pltpu.HBM) for w in weights],
            [pltpu.SemaphoreType.DMA((len(weights) + 1 + blocks,))],
            pl.BlockSpec(memory_space=pl.ANY),
        )

    steps = range(1, tiles)
    left = [fetched(left_tokens[0], step) for step in range(tiles)]
    self_out, reassemble, cross_out, right_own, self_qkv, cross_qkv, taps, half = staged(
        [self_out, reassemble, cross_out, right_tokens[0], self_qkv, cross_qkv, taps]
    )
    right = [right_own, *[from_tile(tied(right_tokens[0], half), s) for s in steps]]
    query, pack = project(left, self_qkv, True, 0)
    (right_pack,) = project(tied(right, pack), cross_qkv, False, 1)
    beside = neighbours(pack, [*stays, *comes])
    right_early = neighbours(right_pack, stays)
    near = [pack, *beside]
    far = [q for p in near for q in across(p)]
    state = begin(query, near)
    halves = tile_pieces(tied(half, right_pack))[1:]
    right_pack = lax.ppermute(right_pack, both, there)
    others = [
        run_kernel(
            unpack_kernel,
            "unpack",
            [(w.shape, BF16) for w in (self_out, reassemble)],
            [half, *across(half)],
        )
        for half in halves
    ]
    map_weights = [reassemble, *[other[1] for other in others]]
    (composed,) = run_kernel(
        compose_kernel, "compose", [((columns, channels), BF16)], [cross_out, *map_weights]
    )
    far, others, composed, map_weights, right_pack, right_early = lax.optimization_barrier(
        (far, others, composed, map_weights, right_pack, right_early)
    )
    (mixed,) = run_kernel(
        end_kernel, "end", [((rows, columns), BF16)], [query, *grouped(far), *state]
    )
    right_pack = tied(right_pack, mixed)
    right_late = neighbours(right_pack, comes)
    mixed = tile_pieces(mixed)
    right_late = tied(right_late, mixed)
    right_near = [right_pack, *[a + b for a, b in zip(right_early, right_late)]]
    right_far = [q for p in right_near for q in across(p)]
    updated, cross_query = run_kernel(
        functools.partial(update_kernel, count=tiles),
        "update",
        [((tiles, rows, share), BF16), ((rows, columns), BF16)],
        [
            *mixed,
            self_out,
            *[other[0] for other in others],
            *left,
            cross_qkv.reshape(3, tiles, share, columns),
        ],
    )
    maps = run_kernel(
        functools.partial(end_map_kernel, count=tiles),
        "end_map",
        [(window, BF16)] * tiles,
        [cross_query, *grouped([*right_near, *right_far]), composed],
        [pltpu.VMEM(board, F32)],
    )
    (carried,) = run_kernel(
        carry_kernel,
        "carry",
        [(window, F32)],
        [tied(updated, maps), *map_weights],
        [pltpu.VMEM(board, F32)],
    )
    received = [from_tile(part, s) for s, part in enumerate(maps) if s > 0]
    (features,) = run_kernel(add_kernel, "add", [(window, BF16)], [carried, maps[0], *received])
    above = lax.ppermute(features[-1:], both, down)
    below = lax.ppermute(features[:1], both, up)
    features = lax.ppermute(features, both, back)
    (joined,) = run_kernel(
        conv_kernel,
        "join",
        [((band_rows, width, channels), BF16)],
        [features, above, below, taps],
    )
    return joined[None]


def solution(mesh):
    placed = (
        P(("groups", "pair"), "blk", "tile"),
        P(("groups", "pair"), "blk", "tile"),
        P(None, None, "tile"),
        P("tile", None),
        P(None, None, "tile"),
        P("tile", None),
        P("tile", None),
        P(),
    )
    return jax.shard_map(
        body,
        mesh=mesh,
        in_specs=placed,
        out_specs=P(("groups", "pair"), "blk", "tile", None),
        check_vma=False,
    )
```

```python
import functools
import math

import jax
import jax.numpy as jnp
from jax import lax
from jax.experimental import pallas as pl
from jax.experimental.pallas import tpu as pltpu
from jax.sharding import PartitionSpec as P

HD = 64
GRID_W = 128
EDGE = 8
F32 = jnp.float32
BF16 = jnp.bfloat16
QUERY_SCALE = math.log2(math.e) * HD**-0.5
VMEM = pl.BlockSpec(memory_space=pltpu.VMEM)
HBM = pl.BlockSpec(memory_space=pl.ANY)


def run_kernel(kernel, name, shapes, operands, scratch=(), space=VMEM):
    return pl.pallas_call(
        kernel,
        out_shape=[jax.ShapeDtypeStruct(*s) for s in shapes],
        in_specs=[space] * len(operands),
        out_specs=[VMEM] * len(shapes),
        scratch_shapes=scratch,
        compiler_params=pltpu.CompilerParams(vmem_limit_bytes=24 << 20),
        cost_estimate=pl.CostEstimate(flops=0, bytes_accessed=0, transcendentals=0),
        name=name,
    )(*operands)


def slot_of(step, count):
    return lax.rem(lax.axis_index("tile") + step, count)


def normalized(pieces):
    widened = [piece.astype(F32) for piece in pieces]
    width = sum(piece.shape[1] for piece in widened)
    mean = sum(jnp.sum(piece, axis=1, keepdims=True) for piece in widened) / width
    centred = [piece - mean for piece in widened]
    variance = sum(jnp.sum(piece * piece, axis=1, keepdims=True) for piece in centred) / width
    scale = lax.rsqrt(variance + 1e-06)
    return [(piece * scale).astype(BF16) for piece in centred]


def dot(left, right):
    return jnp.dot(left, right, preferred_element_type=F32)


def project_kernel(*refs, count, scaled, first):
    pieces, weight, outs = refs[:count], refs[count], refs[count + 1 :]
    normed = normalized([piece[...] for piece in pieces])
    products = []
    for which in range(first, weight.shape[0]):
        products.append(
            sum(dot(normed[step], weight[which, slot_of(step, count)]) for step in range(count))
        )
    if scaled:
        outs[0][...] = (products.pop(0) * QUERY_SCALE).astype(BF16)
    columns = weight.shape[3]
    for which, product in enumerate(products):
        outs[-1][:, which * columns : (which + 1) * columns] = product.astype(BF16)


def attended(query, packs, index):
    columns = query.shape[1]
    start = index * HD
    head = slice(start, start + HD)
    values = slice(columns + start, columns + start + HD)
    asked = query[:, head]
    scores = [
        lax.dot_general(asked, pack[:, head], (((1,), (1,)), ((), ())), preferred_element_type=F32)
        for pack in packs
    ]
    maxima = functools.reduce(
        jnp.maximum, [jnp.max(score, axis=1, keepdims=True) for score in scores]
    )
    mixed = 0.0
    for score, pack in zip(scores, packs):
        value = pack[:, values]
        widened = jnp.concatenate([value, jnp.ones_like(value)], axis=1)
        mixed = mixed + dot(jnp.exp2(score - maxima).astype(BF16), widened)
    return mixed, maxima


def begin_kernel(query, *refs):
    packs, (mixed_out, maxima_out) = refs[:-2], refs[-2:]
    for index in range(query.shape[1] // HD):
        mixed_out[index], maxima_out[index] = attended(query, packs, index)


def ended(query, packs, state):
    heads = []
    for index in range(query.shape[1] // HD):
        mixed, maxima = attended(query, packs, index)
        if state:
            before = state[1][index]
            highest = jnp.maximum(maxima, before)
            mixed = mixed * jnp.exp2(maxima - highest)
            mixed = mixed + state[0][index] * jnp.exp2(before - highest)
        heads.append(mixed[:, :HD] / mixed[:, HD:])
    return jnp.concatenate(heads, axis=1).astype(BF16)


def end_kernel(query, *refs):
    refs[-1][...] = ended(query, refs[:-3], refs[-3:-1])


def fill_board(board, values):
    band_rows, channels = board.shape[0], board.shape[2]
    edge = jnp.zeros((band_rows, EDGE, channels), board.dtype)
    board[:, :EDGE, :] = edge
    board[:, EDGE + GRID_W :, :] = edge
    inner = values.reshape(band_rows, GRID_W, channels)
    board[:, EDGE : EDGE + GRID_W, :] = inner.astype(board.dtype)


def window_of(board, slot, out):
    width = out.shape[1] - 2 * EDGE
    start = pl.multiple_of(slot * width, width)
    out[...] = board[:, pl.ds(start, out.shape[1]), :].astype(out.dtype)


def end_map_kernel(query, *refs, count):
    composed, outs, board = refs[-2 - count], refs[-1 - count : -1], refs[-1]
    fill_board(board, dot(ended(query, refs[: -2 - count], ()), composed[...]))
    for step, out in enumerate(outs):
        window_of(board, slot_of(count - step, count), out)


def carry_kernel(updated, *refs):
    pieces, out, board = refs[:-2], refs[-2], refs[-1]
    fill_board(board, sum(dot(updated[i], piece[...]) for i, piece in enumerate(pieces)))
    window_of(board, lax.axis_index("tile"), out)


def add_kernel(*refs):
    refs[-1][...] = sum(ref[...].astype(F32) for ref in refs[:-1]).astype(BF16)


def stage_kernel(*refs, cores):
    count = (len(refs) - 2) // 2
    sources, outs, half, sems = refs[:count], refs[count : 2 * count], refs[-2], refs[-1]
    core = lax.axis_index("pair")
    pairs = list(zip(sources, outs))
    rows = sources[0].shape[0] // cores
    begin = pl.multiple_of(core * rows, rows)
    pairs.append((sources[0].at[pl.ds(begin, rows)], half.at[pl.ds(0, rows)]))
    start = rows
    blocks = half.shape[1] // sources[1].shape[1]
    block = sources[1].shape[0] // blocks
    rows = block // cores
    for index in range(blocks):
        begin = pl.multiple_of(core * rows + index * block, rows)
        lanes = pl.ds(index * sources[1].shape[1], sources[1].shape[1])
        pairs.append((sources[1].at[pl.ds(begin, rows)], half.at[pl.ds(start, rows), lanes]))
    copies = [pltpu.make_async_copy(a, b, sems.at[i]) for i, (a, b) in enumerate(pairs)]
    for copy in copies:
        copy.start()
    for copy in copies:
        copy.wait()


def unpack_kernel(*refs):
    halves, outs = refs[:-2], refs[-2:]
    for step, half in enumerate(halves):
        core = lax.rem(lax.axis_index("pair") + step, len(halves))
        rows = outs[0].shape[0] // len(halves)
        outs[0][pl.ds(pl.multiple_of(core * rows, rows), rows), :] = half[:rows, :]
        start = rows
        blocks = half.shape[1] // outs[1].shape[1]
        block = outs[1].shape[0] // blocks
        rows = block // len(halves)
        for index in range(blocks):
            first = pl.multiple_of(core * rows + index * block, rows)
            lanes = slice(index * outs[1].shape[1], (index + 1) * outs[1].shape[1])
            outs[1][pl.ds(first, rows), :] = half[start : start + rows, lanes]


def pick(options, slot):
    chosen = options[0]
    for index in range(1, len(options)):
        chosen = jnp.where(slot == index, options[index], chosen)
    return chosen


def feature_shares(whole, count):
    share = whole.shape[1] // count
    options = [whole[:, i * share : (i + 1) * share] for i in range(count)]
    return [pick(options, slot_of(step, count)) for step in range(count)]


def compose_kernel(weight, *refs):
    pieces, out = refs[:-1], refs[-1]
    shares = feature_shares(weight[...].astype(F32), len(pieces))
    out[...] = sum(dot(s.astype(BF16), p[...]) for s, p in zip(shares, pieces)).astype(BF16)


def update_kernel(*refs, count):
    mixed, weights = refs[:count], refs[count : 2 * count]
    tokens, query_weight = refs[2 * count : 3 * count], refs[3 * count]
    updated, query = refs[3 * count + 1 :]
    whole = sum(dot(m[...], w[...]) for m, w in zip(mixed, weights))
    pieces = []
    for step, term in enumerate(feature_shares(whole, count)):
        piece = (tokens[step][...].astype(F32) + term).astype(BF16)
        updated[step] = piece
        pieces.append(piece)
    normed = normalized(pieces)
    product = sum(
        dot(normed[step], query_weight[0, slot_of(step, count)]) for step in range(count)
    )
    query[...] = (product * QUERY_SCALE).astype(BF16)


def conv_kernel(window, above, below, weight, out):
    width = out.shape[1]
    band_rows, channels = out.shape[0], out.shape[2]
    grid = jnp.concatenate([above[...], window[...], below[...]], axis=0).astype(F32)
    active = jnp.maximum(grid, 0.0)
    total = grid[1 : 1 + band_rows, EDGE : EDGE + width, :].reshape(band_rows * width, channels)
    for column in range(3):
        first = EDGE - 1 + column
        shifted = active[:, first : first + width, :].astype(BF16)
        for row in range(3):
            rows = shifted[row : row + band_rows].reshape(band_rows * width, channels)
            total = total + dot(rows, weight[row, column])
    out[...] = total.reshape(out.shape).astype(BF16)


def body(left_tokens, right_tokens, self_qkv, self_out, cross_qkv, cross_out, reassemble, taps):
    bands, tiles, cores = (lax.axis_size(axis) for axis in ("blk", "tile", "pair"))
    span = bands // cores
    both = ("blk", "pair")
    rows, share = left_tokens.shape[1:]
    columns = self_qkv.shape[2]
    channels = reassemble.shape[1]
    width = GRID_W // tiles
    band_rows = rows // GRID_W
    heads = columns // HD
    window = (band_rows, width + 2 * EDGE, channels)
    board = (band_rows, GRID_W + 2 * EDGE, channels)

    def home(band, pair):
        return band * cores + pair

    def worker(band, pair):
        part, index = divmod(band, span)
        if part == pair:
            return band * cores + pair
        shift = (pair - part) % cores
        return (pair * span + span - 1 - index) * cores + (pair - shift) % cores

    places = [(band, pair) for band in range(bands) for pair in range(cores)]
    there = [(home(*p), worker(*p)) for p in places]
    back = [(worker(*p), home(*p)) for p in places]
    down = [(worker(b, p), home(b + 1, p)) for b, p in places if b + 1 < bands]
    up = [(worker(b, p), home(b - 1, p)) for b, p in places if b > 0]

    def fetched(value, step):
        def flat(position, tile):
            return (position // cores * tiles + tile) * cores + position % cores

        pairs = [(flat(s, (i + step) % tiles), flat(d, i)) for s, d in there for i in range(tiles)]
        return lax.ppermute(value, ("blk", "tile", "pair"), pairs)

    def tied(values, *others):
        return lax.optimization_barrier((values, others))[0]

    def from_tile(value, step):
        return lax.ppermute(value, "tile", [((i + step) % tiles, i) for i in range(tiles)])

    def tile_pieces(own):
        return [own, *[from_tile(own, s) for s in range(1, tiles)]]

    def neighbours(pack):
        ring = [(g * span, i) for g in range(cores) for i in range(span)]
        return [
            lax.ppermute(pack, "blk", [(g + (i + s) % span, g + i) for g, i in ring])
            for s in range(1, span)
        ]

    def across(pack):
        return [
            lax.ppermute(pack, "pair", [((i + s) % cores, i) for i in range(cores)])
            for s in range(1, cores)
        ]

    def grouped(packs):
        return packs if len(packs) < 5 else [jnp.concatenate(packs)]

    def project(pieces, weights, scaled, first):
        return run_kernel(
            functools.partial(project_kernel, count=tiles, scaled=scaled, first=first),
            "project",
            [((rows, columns), BF16)] * scaled + [((rows, 2 * columns), BF16)],
            [*pieces, weights.reshape(3, tiles, share, columns)],
        )

    def begin(query, packs):
        shapes = [((heads, rows, 2 * HD), F32), ((heads, rows, 1), F32)]
        return run_kernel(begin_kernel, "begin", shapes, [query, *grouped(packs)])

    def staged(weights):
        blocks = weights[0].shape[1] // channels
        height = (weights[0].shape[0] + share // blocks) // cores
        return run_kernel(
            functools.partial(stage_kernel, cores=cores),
            "stage",
            [(w.shape, BF16) for w in weights] + [((height, weights[0].shape[1]), BF16)],
            [pltpu.with_memory_space_constraint(w, pltpu.HBM) for w in weights],
            [pltpu.SemaphoreType.DMA((len(weights) + 1 + blocks,))],
            pl.BlockSpec(memory_space=pl.ANY),
        )

    steps = range(1, tiles)
    left = [fetched(left_tokens[0], step) for step in range(tiles)]
    self_out, reassemble, cross_out, right_own, self_qkv, cross_qkv, taps, half = staged(
        [self_out, reassemble, cross_out, right_tokens[0], self_qkv, cross_qkv, taps]
    )
    right = [right_own, *[from_tile(tied(right_tokens[0], half), s) for s in steps]]
    query, pack = project(left, self_qkv, True, 0)
    (right_pack,) = project(tied(right, pack), cross_qkv, False, 1)
    beside = neighbours(pack)
    near = [pack, *beside]
    far = [q for p in near for q in across(p)]
    state = begin(query, near)
    halves = tile_pieces(tied(half, right_pack))[1:]
    right_pack = lax.ppermute(right_pack, both, there)
    others = [
        run_kernel(
            unpack_kernel,
            "unpack",
            [(w.shape, BF16) for w in (self_out, reassemble)],
            [half, *across(half)],
        )
        for half in halves
    ]
    map_weights = [reassemble, *[other[1] for other in others]]
    (composed,) = run_kernel(
        compose_kernel, "compose", [((columns, channels), BF16)], [cross_out, *map_weights]
    )
    right_pack = tied(right_pack, state, composed)
    far, others, composed, map_weights, right_pack = lax.optimization_barrier(
        (far, others, composed, map_weights, right_pack)
    )
    (mixed,) = run_kernel(
        end_kernel, "end", [((rows, columns), BF16)], [query, *grouped(far), *state]
    )
    right_near = [right_pack, *neighbours(right_pack)]
    mixed = tile_pieces(mixed)
    right_near = tied(right_near, mixed)
    right_far = [q for p in right_near for q in across(p)]
    updated, cross_query = run_kernel(
        functools.partial(update_kernel, count=tiles),
        "update",
        [((tiles, rows, share), BF16), ((rows, columns), BF16)],
        [
            *mixed,
            self_out,
            *[other[0] for other in others],
            *left,
            cross_qkv.reshape(3, tiles, share, columns),
        ],
    )
    maps = run_kernel(
        functools.partial(end_map_kernel, count=tiles),
        "end_map",
        [(window, BF16)] * tiles,
        [cross_query, *grouped([*right_near, *right_far]), composed],
        [pltpu.VMEM(board, F32)],
    )
    (carried,) = run_kernel(
        carry_kernel,
        "carry",
        [(window, F32)],
        [tied(updated, maps), *map_weights],
        [pltpu.VMEM(board, F32)],
    )
    received = [from_tile(part, s) for s, part in enumerate(maps) if s > 0]
    (features,) = run_kernel(add_kernel, "add", [(window, BF16)], [carried, maps[0], *received])
    above = lax.ppermute(features[-1:], both, down)
    below = lax.ppermute(features[:1], both, up)
    features = lax.ppermute(features, both, back)
    (joined,) = run_kernel(
        conv_kernel,
        "join",
        [((band_rows, width, channels), BF16)],
        [features, above, below, taps],
    )
    return joined[None]


def solution(mesh):
    placed = (
        P(("groups", "pair"), "blk", "tile"),
        P(("groups", "pair"), "blk", "tile"),
        P(None, None, "tile"),
        P("tile", None),
        P(None, None, "tile"),
        P("tile", None),
        P("tile", None),
        P(),
    )
    return jax.shard_map(
        body,
        mesh=mesh,
        in_specs=placed,
        out_specs=P(("groups", "pair"), "blk", "tile", None),
        check_vma=False,
    )
```

```python
import functools
import math

import jax
import jax.numpy as jnp
from jax import lax
from jax.experimental import pallas as pl
from jax.experimental.pallas import tpu as pltpu
from jax.sharding import PartitionSpec as P

HD = 64
GRID_W = 128
EDGE = 8
F32 = jnp.float32
BF16 = jnp.bfloat16
QUERY_SCALE = math.log2(math.e) * HD**-0.5
VMEM = pl.BlockSpec(memory_space=pltpu.VMEM)
HBM = pl.BlockSpec(memory_space=pl.ANY)


def run_kernel(kernel, name, shapes, operands, scratch=(), space=VMEM):
    return pl.pallas_call(
        kernel,
        out_shape=[jax.ShapeDtypeStruct(*s) for s in shapes],
        in_specs=[space] * len(operands),
        out_specs=[VMEM] * len(shapes),
        scratch_shapes=scratch,
        compiler_params=pltpu.CompilerParams(vmem_limit_bytes=24 << 20),
        cost_estimate=pl.CostEstimate(flops=0, bytes_accessed=0, transcendentals=0),
        name=name,
    )(*operands)


def slot_of(step, count):
    return lax.rem(lax.axis_index("tile") + step, count)


def normalized(pieces):
    widened = [piece.astype(F32) for piece in pieces]
    width = sum(piece.shape[1] for piece in widened)
    mean = sum(jnp.sum(piece, axis=1, keepdims=True) for piece in widened) / width
    centred = [piece - mean for piece in widened]
    variance = sum(jnp.sum(piece * piece, axis=1, keepdims=True) for piece in centred) / width
    scale = lax.rsqrt(variance + 1e-06)
    return [(piece * scale).astype(BF16) for piece in centred]


def dot(left, right):
    return jnp.dot(left, right, preferred_element_type=F32)


def project_kernel(*refs, count, scaled, first):
    pieces, weight, outs = refs[:count], refs[count], refs[count + 1 :]
    normed = normalized([piece[...] for piece in pieces])
    products = []
    for which in range(first, weight.shape[0]):
        products.append(
            sum(dot(normed[step], weight[which, slot_of(step, count)]) for step in range(count))
        )
    if scaled:
        outs[0][...] = (products.pop(0) * QUERY_SCALE).astype(BF16)
    columns = weight.shape[3]
    for which, product in enumerate(products):
        outs[-1][:, which * columns : (which + 1) * columns] = product.astype(BF16)


def attended(query, packs, index):
    columns = query.shape[1]
    start = index * HD
    head = slice(start, start + HD)
    values = slice(columns + start, columns + start + HD)
    asked = query[:, head]
    scores = [
        lax.dot_general(asked, pack[:, head], (((1,), (1,)), ((), ())), preferred_element_type=F32)
        for pack in packs
    ]
    maxima = functools.reduce(
        jnp.maximum, [jnp.max(score, axis=1, keepdims=True) for score in scores]
    )
    mixed = 0.0
    for score, pack in zip(scores, packs):
        value = pack[:, values]
        widened = jnp.concatenate([value, jnp.ones_like(value)], axis=1)
        mixed = mixed + dot(jnp.exp2(score - maxima).astype(BF16), widened)
    return mixed, maxima


def begin_kernel(query, *refs):
    packs, (mixed_out, maxima_out) = refs[:-2], refs[-2:]
    for index in range(query.shape[1] // HD):
        mixed_out[index], maxima_out[index] = attended(query, packs, index)


def ended(query, packs, state):
    heads = []
    for index in range(query.shape[1] // HD):
        mixed, maxima = attended(query, packs, index)
        if state:
            before = state[1][index]
            highest = jnp.maximum(maxima, before)
            mixed = mixed * jnp.exp2(maxima - highest)
            mixed = mixed + state[0][index] * jnp.exp2(before - highest)
        heads.append(mixed[:, :HD] / mixed[:, HD:])
    return jnp.concatenate(heads, axis=1).astype(BF16)


def end_kernel(query, *refs):
    refs[-1][...] = ended(query, refs[:-3], refs[-3:-1])


def fill_board(board, values):
    band_rows, channels = board.shape[0], board.shape[2]
    edge = jnp.zeros((band_rows, EDGE, channels), board.dtype)
    board[:, :EDGE, :] = edge
    board[:, EDGE + GRID_W :, :] = edge
    inner = values.reshape(band_rows, GRID_W, channels)
    board[:, EDGE : EDGE + GRID_W, :] = inner.astype(board.dtype)


def window_of(board, slot, out):
    width = out.shape[1] - 2 * EDGE
    start = pl.multiple_of(slot * width, width)
    out[...] = board[:, pl.ds(start, out.shape[1]), :].astype(out.dtype)


def end_map_kernel(query, *refs, count):
    composed, outs, board = refs[-2 - count], refs[-1 - count : -1], refs[-1]
    fill_board(board, dot(ended(query, refs[: -2 - count], ()), composed[...]))
    for step, out in enumerate(outs):
        window_of(board, slot_of(count - step, count), out)


def carry_kernel(updated, *refs):
    pieces, out, board = refs[:-2], refs[-2], refs[-1]
    fill_board(board, sum(dot(updated[i], piece[...]) for i, piece in enumerate(pieces)))
    window_of(board, lax.axis_index("tile"), out)


def add_kernel(*refs):
    refs[-1][...] = sum(ref[...].astype(F32) for ref in refs[:-1]).astype(BF16)


def stage_kernel(*refs, cores):
    count = (len(refs) - 2) // 2
    sources, outs, half, sems = refs[:count], refs[count : 2 * count], refs[-2], refs[-1]
    core = lax.axis_index("pair")
    pairs = list(zip(sources, outs))
    rows = sources[0].shape[0] // cores
    begin = pl.multiple_of(core * rows, rows)
    pairs.append((sources[0].at[pl.ds(begin, rows)], half.at[pl.ds(0, rows)]))
    start = rows
    blocks = half.shape[1] // sources[1].shape[1]
    block = sources[1].shape[0] // blocks
    rows = block // cores
    for index in range(blocks):
        begin = pl.multiple_of(core * rows + index * block, rows)
        lanes = pl.ds(index * sources[1].shape[1], sources[1].shape[1])
        pairs.append((sources[1].at[pl.ds(begin, rows)], half.at[pl.ds(start, rows), lanes]))
    copies = [pltpu.make_async_copy(a, b, sems.at[i]) for i, (a, b) in enumerate(pairs)]
    for copy in copies:
        copy.start()
    for copy in copies:
        copy.wait()


def unpack_kernel(*refs):
    halves, outs = refs[:-2], refs[-2:]
    for step, half in enumerate(halves):
        core = lax.rem(lax.axis_index("pair") + step, len(halves))
        rows = outs[0].shape[0] // len(halves)
        outs[0][pl.ds(pl.multiple_of(core * rows, rows), rows), :] = half[:rows, :]
        start = rows
        blocks = half.shape[1] // outs[1].shape[1]
        block = outs[1].shape[0] // blocks
        rows = block // len(halves)
        for index in range(blocks):
            first = pl.multiple_of(core * rows + index * block, rows)
            lanes = slice(index * outs[1].shape[1], (index + 1) * outs[1].shape[1])
            outs[1][pl.ds(first, rows), :] = half[start : start + rows, lanes]


def pick(options, slot):
    chosen = options[0]
    for index in range(1, len(options)):
        chosen = jnp.where(slot == index, options[index], chosen)
    return chosen


def feature_shares(whole, count):
    share = whole.shape[1] // count
    options = [whole[:, i * share : (i + 1) * share] for i in range(count)]
    return [pick(options, slot_of(step, count)) for step in range(count)]


def compose_kernel(weight, *refs):
    pieces, out = refs[:-1], refs[-1]
    shares = feature_shares(weight[...].astype(F32), len(pieces))
    out[...] = sum(dot(s.astype(BF16), p[...]) for s, p in zip(shares, pieces)).astype(BF16)


def update_kernel(*refs, count):
    mixed, weights = refs[:count], refs[count : 2 * count]
    tokens, query_weight = refs[2 * count : 3 * count], refs[3 * count]
    updated, query = refs[3 * count + 1 :]
    whole = sum(dot(m[...], w[...]) for m, w in zip(mixed, weights))
    pieces = []
    for step, term in enumerate(feature_shares(whole, count)):
        piece = (tokens[step][...].astype(F32) + term).astype(BF16)
        updated[step] = piece
        pieces.append(piece)
    normed = normalized(pieces)
    product = sum(
        dot(normed[step], query_weight[0, slot_of(step, count)]) for step in range(count)
    )
    query[...] = (product * QUERY_SCALE).astype(BF16)


def conv_kernel(window, above, below, weight, out):
    width = out.shape[1]
    band_rows, channels = out.shape[0], out.shape[2]
    grid = jnp.concatenate([above[...], window[...], below[:1]], axis=0).astype(F32)
    active = jnp.maximum(grid, 0.0)
    total = grid[1 : 1 + band_rows, EDGE : EDGE + width, :].reshape(band_rows * width, channels)
    for column in range(3):
        first = EDGE - 1 + column
        shifted = active[:, first : first + width, :].astype(BF16)
        for row in range(3):
            rows = shifted[row : row + band_rows].reshape(band_rows * width, channels)
            total = total + dot(rows, weight[row, column])
    out[...] = total.reshape(out.shape).astype(BF16)


def body(left_tokens, right_tokens, self_qkv, self_out, cross_qkv, cross_out, reassemble, taps):
    bands, tiles, cores = (lax.axis_size(axis) for axis in ("blk", "tile", "pair"))
    span = bands // cores
    both = ("blk", "pair")
    rows, share = left_tokens.shape[1:]
    columns = self_qkv.shape[2]
    channels = reassemble.shape[1]
    width = GRID_W // tiles
    band_rows = rows // GRID_W
    heads = columns // HD
    window = (band_rows, width + 2 * EDGE, channels)
    board = (band_rows, GRID_W + 2 * EDGE, channels)

    def home(band, pair):
        return band * cores + pair

    def worker(band, pair):
        part, index = divmod(band, span)
        if part == pair:
            return band * cores + pair
        shift = (pair - part) % cores
        return (pair * span + span - 1 - index) * cores + (pair - shift) % cores

    places = [(band, pair) for band in range(bands) for pair in range(cores)]
    there = [(home(*p), worker(*p)) for p in places]
    back = [(worker(*p), home(*p)) for p in places]
    down = [(worker(b, p), home(b + 1, p)) for b, p in places if b + 1 < bands]
    up = [(worker(b, p), home(b - 1, p)) for b, p in places if b > 0]

    def fetched(value, step):
        def flat(position, tile):
            return (position // cores * tiles + tile) * cores + position % cores

        pairs = [(flat(s, (i + step) % tiles), flat(d, i)) for s, d in there for i in range(tiles)]
        return lax.ppermute(value, ("blk", "tile", "pair"), pairs)

    def tied(values, *others):
        return lax.optimization_barrier((values, others))[0]

    def from_tile(value, step):
        return lax.ppermute(value, "tile", [((i + step) % tiles, i) for i in range(tiles)])

    def tile_pieces(own):
        return [own, *[from_tile(own, s) for s in range(1, tiles)]]

    def neighbours(pack):
        ring = [(g * span, i) for g in range(cores) for i in range(span)]
        return [
            lax.ppermute(pack, "blk", [(g + (i + s) % span, g + i) for g, i in ring])
            for s in range(1, span)
        ]

    def across(pack):
        return [
            lax.ppermute(pack, "pair", [((i + s) % cores, i) for i in range(cores)])
            for s in range(1, cores)
        ]

    def grouped(packs):
        return packs if len(packs) < 5 else [jnp.concatenate(packs)]

    def project(pieces, weights, scaled, first):
        return run_kernel(
            functools.partial(project_kernel, count=tiles, scaled=scaled, first=first),
            "project",
            [((rows, columns), BF16)] * scaled + [((rows, 2 * columns), BF16)],
            [*pieces, weights.reshape(3, tiles, share, columns)],
        )

    def begin(query, packs):
        shapes = [((heads, rows, 2 * HD), F32), ((heads, rows, 1), F32)]
        return run_kernel(begin_kernel, "begin", shapes, [query, *grouped(packs)])

    def staged(weights):
        blocks = weights[0].shape[1] // channels
        height = (weights[0].shape[0] + share // blocks) // cores
        return run_kernel(
            functools.partial(stage_kernel, cores=cores),
            "stage",
            [(w.shape, BF16) for w in weights] + [((height, weights[0].shape[1]), BF16)],
            [pltpu.with_memory_space_constraint(w, pltpu.HBM) for w in weights],
            [pltpu.SemaphoreType.DMA((len(weights) + 1 + blocks,))],
            pl.BlockSpec(memory_space=pl.ANY),
        )

    steps = range(1, tiles)
    left = [fetched(left_tokens[0], step) for step in reversed(range(tiles))][::-1]
    left[0] = tied(left[0], left[1:])
    self_out, reassemble, cross_out, right_own, self_qkv, cross_qkv, taps, half = staged(
        [self_out, reassemble, cross_out, right_tokens[0], self_qkv, cross_qkv, taps]
    )
    right = [right_own, *[from_tile(tied(right_tokens[0], half), s) for s in steps]]
    query, pack = project(left, self_qkv, True, 0)
    (right_pack,) = project(tied(right, pack), cross_qkv, False, 1)
    beside = neighbours(pack)
    near = [pack, *beside]
    far = [q for p in near for q in across(p)]
    state = begin(query, near)
    halves = tile_pieces(tied(half, right_pack))[1:]
    right_pack = lax.ppermute(right_pack, both, there)
    others = [
        run_kernel(
            unpack_kernel,
            "unpack",
            [(w.shape, BF16) for w in (self_out, reassemble)],
            [half, *across(half)],
        )
        for half in halves
    ]
    map_weights = [reassemble, *[other[1] for other in others]]
    (composed,) = run_kernel(
        compose_kernel, "compose", [((columns, channels), BF16)], [cross_out, *map_weights]
    )
    right_pack = tied(right_pack, state, composed)
    far, others, composed, map_weights, right_pack = lax.optimization_barrier(
        (far, others, composed, map_weights, right_pack)
    )
    (mixed,) = run_kernel(
        end_kernel, "end", [((rows, columns), BF16)], [query, *grouped(far), *state]
    )
    right_near = [right_pack, *neighbours(right_pack)]
    mixed = tile_pieces(mixed)
    right_near = tied(right_near, mixed)
    right_far = [q for p in right_near for q in across(p)]
    updated, cross_query = run_kernel(
        functools.partial(update_kernel, count=tiles),
        "update",
        [((tiles, rows, share), BF16), ((rows, columns), BF16)],
        [
            *mixed,
            self_out,
            *[other[0] for other in others],
            *left,
            cross_qkv.reshape(3, tiles, share, columns),
        ],
    )
    maps = run_kernel(
        functools.partial(end_map_kernel, count=tiles),
        "end_map",
        [(window, BF16)] * tiles,
        [cross_query, *grouped([*right_near, *right_far]), composed],
        [pltpu.VMEM(board, F32)],
    )
    (carried,) = run_kernel(
        carry_kernel,
        "carry",
        [(window, F32)],
        [tied(updated, maps), *map_weights],
        [pltpu.VMEM(board, F32)],
    )
    received = [from_tile(part, s) for s, part in enumerate(maps) if s > 0]
    (features,) = run_kernel(add_kernel, "add", [(window, BF16)], [carried, maps[0], *received])
    below = lax.ppermute(features[:2], both, up)
    above = lax.ppermute(features[-1:], both, down)
    features = lax.ppermute(features, both, back)
    (joined,) = run_kernel(
        conv_kernel,
        "join",
        [((band_rows, width, channels), BF16)],
        [features, above, below, taps],
    )
    return joined[None]


def solution(mesh):
    placed = (
        P(("groups", "pair"), "blk", "tile"),
        P(("groups", "pair"), "blk", "tile"),
        P(None, None, "tile"),
        P("tile", None),
        P(None, None, "tile"),
        P("tile", None),
        P("tile", None),
        P(),
    )
    return jax.shard_map(
        body,
        mesh=mesh,
        in_specs=placed,
        out_specs=P(("groups", "pair"), "blk", "tile", None),
        check_vma=False,
    )
```

```python
import functools
import math

import jax
import jax.numpy as jnp
from jax import lax
from jax.experimental import pallas as pl
from jax.experimental.pallas import tpu as pltpu
from jax.sharding import PartitionSpec as P

HD = 64
GRID_W = 128
EDGE = 8
F32 = jnp.float32
BF16 = jnp.bfloat16
QUERY_SCALE = math.log2(math.e) * HD**-0.5
VMEM = pl.BlockSpec(memory_space=pltpu.VMEM)
HBM = pl.BlockSpec(memory_space=pl.ANY)


def run_kernel(kernel, name, shapes, operands, scratch=(), space=VMEM):
    return pl.pallas_call(
        kernel,
        out_shape=[jax.ShapeDtypeStruct(*s) for s in shapes],
        in_specs=[space] * len(operands),
        out_specs=[VMEM] * len(shapes),
        scratch_shapes=scratch,
        compiler_params=pltpu.CompilerParams(vmem_limit_bytes=24 << 20),
        cost_estimate=pl.CostEstimate(flops=0, bytes_accessed=0, transcendentals=0),
        name=name,
    )(*operands)


def slot_of(step, count):
    return lax.rem(lax.axis_index("tile") + step, count)


def normalized(pieces):
    widened = [piece.astype(F32) for piece in pieces]
    width = sum(piece.shape[1] for piece in widened)
    mean = sum(jnp.sum(piece, axis=1, keepdims=True) for piece in widened) / width
    centred = [piece - mean for piece in widened]
    variance = sum(jnp.sum(piece * piece, axis=1, keepdims=True) for piece in centred) / width
    scale = lax.rsqrt(variance + 1e-06)
    return [(piece * scale).astype(BF16) for piece in centred]


def dot(left, right):
    return jnp.dot(left, right, preferred_element_type=F32)


def project_kernel(*refs, count, scaled, first):
    pieces, weight, outs = refs[:count], refs[count], refs[count + 1 :]
    normed = normalized([piece[...] for piece in pieces])
    products = []
    for which in range(first, weight.shape[0]):
        products.append(
            sum(dot(normed[step], weight[which, slot_of(step, count)]) for step in range(count))
        )
    if scaled:
        outs[0][...] = (products.pop(0) * QUERY_SCALE).astype(BF16)
    columns = weight.shape[3]
    for which, product in enumerate(products):
        outs[-1][:, which * columns : (which + 1) * columns] = product.astype(BF16)


def attended(query, packs, index):
    columns = query.shape[1]
    start = index * HD
    head = slice(start, start + HD)
    values = slice(columns + start, columns + start + HD)
    asked = query[:, head]
    scores = [
        lax.dot_general(asked, pack[:, head], (((1,), (1,)), ((), ())), preferred_element_type=F32)
        for pack in packs
    ]
    maxima = functools.reduce(
        jnp.maximum, [jnp.max(score, axis=1, keepdims=True) for score in scores]
    )
    mixed = 0.0
    for score, pack in zip(scores, packs):
        value = pack[:, values]
        widened = jnp.concatenate([value, jnp.ones_like(value)], axis=1)
        mixed = mixed + dot(jnp.exp2(score - maxima).astype(BF16), widened)
    return mixed, maxima


def begin_kernel(query, *refs):
    packs, (mixed_out, maxima_out) = refs[:-2], refs[-2:]
    for index in range(query.shape[1] // HD):
        mixed_out[index], maxima_out[index] = attended(query, packs, index)


def ended(query, packs, state):
    heads = []
    for index in range(query.shape[1] // HD):
        mixed, maxima = attended(query, packs, index)
        if state:
            before = state[1][index]
            highest = jnp.maximum(maxima, before)
            mixed = mixed * jnp.exp2(maxima - highest)
            mixed = mixed + state[0][index] * jnp.exp2(before - highest)
        heads.append(mixed[:, :HD] / mixed[:, HD:])
    return jnp.concatenate(heads, axis=1).astype(BF16)


def end_kernel(query, *refs):
    refs[-1][...] = ended(query, refs[:-3], refs[-3:-1])


def fill_board(board, values):
    band_rows, channels = board.shape[0], board.shape[2]
    edge = jnp.zeros((band_rows, EDGE, channels), board.dtype)
    board[:, :EDGE, :] = edge
    board[:, EDGE + GRID_W :, :] = edge
    inner = values.reshape(band_rows, GRID_W, channels)
    board[:, EDGE : EDGE + GRID_W, :] = inner.astype(board.dtype)


def window_of(board, slot, out):
    width = out.shape[1] - 2 * EDGE
    start = pl.multiple_of(slot * width, width)
    out[...] = board[:, pl.ds(start, out.shape[1]), :].astype(out.dtype)


def end_map_kernel(query, *refs, count):
    composed, outs, board = refs[-2 - count], refs[-1 - count : -1], refs[-1]
    fill_board(board, dot(ended(query, refs[: -2 - count], ()), composed[...]))
    for step, out in enumerate(outs):
        window_of(board, slot_of(count - step, count), out)


def carry_kernel(updated, *refs):
    pieces, out, board = refs[:-2], refs[-2], refs[-1]
    fill_board(board, sum(dot(updated[i], piece[...]) for i, piece in enumerate(pieces)))
    window_of(board, lax.axis_index("tile"), out)


def add_kernel(*refs):
    total = sum(ref[...].astype(F32) for ref in refs[:-2]).astype(BF16)
    refs[-2][...] = total
    refs[-1][...] = jnp.concatenate([total, total[:1]], axis=0)


def stage_kernel(*refs, cores):
    count = (len(refs) - 2) // 2
    sources, outs, half, sems = refs[:count], refs[count : 2 * count], refs[-2], refs[-1]
    core = lax.axis_index("pair")
    pairs = list(zip(sources, outs))
    rows = sources[0].shape[0] // cores
    begin = pl.multiple_of(core * rows, rows)
    pairs.append((sources[0].at[pl.ds(begin, rows)], half.at[pl.ds(0, rows)]))
    start = rows
    blocks = half.shape[1] // sources[1].shape[1]
    block = sources[1].shape[0] // blocks
    rows = block // cores
    for index in range(blocks):
        begin = pl.multiple_of(core * rows + index * block, rows)
        lanes = pl.ds(index * sources[1].shape[1], sources[1].shape[1])
        pairs.append((sources[1].at[pl.ds(begin, rows)], half.at[pl.ds(start, rows), lanes]))
    copies = [pltpu.make_async_copy(a, b, sems.at[i]) for i, (a, b) in enumerate(pairs)]
    for copy in copies:
        copy.start()
    for copy in copies:
        copy.wait()


def unpack_kernel(*refs):
    halves, outs = refs[:-2], refs[-2:]
    for step, half in enumerate(halves):
        core = lax.rem(lax.axis_index("pair") + step, len(halves))
        rows = outs[0].shape[0] // len(halves)
        outs[0][pl.ds(pl.multiple_of(core * rows, rows), rows), :] = half[:rows, :]
        start = rows
        blocks = half.shape[1] // outs[1].shape[1]
        block = outs[1].shape[0] // blocks
        rows = block // len(halves)
        for index in range(blocks):
            first = pl.multiple_of(core * rows + index * block, rows)
            lanes = slice(index * outs[1].shape[1], (index + 1) * outs[1].shape[1])
            outs[1][pl.ds(first, rows), :] = half[start : start + rows, lanes]


def pick(options, slot):
    chosen = options[0]
    for index in range(1, len(options)):
        chosen = jnp.where(slot == index, options[index], chosen)
    return chosen


def feature_shares(whole, count):
    share = whole.shape[1] // count
    options = [whole[:, i * share : (i + 1) * share] for i in range(count)]
    return [pick(options, slot_of(step, count)) for step in range(count)]


def compose_kernel(weight, *refs):
    pieces, out = refs[:-1], refs[-1]
    shares = feature_shares(weight[...].astype(F32), len(pieces))
    out[...] = sum(dot(s.astype(BF16), p[...]) for s, p in zip(shares, pieces)).astype(BF16)


def update_kernel(*refs, count):
    mixed, weights = refs[:count], refs[count : 2 * count]
    tokens, query_weight = refs[2 * count : 3 * count], refs[3 * count]
    updated, query = refs[3 * count + 1 :]
    whole = sum(dot(m[...], w[...]) for m, w in zip(mixed, weights))
    pieces = []
    for step, term in enumerate(feature_shares(whole, count)):
        piece = (tokens[step][...].astype(F32) + term).astype(BF16)
        updated[step] = piece
        pieces.append(piece)
    normed = normalized(pieces)
    product = sum(
        dot(normed[step], query_weight[0, slot_of(step, count)]) for step in range(count)
    )
    query[...] = (product * QUERY_SCALE).astype(BF16)


def conv_kernel(window, above, below, weight, out):
    width = out.shape[1]
    band_rows, channels = out.shape[0], out.shape[2]
    grid = jnp.concatenate([above[...], window[...], below[:1]], axis=0).astype(F32)
    active = jnp.maximum(grid, 0.0)
    total = grid[1 : 1 + band_rows, EDGE : EDGE + width, :].reshape(band_rows * width, channels)
    for column in range(3):
        first = EDGE - 1 + column
        shifted = active[:, first : first + width, :].astype(BF16)
        for row in range(3):
            rows = shifted[row : row + band_rows].reshape(band_rows * width, channels)
            total = total + dot(rows, weight[row, column])
    out[...] = total.reshape(out.shape).astype(BF16)


def body(left_tokens, right_tokens, self_qkv, self_out, cross_qkv, cross_out, reassemble, taps):
    bands, tiles, cores = (lax.axis_size(axis) for axis in ("blk", "tile", "pair"))
    span = bands // cores
    both = ("blk", "pair")
    rows, share = left_tokens.shape[1:]
    columns = self_qkv.shape[2]
    channels = reassemble.shape[1]
    width = GRID_W // tiles
    band_rows = rows // GRID_W
    heads = columns // HD
    window = (band_rows, width + 2 * EDGE, channels)
    board = (band_rows, GRID_W + 2 * EDGE, channels)

    def home(band, pair):
        return band * cores + pair

    def worker(band, pair):
        part, index = divmod(band, span)
        if part == pair:
            return band * cores + pair
        shift = (pair - part) % cores
        return (pair * span + span - 1 - index) * cores + (pair - shift) % cores

    places = [(band, pair) for band in range(bands) for pair in range(cores)]
    there = [(home(*p), worker(*p)) for p in places]
    back = [(worker(*p), home(*p)) for p in places]
    down = [(worker(b, p), home(b + 1, p)) for b, p in places if b + 1 < bands]
    up = [(worker(b, p), home(b - 1, p)) for b, p in places if b > 0]

    def fetched(value, step):
        def flat(position, tile):
            return (position // cores * tiles + tile) * cores + position % cores

        pairs = [(flat(s, (i + step) % tiles), flat(d, i)) for s, d in there for i in range(tiles)]
        return lax.ppermute(value, ("blk", "tile", "pair"), pairs)

    def tied(values, *others):
        return lax.optimization_barrier((values, others))[0]

    def from_tile(value, step):
        return lax.ppermute(value, "tile", [((i + step) % tiles, i) for i in range(tiles)])

    def tile_pieces(own):
        return [own, *[from_tile(own, s) for s in range(1, tiles)]]

    def neighbours(pack):
        ring = [(g * span, i) for g in range(cores) for i in range(span)]
        return [
            lax.ppermute(pack, "blk", [(g + (i + s) % span, g + i) for g, i in ring])
            for s in range(1, span)
        ]

    def across(pack):
        return [
            lax.ppermute(pack, "pair", [((i + s) % cores, i) for i in range(cores)])
            for s in range(1, cores)
        ]

    def grouped(packs):
        return packs if len(packs) < 5 else [jnp.concatenate(packs)]

    def project(pieces, weights, scaled, first):
        return run_kernel(
            functools.partial(project_kernel, count=tiles, scaled=scaled, first=first),
            "project",
            [((rows, columns), BF16)] * scaled + [((rows, 2 * columns), BF16)],
            [*pieces, weights.reshape(3, tiles, share, columns)],
        )

    def begin(query, packs):
        shapes = [((heads, rows, 2 * HD), F32), ((heads, rows, 1), F32)]
        return run_kernel(begin_kernel, "begin", shapes, [query, *grouped(packs)])

    def staged(weights):
        blocks = weights[0].shape[1] // channels
        height = (weights[0].shape[0] + share // blocks) // cores
        return run_kernel(
            functools.partial(stage_kernel, cores=cores),
            "stage",
            [(w.shape, BF16) for w in weights] + [((height, weights[0].shape[1]), BF16)],
            [pltpu.with_memory_space_constraint(w, pltpu.HBM) for w in weights],
            [pltpu.SemaphoreType.DMA((len(weights) + 1 + blocks,))],
            pl.BlockSpec(memory_space=pl.ANY),
        )

    steps = range(1, tiles)
    left = [fetched(left_tokens[0], step) for step in reversed(range(tiles))][::-1]
    left[0] = tied(left[0], left[1:])
    self_out, reassemble, cross_out, right_own, self_qkv, cross_qkv, taps, half = staged(
        [self_out, reassemble, cross_out, right_tokens[0], self_qkv, cross_qkv, taps]
    )
    right = [right_own, *[from_tile(tied(right_tokens[0], half), s) for s in steps]]
    query, pack = project(left, self_qkv, True, 0)
    (right_pack,) = project(tied(right, pack), cross_qkv, False, 1)
    beside = neighbours(pack)
    near = [pack, *beside]
    far = [q for p in near for q in across(p)]
    state = begin(query, near)
    halves = tile_pieces(tied(half, right_pack))[1:]
    right_pack = lax.ppermute(right_pack, both, there)
    others = [
        run_kernel(
            unpack_kernel,
            "unpack",
            [(w.shape, BF16) for w in (self_out, reassemble)],
            [half, *across(half)],
        )
        for half in halves
    ]
    map_weights = [reassemble, *[other[1] for other in others]]
    (composed,) = run_kernel(
        compose_kernel, "compose", [((columns, channels), BF16)], [cross_out, *map_weights]
    )
    right_pack = tied(right_pack, state, composed)
    far, others, composed, map_weights, right_pack = lax.optimization_barrier(
        (far, others, composed, map_weights, right_pack)
    )
    (mixed,) = run_kernel(
        end_kernel, "end", [((rows, columns), BF16)], [query, *grouped(far), *state]
    )
    right_near = [right_pack, *neighbours(right_pack)]
    mixed = tile_pieces(mixed)
    right_near = tied(right_near, mixed)
    right_far = [q for p in right_near for q in across(p)]
    updated, cross_query = run_kernel(
        functools.partial(update_kernel, count=tiles),
        "update",
        [((tiles, rows, share), BF16), ((rows, columns), BF16)],
        [
            *mixed,
            self_out,
            *[other[0] for other in others],
            *left,
            cross_qkv.reshape(3, tiles, share, columns),
        ],
    )
    maps = run_kernel(
        functools.partial(end_map_kernel, count=tiles),
        "end_map",
        [(window, BF16)] * tiles,
        [cross_query, *grouped([*right_near, *right_far]), composed],
        [pltpu.VMEM(board, F32)],
    )
    (carried,) = run_kernel(
        carry_kernel,
        "carry",
        [(window, F32)],
        [tied(updated, maps), *map_weights],
        [pltpu.VMEM(board, F32)],
    )
    received = [from_tile(part, s) for s, part in enumerate(maps) if s > 0]
    longer = (window[0] + 1, *window[1:])
    features, raised = run_kernel(
        add_kernel, "add", [(window, BF16), (longer, BF16)], [carried, maps[0], *received]
    )
    below = lax.ppermute(raised, both, up)
    above = lax.ppermute(features[-1:], both, down)
    features = lax.ppermute(features, both, back)
    (joined,) = run_kernel(
        conv_kernel,
        "join",
        [((band_rows, width, channels), BF16)],
        [features, above, below, taps],
    )
    return joined[None]


def solution(mesh):
    placed = (
        P(("groups", "pair"), "blk", "tile"),
        P(("groups", "pair"), "blk", "tile"),
        P(None, None, "tile"),
        P("tile", None),
        P(None, None, "tile"),
        P("tile", None),
        P("tile", None),
        P(),
    )
    return jax.shard_map(
        body,
        mesh=mesh,
        in_specs=placed,
        out_specs=P(("groups", "pair"), "blk", "tile", None),
        check_vma=False,
    )
```

```python
import functools
import math

import jax
import jax.numpy as jnp
from jax import lax
from jax.experimental import pallas as pl
from jax.experimental.pallas import tpu as pltpu
from jax.sharding import PartitionSpec as P

HD = 64
GRID_W = 128
EDGE = 8
F32 = jnp.float32
BF16 = jnp.bfloat16
QUERY_SCALE = math.log2(math.e) * HD**-0.5
VMEM = pl.BlockSpec(memory_space=pltpu.VMEM)
HBM = pl.BlockSpec(memory_space=pl.ANY)


def run_kernel(kernel, name, shapes, operands, scratch=(), space=VMEM):
    return pl.pallas_call(
        kernel,
        out_shape=[jax.ShapeDtypeStruct(*s) for s in shapes],
        in_specs=[space] * len(operands),
        out_specs=[VMEM] * len(shapes),
        scratch_shapes=scratch,
        compiler_params=pltpu.CompilerParams(vmem_limit_bytes=24 << 20),
        cost_estimate=pl.CostEstimate(flops=0, bytes_accessed=0, transcendentals=0),
        name=name,
    )(*operands)


def slot_of(step, count):
    return lax.rem(lax.axis_index("tile") + step, count)


def normalized(pieces):
    widened = [piece.astype(F32) for piece in pieces]
    width = sum(piece.shape[1] for piece in widened)
    mean = sum(jnp.sum(piece, axis=1, keepdims=True) for piece in widened) / width
    centred = [piece - mean for piece in widened]
    variance = sum(jnp.sum(piece * piece, axis=1, keepdims=True) for piece in centred) / width
    scale = lax.rsqrt(variance + 1e-06)
    return [(piece * scale).astype(BF16) for piece in centred]


def dot(left, right):
    return jnp.dot(left, right, preferred_element_type=F32)


def project_kernel(*refs, count, scaled, first):
    pieces, weight, outs = refs[:count], refs[count], refs[count + 1 :]
    normed = normalized([piece[...] for piece in pieces])
    products = []
    for which in range(first, weight.shape[0]):
        products.append(
            sum(dot(normed[step], weight[which, slot_of(step, count)]) for step in range(count))
        )
    if scaled:
        outs[0][...] = (products.pop(0) * QUERY_SCALE).astype(BF16)
    columns = weight.shape[3]
    for which, product in enumerate(products):
        outs[-1][:, which * columns : (which + 1) * columns] = product.astype(BF16)


def attended(query, packs, index):
    columns = query.shape[1]
    start = index * HD
    head = slice(start, start + HD)
    values = slice(columns + start, columns + start + HD)
    asked = query[:, head]
    scores = [
        lax.dot_general(asked, pack[:, head], (((1,), (1,)), ((), ())), preferred_element_type=F32)
        for pack in packs
    ]
    maxima = functools.reduce(
        jnp.maximum, [jnp.max(score, axis=1, keepdims=True) for score in scores]
    )
    mixed = 0.0
    for score, pack in zip(scores, packs):
        value = pack[:, values]
        widened = jnp.concatenate([value, jnp.ones_like(value)], axis=1)
        mixed = mixed + dot(jnp.exp2(score - maxima).astype(BF16), widened)
    return mixed, maxima


def begin_kernel(query, *refs):
    packs, (mixed_out, maxima_out) = refs[:-2], refs[-2:]
    for index in range(query.shape[1] // HD):
        mixed_out[index], maxima_out[index] = attended(query, packs, index)


def ended(query, packs, state):
    heads = []
    for index in range(query.shape[1] // HD):
        mixed, maxima = attended(query, packs, index)
        if state:
            before = state[1][index]
            highest = jnp.maximum(maxima, before)
            mixed = mixed * jnp.exp2(maxima - highest)
            mixed = mixed + state[0][index] * jnp.exp2(before - highest)
        heads.append(mixed[:, :HD] / mixed[:, HD:])
    return jnp.concatenate(heads, axis=1).astype(BF16)


def end_kernel(query, *refs):
    refs[-1][...] = ended(query, refs[:-3], refs[-3:-1])


def fill_board(board, values):
    band_rows, channels = board.shape[0], board.shape[2]
    edge = jnp.zeros((band_rows, EDGE, channels), board.dtype)
    board[:, :EDGE, :] = edge
    board[:, EDGE + GRID_W :, :] = edge
    inner = values.reshape(band_rows, GRID_W, channels)
    board[:, EDGE : EDGE + GRID_W, :] = inner.astype(board.dtype)


def window_of(board, slot, out):
    width = out.shape[1] - 2 * EDGE
    start = pl.multiple_of(slot * width, width)
    out[...] = board[:, pl.ds(start, out.shape[1]), :].astype(out.dtype)


def end_map_kernel(query, *refs, count):
    composed, outs, board = refs[-2 - count], refs[-1 - count : -1], refs[-1]
    fill_board(board, dot(ended(query, refs[: -2 - count], ()), composed[...]))
    for step, out in enumerate(outs):
        window_of(board, slot_of(count - step, count), out)


def carry_kernel(updated, *refs):
    pieces, out, board = refs[:-2], refs[-2], refs[-1]
    fill_board(board, sum(dot(updated[i], piece[...]) for i, piece in enumerate(pieces)))
    window_of(board, lax.axis_index("tile"), out)


def add_kernel(*refs):
    total = sum(ref[...].astype(F32) for ref in refs[:-2]).astype(BF16)
    refs[-2][...] = total
    refs[-1][...] = jnp.concatenate([total, total[:1]], axis=0)


def stage_kernel(*refs, cores):
    count = (len(refs) - 2) // 2
    sources, outs, half, sems = refs[:count], refs[count : 2 * count], refs[-2], refs[-1]
    core = lax.axis_index("pair")
    pairs = list(zip(sources, outs))
    rows = sources[0].shape[0] // cores
    begin = pl.multiple_of(core * rows, rows)
    pairs.append((sources[0].at[pl.ds(begin, rows)], half.at[pl.ds(0, rows)]))
    start = rows
    blocks = half.shape[1] // sources[1].shape[1]
    block = sources[1].shape[0] // blocks
    rows = block // cores
    for index in range(blocks):
        begin = pl.multiple_of(core * rows + index * block, rows)
        lanes = pl.ds(index * sources[1].shape[1], sources[1].shape[1])
        pairs.append((sources[1].at[pl.ds(begin, rows)], half.at[pl.ds(start, rows), lanes]))
    copies = [pltpu.make_async_copy(a, b, sems.at[i]) for i, (a, b) in enumerate(pairs)]
    for copy in copies:
        copy.start()
    for copy in copies:
        copy.wait()


def unpack_kernel(*refs):
    halves, outs = refs[:-2], refs[-2:]
    for step, half in enumerate(halves):
        core = lax.rem(lax.axis_index("pair") + step, len(halves))
        rows = outs[0].shape[0] // len(halves)
        outs[0][pl.ds(pl.multiple_of(core * rows, rows), rows), :] = half[:rows, :]
        start = rows
        blocks = half.shape[1] // outs[1].shape[1]
        block = outs[1].shape[0] // blocks
        rows = block // len(halves)
        for index in range(blocks):
            first = pl.multiple_of(core * rows + index * block, rows)
            lanes = slice(index * outs[1].shape[1], (index + 1) * outs[1].shape[1])
            outs[1][pl.ds(first, rows), :] = half[start : start + rows, lanes]


def pick(options, slot):
    chosen = options[0]
    for index in range(1, len(options)):
        chosen = jnp.where(slot == index, options[index], chosen)
    return chosen


def feature_shares(whole, count):
    share = whole.shape[1] // count
    options = [whole[:, i * share : (i + 1) * share] for i in range(count)]
    return [pick(options, slot_of(step, count)) for step in range(count)]


def compose_kernel(weight, *refs):
    pieces, out = refs[:-1], refs[-1]
    shares = feature_shares(weight[...].astype(F32), len(pieces))
    out[...] = sum(dot(s.astype(BF16), p[...]) for s, p in zip(shares, pieces)).astype(BF16)


def update_kernel(*refs, count):
    mixed, weights = refs[:count], refs[count : 2 * count]
    tokens, query_weight = refs[2 * count : 3 * count], refs[3 * count]
    updated, query = refs[3 * count + 1 :]
    whole = sum(dot(m[...], w[...]) for m, w in zip(mixed, weights))
    pieces = []
    for step, term in enumerate(feature_shares(whole, count)):
        piece = (tokens[step][...].astype(F32) + term).astype(BF16)
        updated[step] = piece
        pieces.append(piece)
    normed = normalized(pieces)
    product = sum(
        dot(normed[step], query_weight[0, slot_of(step, count)]) for step in range(count)
    )
    query[...] = (product * QUERY_SCALE).astype(BF16)


def conv_kernel(window, above, below, weight, out):
    width = out.shape[1]
    band_rows, channels = out.shape[0], out.shape[2]
    grid = jnp.concatenate([above[...], window[...], below[:1]], axis=0).astype(F32)
    active = jnp.maximum(grid, 0.0)
    total = grid[1 : 1 + band_rows, EDGE : EDGE + width, :].reshape(band_rows * width, channels)
    for column in range(3):
        first = EDGE - 1 + column
        shifted = active[:, first : first + width, :].astype(BF16)
        for row in range(3):
            rows = shifted[row : row + band_rows].reshape(band_rows * width, channels)
            total = total + dot(rows, weight[row, column])
    out[...] = total.reshape(out.shape).astype(BF16)


def body(left_tokens, right_tokens, self_qkv, self_out, cross_qkv, cross_out, reassemble, taps):
    bands, tiles, cores = (lax.axis_size(axis) for axis in ("blk", "tile", "pair"))
    span = bands // cores
    both = ("blk", "pair")
    rows, share = left_tokens.shape[1:]
    columns = self_qkv.shape[2]
    channels = reassemble.shape[1]
    width = GRID_W // tiles
    band_rows = rows // GRID_W
    heads = columns // HD
    window = (band_rows, width + 2 * EDGE, channels)
    board = (band_rows, GRID_W + 2 * EDGE, channels)

    def home(band, pair):
        return band * cores + pair

    def worker(band, pair):
        part, index = divmod(band, span)
        if part == pair:
            return band * cores + pair
        shift = (pair - part) % cores
        return (pair * span + span - 1 - index) * cores + (pair - shift) % cores

    places = [(band, pair) for band in range(bands) for pair in range(cores)]
    there = [(home(*p), worker(*p)) for p in places]
    back = [(worker(*p), home(*p)) for p in places]
    down = [(worker(b, p), home(b + 1, p)) for b, p in places if b + 1 < bands]
    up = [(worker(b, p), home(b - 1, p)) for b, p in places if b > 0]

    def fetched(value, step):
        def flat(position, tile):
            return (position // cores * tiles + tile) * cores + position % cores

        pairs = [(flat(s, (i + step) % tiles), flat(d, i)) for s, d in there for i in range(tiles)]
        return lax.ppermute(value, ("blk", "tile", "pair"), pairs)

    def tied(values, *others):
        return lax.optimization_barrier((values, others))[0]

    def from_tile(value, step):
        return lax.ppermute(value, "tile", [((i + step) % tiles, i) for i in range(tiles)])

    def tile_pieces(own):
        return [own, *[from_tile(own, s) for s in range(1, tiles)]]

    def neighbours(pack):
        ring = [(g * span, i) for g in range(cores) for i in range(span)]
        return [
            lax.ppermute(pack, "blk", [(g + (i + s) % span, g + i) for g, i in ring])
            for s in range(1, span)
        ]

    def across(pack):
        return [
            lax.ppermute(pack, "pair", [((i + s) % cores, i) for i in range(cores)])
            for s in range(1, cores)
        ]

    def grouped(packs):
        return packs if len(packs) < 5 else [jnp.concatenate(packs)]

    def project(pieces, weights, scaled, first):
        return run_kernel(
            functools.partial(project_kernel, count=tiles, scaled=scaled, first=first),
            "project",
            [((rows, columns), BF16)] * scaled + [((rows, 2 * columns), BF16)],
            [*pieces, weights.reshape(3, tiles, share, columns)],
        )

    def begin(query, packs):
        shapes = [((heads, rows, 2 * HD), F32), ((heads, rows, 1), F32)]
        return run_kernel(begin_kernel, "begin", shapes, [query, *grouped(packs)])

    def staged(weights):
        blocks = weights[0].shape[1] // channels
        height = (weights[0].shape[0] + share // blocks) // cores
        return run_kernel(
            functools.partial(stage_kernel, cores=cores),
            "stage",
            [(w.shape, BF16) for w in weights] + [((height, weights[0].shape[1]), BF16)],
            [pltpu.with_memory_space_constraint(w, pltpu.HBM) for w in weights],
            [pltpu.SemaphoreType.DMA((len(weights) + 1 + blocks,))],
            pl.BlockSpec(memory_space=pl.ANY),
        )

    steps = range(1, tiles)
    left = [fetched(left_tokens[0], step) for step in reversed(range(tiles))][::-1]
    left[0] = tied(left[0], left[1:])
    self_out, reassemble, cross_out, right_own, self_qkv, cross_qkv, taps, half = staged(
        [self_out, reassemble, cross_out, right_tokens[0], self_qkv, cross_qkv, taps]
    )
    right = [right_own, *[from_tile(tied(right_tokens[0], half), s) for s in steps]]
    query, pack = project(left, self_qkv, True, 0)
    (right_pack,) = project(tied(right, pack), cross_qkv, False, 1)
    beside = neighbours(pack)
    near = [pack, *beside, *across(pack)]
    far = [q for p in beside for q in across(p)]
    state = begin(query, near)
    halves = tile_pieces(tied(half, right_pack))[1:]
    right_pack = lax.ppermute(right_pack, both, there)
    others = [
        run_kernel(
            unpack_kernel,
            "unpack",
            [(w.shape, BF16) for w in (self_out, reassemble)],
            [half, *across(half)],
        )
        for half in halves
    ]
    map_weights = [reassemble, *[other[1] for other in others]]
    (composed,) = run_kernel(
        compose_kernel, "compose", [((columns, channels), BF16)], [cross_out, *map_weights]
    )
    right_pack = tied(right_pack, state, composed)
    far, others, composed, map_weights, right_pack = lax.optimization_barrier(
        (far, others, composed, map_weights, right_pack)
    )
    (mixed,) = run_kernel(
        end_kernel, "end", [((rows, columns), BF16)], [query, *grouped(far), *state]
    )
    right_near = [right_pack, *neighbours(right_pack)]
    mixed = tile_pieces(mixed)
    right_near = tied(right_near, mixed)
    right_far = [q for p in right_near for q in across(p)]
    updated, cross_query = run_kernel(
        functools.partial(update_kernel, count=tiles),
        "update",
        [((tiles, rows, share), BF16), ((rows, columns), BF16)],
        [
            *mixed,
            self_out,
            *[other[0] for other in others],
            *left,
            cross_qkv.reshape(3, tiles, share, columns),
        ],
    )
    maps = run_kernel(
        functools.partial(end_map_kernel, count=tiles),
        "end_map",
        [(window, BF16)] * tiles,
        [cross_query, *grouped([*right_near, *right_far]), composed],
        [pltpu.VMEM(board, F32)],
    )
    (carried,) = run_kernel(
        carry_kernel,
        "carry",
        [(window, F32)],
        [tied(updated, maps), *map_weights],
        [pltpu.VMEM(board, F32)],
    )
    received = [from_tile(part, s) for s, part in enumerate(maps) if s > 0]
    longer = (window[0] + 1, *window[1:])
    features, raised = run_kernel(
        add_kernel, "add", [(window, BF16), (longer, BF16)], [carried, maps[0], *received]
    )
    below = lax.ppermute(raised, both, up)
    above = lax.ppermute(features[-1:], both, down)
    features = lax.ppermute(features, both, back)
    (joined,) = run_kernel(
        conv_kernel,
        "join",
        [((band_rows, width, channels), BF16)],
        [features, above, below, taps],
    )
    return joined[None]


def solution(mesh):
    placed = (
        P(("groups", "pair"), "blk", "tile"),
        P(("groups", "pair"), "blk", "tile"),
        P(None, None, "tile"),
        P("tile", None),
        P(None, None, "tile"),
        P("tile", None),
        P("tile", None),
        P(),
    )
    return jax.shard_map(
        body,
        mesh=mesh,
        in_specs=placed,
        out_specs=P(("groups", "pair"), "blk", "tile", None),
        check_vma=False,
    )
```

```python
import functools
import math

import jax
import jax.numpy as jnp
from jax import lax
from jax.experimental import pallas as pl
from jax.experimental.pallas import tpu as pltpu
from jax.sharding import PartitionSpec as P

HD = 64
GRID_W = 128
EDGE = 8
F32 = jnp.float32
BF16 = jnp.bfloat16
QUERY_SCALE = math.log2(math.e) * HD**-0.5
VMEM = pl.BlockSpec(memory_space=pltpu.VMEM)
HBM = pl.BlockSpec(memory_space=pl.ANY)


def run_kernel(kernel, name, shapes, operands, scratch=(), space=VMEM):
    return pl.pallas_call(
        kernel,
        out_shape=[jax.ShapeDtypeStruct(*s) for s in shapes],
        in_specs=[space] * len(operands),
        out_specs=[VMEM] * len(shapes),
        scratch_shapes=scratch,
        compiler_params=pltpu.CompilerParams(vmem_limit_bytes=24 << 20),
        cost_estimate=pl.CostEstimate(flops=0, bytes_accessed=0, transcendentals=0),
        name=name,
    )(*operands)


def slot_of(step, count):
    return lax.rem(lax.axis_index("tile") + step, count)


def normalized(pieces):
    widened = [piece.astype(F32) for piece in pieces]
    width = sum(piece.shape[1] for piece in widened)
    mean = sum(jnp.sum(piece, axis=1, keepdims=True) for piece in widened) / width
    centred = [piece - mean for piece in widened]
    variance = sum(jnp.sum(piece * piece, axis=1, keepdims=True) for piece in centred) / width
    scale = lax.rsqrt(variance + 1e-06)
    return [(piece * scale).astype(BF16) for piece in centred]


def dot(left, right):
    return jnp.dot(left, right, preferred_element_type=F32)


def project_kernel(*refs, count, scaled, first):
    pieces, weight, outs = refs[:count], refs[count], refs[count + 1 :]
    normed = normalized([piece[...] for piece in pieces])
    products = []
    for which in range(first, weight.shape[0]):
        products.append(
            sum(dot(normed[step], weight[which, slot_of(step, count)]) for step in range(count))
        )
    if scaled:
        outs[0][...] = (products.pop(0) * QUERY_SCALE).astype(BF16)
    columns = weight.shape[3]
    for which, product in enumerate(products):
        outs[-1][:, which * columns : (which + 1) * columns] = product.astype(BF16)


def attended(query, packs, index):
    columns = query.shape[1]
    start = index * HD
    head = slice(start, start + HD)
    values = slice(columns + start, columns + start + HD)
    asked = query[:, head]
    scores = [
        lax.dot_general(asked, pack[:, head], (((1,), (1,)), ((), ())), preferred_element_type=F32)
        for pack in packs
    ]
    maxima = functools.reduce(
        jnp.maximum, [jnp.max(score, axis=1, keepdims=True) for score in scores]
    )
    mixed = 0.0
    for score, pack in zip(scores, packs):
        value = pack[:, values]
        widened = jnp.concatenate([value, jnp.ones_like(value)], axis=1)
        mixed = mixed + dot(jnp.exp2(score - maxima).astype(BF16), widened)
    return mixed, maxima


def begin_kernel(query, *refs):
    packs, (mixed_out, maxima_out) = refs[:-2], refs[-2:]
    for index in range(query.shape[1] // HD):
        mixed_out[index], maxima_out[index] = attended(query, packs, index)


def ended(query, packs, state):
    heads = []
    for index in range(query.shape[1] // HD):
        mixed, maxima = attended(query, packs, index)
        if state:
            before = state[1][index]
            highest = jnp.maximum(maxima, before)
            mixed = mixed * jnp.exp2(maxima - highest)
            mixed = mixed + state[0][index] * jnp.exp2(before - highest)
        heads.append(mixed[:, :HD] / mixed[:, HD:])
    return jnp.concatenate(heads, axis=1).astype(BF16)


def end_kernel(query, *refs):
    refs[-1][...] = ended(query, refs[:-3], refs[-3:-1])


def fill_board(board, values):
    band_rows, channels = board.shape[0], board.shape[2]
    edge = jnp.zeros((band_rows, EDGE, channels), board.dtype)
    board[:, :EDGE, :] = edge
    board[:, EDGE + GRID_W :, :] = edge
    inner = values.reshape(band_rows, GRID_W, channels)
    board[:, EDGE : EDGE + GRID_W, :] = inner.astype(board.dtype)


def window_of(board, slot, out):
    width = out.shape[1] - 2 * EDGE
    start = pl.multiple_of(slot * width, width)
    out[...] = board[:, pl.ds(start, out.shape[1]), :].astype(out.dtype)


def end_map_kernel(query, *refs, count):
    composed, outs, board = refs[-2 - count], refs[-1 - count : -1], refs[-1]
    fill_board(board, dot(ended(query, refs[: -2 - count], ()), composed[...]))
    for step, out in enumerate(outs):
        window_of(board, slot_of(count - step, count), out)


def carry_kernel(updated, *refs):
    pieces, out, board = refs[:-2], refs[-2], refs[-1]
    fill_board(board, sum(dot(updated[i], piece[...]) for i, piece in enumerate(pieces)))
    window_of(board, lax.axis_index("tile"), out)


def add_kernel(*refs):
    total = sum(ref[...].astype(F32) for ref in refs[:-2]).astype(BF16)
    refs[-2][...] = total
    refs[-1][...] = jnp.concatenate([total, total[:1]], axis=0)


def stage_kernel(*refs, cores):
    count = (len(refs) - 2) // 2
    sources, outs, half, sems = refs[:count], refs[count : 2 * count], refs[-2], refs[-1]
    core = lax.axis_index("pair")
    pairs = list(zip(sources, outs))
    rows = sources[0].shape[0] // cores
    begin = pl.multiple_of(core * rows, rows)
    pairs.append((sources[0].at[pl.ds(begin, rows)], half.at[pl.ds(0, rows)]))
    start = rows
    blocks = half.shape[1] // sources[1].shape[1]
    block = sources[1].shape[0] // blocks
    rows = block // cores
    for index in range(blocks):
        begin = pl.multiple_of(core * rows + index * block, rows)
        lanes = pl.ds(index * sources[1].shape[1], sources[1].shape[1])
        pairs.append((sources[1].at[pl.ds(begin, rows)], half.at[pl.ds(start, rows), lanes]))
    copies = [pltpu.make_async_copy(a, b, sems.at[i]) for i, (a, b) in enumerate(pairs)]
    for copy in copies:
        copy.start()
    for copy in copies:
        copy.wait()


def unpack_kernel(*refs):
    halves, outs = refs[:-2], refs[-2:]
    for step, half in enumerate(halves):
        core = lax.rem(lax.axis_index("pair") + step, len(halves))
        rows = outs[0].shape[0] // len(halves)
        outs[0][pl.ds(pl.multiple_of(core * rows, rows), rows), :] = half[:rows, :]
        start = rows
        blocks = half.shape[1] // outs[1].shape[1]
        block = outs[1].shape[0] // blocks
        rows = block // len(halves)
        for index in range(blocks):
            first = pl.multiple_of(core * rows + index * block, rows)
            lanes = slice(index * outs[1].shape[1], (index + 1) * outs[1].shape[1])
            outs[1][pl.ds(first, rows), :] = half[start : start + rows, lanes]


def pick(options, slot):
    chosen = options[0]
    for index in range(1, len(options)):
        chosen = jnp.where(slot == index, options[index], chosen)
    return chosen


def feature_shares(whole, count):
    share = whole.shape[1] // count
    options = [whole[:, i * share : (i + 1) * share] for i in range(count)]
    return [pick(options, slot_of(step, count)) for step in range(count)]


def compose_kernel(weight, *refs):
    pieces, out = refs[:-1], refs[-1]
    shares = feature_shares(weight[...].astype(F32), len(pieces))
    out[...] = sum(dot(s.astype(BF16), p[...]) for s, p in zip(shares, pieces)).astype(BF16)


def update_kernel(*refs, count):
    mixed, weights = refs[:count], refs[count : 2 * count]
    tokens, query_weight = refs[2 * count : 3 * count], refs[3 * count]
    updated, query = refs[3 * count + 1 :]
    whole = sum(dot(m[...], w[...]) for m, w in zip(mixed, weights))
    pieces = []
    for step, term in enumerate(feature_shares(whole, count)):
        piece = (tokens[step][...].astype(F32) + term).astype(BF16)
        updated[step] = piece
        pieces.append(piece)
    normed = normalized(pieces)
    product = sum(
        dot(normed[step], query_weight[0, slot_of(step, count)]) for step in range(count)
    )
    query[...] = (product * QUERY_SCALE).astype(BF16)


def conv_kernel(window, above, below, weight, out):
    width = out.shape[1]
    band_rows, channels = out.shape[0], out.shape[2]
    grid = jnp.concatenate(
        [above[band_rows - 1 : band_rows], window[...], below[:1]], axis=0
    ).astype(F32)
    active = jnp.maximum(grid, 0.0)
    total = grid[1 : 1 + band_rows, EDGE : EDGE + width, :].reshape(band_rows * width, channels)
    for column in range(3):
        first = EDGE - 1 + column
        shifted = active[:, first : first + width, :].astype(BF16)
        for row in range(3):
            rows = shifted[row : row + band_rows].reshape(band_rows * width, channels)
            total = total + dot(rows, weight[row, column])
    out[...] = total.reshape(out.shape).astype(BF16)


def body(left_tokens, right_tokens, self_qkv, self_out, cross_qkv, cross_out, reassemble, taps):
    bands, tiles, cores = (lax.axis_size(axis) for axis in ("blk", "tile", "pair"))
    span = bands // cores
    both = ("blk", "pair")
    rows, share = left_tokens.shape[1:]
    columns = self_qkv.shape[2]
    channels = reassemble.shape[1]
    width = GRID_W // tiles
    band_rows = rows // GRID_W
    heads = columns // HD
    window = (band_rows, width + 2 * EDGE, channels)
    board = (band_rows, GRID_W + 2 * EDGE, channels)

    def home(band, pair):
        return band * cores + pair

    def worker(band, pair):
        part, index = divmod(band, span)
        if part == pair:
            return band * cores + pair
        shift = (pair - part) % cores
        return (pair * span + span - 1 - index) * cores + (pair - shift) % cores

    places = [(band, pair) for band in range(bands) for pair in range(cores)]
    there = [(home(*p), worker(*p)) for p in places]
    back = [(worker(*p), home(*p)) for p in places]
    down = [(worker(b, p), home(b + 1, p)) for b, p in places if b + 1 < bands]
    up = [(worker(b, p), home(b - 1, p)) for b, p in places if b > 0]

    def fetched(value, step):
        def flat(position, tile):
            return (position // cores * tiles + tile) * cores + position % cores

        pairs = [(flat(s, (i + step) % tiles), flat(d, i)) for s, d in there for i in range(tiles)]
        return lax.ppermute(value, ("blk", "tile", "pair"), pairs)

    def tied(values, *others):
        return lax.optimization_barrier((values, others))[0]

    def from_tile(value, step):
        return lax.ppermute(value, "tile", [((i + step) % tiles, i) for i in range(tiles)])

    def tile_pieces(own):
        return [own, *[from_tile(own, s) for s in range(1, tiles)]]

    def neighbours(pack):
        ring = [(g * span, i) for g in range(cores) for i in range(span)]
        return [
            lax.ppermute(pack, "blk", [(g + (i + s) % span, g + i) for g, i in ring])
            for s in range(1, span)
        ]

    def across(pack):
        return [
            lax.ppermute(pack, "pair", [((i + s) % cores, i) for i in range(cores)])
            for s in range(1, cores)
        ]

    def grouped(packs):
        return packs if len(packs) < 5 else [jnp.concatenate(packs)]

    def project(pieces, weights, scaled, first):
        return run_kernel(
            functools.partial(project_kernel, count=tiles, scaled=scaled, first=first),
            "project",
            [((rows, columns), BF16)] * scaled + [((rows, 2 * columns), BF16)],
            [*pieces, weights.reshape(3, tiles, share, columns)],
        )

    def begin(query, packs):
        shapes = [((heads, rows, 2 * HD), F32), ((heads, rows, 1), F32)]
        return run_kernel(begin_kernel, "begin", shapes, [query, *grouped(packs)])

    def staged(weights):
        blocks = weights[0].shape[1] // channels
        height = (weights[0].shape[0] + share // blocks) // cores
        return run_kernel(
            functools.partial(stage_kernel, cores=cores),
            "stage",
            [(w.shape, BF16) for w in weights] + [((height, weights[0].shape[1]), BF16)],
            [pltpu.with_memory_space_constraint(w, pltpu.HBM) for w in weights],
            [pltpu.SemaphoreType.DMA((len(weights) + 1 + blocks,))],
            pl.BlockSpec(memory_space=pl.ANY),
        )

    steps = range(1, tiles)
    left = [fetched(left_tokens[0], step) for step in reversed(range(tiles))][::-1]
    left[0] = tied(left[0], left[1:])
    self_out, reassemble, cross_out, right_own, self_qkv, cross_qkv, taps, half = staged(
        [self_out, reassemble, cross_out, right_tokens[0], self_qkv, cross_qkv, taps]
    )
    right = [right_own, *[from_tile(tied(right_tokens[0], half), s) for s in steps]]
    query, pack = project(left, self_qkv, True, 0)
    (right_pack,) = project(tied(right, pack), cross_qkv, False, 1)
    beside = neighbours(pack)
    near = [pack, *beside, *across(pack)]
    far = [q for p in beside for q in across(p)]
    state = begin(query, near)
    halves = tile_pieces(tied(half, right_pack))[1:]
    right_pack = lax.ppermute(right_pack, both, there)
    others = [
        run_kernel(
            unpack_kernel,
            "unpack",
            [(w.shape, BF16) for w in (self_out, reassemble)],
            [half, *across(half)],
        )
        for half in halves
    ]
    map_weights = [reassemble, *[other[1] for other in others]]
    (composed,) = run_kernel(
        compose_kernel, "compose", [((columns, channels), BF16)], [cross_out, *map_weights]
    )
    right_pack = tied(right_pack, state, composed)
    far, others, composed, map_weights, right_pack = lax.optimization_barrier(
        (far, others, composed, map_weights, right_pack)
    )
    (mixed,) = run_kernel(
        end_kernel, "end", [((rows, columns), BF16)], [query, *grouped(far), *state]
    )
    right_near = [right_pack, *neighbours(right_pack)]
    mixed = tile_pieces(mixed)
    right_near = tied(right_near, mixed)
    right_far = [q for p in right_near for q in across(p)]
    updated, cross_query = run_kernel(
        functools.partial(update_kernel, count=tiles),
        "update",
        [((tiles, rows, share), BF16), ((rows, columns), BF16)],
        [
            *mixed,
            self_out,
            *[other[0] for other in others],
            *left,
            cross_qkv.reshape(3, tiles, share, columns),
        ],
    )
    maps = run_kernel(
        functools.partial(end_map_kernel, count=tiles),
        "end_map",
        [(window, BF16)] * tiles,
        [cross_query, *grouped([*right_near, *right_far]), composed],
        [pltpu.VMEM(board, F32)],
    )
    (carried,) = run_kernel(
        carry_kernel,
        "carry",
        [(window, F32)],
        [tied(updated, maps), *map_weights],
        [pltpu.VMEM(board, F32)],
    )
    received = [from_tile(part, s) for s, part in enumerate(maps) if s > 0]
    longer = (window[0] + 1, *window[1:])
    features, raised = run_kernel(
        add_kernel, "add", [(window, BF16), (longer, BF16)], [carried, maps[0], *received]
    )
    below = lax.ppermute(raised, both, up)
    above = lax.ppermute(raised, both, down)
    features = lax.ppermute(features, both, back)
    (joined,) = run_kernel(
        conv_kernel,
        "join",
        [((band_rows, width, channels), BF16)],
        [features, above, below, taps],
    )
    return joined[None]


def solution(mesh):
    placed = (
        P(("groups", "pair"), "blk", "tile"),
        P(("groups", "pair"), "blk", "tile"),
        P(None, None, "tile"),
        P("tile", None),
        P(None, None, "tile"),
        P("tile", None),
        P("tile", None),
        P(),
    )
    return jax.shard_map(
        body,
        mesh=mesh,
        in_specs=placed,
        out_specs=P(("groups", "pair"), "blk", "tile", None),
        check_vma=False,
    )
```
